32 devices in a mesh: dp: 2 (over x), lat: 4 (over y, core), lon: 4 (over z).
Axes of the slice: x: 2, y: 2, z: 4, core: 2. Of those that a mesh axis runs over, the one named last changes fastest.
Arguments:
- inputs: bfloat16 [2, 128, 64, 1024], P('dp', 'lat', 'lon'), may hold values from -40 to 40
- grad_out: bfloat16 [2, 128, 64, 1024], P('dp', 'lat', 'lon'), may hold values from -6 to 6
- w_qkv: bfloat16 [1024, 3072], replicated, may hold values from -0.1875 to 0.1875
Outputs:
- grad_inputs: bfloat16 [2, 128, 64, 1024], P('dp', 'lat', 'lon')
- grad_w_qkv: float32 [1024, 3072], P(('dp', 'lat', 'lon'))
The draws below stay inside these ranges and needn't reach their ends.
All inputs are finite; a program needn't handle non-finite values.
Results may differ from the reference program's by a relative error of at most 0.011.
Values may be sent and summed in bfloat16 or wider, within the bound.
No kernel may reach another device: no remote copies, remote signals or barrier semaphores. Data moves between devices by JAX's collectives and lax.ppermute only.
A program may use at most 192 MiB of HBM per device.

```python
import jax
import jax.numpy as jnp
from jax import lax

D = 1024
HEADS = 16
WIN = 13
LAT_DEV = 32
LON_DEV = 16
TILE_R = 8
TILE_C = 16
GROUP = 4
SAMPLES = 2
ROWS = 128
COLS = 64
TOKENS = 16384
N_LAT = 4
N_LON = 4
DEVICES = 32


def draw_inputs(key, part):
    base_key = jax.random.fold_in(key, 11)
    noise_key, pair_key = jax.random.split(base_key, 2)
    noise_field = jnp.clip(jax.random.normal(noise_key, (SAMPLES, ROWS, COLS, D), jnp.float32), -5.0, 5.0)
    sample_ids = jnp.arange(SAMPLES, dtype=jnp.int32)[:, None, None]
    band_ids = (jnp.arange(ROWS, dtype=jnp.int32) // LAT_DEV)[None, :, None]
    column_ids = (jnp.arange(COLS, dtype=jnp.int32) // LON_DEV)[None, None, :]
    owner_ids = (sample_ids * N_LAT + band_ids) * N_LON + column_ids
    pairing = jax.random.permutation(pair_key, DEVICES).astype(jnp.int32)
    target = pairing[owner_ids]
    feature_block = jnp.arange(D, dtype=jnp.int32) // (D // DEVICES)
    factor = jnp.where(target[..., None] == feature_block, 4.0, 1.0)
    values = noise_field * factor
    return values.astype(jnp.bfloat16)


def level_of(key, extent, cuts, least, high):
    gain, own = 1.0, jax.random.fold_in(key, 6)
    for position, blocks in cuts:
        heights = jnp.exp(jax.random.uniform(jax.random.fold_in(own, position), (blocks,), jnp.float32, least / len(cuts), high / len(cuts)))
        gain = gain * jnp.repeat(heights, extent[position] // blocks).reshape([-1 if axis == position else 1 for axis in range(len(extent))])
    return gain


def noise(key, dims, deviation, limit, cuts=(), held_as=jnp.bfloat16):
    entries = deviation * jax.random.normal(key, dims, jnp.float32)
    if cuts:
        entries = entries * level_of(key, dims, cuts, -0.22, 0.18)
    return jnp.clip(entries, -limit, limit).astype(held_as)


def setup_inputs(seed: int = 0) -> dict:
    seeds = jax.random.split(jax.random.key(seed), 4)
    inputs = draw_inputs(jax.random.fold_in(seeds[3], 71), 0)
    grad_out = noise(seeds[1], (SAMPLES, ROWS, COLS, D), 1.0, 6.0, ((0, 2), (1, 4), (2, 4)))
    w_qkv = noise(seeds[2], (D, 3 * D), D ** -0.5, 0.1875)
    return dict(inputs=inputs, grad_out=grad_out, w_qkv=w_qkv)


def tile_layout(row_tile, band_start, band_rows, total_rows):
    margin = WIN // 2
    first_row = band_start + row_tile * TILE_R
    window_top = jnp.clip(first_row - margin, 0, total_rows - WIN)
    region_top = jnp.minimum(window_top - band_start + margin, band_rows - TILE_R)
    query_rows = first_row + jnp.arange(TILE_R, dtype=jnp.int32)
    key_rows = region_top + band_start - margin + jnp.arange(TILE_R + WIN - 1, dtype=jnp.int32)
    return region_top, query_rows, key_rows


def window_mask(query_rows, key_rows, total_rows):
    margin = WIN // 2
    starts = jnp.clip(query_rows - margin, 0, total_rows - WIN)
    row_inside = (key_rows[:, None] >= starts[None, :]) & (key_rows[:, None] <= starts[None, :] + WIN - 1)
    query_cols = jnp.arange(TILE_C, dtype=jnp.int32)
    key_cols = jnp.arange(TILE_C + WIN - 1, dtype=jnp.int32)
    col_inside = (key_cols[:, None] >= query_cols[None, :]) & (key_cols[:, None] <= query_cols[None, :] + WIN - 1)
    inside = row_inside[:, None, :, None] & col_inside[None, :, None, :]
    return inside.reshape((TILE_R + WIN - 1) * (TILE_C + WIN - 1), TILE_R * TILE_C)


def rounded(tensor):
    narrow = lax.optimization_barrier(tensor.astype(jnp.bfloat16))
    return narrow.astype(jnp.float32)


def tile_grads(query_tile, grad_tile, region, inside):
    query_count, width = query_tile.shape
    key_count = region.shape[0]
    head_width = width // HEADS
    norm_scale = head_width ** -0.5
    head_queries = query_tile.astype(jnp.float32).reshape(query_count, HEADS, head_width)
    head_grads = grad_tile.astype(jnp.float32).reshape(query_count, HEADS, head_width)
    head_keys = region[:, :width].astype(jnp.float32).reshape(key_count, HEADS, head_width)
    head_values = region[:, width:].astype(jnp.float32).reshape(key_count, HEADS, head_width)
    scores = jnp.einsum('khd,ihd->hki', head_keys, head_queries) * norm_scale
    scores = jnp.where(inside[None], scores, -1e30)
    maxima = jnp.max(scores, axis=1, keepdims=True)
    exponent = jnp.exp(scores - maxima)
    attn_weights = exponent / jnp.sum(exponent, axis=1, keepdims=True)
    attn_rounded = rounded(attn_weights)
    value_dots = jnp.einsum('khd,ihd->hki', head_values, head_grads)
    delta_terms = jnp.sum(attn_weights * value_dots, axis=1, keepdims=True)
    score_grads = rounded(attn_weights * (value_dots - delta_terms))
    query_grad = jnp.einsum('hki,khd->ihd', score_grads, head_keys) * norm_scale
    key_grad = jnp.einsum('hki,ihd->khd', score_grads, head_queries) * norm_scale
    value_grad = jnp.einsum('hki,ihd->khd', attn_rounded, head_grads)
    region_grad = jnp.concatenate([key_grad.reshape(key_count, width), value_grad.reshape(key_count, width)], axis=1)
    return query_grad.reshape(query_count, width), region_grad


def run_tiles(queries, grad_out, key_values, band_start, total_rows):
    samples, band_rows, band_cols, width = queries.shape
    region_rows = TILE_R + WIN - 1
    region_cols = TILE_C + WIN - 1
    row_tiles = band_rows // TILE_R
    col_tiles = band_cols // TILE_C
    tile_count = samples * row_tiles * col_tiles
    anchor = jnp.zeros((), jnp.int32)

    def one_tile(tile_index):
        sample = tile_index // (row_tiles * col_tiles)
        row_tile = (tile_index // col_tiles) % row_tiles
        col_tile = tile_index % col_tiles
        region_top, query_rows, key_rows = tile_layout(row_tile, band_start, band_rows, total_rows)
        first_col = col_tile * TILE_C
        query_tile = lax.dynamic_slice(queries, (sample, row_tile * TILE_R, first_col, anchor), (1, TILE_R, TILE_C, width)).reshape(TILE_R * TILE_C, width)
        grad_tile = lax.dynamic_slice(grad_out, (sample, row_tile * TILE_R, first_col, anchor), (1, TILE_R, TILE_C, width)).reshape(TILE_R * TILE_C, width)
        region = lax.dynamic_slice(key_values, (sample, region_top, first_col, anchor), (1, region_rows, region_cols, 2 * width)).reshape(region_rows * region_cols, 2 * width)
        query_grad, region_grad = tile_grads(query_tile, grad_tile, region, window_mask(query_rows, key_rows, total_rows))
        return query_grad, region_grad, sample, region_top, first_col

    def group_step(totals, group_index):
        tile_ids = group_index * GROUP + jnp.arange(GROUP, dtype=jnp.int32)
        query_grads, region_grads, sample_ids, region_tops, region_lefts = jax.vmap(one_tile)(tile_ids)
        for member in range(GROUP):
            corner = (sample_ids[member], region_tops[member], region_lefts[member], anchor)
            current = lax.dynamic_slice(totals, corner, (1, region_rows, region_cols, 2 * width))
            totals = lax.dynamic_update_slice(totals, current + region_grads[member].reshape(1, region_rows, region_cols, 2 * width), corner)
        return totals, query_grads

    initial = jnp.zeros((samples, band_rows + WIN - 1, band_cols + WIN - 1, 2 * width), jnp.float32)
    totals, query_grads = lax.scan(group_step, initial, jnp.arange(tile_count // GROUP, dtype=jnp.int32))
    query_grads = query_grads.reshape(samples, row_tiles, col_tiles, TILE_R, TILE_C, width)
    query_grads = query_grads.transpose(0, 1, 3, 2, 4, 5).reshape(samples, band_rows, band_cols, width)
    return query_grads, totals


def reference(inputs, grad_out, w_qkv):
    samples, total_rows, total_cols, width = inputs.shape
    margin = WIN // 2
    flat_inputs = inputs.reshape(-1, width)
    projected = jnp.dot(flat_inputs, w_qkv, preferred_element_type=jnp.float32).astype(jnp.bfloat16)
    projected = projected.reshape(samples, total_rows, total_cols, 3 * width)
    queries = projected[..., :width]
    key_values = projected[..., width:]
    key_values = jnp.concatenate([key_values[:, :, total_cols - margin:], key_values, key_values[:, :, :margin]], axis=2)
    zero_rows = jnp.zeros((samples, margin, total_cols + 2 * margin, 2 * width), key_values.dtype)
    key_values = jnp.concatenate([zero_rows, key_values, zero_rows], axis=1)
    band_start = jnp.zeros((), jnp.int32)
    query_grads, totals = run_tiles(queries, grad_out, key_values, band_start, total_rows)
    totals = totals[:, margin:total_rows + margin]
    interior = totals[:, :, margin:total_cols + margin]
    interior = interior.at[:, :, :margin].add(totals[:, :, total_cols + margin:])
    interior = interior.at[:, :, total_cols - margin:].add(totals[:, :, :margin])
    grad_proj = jnp.concatenate([query_grads.astype(jnp.bfloat16), interior.astype(jnp.bfloat16)], axis=-1).reshape(-1, 3 * width)
    grad_inputs = jnp.dot(grad_proj, w_qkv.T, preferred_element_type=jnp.float32).astype(jnp.bfloat16)
    grad_inputs = grad_inputs.reshape(inputs.shape)
    grad_w_qkv = jnp.dot(flat_inputs.T, grad_proj, preferred_element_type=jnp.float32) * (float(TOKENS) ** -0.5)
    return grad_inputs, grad_w_qkv
```

```python
import functools

import jax
import jax.numpy as jnp
from jax import lax
from jax.experimental import pallas as pl
from jax.experimental.pallas import tpu as pltpu
from jax.sharding import PartitionSpec as P

HEADS = 16
WIN = 13
MARGIN = WIN // 2
TILE_R = 4
GROUP = 4
KEY_COLS = 32
REGION_R = 16
NEG = -1e30

NT = (((1,), (1,)), ((), ()))
TN = (((0,), (0,)), ((), ()))
NN = (((1,), (0,)), ((), ()))


def dot(a, b, dims):
    return lax.dot_general(a, b, dims, preferred_element_type=jnp.float32)


def region_top(tile, band_start, band_rows, total_rows):
    lowest = jnp.where(band_start == 0, TILE_R, 0)
    highest = jnp.where(band_start + band_rows == total_rows, band_rows - 2 * TILE_R, band_rows)
    return jnp.clip(tile * TILE_R, lowest, highest)


def attention_kernel(
    band_rows, band_cols, total_rows, head_width,
    start_ref, region_ref, own_ref, grad_ref, wq_ref, wk_ref, wv_ref,
    dq_ref, top_ref, mid_ref, bottom_ref,
    mask_ref, q_ref, k_ref, v_ref, dk_ref, dv_ref,
):
    band_start = start_ref[0]
    tiles = band_rows // TILE_R
    queries = TILE_R * band_cols
    keys = REGION_R * KEY_COLS
    width = GROUP * head_width
    lanes = GROUP * queries

    @pl.when(pl.program_id(0) == 0)
    def _():
        def build(tile, carry):
            first = region_top(tile, band_start, band_rows, total_rows)
            key = lax.broadcasted_iota(jnp.int32, (keys, 2 * queries), 0)
            query = lax.broadcasted_iota(jnp.int32, (keys, 2 * queries), 1) % queries
            key_row = band_start - MARGIN + first + key // KEY_COLS
            place = key % KEY_COLS
            query_row = band_start + tile * TILE_R + query // band_cols
            query_col = query % band_cols
            window = jnp.clip(query_row - MARGIN, 0, total_rows - WIN)
            row_inside = (key_row >= window) & (key_row < window + WIN)
            key_col = jnp.where(
                place < band_cols,
                place,
                jnp.where(place < band_cols + MARGIN, place - band_cols - MARGIN, place - MARGIN),
            )
            col_inside = (jnp.abs(key_col - query_col) <= MARGIN) & (
                place < band_cols + 2 * MARGIN
            )
            mask_ref[tile] = jnp.where(row_inside & col_inside, 0.0, NEG)
            return carry

        lax.fori_loop(0, tiles, build, 0)

    q_ref[...] = (
        dot(own_ref[...], wq_ref[...], NN).astype(jnp.bfloat16) * jnp.bfloat16(head_width**-0.5)
    )
    k_ref[...] = dot(region_ref[...], wk_ref[...], NN).astype(jnp.bfloat16)
    v_ref[...] = dot(region_ref[...], wv_ref[...], NN).astype(jnp.bfloat16)
    dk_ref[...] = jnp.zeros_like(dk_ref)
    dv_ref[...] = jnp.zeros_like(dv_ref)

    def spread(rows):
        block = jnp.concatenate([rows] * GROUP, axis=0)
        head_row = lax.broadcasted_iota(jnp.int32, (lanes, width), 0) // queries
        head_col = lax.broadcasted_iota(jnp.int32, (lanes, width), 1) // head_width
        return jnp.where(head_row == head_col, block, jnp.zeros_like(block))

    def one_tile(tile, carry):
        first = region_top(tile, band_start, band_rows, total_rows)
        region = pl.ds(pl.multiple_of(first * KEY_COLS, TILE_R * KEY_COLS), keys)
        mine = pl.ds(pl.multiple_of(tile * queries, queries), queries)
        q_wide = spread(q_ref[mine, :])
        g_wide = spread(grad_ref[mine, :])
        mask = mask_ref[tile]
        scores = dot(k_ref[region, :], q_wide, NT) + jnp.concatenate([mask, mask], axis=1)
        dots = dot(v_ref[region, :], g_wide, NT)
        exponent = jnp.exp(scores - jnp.max(scores, axis=0, keepdims=True))
        inverse = 1.0 / jnp.sum(exponent, axis=0, keepdims=True)
        attn = exponent * inverse
        delta = jnp.sum(attn * dots, axis=0, keepdims=True)
        dscore = (attn * (dots - delta)).astype(jnp.bfloat16)
        dv_ref[region, :] += dot(attn.astype(jnp.bfloat16), g_wide, NN)
        dk_ref[region, :] += dot(dscore, q_wide, NN)
        dq_wide = dot(dscore, k_ref[region, :], TN)
        head_col = lax.broadcasted_iota(jnp.int32, (queries, width), 1) // head_width
        dq = jnp.zeros((queries, width), jnp.float32)
        for head in range(GROUP):
            dq = jnp.where(head_col == head, dq_wide[head * queries : (head + 1) * queries], dq)
        dq_ref[mine, :] = (dq * head_width**-0.5).astype(jnp.bfloat16)
        return carry

    lax.fori_loop(0, tiles, one_tile, 0)

    edge = MARGIN * KEY_COLS
    inner = band_rows * KEY_COLS
    for part, total in enumerate((dk_ref, dv_ref)):
        top_ref[part] = total[:edge, :].astype(jnp.bfloat16)
        mid_ref[part] = total[edge : edge + inner, :].astype(jnp.bfloat16)
        bottom_ref[part] = total[edge + inner :, :].astype(jnp.bfloat16)


def attention_grads(region, own, grad_out, w_qkv, band_start, band_rows, band_cols, total_rows):
    tokens, width = own.shape
    head_width = width // HEADS
    block = GROUP * head_width
    groups = HEADS // GROUP
    edge = MARGIN * KEY_COLS
    inner = band_rows * KEY_COLS
    region_tokens = inner + 2 * edge
    tiles = band_rows // TILE_R
    queries = TILE_R * band_cols
    keys = REGION_R * KEY_COLS
    whole = lambda g: (0, 0)
    return pl.pallas_call(
        functools.partial(attention_kernel, band_rows, band_cols, total_rows, head_width),
        grid=(groups,),
        in_specs=[
            pl.BlockSpec(memory_space=pltpu.SMEM),
            pl.BlockSpec((region_tokens, width), whole),
            pl.BlockSpec((tokens, width), whole),
            pl.BlockSpec((tokens, block), lambda g: (0, g)),
            pl.BlockSpec((width, block), lambda g: (0, g)),
            pl.BlockSpec((width, block), lambda g: (0, groups + g)),
            pl.BlockSpec((width, block), lambda g: (0, 2 * groups + g)),
        ],
        out_specs=[
            pl.BlockSpec((tokens, block), lambda g: (0, g)),
            pl.BlockSpec((2, edge, block), lambda g: (0, 0, g)),
            pl.BlockSpec((2, inner, block), lambda g: (0, 0, g)),
            pl.BlockSpec((2, edge, block), lambda g: (0, 0, g)),
        ],
        out_shape=[
            jax.ShapeDtypeStruct((tokens, width), jnp.bfloat16),
            jax.ShapeDtypeStruct((2, edge, width), jnp.bfloat16),
            jax.ShapeDtypeStruct((2, inner, width), jnp.bfloat16),
            jax.ShapeDtypeStruct((2, edge, width), jnp.bfloat16),
        ],
        scratch_shapes=[
            pltpu.VMEM((tiles, keys, 2 * queries), jnp.float32),
            pltpu.VMEM((tokens, block), jnp.bfloat16),
            pltpu.VMEM((region_tokens, block), jnp.bfloat16),
            pltpu.VMEM((region_tokens, block), jnp.bfloat16),
            pltpu.VMEM((region_tokens, block), jnp.float32),
            pltpu.VMEM((region_tokens, block), jnp.float32),
        ],
        compiler_params=pltpu.CompilerParams(
            dimension_semantics=("arbitrary",), vmem_limit_bytes=50 * 1024 * 1024
        ),
    )(band_start.reshape(1), region, own, grad_out, w_qkv, w_qkv, w_qkv)


def shifted(array, axis, by, wrap):
    size = lax.axis_size(axis)
    route = [(i, (i + by) % size) for i in range(size) if wrap or 0 <= i + by < size]
    return lax.ppermute(array, axis, route)


def body(inputs, grad_out, w_qkv):
    _, band_rows, band_cols, width = inputs.shape
    lat_count = lax.axis_size("lat")
    devices_all = lat_count * lax.axis_size("lon") * lax.axis_size("dp")
    band_start = lax.axis_index("lat") * band_rows
    total_rows = band_rows * lat_count
    tokens = band_rows * band_cols
    own = inputs.reshape(band_rows, band_cols, width)
    flat_inputs = inputs.reshape(tokens, width)

    left = shifted(own[:, band_cols - MARGIN :], "lon", 1, True)
    right = shifted(own[:, :MARGIN], "lon", -1, True)
    pad = jnp.zeros((band_rows, KEY_COLS - band_cols - 2 * MARGIN, width), own.dtype)
    middle = jnp.concatenate([own, left, right, pad], axis=1)
    above = shifted(middle[band_rows - MARGIN :], "lat", 1, False)
    below = shifted(middle[:MARGIN], "lat", -1, False)
    region = jnp.concatenate([above, middle, below], axis=0)
    region = region.reshape(-1, width)

    dq, top, mid, bottom = attention_grads(
        region, flat_inputs, grad_out.reshape(tokens, width), w_qkv,
        band_start, band_rows, band_cols, total_rows,
    )
    from_below = shifted(top, "lat", -1, False)
    from_above = shifted(bottom, "lat", 1, False)
    edge = MARGIN * KEY_COLS
    mid = mid.astype(jnp.float32)
    mid = mid.at[:, :edge].add(from_above.astype(jnp.float32))
    mid = mid.at[:, mid.shape[1] - edge :].add(from_below.astype(jnp.float32))
    mid = mid.reshape(2, band_rows, KEY_COLS, width)
    to_left = mid[:, :, band_cols : band_cols + MARGIN].astype(jnp.bfloat16)
    to_right = mid[:, :, band_cols + MARGIN : band_cols + 2 * MARGIN].astype(jnp.bfloat16)
    from_right = shifted(to_left, "lon", -1, True)
    from_left = shifted(to_right, "lon", 1, True)
    mid = mid[:, :, :band_cols]
    mid = mid.at[:, :, :MARGIN].add(from_left.astype(jnp.float32))
    mid = mid.at[:, :, band_cols - MARGIN :].add(from_right.astype(jnp.float32))
    dkv = mid.astype(jnp.bfloat16).reshape(2, tokens, width)
    grad_proj = jnp.concatenate([dq, dkv[0], dkv[1]], axis=-1)
    grad_inputs = dot(grad_proj, w_qkv, NT).astype(jnp.bfloat16).reshape(inputs.shape)
    grad_scale = float(tokens * devices_all) ** -0.5
    grad_w = (dot(flat_inputs, grad_proj, TN) * grad_scale).astype(jnp.bfloat16)
    grad_w = lax.psum_scatter(grad_w, ("dp", "lat", "lon"), scatter_dimension=0, tiled=True)
    return (grad_inputs, grad_w.astype(jnp.float32))


def solution(mesh):
    in_specs = (P("dp", "lat", "lon", None), P("dp", "lat", "lon", None), P())
    out_specs = (P("dp", "lat", "lon", None), P(("dp", "lat", "lon"), None))
    return jax.shard_map(body, mesh=mesh, in_specs=in_specs, out_specs=out_specs, check_vma=False)
```

```python
import functools

import jax
import jax.numpy as jnp
import numpy as np
from jax import lax
from jax.experimental import pallas as pl
from jax.experimental.pallas import tpu as pltpu
from jax.sharding import PartitionSpec as P

HEADS = 16
WIN = 13
MARGIN = WIN // 2
TILE_R = 4
GROUP = 4
KEY_COLS = 32
HALO_COLS = 16
REGION_R = 16
PAD_R = 2
EDGE_R = MARGIN + PAD_R
NEG = -1e30
BF = jnp.bfloat16
F32 = jnp.float32
MIB = 1024 * 1024
LANES = 128

NT = (((1,), (1,)), ((), ()))
TN = (((0,), (0,)), ((), ()))
NN = (((1,), (0,)), ((), ()))


def dot(a, b, dims=NN):
    return lax.dot_general(a, b, dims, preferred_element_type=F32)


def region_top(tile, band_start, band_rows, total_rows):
    lowest = jnp.where(band_start == 0, TILE_R, 0)
    highest = jnp.where(band_start + band_rows == total_rows, band_rows - 2 * TILE_R, band_rows)
    return jnp.clip(tile * TILE_R, lowest, highest)


def mask_kernel(band_rows, band_cols, total_rows, start_ref, mask_ref):
    band_start = start_ref[0]
    tile = pl.program_id(0)
    shape = mask_ref.shape[1:]
    first = region_top(tile, band_start, band_rows, total_rows)
    key = lax.broadcasted_iota(jnp.int32, shape, 0)
    query = lax.broadcasted_iota(jnp.int32, shape, 1) % (TILE_R * band_cols)
    key_row = band_start - MARGIN + first + key // KEY_COLS
    place = key % KEY_COLS
    query_row = band_start + tile * TILE_R + query // band_cols
    query_col = query % band_cols
    window = jnp.clip(query_row - MARGIN, 0, total_rows - WIN)
    row_inside = (key_row >= window) & (key_row < window + WIN)
    key_col = jnp.where(
        place < band_cols,
        place,
        jnp.where(place < band_cols + MARGIN, place - band_cols - MARGIN, place - MARGIN),
    )
    col_inside = (jnp.abs(key_col - query_col) <= MARGIN) & (place < band_cols + 2 * MARGIN)
    mask_ref[0] = jnp.where(row_inside & col_inside, 0.0, NEG).astype(BF)


def window_masks(start, band_rows, band_cols, total_rows):
    tiles = band_rows // TILE_R
    shape = (REGION_R * KEY_COLS, 2 * TILE_R * band_cols)
    return pl.pallas_call(
        functools.partial(mask_kernel, band_rows, band_cols, total_rows),
        grid=(tiles,),
        in_specs=[pl.BlockSpec(memory_space=pltpu.SMEM)],
        out_specs=pl.BlockSpec((1,) + shape, lambda t: (t, 0, 0)),
        out_shape=jax.ShapeDtypeStruct((tiles,) + shape, BF),
        cost_estimate=pl.CostEstimate(flops=10**7, bytes_accessed=2**21, transcendentals=0),
    )(start)


def attention_kernel(band_rows, band_cols, total_rows, head_width, aliased, *refs):
    (start_ref, mask_ref, left_ref, right_ref, above_ref, below_ref, cl_ref, cr_ref,
     oq_ref, ok_ref, ov_ref, grad_ref, wk_ref, wv_ref) = refs[:14]
    (dq_ref, top_ref, bottom_ref, mid_ref, to_left_ref, to_right_ref,
     halo_ref, spot_ref, q_ref, k_ref, v_ref, dk_ref, dv_ref) = refs[14 + aliased :]
    band_start = start_ref[0]
    tiles = band_rows // TILE_R
    queries = TILE_R * band_cols
    keys = REGION_R * KEY_COLS
    width = GROUP * head_width
    lanes = GROUP * queries
    region_rows = band_rows + 2 * MARGIN
    side = MARGIN * band_rows
    edge = MARGIN * band_cols
    corner = 2 * MARGIN * MARGIN
    at_above = 2 * side
    at_below = at_above + edge
    at_cl = at_below + edge
    at_cr = at_cl + -(-corner // 16) * 16
    halves = [(i, slice(i * LANES, (i + 1) * LANES)) for i in range(width // LANES)]

    @pl.when(pl.program_id(0) == 0)
    def _():
        halo_ref[:side] = left_ref[...]
        halo_ref[side:at_above] = right_ref[...]
        halo_ref[at_above:at_below] = above_ref[...]
        halo_ref[at_below:at_cl] = below_ref[...]
        halo_ref[at_cl : at_cl + corner] = cl_ref[...]
        halo_ref[at_cr : at_cr + corner] = cr_ref[...]
        spot_ref[...] = jnp.zeros_like(spot_ref)

    def place(target, own, weights):
        fresh = dot(halo_ref[...], weights)
        for col in range(MARGIN):
            start = MARGIN * HALO_COLS + col
            for part, at in halves:
                spot_ref[part, pl.ds(start, band_rows, stride=HALO_COLS), :] = fresh[
                    col * band_rows : (col + 1) * band_rows, at
                ]
                spot_ref[part, pl.ds(start + MARGIN, band_rows, stride=HALO_COLS), :] = fresh[
                    side + col * band_rows : side + (col + 1) * band_rows, at
                ]
        for row in range(2 * MARGIN):
            spot = (row if row < MARGIN else row + band_rows) * HALO_COLS
            for part, at in halves:
                spot_ref[part, spot : spot + MARGIN, :] = fresh[
                    at_cl + row * MARGIN : at_cl + (row + 1) * MARGIN, at
                ]
                spot_ref[part, spot + MARGIN : spot + 2 * MARGIN, :] = fresh[
                    at_cr + row * MARGIN : at_cr + (row + 1) * MARGIN, at
                ]
        for row in range(region_rows):
            base = row * KEY_COLS
            inner = row - MARGIN
            if inner < 0:
                ours = fresh[at_above + row * band_cols : at_above + (row + 1) * band_cols].astype(BF)
            elif inner < band_rows:
                ours = own[inner * band_cols : (inner + 1) * band_cols, :]
            else:
                past = at_below + (inner - band_rows) * band_cols
                ours = fresh[past : past + band_cols].astype(BF)
            target[base : base + band_cols, :] = ours
            for part, at in halves:
                target[base + band_cols : base + KEY_COLS, at] = spot_ref[
                    part, row * HALO_COLS : (row + 1) * HALO_COLS, :
                ].astype(BF)

    place(k_ref, ok_ref, wk_ref[...])
    place(v_ref, ov_ref, wv_ref[...])
    q_ref[...] = oq_ref[...] * BF(head_width**-0.5)
    dk_ref[...] = jnp.zeros_like(dk_ref)
    dv_ref[...] = jnp.zeros_like(dv_ref)

    def spread(rows):
        block = jnp.concatenate([rows] * GROUP, axis=0)
        head_row = lax.broadcasted_iota(jnp.int32, (lanes, width), 0) // queries
        head_col = lax.broadcasted_iota(jnp.int32, (lanes, width), 1) // head_width
        return jnp.where(head_row == head_col, block, jnp.zeros_like(block))

    def one_tile(tile, carry):
        first = region_top(tile, band_start, band_rows, total_rows)
        region = pl.ds(pl.multiple_of(first * KEY_COLS, TILE_R * KEY_COLS), keys)
        total = pl.ds(pl.multiple_of((first + PAD_R) * KEY_COLS, PAD_R * KEY_COLS), keys)
        mine = pl.ds(pl.multiple_of(tile * queries, queries), queries)
        q_wide = spread(q_ref[mine, :])
        g_wide = spread(grad_ref[mine, :])
        mask = mask_ref[tile].astype(F32)
        scores = dot(k_ref[region, :], q_wide, NT) + jnp.concatenate([mask, mask], axis=1)
        dots = dot(v_ref[region, :], g_wide, NT)
        exponent = jnp.exp(scores - jnp.max(scores, axis=0, keepdims=True))
        inverse = 1.0 / jnp.sum(exponent, axis=0, keepdims=True)
        attn = exponent * inverse
        delta = jnp.sum(attn * dots, axis=0, keepdims=True)
        dscore = (attn * (dots - delta)).astype(BF)
        dv = dot(attn.astype(BF), g_wide)
        dk = dot(dscore, q_wide)
        for part, at in halves:
            dv_ref[part, total, :] += dv[:, at]
            dk_ref[part, total, :] += dk[:, at]
        dq_wide = dot(dscore, k_ref[region, :], TN)
        head_col = lax.broadcasted_iota(jnp.int32, (queries, width), 1) // head_width
        dq = jnp.zeros((queries, width), F32)
        for head in range(GROUP):
            dq = jnp.where(head_col == head, dq_wide[head * queries : (head + 1) * queries], dq)
        dq_ref[mine, :] = (dq * head_width**-0.5).astype(BF)
        return carry

    lax.fori_loop(0, tiles, one_tile, 0)

    middle = (PAD_R + MARGIN) * KEY_COLS
    below = (PAD_R + MARGIN + band_rows) * KEY_COLS
    for part, acc in enumerate((dk_ref, dv_ref)):
        for lane, at in halves:
            for row in range(MARGIN):
                here = slice(row * band_cols, (row + 1) * band_cols)
                for start, out in ((PAD_R * KEY_COLS, top_ref), (below, bottom_ref)):
                    start = start + row * KEY_COLS
                    out[part, here, at] = acc[lane, start : start + band_cols, :].astype(BF)
            for pair in range(MARGIN):
                here = slice(edge + pair * 2 * EDGE_R, edge + (pair + 1) * 2 * EDGE_R)
                for start, out in ((0, top_ref), (below, bottom_ref)):
                    start = start + band_cols + 2 * pair
                    out[part, here, at] = jnp.concatenate(
                        [
                            acc[lane, pl.ds(start, EDGE_R, stride=KEY_COLS), :],
                            acc[lane, pl.ds(start + 1, EDGE_R, stride=KEY_COLS), :],
                        ],
                        axis=0,
                    ).astype(BF)
            for row in range(band_rows):
                base = middle + row * KEY_COLS
                mid_ref[part, row * band_cols : (row + 1) * band_cols, at] = acc[
                    lane, base : base + band_cols, :
                ].astype(BF)
            for col in range(MARGIN):
                here = slice(col * band_rows, (col + 1) * band_rows)
                start = middle + band_cols + col
                to_left_ref[part, here, at] = acc[
                    lane, pl.ds(start, band_rows, stride=KEY_COLS), :
                ].astype(BF)
                to_right_ref[part, here, at] = acc[
                    lane, pl.ds(start + MARGIN, band_rows, stride=KEY_COLS), :
                ].astype(BF)


def attention_grads(first, count, slots, start, masks, halo, qkv, grad_out, w_qkv, shape, before):
    band_rows, band_cols, total_rows = shape
    tokens, width = grad_out.shape
    head_width = width // HEADS
    block = GROUP * head_width
    groups = HEADS // GROUP
    region_tokens = (band_rows + 2 * MARGIN) * KEY_COLS
    total_tokens = (band_rows + 2 * MARGIN + 2 * PAD_R) * KEY_COLS
    side = MARGIN * band_rows
    edge = MARGIN * (band_cols + 2 * EDGE_R)
    corner = -(-2 * MARGIN * MARGIN // 16) * 16
    halo_tokens = 2 * (side + MARGIN * band_cols + corner)
    whole = lambda g: (0, 0)
    column = lambda offset: (lambda g: (0, offset + first + g))
    slot = lambda g: (0, 0, first % slots + g)
    halves = [(2, edge), (2, edge), (2, tokens), (2, side), (2, side)]
    out_shape = [jax.ShapeDtypeStruct((tokens, width), BF)] + [
        jax.ShapeDtypeStruct(s + (slots * block,), BF) for s in halves
    ]
    aliases = {}
    if before:
        aliases = {14 + i: place for i, (place, _) in enumerate(before)}
    return pl.pallas_call(
        functools.partial(
            attention_kernel, band_rows, band_cols, total_rows, head_width, len(before)
        ),
        grid=(count,),
        in_specs=[
            pl.BlockSpec(memory_space=pltpu.SMEM),
            pl.BlockSpec(masks.shape, lambda g: (0, 0, 0)),
        ]
        + [pl.BlockSpec(piece.shape, whole) for piece in halo]
        + [
            pl.BlockSpec((tokens, block), column(0)),
            pl.BlockSpec((tokens, block), column(groups)),
            pl.BlockSpec((tokens, block), column(2 * groups)),
            pl.BlockSpec((tokens, block), column(0)),
            pl.BlockSpec((width, block), column(groups)),
            pl.BlockSpec((width, block), column(2 * groups)),
        ]
        + [pl.BlockSpec(memory_space=pl.ANY)] * len(before),
        out_specs=[pl.BlockSpec((tokens, block), column(0))]
        + [pl.BlockSpec(s + (block,), slot) for s in halves],
        out_shape=out_shape,
        input_output_aliases=aliases,
        scratch_shapes=[
            pltpu.VMEM((halo_tokens, width), BF),
            pltpu.VMEM((block // LANES, (band_rows + 2 * MARGIN) * HALO_COLS, LANES), F32),
            pltpu.VMEM((tokens, block), BF),
            pltpu.VMEM((region_tokens, block), BF),
            pltpu.VMEM((region_tokens, block), BF),
            pltpu.VMEM((block // LANES, total_tokens, LANES), F32),
            pltpu.VMEM((block // LANES, total_tokens, LANES), F32),
        ],
        compiler_params=pltpu.CompilerParams(
            dimension_semantics=("arbitrary",), vmem_limit_bytes=44 * MIB
        ),
        cost_estimate=pl.CostEstimate(
            flops=count * 9 * 10**9, bytes_accessed=count * 8 * MIB, transcendentals=count * 10**6
        ),
    )(start, masks, *halo, qkv, qkv, qkv, grad_out, w_qkv, w_qkv, *[a for _, a in before])


def merge_kernel(band_rows, edge, left_ref, right_ref, above_ref, below_ref, ol_ref, or_ref):
    for part in range(2):
        for col in range(2 * MARGIN):
            source, target = (left_ref, ol_ref) if col < MARGIN else (right_ref, or_ref)
            base = (col % MARGIN) * band_rows
            pair = slice(edge + (col // 2) * 2 * EDGE_R, edge + (col // 2 + 1) * 2 * EDGE_R)
            odd = slice((col % 2) * EDGE_R, (col % 2 + 1) * EDGE_R)
            rows = source[part, base : base + band_rows, :].astype(F32)
            first = rows[:EDGE_R] + above_ref[part, pair, :].astype(F32)[odd]
            last = rows[band_rows - EDGE_R :] + below_ref[part, pair, :].astype(F32)[odd]
            target[part, base : base + band_rows, :] = jnp.concatenate(
                [first, rows[EDGE_R : band_rows - EDGE_R], last], axis=0
            ).astype(BF)


def merge_sides(left, right, above, below, band_rows, band_cols, block):
    width = left.shape[2]
    spec = lambda a: pl.BlockSpec((2, a.shape[1], block), lambda g: (0, 0, g))
    return pl.pallas_call(
        functools.partial(merge_kernel, band_rows, MARGIN * band_cols),
        grid=(width // block,),
        in_specs=[spec(left), spec(right), spec(above), spec(below)],
        out_specs=[spec(left), spec(right)],
        out_shape=[jax.ShapeDtypeStruct(left.shape, BF), jax.ShapeDtypeStruct(right.shape, BF)],
        cost_estimate=pl.CostEstimate(flops=10**6, bytes_accessed=4 * MIB, transcendentals=0),
    )(left, right, above, below)


def finish_kernel(band_rows, band_cols, own_ref, above_ref, below_ref, left_ref, right_ref, out_ref, acc_ref):
    edge = MARGIN * band_cols
    tokens = band_rows * band_cols
    for lane in range(acc_ref.shape[0]):
        at = slice(lane * LANES, (lane + 1) * LANES)
        acc_ref[lane] = own_ref[0, :, at].astype(F32)
        acc_ref[lane, :edge, :] += above_ref[0, :edge, at].astype(F32)
        acc_ref[lane, tokens - edge :, :] += below_ref[0, :edge, at].astype(F32)
        for col in range(MARGIN):
            here = slice(col * band_rows, (col + 1) * band_rows)
            first = pl.ds(col, band_rows, stride=band_cols)
            last = pl.ds(band_cols - MARGIN + col, band_rows, stride=band_cols)
            acc_ref[lane, first, :] += left_ref[0, here, at].astype(F32)
            acc_ref[lane, last, :] += right_ref[0, here, at].astype(F32)
        out_ref[:, at] = acc_ref[lane].astype(BF)


def finish(own, above, below, left, right, band_rows, band_cols, block):
    _, tokens, width = own.shape
    count = width // block
    spec = lambda a: pl.BlockSpec((1, a.shape[1], block), lambda p, g: (p, 0, g))
    return pl.pallas_call(
        functools.partial(finish_kernel, band_rows, band_cols),
        grid=(2, count),
        in_specs=[spec(a) for a in (own, above, below, left, right)],
        out_specs=pl.BlockSpec((tokens, block), lambda p, g: (0, p * count + g)),
        out_shape=jax.ShapeDtypeStruct((tokens, 2 * width), BF),
        scratch_shapes=[pltpu.VMEM((block // LANES, tokens, LANES), F32)],
        cost_estimate=pl.CostEstimate(flops=10**6, bytes_accessed=4 * MIB, transcendentals=0),
    )(own, above, below, left, right)


def shifted(array, axis, by, wrap):
    size = lax.axis_size(axis)
    route = [(i, (i + by) % size) for i in range(size) if wrap or 0 <= i + by < size]
    return lax.ppermute(array, axis, route)


def exchanged(array, axis, flip):
    return lax.ppermute(array, axis, [(i, i ^ flip) for i in range(lax.axis_size(axis))])


def bits_of(axis):
    return [(axis, 1 << b) for b in range((lax.axis_size(axis) - 1).bit_length())]


def feature_order(stages):
    n_lon, n_lat = lax.axis_size("lon"), lax.axis_size("lat")
    unit = {"lon": 1, "lat": n_lon, "dp": n_lon * n_lat}
    order = np.arange(n_lon)
    for axis, bit in reversed(stages):
        order = np.concatenate([order, order + unit[axis] * bit])
    return order.astype(np.int32)


def reduce_rows(rows, columns, stages, scale):
    half = rows.shape[0] // 2
    send = (dot(rows[half:], columns) * scale).astype(BF)
    keep = dot(rows[:half], columns) * scale
    axis, bit = stages[0]
    total = keep + exchanged(send, axis, bit).astype(F32)
    for axis, bit in stages[1:]:
        half = total.shape[0] // 2
        total = total[:half] + exchanged(total[half:].astype(BF), axis, bit).astype(F32)
    n_lon = lax.axis_size("lon")
    block = total.shape[0] // n_lon
    result = total[:block]
    for flip in range(1, n_lon):
        part = total[flip * block : (flip + 1) * block].astype(BF)
        result = result + exchanged(part, "lon", flip).astype(F32)
    return result


def body(inputs, grad_out, w_qkv):
    _, band_rows, band_cols, width = inputs.shape
    n_lat, n_lon, n_dp = lax.axis_size("lat"), lax.axis_size("lon"), lax.axis_size("dp")
    band_start = lax.axis_index("lat") * band_rows
    total_rows = band_rows * n_lat
    tokens = band_rows * band_cols
    block = GROUP * (width // HEADS)
    slots = HEADS // GROUP // 2
    shape = (band_rows, band_cols, total_rows)
    own = inputs.reshape(band_rows, band_cols, width)
    flat_inputs = inputs.reshape(tokens, width)
    flat_grad = grad_out.reshape(tokens, width)

    side = MARGIN * band_rows
    swap = lambda a: a.transpose(1, 0, 2).reshape(side, width)
    above = shifted(own[band_rows - MARGIN :], "lat", 1, False)
    below = shifted(own[:MARGIN], "lat", -1, False)
    left = shifted(swap(own[:, band_cols - MARGIN :]), "lon", 1, True)
    right = shifted(swap(own[:, :MARGIN]), "lon", -1, True)
    corner = 2 * MARGIN * MARGIN
    rims = jnp.stack([above, below])
    corner_left = shifted(rims[:, :, band_cols - MARGIN :].reshape(corner, width), "lon", 1, True)
    corner_right = shifted(rims[:, :, :MARGIN].reshape(corner, width), "lon", -1, True)
    above, below = above.reshape(-1, width), below.reshape(-1, width)
    halo = (left, right, above, below, corner_left, corner_right)

    start = band_start.reshape(1)
    masks = window_masks(start, band_rows, band_cols, total_rows)
    qkv = dot(flat_inputs, w_qkv).astype(BF)
    lat_bits = bits_of("lat")
    x_first = lat_bits[:1] + bits_of("dp") + lat_bits[1:]
    y_first = lat_bits + bits_of("dp")
    me = (lax.axis_index("dp") * n_lat + lax.axis_index("lat")) * n_lon + lax.axis_index("lon")
    blocks = flat_inputs.T.reshape(n_dp * n_lat * n_lon, -1, tokens)
    rows_x = blocks[me ^ feature_order(x_first)].reshape(width, tokens)
    rows_y = blocks[me ^ feature_order(y_first)].reshape(width, tokens)
    scale = float(tokens * n_dp * n_lat * n_lon) ** -0.5

    attend = lambda first, count, before: attention_grads(
        first, count, slots, start, masks, halo, qkv, flat_grad, w_qkv, shape, before
    )
    one = attend(0, slots, [])
    two = attend(slots, 1, [(0, one[0])])
    two = attend(slots + 1, 1, list(enumerate(two)))
    dq = two[0]

    pieces = []
    for _, top, bottom, mid, to_left, to_right in (one, two):
        from_below = shifted(top, "lat", -1, False)
        from_above = shifted(bottom, "lat", 1, False)
        to_left, to_right = merge_sides(
            to_left, to_right, from_above, from_below, band_rows, band_cols, block
        )
        from_right = shifted(to_left, "lon", -1, True)
        from_left = shifted(to_right, "lon", 1, True)
        pieces.append(
            finish(mid, from_above, from_below, from_left, from_right, band_rows, band_cols, block)
        )

    half = slots * block
    gw_q = reduce_rows(rows_x, dq, x_first, scale)
    gw_1 = reduce_rows(rows_y, pieces[0], y_first, scale)
    gw_2 = reduce_rows(rows_x, pieces[1], x_first, scale)
    grad_w = jnp.concatenate(
        [gw_q, gw_1[:, :half], gw_2[:, :half], gw_1[:, half:], gw_2[:, half:]], axis=1
    )
    grad_proj = jnp.concatenate(
        [dq, pieces[0][:, :half], pieces[1][:, :half], pieces[0][:, half:], pieces[1][:, half:]],
        axis=1,
    )
    grad_inputs = dot(grad_proj, w_qkv, NT).astype(BF).reshape(inputs.shape)
    return (grad_inputs, grad_w)


def solution(mesh):
    in_specs = (P("dp", "lat", "lon", None), P("dp", "lat", "lon", None), P())
    out_specs = (P("dp", "lat", "lon", None), P(("dp", "lat", "lon"), None))
    return jax.shard_map(body, mesh=mesh, in_specs=in_specs, out_specs=out_specs, check_vma=False)
```

```python
import functools

import jax
import jax.numpy as jnp
import numpy as np
from jax import lax
from jax.experimental import pallas as pl
from jax.experimental.pallas import tpu as pltpu
from jax.sharding import PartitionSpec as P

HEADS = 16
WIN = 13
MARGIN = WIN // 2
TILE_R = 4
GROUP = 4
KEY_COLS = 32
HALO_COLS = 16
REGION_R = 16
PAD_R = 2
EDGE_R = MARGIN + PAD_R
NEG = -1e30
BF = jnp.bfloat16
F32 = jnp.float32
MIB = 1024 * 1024
FINISH_FLOPS = 6 * 10**9
LANES = 128

NT = (((1,), (1,)), ((), ()))
TN = (((0,), (0,)), ((), ()))
NN = (((1,), (0,)), ((), ()))


def dot(a, b, dims=NN):
    return lax.dot_general(a, b, dims, preferred_element_type=F32)


def region_top(tile, band_start, band_rows, total_rows):
    lowest = jnp.where(band_start == 0, TILE_R, 0)
    highest = jnp.where(band_start + band_rows == total_rows, band_rows - 2 * TILE_R, band_rows)
    return jnp.clip(tile * TILE_R, lowest, highest)


def mask_kernel(band_rows, band_cols, total_rows, start_ref, mask_ref):
    band_start = start_ref[0]
    tile = pl.program_id(0)
    shape = mask_ref.shape[1:]
    first = region_top(tile, band_start, band_rows, total_rows)
    key = lax.broadcasted_iota(jnp.int32, shape, 0)
    query = lax.broadcasted_iota(jnp.int32, shape, 1) % (TILE_R * band_cols)
    key_row = band_start - MARGIN + first + key // KEY_COLS
    place = key % KEY_COLS
    query_row = band_start + tile * TILE_R + query // band_cols
    query_col = query % band_cols
    window = jnp.clip(query_row - MARGIN, 0, total_rows - WIN)
    row_inside = (key_row >= window) & (key_row < window + WIN)
    key_col = jnp.where(
        place < band_cols,
        place,
        jnp.where(place < band_cols + MARGIN, place - band_cols - MARGIN, place - MARGIN),
    )
    col_inside = (jnp.abs(key_col - query_col) <= MARGIN) & (place < band_cols + 2 * MARGIN)
    mask_ref[0] = jnp.where(row_inside & col_inside, 0.0, NEG).astype(BF)


def window_masks(start, band_rows, band_cols, total_rows):
    tiles = band_rows // TILE_R
    shape = (REGION_R * KEY_COLS, 2 * TILE_R * band_cols)
    return pl.pallas_call(
        functools.partial(mask_kernel, band_rows, band_cols, total_rows),
        grid=(tiles,),
        in_specs=[pl.BlockSpec(memory_space=pltpu.SMEM)],
        out_specs=pl.BlockSpec((1,) + shape, lambda t: (t, 0, 0)),
        out_shape=jax.ShapeDtypeStruct((tiles,) + shape, BF),
        cost_estimate=pl.CostEstimate(flops=10**7, bytes_accessed=2**21, transcendentals=0),
    )(start)


def attention_kernel(band_rows, band_cols, total_rows, head_width, extra, *refs):
    (start_ref, mask_ref, left_ref, right_ref, above_ref, below_ref, cl_ref, cr_ref,
     oq_ref, ok_ref, ov_ref, grad_ref, wk_ref, wv_ref) = refs[:14]
    (dq_ref, top_ref, bottom_ref, mid_ref, to_left_ref, to_right_ref,
     halo_ref, spot_ref, q_ref, k_ref, v_ref, dk_ref, dv_ref) = refs[14 + extra :]
    band_start = start_ref[0]
    tiles = band_rows // TILE_R
    queries = TILE_R * band_cols
    keys = REGION_R * KEY_COLS
    width = GROUP * head_width
    lanes = GROUP * queries
    region_rows = band_rows + 2 * MARGIN
    side = MARGIN * band_rows
    edge = MARGIN * band_cols
    corner = 2 * MARGIN * EDGE_R
    at_above = 2 * side
    at_below = at_above + edge
    at_cl = at_below + edge
    at_cr = at_cl + corner
    halves = [(i, slice(i * LANES, (i + 1) * LANES)) for i in range(width // LANES)]

    @pl.when(pl.program_id(0) == 0)
    def _():
        halo_ref[:side] = left_ref[...]
        halo_ref[side:at_above] = right_ref[...]
        halo_ref[at_above:at_below] = above_ref[...]
        halo_ref[at_below:at_cl] = below_ref[...]
        halo_ref[at_cl : at_cl + corner] = cl_ref[...]
        halo_ref[at_cr : at_cr + corner] = cr_ref[...]
        spot_ref[...] = jnp.zeros_like(spot_ref)

    def place(target, own, weights):
        fresh = dot(halo_ref[...], weights)
        for col in range(MARGIN):
            start = MARGIN * HALO_COLS + col
            for part, at in halves:
                spot_ref[part, pl.ds(start, band_rows, stride=HALO_COLS), :] = fresh[
                    col * band_rows : (col + 1) * band_rows, at
                ]
                spot_ref[part, pl.ds(start + MARGIN, band_rows, stride=HALO_COLS), :] = fresh[
                    side + col * band_rows : side + (col + 1) * band_rows, at
                ]
        for corner_at, offset in ((at_cl, 0), (at_cr, MARGIN)):
            for rim in range(2):
                first = rim * (MARGIN + band_rows) * HALO_COLS + offset
                for col in range(MARGIN):
                    base = corner_at + (rim * MARGIN + col) * EDGE_R
                    for part, at in halves:
                        spot_ref[part, pl.ds(first + col, MARGIN, stride=HALO_COLS), :] = fresh[
                            base : base + MARGIN, at
                        ]
        for row in range(region_rows):
            base = row * KEY_COLS
            inner = row - MARGIN
            if inner < 0:
                ours = fresh[at_above + row * band_cols : at_above + (row + 1) * band_cols].astype(BF)
            elif inner < band_rows:
                ours = own[inner * band_cols : (inner + 1) * band_cols, :]
            else:
                past = at_below + (inner - band_rows) * band_cols
                ours = fresh[past : past + band_cols].astype(BF)
            target[base : base + band_cols, :] = ours
            for part, at in halves:
                target[base + band_cols : base + KEY_COLS, at] = spot_ref[
                    part, row * HALO_COLS : (row + 1) * HALO_COLS, :
                ].astype(BF)

    place(k_ref, ok_ref, wk_ref[...])
    place(v_ref, ov_ref, wv_ref[...])
    q_ref[...] = oq_ref[...] * BF(head_width**-0.5)
    dk_ref[...] = jnp.zeros_like(dk_ref)
    dv_ref[...] = jnp.zeros_like(dv_ref)

    def spread(rows):
        block = jnp.concatenate([rows] * GROUP, axis=0)
        head_row = lax.broadcasted_iota(jnp.int32, (lanes, width), 0) // queries
        head_col = lax.broadcasted_iota(jnp.int32, (lanes, width), 1) // head_width
        return jnp.where(head_row == head_col, block, jnp.zeros_like(block))

    def one_tile(tile, carry):
        first = region_top(tile, band_start, band_rows, total_rows)
        region = pl.ds(pl.multiple_of(first * KEY_COLS, TILE_R * KEY_COLS), keys)
        total = pl.ds(pl.multiple_of((first + PAD_R) * KEY_COLS, PAD_R * KEY_COLS), keys)
        mine = pl.ds(pl.multiple_of(tile * queries, queries), queries)
        q_wide = spread(q_ref[mine, :])
        g_wide = spread(grad_ref[mine, :])
        mask = mask_ref[tile].astype(F32)
        scores = dot(k_ref[region, :], q_wide, NT) + jnp.concatenate([mask, mask], axis=1)
        dots = dot(v_ref[region, :], g_wide, NT)
        exponent = jnp.exp(scores - jnp.max(scores, axis=0, keepdims=True))
        inverse = 1.0 / jnp.sum(exponent, axis=0, keepdims=True)
        delta = jnp.sum(exponent * dots, axis=0, keepdims=True) * inverse
        attn = exponent * inverse
        dscore = (attn * (dots - delta)).astype(BF)
        dv = dot(attn.astype(BF), g_wide)
        dk = dot(dscore, q_wide)
        for part, at in halves:
            dv_ref[part, total, :] += dv[:, at]
            dk_ref[part, total, :] += dk[:, at]
        dq_wide = dot(dscore, k_ref[region, :], TN)
        head_col = lax.broadcasted_iota(jnp.int32, (queries, width), 1) // head_width
        dq = jnp.zeros((queries, width), F32)
        for head in range(GROUP):
            dq = jnp.where(head_col == head, dq_wide[head * queries : (head + 1) * queries], dq)
        dq_ref[mine, :] = (dq * head_width**-0.5).astype(BF)
        return carry

    lax.fori_loop(0, tiles, one_tile, 0, unroll=2)

    middle = (PAD_R + MARGIN) * KEY_COLS
    below = (PAD_R + MARGIN + band_rows) * KEY_COLS
    for part, acc in enumerate((dk_ref, dv_ref)):
        for lane, at in halves:
            for row in range(MARGIN):
                here = slice(row * band_cols, (row + 1) * band_cols)
                for start, out in ((PAD_R * KEY_COLS, top_ref), (below, bottom_ref)):
                    start = start + row * KEY_COLS
                    out[part, here, at] = acc[lane, start : start + band_cols, :].astype(BF)
            for pair in range(MARGIN):
                here = slice(edge + pair * 2 * EDGE_R, edge + (pair + 1) * 2 * EDGE_R)
                for start, out in ((0, top_ref), (below, bottom_ref)):
                    start = start + band_cols + 2 * pair
                    out[part, here, at] = jnp.concatenate(
                        [
                            acc[lane, pl.ds(start, EDGE_R, stride=KEY_COLS), :],
                            acc[lane, pl.ds(start + 1, EDGE_R, stride=KEY_COLS), :],
                        ],
                        axis=0,
                    ).astype(BF)
            for row in range(band_rows):
                base = middle + row * KEY_COLS
                mid_ref[part, row * band_cols : (row + 1) * band_cols, at] = acc[
                    lane, base : base + band_cols, :
                ].astype(BF)
            for col in range(MARGIN):
                here = slice(col * band_rows, (col + 1) * band_rows)
                start = middle + band_cols + col
                to_left_ref[part, here, at] = acc[
                    lane, pl.ds(start, band_rows, stride=KEY_COLS), :
                ].astype(BF)
                to_right_ref[part, here, at] = acc[
                    lane, pl.ds(start + MARGIN, band_rows, stride=KEY_COLS), :
                ].astype(BF)


def attention_grads(
    first, count, slots, start, masks, halo, qkv, grad_out, w_qkv, shape, before, after
):
    band_rows, band_cols, total_rows = shape
    tokens, width = grad_out.shape
    head_width = width // HEADS
    block = GROUP * head_width
    groups = HEADS // GROUP
    region_tokens = (band_rows + 2 * MARGIN) * KEY_COLS
    total_tokens = (band_rows + 2 * MARGIN + 2 * PAD_R) * KEY_COLS
    side = MARGIN * band_rows
    edge = MARGIN * (band_cols + 2 * EDGE_R)
    corner = 2 * MARGIN * EDGE_R
    halo_tokens = 2 * (side + MARGIN * band_cols + corner)
    whole = lambda g: (0, 0)
    column = lambda offset: (lambda g: (0, offset + first + g))
    slot = lambda g: (0, 0, first % slots + g)
    halves = [(2, edge), (2, edge), (2, tokens), (2, side), (2, side)]
    out_shape = [jax.ShapeDtypeStruct((tokens, width), BF)] + [
        jax.ShapeDtypeStruct(s + (slots * block,), BF) for s in halves
    ]
    aliases = {}
    if before:
        aliases = {14 + i: place for i, (place, _) in enumerate(before)}
    return pl.pallas_call(
        functools.partial(
            attention_kernel, band_rows, band_cols, total_rows, head_width, len(before) + len(after)
        ),
        grid=(count,),
        in_specs=[
            pl.BlockSpec(memory_space=pltpu.SMEM),
            pl.BlockSpec(masks.shape, lambda g: (0, 0, 0)),
        ]
        + [pl.BlockSpec(piece.shape, whole) for piece in halo]
        + [
            pl.BlockSpec((tokens, block), column(0)),
            pl.BlockSpec((tokens, block), column(groups)),
            pl.BlockSpec((tokens, block), column(2 * groups)),
            pl.BlockSpec((tokens, block), column(0)),
            pl.BlockSpec((width, block), column(groups)),
            pl.BlockSpec((width, block), column(2 * groups)),
        ]
        + [pl.BlockSpec(memory_space=pl.ANY)] * (len(before) + len(after)),
        out_specs=[pl.BlockSpec((tokens, block), column(0))]
        + [pl.BlockSpec(s + (block,), slot) for s in halves],
        out_shape=out_shape,
        input_output_aliases=aliases,
        scratch_shapes=[
            pltpu.VMEM((halo_tokens, width), BF),
            pltpu.VMEM((block // LANES, (band_rows + 2 * MARGIN) * HALO_COLS, LANES), F32),
            pltpu.VMEM((tokens, block), BF),
            pltpu.VMEM((region_tokens, block), BF),
            pltpu.VMEM((region_tokens, block), BF),
            pltpu.VMEM((block // LANES, total_tokens, LANES), F32),
            pltpu.VMEM((block // LANES, total_tokens, LANES), F32),
        ],
        compiler_params=pltpu.CompilerParams(
            dimension_semantics=("arbitrary",), vmem_limit_bytes=30 * MIB
        ),
        cost_estimate=pl.CostEstimate(
            flops=count * 14 * 10**9, bytes_accessed=count * 8 * MIB, transcendentals=count * 10**6
        ),
    )(start, masks, *halo, qkv, qkv, qkv, grad_out, w_qkv, w_qkv, *[a for _, a in before], *after)


def on_chip(kernel, out_shape, operands, after=(), scratch=(), flops=10**5):
    count = len(operands)

    def run(*refs):
        kernel(*refs[:count], *refs[count + len(after) :])

    return pl.pallas_call(
        run,
        in_specs=[pl.BlockSpec(memory_space=pltpu.VMEM)] * count
        + [pl.BlockSpec(memory_space=pl.ANY)] * len(after),
        out_specs=[pl.BlockSpec(memory_space=pltpu.VMEM)] * len(out_shape),
        out_shape=[jax.ShapeDtypeStruct(s, d) for s, d in out_shape],
        scratch_shapes=list(scratch),
        compiler_params=pltpu.CompilerParams(vmem_limit_bytes=24 * MIB),
        cost_estimate=pl.CostEstimate(flops=flops, bytes_accessed=10**4, transcendentals=0),
    )(*operands, *after)


def lanes_of(width):
    return [(i, slice(i * LANES, (i + 1) * LANES)) for i in range(width // LANES)]


def pack_sides(own, band_rows, band_cols):
    tokens, width = own.shape

    def kernel(own_ref, last_ref, first_ref, wide_ref):
        for lane, at in lanes_of(width):
            wide_ref[lane] = own_ref[:, at].astype(F32)
            for col in range(MARGIN):
                here = slice(col * band_rows, (col + 1) * band_rows)
                last = pl.ds(band_cols - MARGIN + col, band_rows, stride=band_cols)
                last_ref[here, at] = wide_ref[lane, last, :].astype(BF)
                first = pl.ds(col, band_rows, stride=band_cols)
                first_ref[here, at] = wide_ref[lane, first, :].astype(BF)

    out = ((MARGIN * band_rows, width), BF)
    scratch = [pltpu.VMEM((width // LANES, tokens, LANES), F32)]
    return on_chip(kernel, [out, out], [own], scratch=scratch)


def pack_rows(own, band_cols, after):
    tokens, width = own.shape
    edge = MARGIN * band_cols

    def kernel(own_ref, last_ref, first_ref):
        last_ref[...] = own_ref[tokens - edge :, :]
        first_ref[...] = own_ref[:edge, :]

    out = ((edge, width), BF)
    return on_chip(kernel, [out, out], [own], after=after)


def pack_corners(above, below, band_cols):
    edge, width = above.shape

    def kernel(above_ref, below_ref, last_ref, first_ref, wide_ref):
        wide_ref[:, edge:, :] = jnp.zeros_like(wide_ref[:, edge:, :])
        for rim, rim_ref in enumerate((above_ref, below_ref)):
            for lane, at in lanes_of(width):
                wide_ref[lane, :edge, :] = rim_ref[:, at].astype(F32)
                for out_ref, offset in ((last_ref, band_cols - MARGIN), (first_ref, 0)):
                    for col in range(0, MARGIN, 2):
                        base = (rim * MARGIN + col) * EDGE_R
                        pair = [
                            wide_ref[lane, pl.ds(offset + c, EDGE_R, stride=band_cols), :]
                            for c in (col, col + 1)
                        ]
                        out_ref[base : base + 2 * EDGE_R, at] = jnp.concatenate(pair).astype(BF)

    out = ((2 * MARGIN * EDGE_R, width), BF)
    scratch = [pltpu.VMEM((width // LANES, EDGE_R * band_cols, LANES), F32)]
    return on_chip(kernel, [out, out], [above, below], scratch=scratch)


def merge_sides(left, right, above, below, band_rows, band_cols, after=()):
    edge = MARGIN * band_cols

    def kernel(left_ref, right_ref, above_ref, below_ref, ol_ref, or_ref):
        for part in range(2):
            for col in range(2 * MARGIN):
                source, target = (left_ref, ol_ref) if col < MARGIN else (right_ref, or_ref)
                base = (col % MARGIN) * band_rows
                pair = slice(edge + (col // 2) * 2 * EDGE_R, edge + (col // 2 + 1) * 2 * EDGE_R)
                odd = slice((col % 2) * EDGE_R, (col % 2 + 1) * EDGE_R)
                rows = source[part, base : base + band_rows, :].astype(F32)
                first = rows[:EDGE_R] + above_ref[part, pair, :].astype(F32)[odd]
                last = rows[band_rows - EDGE_R :] + below_ref[part, pair, :].astype(F32)[odd]
                target[part, base : base + band_rows, :] = jnp.concatenate(
                    [first, rows[EDGE_R : band_rows - EDGE_R], last], axis=0
                ).astype(BF)

    out = [(left.shape, BF), (right.shape, BF)]
    return on_chip(kernel, out, [left, right, above, below], after=after)


def finish(mid, above, below, left, right, band_rows, band_cols, after, flops):
    _, tokens, width = mid.shape
    edge = MARGIN * band_cols

    def kernel(mid_ref, above_ref, below_ref, left_ref, right_ref, out_ref, acc_ref):
        for part in range(2):
            for block in range(width // (2 * LANES)):
                for lane in range(2):
                    at = slice((2 * block + lane) * LANES, (2 * block + lane + 1) * LANES)
                    acc_ref[lane] = mid_ref[part, :, at].astype(F32)
                    acc_ref[lane, :edge, :] += above_ref[part, :edge, at].astype(F32)
                    acc_ref[lane, tokens - edge :, :] += below_ref[part, :edge, at].astype(F32)
                    for col in range(MARGIN):
                        here = slice(col * band_rows, (col + 1) * band_rows)
                        first = pl.ds(col, band_rows, stride=band_cols)
                        last = pl.ds(band_cols - MARGIN + col, band_rows, stride=band_cols)
                        acc_ref[lane, first, :] += left_ref[part, here, at].astype(F32)
                        acc_ref[lane, last, :] += right_ref[part, here, at].astype(F32)
                both = jnp.concatenate([acc_ref[0], acc_ref[1]], axis=1).astype(BF)
                start = part * width + block * 2 * LANES
                out_ref[:, start : start + 2 * LANES] = both

    out = [((tokens, 2 * width), BF)]
    scratch = [pltpu.VMEM((2, tokens, LANES), F32)]
    operands = [mid, above, below, left, right]
    return on_chip(kernel, out, operands, after, scratch, flops)[0]


def grad_rows(rows, columns, scale, kind, after=()):
    features, width = rows.shape[0], columns.shape[1]

    def kernel(rows_ref, columns_ref, out_ref):
        for start in range(0, width, 2 * LANES):
            here = slice(start, start + 2 * LANES)
            out_ref[:, here] = (dot(rows_ref[...], columns_ref[:, here]) * scale).astype(kind)

    return on_chip(kernel, [((features, width), kind)], [rows, columns], after)[0]


def add_split(keep, received, after=()):
    half, columns = keep.shape[0] // 2, keep.shape[1]
    part = columns // len(received)

    def kernel(keep_ref, *refs):
        sums = refs[len(received)]
        for i, received_ref in enumerate(refs[: len(received)]):
            at = slice(i * part, (i + 1) * part)
            sums[:, at] = keep_ref[:half, at] + received_ref[:half, :].astype(F32)
            refs[len(received) + 1 + i][...] = (
                keep_ref[half:, at] + received_ref[half:, :].astype(F32)
            ).astype(BF)

    out = [((half, columns), F32)] + [((half, part), BF)] * len(received)
    keep, *send = on_chip(kernel, out, [keep, *received], after=after)
    return keep, send


def add_blocks(keep, received, blocks):
    rows, columns = keep.shape
    part = columns // len(received)
    size = rows // blocks

    def kernel(keep_ref, *refs):
        sums, *send = refs[len(received) :]
        for i, received_ref in enumerate(refs[: len(received)]):
            at = slice(i * part, (i + 1) * part)
            total = keep_ref[:, at] + received_ref[...].astype(F32)
            sums[:, at] = total[:size]
            for b in range(1, blocks):
                send[b - 1][:, at] = total[b * size : (b + 1) * size].astype(BF)

    out = [((size, columns), F32)] + [((size, columns), BF)] * (blocks - 1)
    keep, *send = on_chip(kernel, out, [keep, *received])
    return keep, send


def gather_sums(groups, places, width):
    flat = [a for group in groups for a in group]

    def kernel(*refs):
        out_ref = refs[-1]
        at = 0
        for group, moves in zip(groups, places):
            total = refs[at][...]
            for ref in refs[at + 1 : at + len(group)]:
                total = total + ref[...].astype(F32)
            at += len(group)
            for source, size, target in moves:
                out_ref[:, target : target + size] = total[:, source : source + size]

    return on_chip(kernel, [((flat[0].shape[0], width), F32)], flat)[0]


def shifted(array, axis, by, wrap):
    size = lax.axis_size(axis)
    route = [(i, (i + by) % size) for i in range(size) if wrap or 0 <= i + by < size]
    return lax.ppermute(array, axis, route)


def exchanged(array, axis, flip):
    return lax.ppermute(array, axis, [(i, i ^ flip) for i in range(lax.axis_size(axis))])


def bits_of(axis):
    return [(axis, 1 << b) for b in range((lax.axis_size(axis) - 1).bit_length())]


def feature_order(stages):
    n_lon, n_lat = lax.axis_size("lon"), lax.axis_size("lat")
    unit = {"lon": 1, "lat": n_lon, "dp": n_lon * n_lat}
    order = np.arange(n_lon)
    for axis, bit in reversed(stages):
        order = np.concatenate([order, order + unit[axis] * bit])
    return order.astype(np.int32)


def body(inputs, grad_out, w_qkv):
    _, band_rows, band_cols, width = inputs.shape
    n_lat, n_lon, n_dp = lax.axis_size("lat"), lax.axis_size("lon"), lax.axis_size("dp")
    band_start = lax.axis_index("lat") * band_rows
    total_rows = band_rows * n_lat
    tokens = band_rows * band_cols
    slots = HEADS // GROUP // 2
    shape = (band_rows, band_cols, total_rows)
    own = inputs.reshape(tokens, width)
    flat_grad = grad_out.reshape(tokens, width)

    last_cols, first_cols = pack_sides(own, band_rows, band_cols)
    left = shifted(last_cols, "lon", 1, True)
    right = shifted(first_cols, "lon", -1, True)
    last_rows, first_rows = pack_rows(own, band_cols, [last_cols])
    above = shifted(last_rows, "lat", 1, False)
    below = shifted(first_rows, "lat", -1, False)
    last_corners, first_corners = pack_corners(above, below, band_cols)
    corner_left = shifted(last_corners, "lon", 1, True)
    corner_right = shifted(first_corners, "lon", -1, True)
    halo = (left, right, above, below, corner_left, corner_right)

    start = band_start.reshape(1)
    masks = window_masks(start, band_rows, band_cols, total_rows)
    qkv = dot(own, w_qkv).astype(BF)
    lat_bits = bits_of("lat")
    x_first = lat_bits[:1] + bits_of("dp") + lat_bits[1:]
    y_first = lat_bits + bits_of("dp")
    me = (lax.axis_index("dp") * n_lat + lax.axis_index("lat")) * n_lon + lax.axis_index("lon")
    blocks = own.T.reshape(n_dp * n_lat * n_lon, -1, tokens)
    rows_x = blocks[me ^ feature_order(x_first)].reshape(width, tokens)
    rows_y = blocks[me ^ feature_order(y_first)].reshape(width, tokens)
    half = width // 2
    rows_x, rows_y = ((r[:half], r[half:]) for r in (rows_x, rows_y))
    scale = float(tokens * n_dp * n_lat * n_lon) ** -0.5

    attend = lambda first, count, before, after: attention_grads(
        first, count, slots, start, masks, halo, qkv, flat_grad, w_qkv, shape, before, after
    )

    def return_rows(grads):
        from_below = shifted(grads[1], "lat", -1, False)
        from_above = shifted(grads[2], "lat", 1, False)
        return from_above, from_below

    def return_sides(grads, rims, after):
        to_left, to_right = merge_sides(grads[4], grads[5], *rims, band_rows, band_cols, after)
        from_right = shifted(to_left, "lon", -1, True)
        from_left = shifted(to_right, "lon", 1, True)
        return to_left, from_left, from_right

    one = attend(0, slots, [], [*rows_x, *rows_y])
    rims_1 = return_rows(one)
    two = attend(slots, 1, [(0, one[0])], [])
    sent, *sides_1 = return_sides(one, rims_1, [two[1]])
    two = attend(slots + 1, 1, list(enumerate(two)), [sent])
    rims_2 = return_rows(two)
    dq = two[0]

    send_q = grad_rows(rows_x[1], dq, scale, BF, after=sides_1)
    keep_q = dot(rows_x[0], dq) * scale
    sent, *sides_2 = return_sides(two, rims_2, [send_q])
    dkv_1 = finish(one[3], *rims_1, *sides_1, band_rows, band_cols, [sent], 10**5)
    send_1 = grad_rows(rows_y[1], dkv_1, scale, BF)
    keep_1 = dot(rows_y[0], dkv_1) * scale
    received = [exchanged(send_q, *x_first[0]), exchanged(send_1, *y_first[0])]
    keep, send = add_split(jnp.concatenate([keep_q, keep_1], axis=1), received)

    dkv_2 = finish(two[3], *rims_2, *sides_2, band_rows, band_cols, [keep], FINISH_FLOPS)
    for step_x, step_y in zip(x_first[1:-1], y_first[1:-1]):
        received = [exchanged(send[0], *step_x), exchanged(send[1], *step_y)]
        keep, send = add_split(keep, received, [dkv_2])
    send_2 = grad_rows(rows_x[1], dkv_2, scale, BF, after=[keep])
    received_2 = [exchanged(send_2, *x_first[0])]
    keep_2 = grad_rows(rows_x[0], dkv_2, scale, F32, after=[keep])
    received = [exchanged(send[0], *x_first[-1]), exchanged(send[1], *y_first[-1])]
    keep, send = add_blocks(keep, received, n_lon)
    group_1 = [keep] + [exchanged(a, "lon", i + 1) for i, a in enumerate(send)]
    for axis, bit in x_first[1:]:
        keep_2, send = add_split(keep_2, received_2)
        received_2 = [exchanged(send[0], axis, bit)]
    keep_2, send = add_blocks(keep_2, received_2, n_lon)
    group_2 = [keep_2] + [exchanged(a, "lon", i + 1) for i, a in enumerate(send)]
    places = [
        [(0, width, 0), (width, half, width), (width + half, half, 2 * width)],
        [(0, half, width + half), (half, half, 2 * width + half)],
    ]
    grad_w = gather_sums([group_1, group_2], places, 3 * width)

    grad_proj = jnp.concatenate(
        [dq, dkv_1[:, :half], dkv_2[:, :half], dkv_1[:, half:], dkv_2[:, half:]], axis=1
    )
    grad_inputs = dot(grad_proj, w_qkv, NT).astype(BF).reshape(inputs.shape)
    return (grad_inputs, grad_w)


def solution(mesh):
    in_specs = (P("dp", "lat", "lon", None), P("dp", "lat", "lon", None), P())
    out_specs = (P("dp", "lat", "lon", None), P(("dp", "lat", "lon"), None))
    return jax.shard_map(body, mesh=mesh, in_specs=in_specs, out_specs=out_specs, check_vma=False)
```

```python
import functools

import jax
import jax.numpy as jnp
import numpy as np
from jax import lax
from jax.experimental import pallas as pl
from jax.experimental.pallas import tpu as pltpu
from jax.sharding import PartitionSpec as P

HEADS = 16
WIN = 13
MARGIN = WIN // 2
TILE_R = 4
GROUP = 4
KEY_COLS = 32
HALO_COLS = 16
REGION_R = 16
PAD_R = 2
EDGE_R = MARGIN + PAD_R
NEG = -1e30
BF = jnp.bfloat16
F32 = jnp.float32
MIB = 1024 * 1024
FINISH_FLOPS = 6 * 10**9
LANES = 128

NT = (((1,), (1,)), ((), ()))
TN = (((0,), (0,)), ((), ()))
NN = (((1,), (0,)), ((), ()))


def dot(a, b, dims=NN):
    return lax.dot_general(a, b, dims, preferred_element_type=F32)


def region_top(tile, band_start, band_rows, total_rows):
    lowest = jnp.where(band_start == 0, TILE_R, 0)
    highest = jnp.where(band_start + band_rows == total_rows, band_rows - 2 * TILE_R, band_rows)
    return jnp.clip(tile * TILE_R, lowest, highest)


def mask_kernel(band_rows, band_cols, total_rows, start_ref, mask_ref):
    band_start = start_ref[0]
    tile = pl.program_id(0)
    shape = mask_ref.shape[1:]
    first = region_top(tile, band_start, band_rows, total_rows)
    key = lax.broadcasted_iota(jnp.int32, shape, 0)
    query = lax.broadcasted_iota(jnp.int32, shape, 1) % (TILE_R * band_cols)
    key_row = band_start - MARGIN + first + key // KEY_COLS
    place = key % KEY_COLS
    query_row = band_start + tile * TILE_R + query // band_cols
    query_col = query % band_cols
    window = jnp.clip(query_row - MARGIN, 0, total_rows - WIN)
    row_inside = (key_row >= window) & (key_row < window + WIN)
    key_col = jnp.where(
        place < band_cols,
        place,
        jnp.where(place < band_cols + MARGIN, place - band_cols - MARGIN, place - MARGIN),
    )
    col_inside = (jnp.abs(key_col - query_col) <= MARGIN) & (place < band_cols + 2 * MARGIN)
    mask_ref[0] = jnp.where(row_inside & col_inside, 0.0, NEG).astype(BF)


def window_masks(start, band_rows, band_cols, total_rows):
    tiles = band_rows // TILE_R
    shape = (REGION_R * KEY_COLS, 2 * TILE_R * band_cols)
    return pl.pallas_call(
        functools.partial(mask_kernel, band_rows, band_cols, total_rows),
        grid=(tiles,),
        in_specs=[pl.BlockSpec(memory_space=pltpu.SMEM)],
        out_specs=pl.BlockSpec((1,) + shape, lambda t: (t, 0, 0)),
        out_shape=jax.ShapeDtypeStruct((tiles,) + shape, BF),
        cost_estimate=pl.CostEstimate(flops=10**7, bytes_accessed=2**21, transcendentals=0),
    )(start)


def attention_kernel(band_rows, band_cols, total_rows, head_width, extra, first, count, *refs):
    (start_ref, mask_ref, left_ref, right_ref, above_ref, below_ref, cl_ref, cr_ref,
     qkv_hbm, grad_hbm, w_hbm) = refs[:11]
    (dq_ref, top_ref, bottom_ref, mid_ref, to_left_ref, to_right_ref,
     halo_ref, spot_ref, q_ref, k_ref, v_ref, dk_ref, dv_ref,
     own_refs, w_refs, own_sem, w_sem) = refs[11 + extra :]
    band_start = start_ref[0]
    tiles = band_rows // TILE_R
    queries = TILE_R * band_cols
    keys = REGION_R * KEY_COLS
    width = GROUP * head_width
    lanes = GROUP * queries
    region_rows = band_rows + 2 * MARGIN
    side = MARGIN * band_rows
    edge = MARGIN * band_cols
    corner = 2 * MARGIN * EDGE_R
    at_above = 2 * side
    at_below = at_above + edge
    at_cl = at_below + edge
    at_cr = at_cl + corner
    halves = [(i, slice(i * LANES, (i + 1) * LANES)) for i in range(width // LANES)]

    step = pl.program_id(0)
    groups = HEADS // GROUP

    def copies(slot):
        at = lambda part: pl.ds((part * groups + first + slot) * width, width)
        own = [
            pltpu.make_async_copy(source.at[:, at(part)], own_refs.at[slot, i], own_sem.at[slot, i])
            for i, (source, part) in enumerate(
                ((qkv_hbm, 0), (qkv_hbm, 1), (qkv_hbm, 2), (grad_hbm, 0))
            )
        ]
        weights = [
            pltpu.make_async_copy(w_hbm.at[:, at(1 + i)], w_refs.at[slot, i], w_sem.at[slot, i])
            for i in range(2)
        ]
        return weights + own

    @pl.when(step == 0)
    def _():
        for slot in range(count):
            for copy in copies(slot):
                copy.start()
        halo_ref[:side] = left_ref[...]
        halo_ref[side:at_above] = right_ref[...]
        halo_ref[at_above:at_below] = above_ref[...]
        halo_ref[at_below:at_cl] = below_ref[...]
        halo_ref[at_cl : at_cl + corner] = cl_ref[...]
        halo_ref[at_cr : at_cr + corner] = cr_ref[...]
        spot_ref[...] = jnp.zeros_like(spot_ref)

    def place(target, own, weights):
        fresh = dot(halo_ref[...], weights)
        for col in range(MARGIN):
            start = MARGIN * HALO_COLS + col
            for part, at in halves:
                spot_ref[part, pl.ds(start, band_rows, stride=HALO_COLS), :] = fresh[
                    col * band_rows : (col + 1) * band_rows, at
                ]
                spot_ref[part, pl.ds(start + MARGIN, band_rows, stride=HALO_COLS), :] = fresh[
                    side + col * band_rows : side + (col + 1) * band_rows, at
                ]
        for corner_at, offset in ((at_cl, 0), (at_cr, MARGIN)):
            for rim in range(2):
                first = rim * (MARGIN + band_rows) * HALO_COLS + offset
                for col in range(MARGIN):
                    base = corner_at + (rim * MARGIN + col) * EDGE_R
                    for part, at in halves:
                        spot_ref[part, pl.ds(first + col, MARGIN, stride=HALO_COLS), :] = fresh[
                            base : base + MARGIN, at
                        ]
        for row in range(region_rows):
            base = row * KEY_COLS
            inner = row - MARGIN
            if inner < 0:
                ours = fresh[at_above + row * band_cols : at_above + (row + 1) * band_cols].astype(BF)
            elif inner < band_rows:
                ours = own[inner * band_cols : (inner + 1) * band_cols, :]
            else:
                past = at_below + (inner - band_rows) * band_cols
                ours = fresh[past : past + band_cols].astype(BF)
            target[base : base + band_cols, :] = ours
            for part, at in halves:
                target[base + band_cols : base + KEY_COLS, at] = spot_ref[
                    part, row * HALO_COLS : (row + 1) * HALO_COLS, :
                ].astype(BF)

    for slot in range(count):

        @pl.when(step == slot)
        def _():
            for copy in copies(slot):
                copy.wait()

    grad_ref = own_refs.at[step, 3]
    place(k_ref, own_refs.at[step, 1], w_refs[step, 0])
    place(v_ref, own_refs.at[step, 2], w_refs[step, 1])
    q_ref[...] = own_refs[step, 0] * BF(head_width**-0.5)
    dk_ref[...] = jnp.zeros_like(dk_ref)
    dv_ref[...] = jnp.zeros_like(dv_ref)

    def spread(rows):
        block = jnp.concatenate([rows] * GROUP, axis=0)
        head_row = lax.broadcasted_iota(jnp.int32, (lanes, width), 0) // queries
        head_col = lax.broadcasted_iota(jnp.int32, (lanes, width), 1) // head_width
        return jnp.where(head_row == head_col, block, jnp.zeros_like(block))

    def one_tile(tile, carry):
        first = region_top(tile, band_start, band_rows, total_rows)
        region = pl.ds(pl.multiple_of(first * KEY_COLS, TILE_R * KEY_COLS), keys)
        total = pl.ds(pl.multiple_of((first + PAD_R) * KEY_COLS, PAD_R * KEY_COLS), keys)
        mine = pl.ds(pl.multiple_of(tile * queries, queries), queries)
        q_wide = spread(q_ref[mine, :])
        g_wide = spread(grad_ref[mine, :])
        mask = mask_ref[tile].astype(F32)
        scores = dot(k_ref[region, :], q_wide, NT) + jnp.concatenate([mask, mask], axis=1)
        dots = dot(v_ref[region, :], g_wide, NT)
        exponent = jnp.exp(scores - jnp.max(scores, axis=0, keepdims=True))
        inverse = 1.0 / jnp.sum(exponent, axis=0, keepdims=True)
        delta = jnp.sum(exponent * dots, axis=0, keepdims=True) * inverse
        attn = exponent * inverse
        dscore = (attn * (dots - delta)).astype(BF)
        dv = dot(attn.astype(BF), g_wide)
        dk = dot(dscore, q_wide)
        for part, at in halves:
            dv_ref[part, total, :] += dv[:, at]
            dk_ref[part, total, :] += dk[:, at]
        dq_wide = dot(dscore, k_ref[region, :], TN)
        head_col = lax.broadcasted_iota(jnp.int32, (queries, width), 1) // head_width
        dq = jnp.zeros((queries, width), F32)
        for head in range(GROUP):
            dq = jnp.where(head_col == head, dq_wide[head * queries : (head + 1) * queries], dq)
        dq_ref[mine, :] = (dq * head_width**-0.5).astype(BF)
        return carry

    lax.fori_loop(0, tiles, one_tile, 0, unroll=4)

    middle = (PAD_R + MARGIN) * KEY_COLS
    below = (PAD_R + MARGIN + band_rows) * KEY_COLS
    for part, acc in enumerate((dk_ref, dv_ref)):
        for lane, at in halves:
            for row in range(MARGIN):
                here = slice(row * band_cols, (row + 1) * band_cols)
                for start, out in ((PAD_R * KEY_COLS, top_ref), (below, bottom_ref)):
                    start = start + row * KEY_COLS
                    out[part, here, at] = acc[lane, start : start + band_cols, :].astype(BF)
            for pair in range(MARGIN):
                here = slice(edge + pair * 2 * EDGE_R, edge + (pair + 1) * 2 * EDGE_R)
                for start, out in ((0, top_ref), (below, bottom_ref)):
                    start = start + band_cols + 2 * pair
                    out[part, here, at] = jnp.concatenate(
                        [
                            acc[lane, pl.ds(start, EDGE_R, stride=KEY_COLS), :],
                            acc[lane, pl.ds(start + 1, EDGE_R, stride=KEY_COLS), :],
                        ],
                        axis=0,
                    ).astype(BF)
            for row in range(band_rows):
                base = middle + row * KEY_COLS
                mid_ref[part, row * band_cols : (row + 1) * band_cols, at] = acc[
                    lane, base : base + band_cols, :
                ].astype(BF)
            for col in range(MARGIN):
                here = slice(col * band_rows, (col + 1) * band_rows)
                start = middle + band_cols + col
                to_left_ref[part, here, at] = acc[
                    lane, pl.ds(start, band_rows, stride=KEY_COLS), :
                ].astype(BF)
                to_right_ref[part, here, at] = acc[
                    lane, pl.ds(start + MARGIN, band_rows, stride=KEY_COLS), :
                ].astype(BF)


def attention_grads(
    first, count, slots, start, masks, halo, qkv, grad_out, w_qkv, shape, before, after
):
    band_rows, band_cols, total_rows = shape
    tokens, width = grad_out.shape
    head_width = width // HEADS
    block = GROUP * head_width
    region_tokens = (band_rows + 2 * MARGIN) * KEY_COLS
    total_tokens = (band_rows + 2 * MARGIN + 2 * PAD_R) * KEY_COLS
    side = MARGIN * band_rows
    edge = MARGIN * (band_cols + 2 * EDGE_R)
    corner = 2 * MARGIN * EDGE_R
    halo_tokens = 2 * (side + MARGIN * band_cols + corner)
    whole = lambda g: (0, 0)
    column = lambda offset: (lambda g: (0, offset + first + g))
    slot = lambda g: (0, 0, first % slots + g)
    halves = [(2, edge), (2, edge), (2, tokens), (2, side), (2, side)]
    out_shape = [jax.ShapeDtypeStruct((tokens, width), BF)] + [
        jax.ShapeDtypeStruct(s + (slots * block,), BF) for s in halves
    ]
    aliases = {}
    if before:
        aliases = {11 + i: place for i, (place, _) in enumerate(before)}
    return pl.pallas_call(
        functools.partial(
            attention_kernel, band_rows, band_cols, total_rows, head_width,
            len(before) + len(after), first, count,
        ),
        grid=(count,),
        in_specs=[
            pl.BlockSpec(memory_space=pltpu.SMEM),
            pl.BlockSpec(masks.shape, lambda g: (0, 0, 0)),
        ]
        + [pl.BlockSpec(piece.shape, whole) for piece in halo]
        + [pl.BlockSpec(memory_space=pltpu.HBM)] * 3
        + [pl.BlockSpec(memory_space=pl.ANY)] * (len(before) + len(after)),
        out_specs=[pl.BlockSpec((tokens, block), column(0))]
        + [pl.BlockSpec(s + (block,), slot) for s in halves],
        out_shape=out_shape,
        input_output_aliases=aliases,
        scratch_shapes=[
            pltpu.VMEM((halo_tokens, width), BF),
            pltpu.VMEM((block // LANES, (band_rows + 2 * MARGIN) * HALO_COLS, LANES), F32),
            pltpu.VMEM((tokens, block), BF),
            pltpu.VMEM((region_tokens, block), BF),
            pltpu.VMEM((region_tokens, block), BF),
            pltpu.VMEM((block // LANES, total_tokens, LANES), F32),
            pltpu.VMEM((block // LANES, total_tokens, LANES), F32),
            pltpu.VMEM((count, 4, tokens, block), BF),
            pltpu.VMEM((count, 2, width, block), BF),
            pltpu.SemaphoreType.DMA((count, 4)),
            pltpu.SemaphoreType.DMA((count, 2)),
        ],
        compiler_params=pltpu.CompilerParams(
            dimension_semantics=("arbitrary",), vmem_limit_bytes=30 * MIB
        ),
        cost_estimate=pl.CostEstimate(
            flops=count * 14 * 10**9, bytes_accessed=count * 8 * MIB, transcendentals=count * 10**6
        ),
    )(start, masks, *halo, qkv, grad_out, w_qkv, *[a for _, a in before], *after)


def on_chip(kernel, out_shape, operands, after=(), scratch=(), flops=10**5):
    count = len(operands)

    def run(*refs):
        kernel(*refs[:count], *refs[count + len(after) :])

    return pl.pallas_call(
        run,
        in_specs=[pl.BlockSpec(memory_space=pltpu.VMEM)] * count
        + [pl.BlockSpec(memory_space=pl.ANY)] * len(after),
        out_specs=[pl.BlockSpec(memory_space=pltpu.VMEM)] * len(out_shape),
        out_shape=[jax.ShapeDtypeStruct(s, d) for s, d in out_shape],
        scratch_shapes=list(scratch),
        compiler_params=pltpu.CompilerParams(vmem_limit_bytes=24 * MIB),
        cost_estimate=pl.CostEstimate(flops=flops, bytes_accessed=10**4, transcendentals=0),
    )(*operands, *after)


def lanes_of(width):
    return [(i, slice(i * LANES, (i + 1) * LANES)) for i in range(width // LANES)]


def project(own, w_qkv, after):
    tokens, width = own.shape
    columns = w_qkv.shape[1]
    block = 4 * LANES

    def kernel(own_ref, w_ref, *refs):
        refs[-1][...] = dot(own_ref[...], w_ref[...]).astype(BF)

    return pl.pallas_call(
        kernel,
        grid=(columns // block,),
        in_specs=[
            pl.BlockSpec((tokens, width), lambda g: (0, 0)),
            pl.BlockSpec((width, block), lambda g: (0, g)),
        ]
        + [pl.BlockSpec(memory_space=pl.ANY)] * len(after),
        out_specs=pl.BlockSpec((tokens, block), lambda g: (0, g)),
        out_shape=jax.ShapeDtypeStruct((tokens, columns), BF),
        compiler_params=pltpu.CompilerParams(vmem_limit_bytes=24 * MIB),
        cost_estimate=pl.CostEstimate(flops=10**9, bytes_accessed=MIB, transcendentals=0),
    )(own, w_qkv, *after)


def row_blocks(me, own, orders, after):
    tokens, width = own.shape
    devices = len(orders[0])
    size = width // devices
    step = max(1, 16 // size)

    def kernel(me_ref, own_ref, *refs):
        out_refs, wide_ref = refs[len(after) : -1], refs[-1]
        for at in range(0, width, 2 * LANES):
            wide_ref[at : at + 2 * LANES, :] = own_ref[:, at : at + 2 * LANES].astype(F32).T
        me = me_ref[0]
        for i, order in enumerate(orders):
            for j in range(0, devices, step):
                rows = [
                    wide_ref[pl.ds(pl.multiple_of((me ^ int(order[k])) * size, size), size), :]
                    for k in range(j, j + step)
                ]
                half, base = divmod(j * size, width // 2)
                block = rows[0] if step == 1 else jnp.concatenate(rows, axis=0)
                out_refs[2 * i + half][base : base + step * size, :] = block.astype(BF)

    count = 2 * len(orders)
    out = pl.pallas_call(
        kernel,
        in_specs=[pl.BlockSpec(memory_space=pltpu.SMEM), pl.BlockSpec(memory_space=pltpu.VMEM)]
        + [pl.BlockSpec(memory_space=pl.ANY)] * len(after),
        out_specs=[pl.BlockSpec(memory_space=pltpu.VMEM)] * count,
        out_shape=[jax.ShapeDtypeStruct((width // 2, tokens), BF)] * count,
        scratch_shapes=[pltpu.VMEM((width, tokens), F32)],
        compiler_params=pltpu.CompilerParams(vmem_limit_bytes=16 * MIB),
        cost_estimate=pl.CostEstimate(flops=10**9, bytes_accessed=MIB, transcendentals=0),
    )(me, own, *after)
    return [out[2 * i : 2 * i + 2] for i in range(len(orders))]


def pack_sides(own, band_rows, band_cols):
    tokens, width = own.shape

    def kernel(own_ref, last_ref, first_ref, wide_ref):
        for lane, at in lanes_of(width):
            wide_ref[lane] = own_ref[:, at].astype(F32)
            for col in range(MARGIN):
                here = slice(col * band_rows, (col + 1) * band_rows)
                last = pl.ds(band_cols - MARGIN + col, band_rows, stride=band_cols)
                last_ref[here, at] = wide_ref[lane, last, :].astype(BF)
                first = pl.ds(col, band_rows, stride=band_cols)
                first_ref[here, at] = wide_ref[lane, first, :].astype(BF)

    out = ((MARGIN * band_rows, width), BF)
    scratch = [pltpu.VMEM((width // LANES, tokens, LANES), F32)]
    return on_chip(kernel, [out, out], [own], scratch=scratch)


def pack_rows(own, band_cols, after):
    tokens, width = own.shape
    edge = MARGIN * band_cols

    def kernel(own_ref, last_ref, first_ref):
        last_ref[...] = own_ref[tokens - edge :, :]
        first_ref[...] = own_ref[:edge, :]

    out = ((edge, width), BF)
    return on_chip(kernel, [out, out], [own], after=after)


def pack_corners(above, below, band_cols):
    edge, width = above.shape

    def kernel(above_ref, below_ref, last_ref, first_ref, wide_ref):
        wide_ref[:, edge:, :] = jnp.zeros_like(wide_ref[:, edge:, :])
        for rim, rim_ref in enumerate((above_ref, below_ref)):
            for lane, at in lanes_of(width):
                wide_ref[lane, :edge, :] = rim_ref[:, at].astype(F32)
                for out_ref, offset in ((last_ref, band_cols - MARGIN), (first_ref, 0)):
                    for col in range(0, MARGIN, 2):
                        base = (rim * MARGIN + col) * EDGE_R
                        pair = [
                            wide_ref[lane, pl.ds(offset + c, EDGE_R, stride=band_cols), :]
                            for c in (col, col + 1)
                        ]
                        out_ref[base : base + 2 * EDGE_R, at] = jnp.concatenate(pair).astype(BF)

    out = ((2 * MARGIN * EDGE_R, width), BF)
    scratch = [pltpu.VMEM((width // LANES, EDGE_R * band_cols, LANES), F32)]
    return on_chip(kernel, [out, out], [above, below], scratch=scratch)


def merge_sides(left, right, above, below, band_rows, band_cols, after=()):
    edge = MARGIN * band_cols

    def kernel(left_ref, right_ref, above_ref, below_ref, ol_ref, or_ref):
        for part in range(2):
            for col in range(2 * MARGIN):
                source, target = (left_ref, ol_ref) if col < MARGIN else (right_ref, or_ref)
                base = (col % MARGIN) * band_rows
                pair = slice(edge + (col // 2) * 2 * EDGE_R, edge + (col // 2 + 1) * 2 * EDGE_R)
                odd = slice((col % 2) * EDGE_R, (col % 2 + 1) * EDGE_R)
                rows = source[part, base : base + band_rows, :].astype(F32)
                first = rows[:EDGE_R] + above_ref[part, pair, :].astype(F32)[odd]
                last = rows[band_rows - EDGE_R :] + below_ref[part, pair, :].astype(F32)[odd]
                target[part, base : base + band_rows, :] = jnp.concatenate(
                    [first, rows[EDGE_R : band_rows - EDGE_R], last], axis=0
                ).astype(BF)

    out = [(left.shape, BF), (right.shape, BF)]
    return on_chip(kernel, out, [left, right, above, below], after=after)


def finish(mid, above, below, left, right, band_rows, band_cols, after, flops):
    _, tokens, width = mid.shape
    edge = MARGIN * band_cols

    def kernel(mid_ref, above_ref, below_ref, left_ref, right_ref, out_ref, acc_ref):
        for part in range(2):
            for block in range(width // (2 * LANES)):
                for lane in range(2):
                    at = slice((2 * block + lane) * LANES, (2 * block + lane + 1) * LANES)
                    acc_ref[lane] = mid_ref[part, :, at].astype(F32)
                    acc_ref[lane, :edge, :] += above_ref[part, :edge, at].astype(F32)
                    acc_ref[lane, tokens - edge :, :] += below_ref[part, :edge, at].astype(F32)
                    for col in range(MARGIN):
                        here = slice(col * band_rows, (col + 1) * band_rows)
                        first = pl.ds(col, band_rows, stride=band_cols)
                        last = pl.ds(band_cols - MARGIN + col, band_rows, stride=band_cols)
                        acc_ref[lane, first, :] += left_ref[part, here, at].astype(F32)
                        acc_ref[lane, last, :] += right_ref[part, here, at].astype(F32)
                both = jnp.concatenate([acc_ref[0], acc_ref[1]], axis=1).astype(BF)
                start = part * width + block * 2 * LANES
                out_ref[:, start : start + 2 * LANES] = both

    out = [((tokens, 2 * width), BF)]
    scratch = [pltpu.VMEM((2, tokens, LANES), F32)]
    operands = [mid, above, below, left, right]
    return on_chip(kernel, out, operands, after, scratch, flops)[0]


def grad_rows(rows, columns, scale, kind, after=()):
    features, width = rows[0].shape[0], columns.shape[1]

    def kernel(*refs):
        *rows_refs, columns_ref, out_ref = refs
        for start in range(0, width, 2 * LANES):
            here = slice(start, start + 2 * LANES)
            rows_ref = rows_refs[start * len(rows) // width]
            out_ref[:, here] = (dot(rows_ref[...], columns_ref[:, here]) * scale).astype(kind)

    return on_chip(kernel, [((features, width), kind)], [*rows, columns], after)[0]


def add_split(keep, received, after=(), parts=None):
    half, columns = keep.shape[0] // 2, keep.shape[1]
    parts = parts or len(received)
    part = columns // parts
    each = columns // len(received)

    def kernel(keep_ref, *refs):
        sums, *sends = refs[len(received) :]
        for i in range(parts):
            at = slice(i * part, (i + 1) * part)
            received_ref = refs[i * part // each]
            there = slice(i * part % each, i * part % each + part)
            sums[:, at] = keep_ref[:half, at] + received_ref[:half, there].astype(F32)
            sends[i][...] = (keep_ref[half:, at] + received_ref[half:, there].astype(F32)).astype(BF)

    out = [((half, columns), F32)] + [((half, part), BF)] * parts
    keep, *send = on_chip(kernel, out, [keep, *received], after=after)
    return keep, send


def add_blocks(keep, received, blocks):
    rows, columns = keep.shape
    part = columns // len(received)
    size = rows // blocks

    def kernel(keep_ref, *refs):
        sums, *send = refs[len(received) :]
        for i, received_ref in enumerate(refs[: len(received)]):
            at = slice(i * part, (i + 1) * part)
            total = keep_ref[:, at] + received_ref[...].astype(F32)
            sums[:, at] = total[:size]
            for b in range(1, blocks):
                send[b - 1][:, at] = total[b * size : (b + 1) * size].astype(BF)

    out = [((size, columns), F32)] + [((size, columns), BF)] * (blocks - 1)
    keep, *send = on_chip(kernel, out, [keep, *received])
    return keep, send


def gather_sums(groups, places, width):
    flat = [a for group in groups for a in group]

    def kernel(*refs):
        out_ref = refs[-1]
        at = 0
        for group, moves in zip(groups, places):
            total = refs[at][...]
            for ref in refs[at + 1 : at + len(group)]:
                total = total + ref[...].astype(F32)
            at += len(group)
            for source, size, target in moves:
                out_ref[:, target : target + size] = total[:, source : source + size]

    return on_chip(kernel, [((flat[0].shape[0], width), F32)], flat)[0]


def shifted(array, axis, by, wrap):
    size = lax.axis_size(axis)
    route = [(i, (i + by) % size) for i in range(size) if wrap or 0 <= i + by < size]
    return lax.ppermute(array, axis, route)


def exchanged(array, axis, flip):
    return lax.ppermute(array, axis, [(i, i ^ flip) for i in range(lax.axis_size(axis))])


def bits_of(axis):
    return [(axis, 1 << b) for b in range((lax.axis_size(axis) - 1).bit_length())]


def feature_order(stages):
    n_lon, n_lat = lax.axis_size("lon"), lax.axis_size("lat")
    unit = {"lon": 1, "lat": n_lon, "dp": n_lon * n_lat}
    order = np.arange(n_lon)
    for axis, bit in reversed(stages):
        order = np.concatenate([order, order + unit[axis] * bit])
    return order.astype(np.int32)


def body(inputs, grad_out, w_qkv):
    _, band_rows, band_cols, width = inputs.shape
    n_lat, n_lon, n_dp = lax.axis_size("lat"), lax.axis_size("lon"), lax.axis_size("dp")
    band_start = lax.axis_index("lat") * band_rows
    total_rows = band_rows * n_lat
    tokens = band_rows * band_cols
    slots = HEADS // GROUP // 2
    shape = (band_rows, band_cols, total_rows)
    own = inputs.reshape(tokens, width)
    flat_grad = grad_out.reshape(tokens, width)

    last_cols, first_cols = pack_sides(own, band_rows, band_cols)
    left = shifted(last_cols, "lon", 1, True)
    right = shifted(first_cols, "lon", -1, True)
    last_rows, first_rows = pack_rows(own, band_cols, [last_cols])
    above = shifted(last_rows, "lat", 1, False)
    below = shifted(first_rows, "lat", -1, False)
    last_corners, first_corners = pack_corners(above, below, band_cols)
    corner_left = shifted(last_corners, "lon", 1, True)
    corner_right = shifted(first_corners, "lon", -1, True)
    halo = (left, right, above, below, corner_left, corner_right)

    start = band_start.reshape(1)
    masks = window_masks(start, band_rows, band_cols, total_rows)
    qkv = project(own, w_qkv, [last_corners])
    lat_bits = bits_of("lat")
    x_first = lat_bits[:1] + bits_of("dp") + lat_bits[1:]
    y_first = lat_bits + bits_of("dp")
    me = (lax.axis_index("dp") * n_lat + lax.axis_index("lat")) * n_lon + lax.axis_index("lon")
    half = width // 2
    rows_x, rows_y = row_blocks(
        me.reshape(1), own, [feature_order(x_first), feature_order(y_first)], [last_corners]
    )
    scale = float(tokens * n_dp * n_lat * n_lon) ** -0.5

    attend = lambda first, count, before, after: attention_grads(
        first, count, slots, start, masks, halo, qkv, flat_grad, w_qkv, shape, before, after
    )

    def return_rows(grads):
        from_below = shifted(grads[1], "lat", -1, False)
        from_above = shifted(grads[2], "lat", 1, False)
        return from_above, from_below

    def return_sides(grads, rims, after):
        to_left, to_right = merge_sides(grads[4], grads[5], *rims, band_rows, band_cols, after)
        from_right = shifted(to_left, "lon", -1, True)
        from_left = shifted(to_right, "lon", 1, True)
        return to_left, from_left, from_right

    one = attend(0, slots, [], [*rows_x, *rows_y])
    rims_1 = return_rows(one)
    two = attend(slots, 1, [(0, one[0])], [])
    sent, *sides_1 = return_sides(one, rims_1, [two[1]])
    two = attend(slots + 1, 1, list(enumerate(two)), [sent])
    rims_2 = return_rows(two)
    dq = two[0]

    send_q = grad_rows([rows_x[1]], dq, scale, BF, after=sides_1)
    keep_q = dot(rows_x[0], dq) * scale
    sent, *sides_2 = return_sides(two, rims_2, [send_q])
    dkv_1 = finish(one[3], *rims_1, *sides_1, band_rows, band_cols, [sent], 10**5)
    send_1 = grad_rows([rows_y[1]], dkv_1, scale, BF)
    keep_1 = dot(rows_y[0], dkv_1) * scale
    received = [exchanged(send_q, *x_first[0]), exchanged(send_1, *y_first[0])]
    keep, send = add_split(jnp.concatenate([keep_q, keep_1], axis=1), received)

    dkv_2 = finish(two[3], *rims_2, *sides_2, band_rows, band_cols, [keep], FINISH_FLOPS)
    for step_x, step_y in zip(x_first[1:-1], y_first[1:-1]):
        received = [exchanged(send[0], *step_x), exchanged(send[1], *step_y)]
        keep, send = add_split(keep, received, [dkv_2])
    send_2 = grad_rows((rows_x[1], rows_y[1]), dkv_2, scale, BF, after=[keep])
    received_2 = [exchanged(send_2, *x_first[0])]
    keep_2 = grad_rows((rows_x[0], rows_y[0]), dkv_2, scale, F32, after=[keep])
    received = [exchanged(send[0], *x_first[-1]), exchanged(send[1], *y_first[-1])]
    keep, send = add_blocks(keep, received, n_lon)
    group_1 = [keep] + [exchanged(a, "lon", i + 1) for i, a in enumerate(send)]
    for step_x, step_y in zip(x_first[1:], y_first[1:]):
        keep_2, send = add_split(keep_2, received_2, parts=2)
        received_2 = [exchanged(send[0], *step_x), exchanged(send[1], *step_y)]
    keep_2, send = add_blocks(keep_2, received_2, n_lon)
    group_2 = [keep_2] + [exchanged(a, "lon", i + 1) for i, a in enumerate(send)]
    places = [
        [(0, width, 0), (width, half, width), (width + half, half, 2 * width)],
        [(0, half, width + half), (half, half, 2 * width + half)],
    ]
    grad_w = gather_sums([group_1, group_2], places, 3 * width)

    grad_proj = jnp.concatenate(
        [dq, dkv_1[:, :half], dkv_2[:, :half], dkv_1[:, half:], dkv_2[:, half:]], axis=1
    )
    grad_inputs = dot(grad_proj, w_qkv, NT).astype(BF).reshape(inputs.shape)
    return (grad_inputs, grad_w)


def solution(mesh):
    in_specs = (P("dp", "lat", "lon", None), P("dp", "lat", "lon", None), P())
    out_specs = (P("dp", "lat", "lon", None), P(("dp", "lat", "lon"), None))
    return jax.shard_map(body, mesh=mesh, in_specs=in_specs, out_specs=out_specs, check_vma=False)
```

```python
import functools

import jax
import jax.numpy as jnp
import numpy as np
from jax import lax
from jax.experimental import pallas as pl
from jax.experimental.pallas import tpu as pltpu
from jax.sharding import PartitionSpec as P

HEADS = 16
WIN = 13
MARGIN = WIN // 2
TILE_R = 4
GROUP = 4
KEY_COLS = 32
HALO_COLS = 16
REGION_R = 16
PAD_R = 2
EDGE_R = MARGIN + PAD_R
NEG = -1e30
BF = jnp.bfloat16
F32 = jnp.float32
MIB = 1024 * 1024
FINISH_FLOPS = 6 * 10**9
LANES = 128
ATTENTION_MIB = 46

NT = (((1,), (1,)), ((), ()))
TN = (((0,), (0,)), ((), ()))
NN = (((1,), (0,)), ((), ()))


def dot(a, b, dims=NN):
    return lax.dot_general(a, b, dims, preferred_element_type=F32)


def region_top(tile, band_start, band_rows, total_rows):
    lowest = jnp.where(band_start == 0, TILE_R, 0)
    highest = jnp.where(band_start + band_rows == total_rows, band_rows - 2 * TILE_R, band_rows)
    return jnp.clip(tile * TILE_R, lowest, highest)


def mask_kernel(band_rows, band_cols, total_rows, start_ref, mask_ref):
    band_start = start_ref[0]
    tile = pl.program_id(0)
    shape = mask_ref.shape[1:]
    first = region_top(tile, band_start, band_rows, total_rows)
    key = lax.broadcasted_iota(jnp.int32, shape, 0)
    query = lax.broadcasted_iota(jnp.int32, shape, 1) % (TILE_R * band_cols)
    key_row = band_start - MARGIN + first + key // KEY_COLS
    place = key % KEY_COLS
    query_row = band_start + tile * TILE_R + query // band_cols
    query_col = query % band_cols
    window = jnp.clip(query_row - MARGIN, 0, total_rows - WIN)
    row_inside = (key_row >= window) & (key_row < window + WIN)
    key_col = jnp.where(
        place < band_cols,
        place,
        jnp.where(place < band_cols + MARGIN, place - band_cols - MARGIN, place - MARGIN),
    )
    col_inside = (jnp.abs(key_col - query_col) <= MARGIN) & (place < band_cols + 2 * MARGIN)
    mask_ref[0] = jnp.where(row_inside & col_inside, 0.0, NEG).astype(BF)


def window_masks(start, band_rows, band_cols, total_rows):
    tiles = band_rows // TILE_R
    shape = (REGION_R * KEY_COLS, 2 * TILE_R * band_cols)
    return pl.pallas_call(
        functools.partial(mask_kernel, band_rows, band_cols, total_rows),
        grid=(tiles,),
        in_specs=[pl.BlockSpec(memory_space=pltpu.SMEM)],
        out_specs=pl.BlockSpec((1,) + shape, lambda t: (t, 0, 0)),
        out_shape=jax.ShapeDtypeStruct((tiles,) + shape, BF),
        cost_estimate=pl.CostEstimate(flops=10**7, bytes_accessed=2**21, transcendentals=0),
    )(start)


def attention_kernel(band_rows, band_cols, total_rows, head_width, extra, first, count, *refs):
    (place_ref, mask_ref, left_ref, right_ref, rows_a, rows_b, corners_a, corners_b,
     qkv_hbm, grad_hbm, w_hbm) = refs[:11]
    (dq_ref, out_a, out_b, mid_ref, to_left_ref, to_right_ref,
     halo_ref, spot_ref, q_ref, k_ref, v_ref, dk_ref, dv_ref,
     own_refs, w_refs, own_sem, w_sem) = refs[11 + extra :]
    band_start = place_ref[0]
    even = place_ref[1] == 0
    tiles = band_rows // TILE_R
    queries = TILE_R * band_cols
    keys = REGION_R * KEY_COLS
    width = GROUP * head_width
    lanes = GROUP * queries
    region_rows = band_rows + 2 * MARGIN
    side = MARGIN * band_rows
    edge = MARGIN * band_cols
    corner = 2 * MARGIN * EDGE_R
    at_above = 2 * side
    at_below = at_above + edge
    at_cl = at_below + edge
    at_cr = at_cl + corner
    halves = [(i, slice(i * LANES, (i + 1) * LANES)) for i in range(width // LANES)]

    step = pl.program_id(0)
    groups = HEADS // GROUP

    def copies(slot):
        at = lambda part: pl.ds((part * groups + first + slot) * width, width)
        own = [
            pltpu.make_async_copy(source.at[:, at(part)], own_refs.at[slot, i], own_sem.at[slot, i])
            for i, (source, part) in enumerate(
                ((qkv_hbm, 0), (qkv_hbm, 1), (qkv_hbm, 2), (grad_hbm, 0))
            )
        ]
        weights = [
            pltpu.make_async_copy(w_hbm.at[:, at(1 + i)], w_refs.at[slot, i], w_sem.at[slot, i])
            for i in range(2)
        ]
        return weights + own

    @pl.when(step == 0)
    def _():
        for slot in range(count):
            for copy in copies(slot):
                copy.start()
        halo_ref[:side] = left_ref[...]
        halo_ref[side:at_above] = right_ref[...]
        for above, below, size, refs_ab in (
            (at_above, at_below, edge, (rows_a, rows_b)),
            (at_cl, at_cr, corner, (corners_a, corners_b)),
        ):
            for ref, at in zip(refs_ab, (jnp.where(even, below, above), jnp.where(even, above, below))):
                halo_ref[pl.ds(pl.multiple_of(at, 16), size), :] = ref[...]
        spot_ref[...] = jnp.zeros_like(spot_ref)

    def place(target, own, weights):
        fresh = dot(halo_ref[...], weights)
        for col in range(MARGIN):
            start = MARGIN * HALO_COLS + col
            for part, at in halves:
                spot_ref[part, pl.ds(start, band_rows, stride=HALO_COLS), :] = fresh[
                    col * band_rows : (col + 1) * band_rows, at
                ]
                spot_ref[part, pl.ds(start + MARGIN, band_rows, stride=HALO_COLS), :] = fresh[
                    side + col * band_rows : side + (col + 1) * band_rows, at
                ]
        for corner_at, skip, row in ((at_cl, PAD_R, 0), (at_cr, 0, MARGIN + band_rows)):
            for col in range(2 * MARGIN):
                base = corner_at + col * EDGE_R + skip
                spot = pl.ds(row * HALO_COLS + col, MARGIN, stride=HALO_COLS)
                for part, at in halves:
                    spot_ref[part, spot, :] = fresh[base : base + MARGIN, at]
        for row in range(region_rows):
            base = row * KEY_COLS
            inner = row - MARGIN
            if inner < 0:
                ours = fresh[at_above + row * band_cols : at_above + (row + 1) * band_cols].astype(BF)
            elif inner < band_rows:
                ours = own[inner * band_cols : (inner + 1) * band_cols, :]
            else:
                past = at_below + (inner - band_rows) * band_cols
                ours = fresh[past : past + band_cols].astype(BF)
            target[base : base + band_cols, :] = ours
            for part, at in halves:
                target[base + band_cols : base + KEY_COLS, at] = spot_ref[
                    part, row * HALO_COLS : (row + 1) * HALO_COLS, :
                ].astype(BF)

    for slot in range(count):

        @pl.when(step == slot)
        def _():
            for copy in copies(slot):
                copy.wait()

    grad_ref = own_refs.at[step, 3]
    place(k_ref, own_refs.at[step, 1], w_refs[step, 0])
    place(v_ref, own_refs.at[step, 2], w_refs[step, 1])
    q_ref[...] = own_refs[step, 0] * BF(head_width**-0.5)
    dk_ref[...] = jnp.zeros_like(dk_ref)
    dv_ref[...] = jnp.zeros_like(dv_ref)

    def spread(rows):
        block = jnp.concatenate([rows] * GROUP, axis=0)
        head_row = lax.broadcasted_iota(jnp.int32, (lanes, width), 0) // queries
        head_col = lax.broadcasted_iota(jnp.int32, (lanes, width), 1) // head_width
        return jnp.where(head_row == head_col, block, jnp.zeros_like(block))

    def one_tile(tile, carry):
        first = region_top(tile, band_start, band_rows, total_rows)
        region = pl.ds(pl.multiple_of(first * KEY_COLS, TILE_R * KEY_COLS), keys)
        total = pl.ds(pl.multiple_of((first + PAD_R) * KEY_COLS, PAD_R * KEY_COLS), keys)
        mine = pl.ds(pl.multiple_of(tile * queries, queries), queries)
        q_wide = spread(q_ref[mine, :])
        g_wide = spread(grad_ref[mine, :])
        mask = mask_ref[tile].astype(F32)
        scores = dot(k_ref[region, :], q_wide, NT) + jnp.concatenate([mask, mask], axis=1)
        dots = dot(v_ref[region, :], g_wide, NT)
        exponent = jnp.exp(scores - jnp.max(scores, axis=0, keepdims=True))
        inverse = 1.0 / jnp.sum(exponent, axis=0, keepdims=True)
        delta = jnp.sum(exponent * dots, axis=0, keepdims=True) * inverse
        attn = exponent * inverse
        dscore = (attn * (dots - delta)).astype(BF)
        dv = dot(attn.astype(BF), g_wide)
        dk = dot(dscore, q_wide)
        for part, at in halves:
            dv_ref[part, total, :] += dv[:, at]
            dk_ref[part, total, :] += dk[:, at]
        dq_wide = dot(dscore, k_ref[region, :], TN)
        head_col = lax.broadcasted_iota(jnp.int32, (queries, width), 1) // head_width
        dq = jnp.zeros((queries, width), F32)
        for head in range(GROUP):
            dq = jnp.where(head_col == head, dq_wide[head * queries : (head + 1) * queries], dq)
        dq_ref[mine, :] = (dq * head_width**-0.5).astype(BF)
        return carry

    lax.fori_loop(0, tiles, one_tile, 0, unroll=4)

    middle = (PAD_R + MARGIN) * KEY_COLS
    below = (PAD_R + MARGIN + band_rows) * KEY_COLS
    for part, acc in enumerate((dk_ref, dv_ref)):
        for lane, at in halves:
            for out, own_at, side_at in (
                (out_a, jnp.where(even, below, PAD_R * KEY_COLS), jnp.where(even, below, 0)),
                (out_b, jnp.where(even, PAD_R * KEY_COLS, below), jnp.where(even, 0, below)),
            ):
                for row in range(MARGIN):
                    start = pl.multiple_of(own_at + row * KEY_COLS, KEY_COLS)
                    out[part, row * band_cols : (row + 1) * band_cols, at] = acc[
                        lane, pl.ds(start, band_cols), :
                    ].astype(BF)
                for pair in range(MARGIN):
                    here = slice(edge + pair * 2 * EDGE_R, edge + (pair + 1) * 2 * EDGE_R)
                    start = side_at + band_cols + 2 * pair
                    out[part, here, at] = jnp.concatenate(
                        [
                            acc[lane, pl.ds(start, EDGE_R, stride=KEY_COLS), :],
                            acc[lane, pl.ds(start + 1, EDGE_R, stride=KEY_COLS), :],
                        ],
                        axis=0,
                    ).astype(BF)
            for row in range(band_rows):
                base = middle + row * KEY_COLS
                mid_ref[part, row * band_cols : (row + 1) * band_cols, at] = acc[
                    lane, base : base + band_cols, :
                ].astype(BF)
            for col in range(MARGIN):
                here = slice(col * band_rows, (col + 1) * band_rows)
                start = middle + band_cols + col
                to_left_ref[part, here, at] = acc[
                    lane, pl.ds(start, band_rows, stride=KEY_COLS), :
                ].astype(BF)
                to_right_ref[part, here, at] = acc[
                    lane, pl.ds(start + MARGIN, band_rows, stride=KEY_COLS), :
                ].astype(BF)


def attention_grads(
    first, count, slots, start, masks, halo, qkv, grad_out, w_qkv, shape, before, after
):
    band_rows, band_cols, total_rows = shape
    tokens, width = grad_out.shape
    head_width = width // HEADS
    block = GROUP * head_width
    region_tokens = (band_rows + 2 * MARGIN) * KEY_COLS
    total_tokens = (band_rows + 2 * MARGIN + 2 * PAD_R) * KEY_COLS
    side = MARGIN * band_rows
    edge = MARGIN * (band_cols + 2 * EDGE_R)
    corner = 2 * MARGIN * EDGE_R
    halo_tokens = 2 * (side + MARGIN * band_cols + corner)
    whole = lambda g: (0, 0)
    column = lambda offset: (lambda g: (0, offset + first + g))
    slot = lambda g: (0, 0, first % slots + g)
    halves = [(2, edge), (2, edge), (2, tokens), (2, side), (2, side)]
    out_shape = [jax.ShapeDtypeStruct((tokens, width), BF)] + [
        jax.ShapeDtypeStruct(s + (slots * block,), BF) for s in halves
    ]
    aliases = {}
    if before:
        aliases = {11 + i: place for i, (place, _) in enumerate(before)}
    return pl.pallas_call(
        functools.partial(
            attention_kernel, band_rows, band_cols, total_rows, head_width,
            len(before) + len(after), first, count,
        ),
        grid=(count,),
        in_specs=[
            pl.BlockSpec(memory_space=pltpu.SMEM),
            pl.BlockSpec(masks.shape, lambda g: (0, 0, 0)),
        ]
        + [pl.BlockSpec(piece.shape, whole) for piece in halo]
        + [pl.BlockSpec(memory_space=pltpu.HBM)] * 3
        + [pl.BlockSpec(memory_space=pl.ANY)] * (len(before) + len(after)),
        out_specs=[pl.BlockSpec((tokens, block), column(0))]
        + [pl.BlockSpec(s + (block,), slot) for s in halves],
        out_shape=out_shape,
        input_output_aliases=aliases,
        scratch_shapes=[
            pltpu.VMEM((halo_tokens, width), BF),
            pltpu.VMEM((block // LANES, (band_rows + 2 * MARGIN) * HALO_COLS, LANES), F32),
            pltpu.VMEM((tokens, block), BF),
            pltpu.VMEM((region_tokens, block), BF),
            pltpu.VMEM((region_tokens, block), BF),
            pltpu.VMEM((block // LANES, total_tokens, LANES), F32),
            pltpu.VMEM((block // LANES, total_tokens, LANES), F32),
            pltpu.VMEM((count, 4, tokens, block), BF),
            pltpu.VMEM((count, 2, width, block), BF),
            pltpu.SemaphoreType.DMA((count, 4)),
            pltpu.SemaphoreType.DMA((count, 2)),
        ],
        compiler_params=pltpu.CompilerParams(
            dimension_semantics=("arbitrary",), vmem_limit_bytes=ATTENTION_MIB * MIB
        ),
        cost_estimate=pl.CostEstimate(
            flops=count * 14 * 10**9, bytes_accessed=count * 8 * MIB, transcendentals=count * 10**6
        ),
    )(start, masks, *halo, qkv, grad_out, w_qkv, *[a for _, a in before], *after)


def on_chip(kernel, out_shape, operands, after=(), scratch=(), flops=10**5, place=()):
    count = len(operands) + len(place)

    def run(*refs):
        kernel(*refs[:count], *refs[count + len(after) :])

    return pl.pallas_call(
        run,
        in_specs=[pl.BlockSpec(memory_space=pltpu.SMEM)] * len(place)
        + [pl.BlockSpec(memory_space=pltpu.VMEM)] * len(operands)
        + [pl.BlockSpec(memory_space=pl.ANY)] * len(after),
        out_specs=[pl.BlockSpec(memory_space=pltpu.VMEM)] * len(out_shape),
        out_shape=[jax.ShapeDtypeStruct(s, d) for s, d in out_shape],
        scratch_shapes=list(scratch),
        compiler_params=pltpu.CompilerParams(vmem_limit_bytes=24 * MIB),
        cost_estimate=pl.CostEstimate(flops=flops, bytes_accessed=10**4, transcendentals=0),
    )(*place, *operands, *after)


def lanes_of(width):
    return [(i, slice(i * LANES, (i + 1) * LANES)) for i in range(width // LANES)]


def project(own, w_qkv, after):
    tokens, width = own.shape
    columns = w_qkv.shape[1]
    block = 4 * LANES

    def kernel(own_ref, w_ref, *refs):
        refs[-1][...] = dot(own_ref[...], w_ref[...]).astype(BF)

    return pl.pallas_call(
        kernel,
        grid=(columns // block,),
        in_specs=[
            pl.BlockSpec((tokens, width), lambda g: (0, 0)),
            pl.BlockSpec((width, block), lambda g: (0, g)),
        ]
        + [pl.BlockSpec(memory_space=pl.ANY)] * len(after),
        out_specs=pl.BlockSpec((tokens, block), lambda g: (0, g)),
        out_shape=jax.ShapeDtypeStruct((tokens, columns), BF),
        compiler_params=pltpu.CompilerParams(vmem_limit_bytes=56 * MIB),
        cost_estimate=pl.CostEstimate(flops=10**9, bytes_accessed=MIB, transcendentals=0),
    )(own, w_qkv, *after)


def row_blocks(me, own, orders, after):
    tokens, width = own.shape
    devices = len(orders[0])
    size = width // devices
    step = max(1, 16 // size)

    def kernel(me_ref, own_ref, *refs):
        out_refs, wide_ref = refs[len(after) : -1], refs[-1]
        for at in range(0, width, 2 * LANES):
            wide_ref[at : at + 2 * LANES, :] = own_ref[:, at : at + 2 * LANES].astype(F32).T
        me = me_ref[2]
        for i, order in enumerate(orders):
            for j in range(0, devices, step):
                rows = [
                    wide_ref[pl.ds(pl.multiple_of((me ^ int(order[k])) * size, size), size), :]
                    for k in range(j, j + step)
                ]
                half, base = divmod(j * size, width // 2)
                block = rows[0] if step == 1 else jnp.concatenate(rows, axis=0)
                out_refs[2 * i + half][base : base + step * size, :] = block.astype(BF)

    count = 2 * len(orders)
    out = pl.pallas_call(
        kernel,
        in_specs=[pl.BlockSpec(memory_space=pltpu.SMEM), pl.BlockSpec(memory_space=pltpu.VMEM)]
        + [pl.BlockSpec(memory_space=pl.ANY)] * len(after),
        out_specs=[pl.BlockSpec(memory_space=pltpu.VMEM)] * count,
        out_shape=[jax.ShapeDtypeStruct((width // 2, tokens), BF)] * count,
        scratch_shapes=[pltpu.VMEM((width, tokens), F32)],
        compiler_params=pltpu.CompilerParams(vmem_limit_bytes=16 * MIB),
        cost_estimate=pl.CostEstimate(flops=10**9, bytes_accessed=MIB, transcendentals=0),
    )(me, own, *after)
    return [out[2 * i : 2 * i + 2] for i in range(len(orders))]


def pack_sides(own, band_rows, band_cols):
    tokens, width = own.shape

    def kernel(own_ref, last_ref, first_ref, wide_ref):
        for lane, at in lanes_of(width):
            wide_ref[lane] = own_ref[:, at].astype(F32)
            for col in range(MARGIN):
                here = slice(col * band_rows, (col + 1) * band_rows)
                last = pl.ds(band_cols - MARGIN + col, band_rows, stride=band_cols)
                last_ref[here, at] = wide_ref[lane, last, :].astype(BF)
                first = pl.ds(col, band_rows, stride=band_cols)
                first_ref[here, at] = wide_ref[lane, first, :].astype(BF)

    out = ((MARGIN * band_rows, width), BF)
    scratch = [pltpu.VMEM((width // LANES, tokens, LANES), F32)]
    return on_chip(kernel, [out, out], [own], scratch=scratch)


def pack_rows(place, own, band_cols, after):
    tokens, width = own.shape
    edge = MARGIN * band_cols

    def kernel(place_ref, own_ref, out_a, out_b):
        even = place_ref[1] == 0
        last, first = own_ref[tokens - edge :, :], own_ref[:edge, :]
        out_a[...] = jnp.where(even, last, first)
        out_b[...] = jnp.where(even, first, last)

    out = ((edge, width), BF)
    return on_chip(kernel, [out, out], [own], after=after, place=[place])


def pack_corners(place, left, right, band_rows, after):
    width = left.shape[1]

    def kernel(place_ref, left_ref, right_ref, out_a, out_b):
        even = place_ref[1] == 0
        for side, side_ref in enumerate((left_ref, right_ref)):
            for col in range(0, MARGIN, 2):
                base = (side * MARGIN + col) * EDGE_R
                last, first = (
                    jnp.concatenate(
                        [
                            side_ref[at : at + EDGE_R, :].astype(F32)
                            for at in (start, start + band_rows)
                        ]
                    )
                    for start in ((col + 1) * band_rows - EDGE_R, col * band_rows)
                )
                here = slice(base, base + 2 * EDGE_R)
                out_a[here, :] = jnp.where(even, last, first).astype(BF)
                out_b[here, :] = jnp.where(even, first, last).astype(BF)

    out = ((2 * MARGIN * EDGE_R, width), BF)
    return on_chip(kernel, [out, out], [left, right], after=after, place=[place])


def merge_sides(place, left, right, rim_a, rim_b, band_rows, band_cols, after=()):
    edge = MARGIN * band_cols

    def kernel(place_ref, left_ref, right_ref, a_ref, b_ref, ol_ref, or_ref):
        even = place_ref[1] == 0
        for part in range(2):
            for col in range(2 * MARGIN):
                source, target = (left_ref, ol_ref) if col < MARGIN else (right_ref, or_ref)
                base = (col % MARGIN) * band_rows
                pair = slice(edge + (col // 2) * 2 * EDGE_R, edge + (col // 2 + 1) * 2 * EDGE_R)
                odd = slice((col % 2) * EDGE_R, (col % 2 + 1) * EDGE_R)
                rows = source[part, base : base + band_rows, :].astype(F32)
                rim_a, rim_b = (ref[part, pair, :].astype(F32)[odd] for ref in (a_ref, b_ref))
                first = rows[:EDGE_R] + jnp.where(even, rim_b, rim_a)
                last = rows[band_rows - EDGE_R :] + jnp.where(even, rim_a, rim_b)
                target[part, base : base + band_rows, :] = jnp.concatenate(
                    [first, rows[EDGE_R : band_rows - EDGE_R], last], axis=0
                ).astype(BF)

    out = [(left.shape, BF), (right.shape, BF)]
    return on_chip(kernel, out, [left, right, rim_a, rim_b], after=after, place=[place])


def finish(place, mid, rim_a, rim_b, left, right, band_rows, band_cols, after, flops):
    _, tokens, width = mid.shape
    edge = MARGIN * band_cols

    def kernel(place_ref, mid_ref, a_ref, b_ref, left_ref, right_ref, out_ref, acc_ref):
        even = place_ref[1] == 0
        for part in range(2):
            for block in range(width // (2 * LANES)):
                for lane in range(2):
                    at = slice((2 * block + lane) * LANES, (2 * block + lane + 1) * LANES)
                    acc_ref[lane] = mid_ref[part, :, at].astype(F32)
                    from_a, from_b = (r[part, :edge, at].astype(F32) for r in (a_ref, b_ref))
                    acc_ref[lane, :edge, :] += jnp.where(even, from_b, from_a)
                    acc_ref[lane, tokens - edge :, :] += jnp.where(even, from_a, from_b)
                    for col in range(MARGIN):
                        here = slice(col * band_rows, (col + 1) * band_rows)
                        first = pl.ds(col, band_rows, stride=band_cols)
                        last = pl.ds(band_cols - MARGIN + col, band_rows, stride=band_cols)
                        acc_ref[lane, first, :] += left_ref[part, here, at].astype(F32)
                        acc_ref[lane, last, :] += right_ref[part, here, at].astype(F32)
                both = jnp.concatenate([acc_ref[0], acc_ref[1]], axis=1).astype(BF)
                start = part * width + block * 2 * LANES
                out_ref[:, start : start + 2 * LANES] = both

    out = [((tokens, 2 * width), BF)]
    scratch = [pltpu.VMEM((2, tokens, LANES), F32)]
    operands = [mid, rim_a, rim_b, left, right]
    return on_chip(kernel, out, operands, after, scratch, flops, [place])[0]


def grad_rows(rows, columns, scale, kind, after=()):
    features, width = rows[0].shape[0], columns.shape[1]

    def kernel(*refs):
        *rows_refs, columns_ref, out_ref = refs
        for start in range(0, width, 2 * LANES):
            here = slice(start, start + 2 * LANES)
            rows_ref = rows_refs[start * len(rows) // width]
            out_ref[:, here] = (dot(rows_ref[...], columns_ref[:, here]) * scale).astype(kind)

    return on_chip(kernel, [((features, width), kind)], [*rows, columns], after)[0]


def add_split(keep, received, after=(), parts=None):
    half, columns = keep.shape[0] // 2, keep.shape[1]
    parts = parts or len(received)
    part = columns // parts
    each = columns // len(received)

    def kernel(keep_ref, *refs):
        sums, *sends = refs[len(received) :]
        for i in range(parts):
            at = slice(i * part, (i + 1) * part)
            received_ref = refs[i * part // each]
            there = slice(i * part % each, i * part % each + part)
            sums[:, at] = keep_ref[:half, at] + received_ref[:half, there].astype(F32)
            sends[i][...] = (keep_ref[half:, at] + received_ref[half:, there].astype(F32)).astype(BF)

    out = [((half, columns), F32)] + [((half, part), BF)] * parts
    keep, *send = on_chip(kernel, out, [keep, *received], after=after)
    return keep, send


def add_blocks(keep, received, blocks):
    rows, columns = keep.shape
    part = columns // len(received)
    size = rows // blocks

    def kernel(keep_ref, *refs):
        sums, *send = refs[len(received) :]
        for i, received_ref in enumerate(refs[: len(received)]):
            at = slice(i * part, (i + 1) * part)
            total = keep_ref[:, at] + received_ref[...].astype(F32)
            sums[:, at] = total[:size]
            for b in range(1, blocks):
                send[b - 1][:, at] = total[b * size : (b + 1) * size].astype(BF)

    out = [((size, columns), F32)] + [((size, columns), BF)] * (blocks - 1)
    keep, *send = on_chip(kernel, out, [keep, *received])
    return keep, send


def gather_sums(groups, places, width):
    flat = [a for group in groups for a in group]

    def kernel(*refs):
        out_ref = refs[-1]
        at = 0
        for group, moves in zip(groups, places):
            total = refs[at][...]
            for ref in refs[at + 1 : at + len(group)]:
                total = total + ref[...].astype(F32)
            at += len(group)
            for source, size, target in moves:
                out_ref[:, target : target + size] = total[:, source : source + size]

    return on_chip(kernel, [((flat[0].shape[0], width), F32)], flat)[0]


def shifted(array, axis, by, wrap):
    size = lax.axis_size(axis)
    route = [(i, (i + by) % size) for i in range(size) if wrap or 0 <= i + by < size]
    return lax.ppermute(array, axis, route)


def swapped(array_a, array_b, axis):
    size = lax.axis_size(axis)
    pairs = [(i, i + 1) for i in range(size - 1)]
    route = lambda chosen: chosen + [(j, i) for i, j in chosen]
    return [
        lax.ppermute(array, axis, route(pairs[offset::2]))
        for array, offset in ((array_a, 0), (array_b, 1))
    ]


def exchanged(array, axis, flip):
    return lax.ppermute(array, axis, [(i, i ^ flip) for i in range(lax.axis_size(axis))])


def bits_of(axis):
    return [(axis, 1 << b) for b in range((lax.axis_size(axis) - 1).bit_length())]


def feature_order(stages):
    n_lon, n_lat = lax.axis_size("lon"), lax.axis_size("lat")
    unit = {"lon": 1, "lat": n_lon, "dp": n_lon * n_lat}
    order = np.arange(n_lon)
    for axis, bit in reversed(stages):
        order = np.concatenate([order, order + unit[axis] * bit])
    return order.astype(np.int32)


def body(inputs, grad_out, w_qkv):
    _, band_rows, band_cols, width = inputs.shape
    n_lat, n_lon, n_dp = lax.axis_size("lat"), lax.axis_size("lon"), lax.axis_size("dp")
    band_start = lax.axis_index("lat") * band_rows
    total_rows = band_rows * n_lat
    tokens = band_rows * band_cols
    slots = HEADS // GROUP // 2
    shape = (band_rows, band_cols, total_rows)
    own = inputs.reshape(tokens, width)
    flat_grad = grad_out.reshape(tokens, width)

    last_cols, first_cols = pack_sides(own, band_rows, band_cols)
    left = shifted(last_cols, "lon", 1, True)
    right = shifted(first_cols, "lon", -1, True)
    me = (lax.axis_index("dp") * n_lat + lax.axis_index("lat")) * n_lon + lax.axis_index("lon")
    start = jnp.stack([band_start, lax.axis_index("lat") % 2, me])
    rim_rows = swapped(*pack_rows(start, own, band_cols, [last_cols]), "lat")

    masks = window_masks(start, band_rows, band_cols, total_rows)
    qkv = project(own, w_qkv, [last_cols])
    lat_bits = bits_of("lat")
    x_first = lat_bits[:1] + bits_of("dp") + lat_bits[1:]
    y_first = lat_bits + bits_of("dp")
    half = width // 2
    rows_x, rows_y = row_blocks(
        start, own, [feature_order(x_first), feature_order(y_first)], [last_cols]
    )
    corners = pack_corners(start, left, right, band_rows, [masks, qkv, *rows_x, *rows_y])
    halo = (left, right, *rim_rows, *swapped(*corners, "lat"))
    scale = float(tokens * n_dp * n_lat * n_lon) ** -0.5

    attend = lambda first, count, before, after: attention_grads(
        first, count, slots, start, masks, halo, qkv, flat_grad, w_qkv, shape, before, after
    )

    def return_sides(grads, rims, after):
        to_left, to_right = merge_sides(
            start, grads[4], grads[5], *rims, band_rows, band_cols, after
        )
        from_right = shifted(to_left, "lon", -1, True)
        from_left = shifted(to_right, "lon", 1, True)
        return to_left, from_left, from_right

    one = attend(0, slots, [], [*rows_x, *rows_y])
    rims_1 = swapped(one[1], one[2], "lat")
    two = attend(slots, 1, [(0, one[0])], [])
    sent, *sides_1 = return_sides(one, rims_1, [two[1]])
    two = attend(slots + 1, 1, list(enumerate(two)), [sent])
    rims_2 = swapped(two[1], two[2], "lat")
    dq = two[0]

    send_q = grad_rows([rows_x[1]], dq, scale, BF, after=sides_1)
    keep_q = dot(rows_x[0], dq) * scale
    sent, *sides_2 = return_sides(two, rims_2, [send_q])
    dkv_1 = finish(start, one[3], *rims_1, *sides_1, band_rows, band_cols, [sent], 10**5)
    send_1 = grad_rows([rows_y[1]], dkv_1, scale, BF)
    keep_1 = dot(rows_y[0], dkv_1) * scale
    received = [exchanged(send_q, *x_first[0]), exchanged(send_1, *y_first[0])]
    keep, send = add_split(jnp.concatenate([keep_q, keep_1], axis=1), received)

    dkv_2 = finish(start, two[3], *rims_2, *sides_2, band_rows, band_cols, [keep], FINISH_FLOPS)
    for step_x, step_y in zip(x_first[1:-1], y_first[1:-1]):
        received = [exchanged(send[0], *step_x), exchanged(send[1], *step_y)]
        keep, send = add_split(keep, received, [dkv_2])
    send_2 = grad_rows((rows_x[1], rows_y[1]), dkv_2, scale, BF, after=[keep])
    received_2 = [exchanged(send_2, *x_first[0])]
    keep_2 = grad_rows((rows_x[0], rows_y[0]), dkv_2, scale, F32, after=[keep])
    received = [exchanged(send[0], *x_first[-1]), exchanged(send[1], *y_first[-1])]
    keep, send = add_blocks(keep, received, n_lon)
    group_1 = [keep] + [exchanged(a, "lon", i + 1) for i, a in enumerate(send)]
    for step_x, step_y in zip(x_first[1:], y_first[1:]):
        keep_2, send = add_split(keep_2, received_2, parts=2)
        received_2 = [exchanged(send[0], *step_x), exchanged(send[1], *step_y)]
    keep_2, send = add_blocks(keep_2, received_2, n_lon)
    group_2 = [keep_2] + [exchanged(a, "lon", i + 1) for i, a in enumerate(send)]
    places = [
        [(0, width, 0), (width, half, width), (width + half, half, 2 * width)],
        [(0, half, width + half), (half, half, 2 * width + half)],
    ]
    grad_w = gather_sums([group_1, group_2], places, 3 * width)

    grad_proj = jnp.concatenate(
        [dq, dkv_1[:, :half], dkv_2[:, :half], dkv_1[:, half:], dkv_2[:, half:]], axis=1
    )
    grad_inputs = dot(grad_proj, w_qkv, NT).astype(BF).reshape(inputs.shape)
    return (grad_inputs, grad_w)


def solution(mesh):
    in_specs = (P("dp", "lat", "lon", None), P("dp", "lat", "lon", None), P())
    out_specs = (P("dp", "lat", "lon", None), P(("dp", "lat", "lon"), None))
    return jax.shard_map(body, mesh=mesh, in_specs=in_specs, out_specs=out_specs, check_vma=False)
```

```python
import functools

import jax
import jax.numpy as jnp
import numpy as np
from jax import lax
from jax.experimental import pallas as pl
from jax.experimental.pallas import tpu as pltpu
from jax.sharding import PartitionSpec as P

HEADS = 16
WIN = 13
MARGIN = WIN // 2
TILE_R = 4
GROUP = 4
KEY_COLS = 32
HALO_COLS = 16
REGION_R = 16
PAD_R = 2
EDGE_R = MARGIN + PAD_R
NEG = -1e30
BF = jnp.bfloat16
F32 = jnp.float32
MIB = 1024 * 1024
FINISH_FLOPS = 9 * 10**9
LANES = 128
ATTENTION_MIB = 46

NT = (((1,), (1,)), ((), ()))
TN = (((0,), (0,)), ((), ()))
NN = (((1,), (0,)), ((), ()))


def dot(a, b, dims=NN):
    return lax.dot_general(a, b, dims, preferred_element_type=F32)


def region_top(tile, band_start, band_rows, total_rows):
    lowest = jnp.where(band_start == 0, TILE_R, 0)
    highest = jnp.where(band_start + band_rows == total_rows, band_rows - 2 * TILE_R, band_rows)
    return jnp.clip(tile * TILE_R, lowest, highest)


def mask_kernel(band_rows, band_cols, total_rows, start_ref, mask_ref):
    band_start = start_ref[0]
    tile = pl.program_id(0)
    shape = mask_ref.shape[1:]
    first = region_top(tile, band_start, band_rows, total_rows)
    key = lax.broadcasted_iota(jnp.int32, shape, 0)
    query = lax.broadcasted_iota(jnp.int32, shape, 1) & (TILE_R * band_cols - 1)
    key_row = band_start - MARGIN + first + (key >> (KEY_COLS.bit_length() - 1))
    place = key & (KEY_COLS - 1)
    query_row = band_start + tile * TILE_R + (query >> (band_cols.bit_length() - 1))
    query_col = query & (band_cols - 1)
    window = jnp.clip(query_row - MARGIN, 0, total_rows - WIN)
    row_inside = (key_row >= window) & (key_row < window + WIN)
    key_col = jnp.where(
        place < band_cols,
        place,
        jnp.where(place < band_cols + MARGIN, place - band_cols - MARGIN, place - MARGIN),
    )
    col_inside = (jnp.abs(key_col - query_col) <= MARGIN) & (place < band_cols + 2 * MARGIN)
    mask_ref[0] = jnp.where(row_inside & col_inside, 0.0, NEG).astype(BF)


def window_masks(start, band_rows, band_cols, total_rows):
    tiles = band_rows // TILE_R
    shape = (REGION_R * KEY_COLS, 2 * TILE_R * band_cols)
    return pl.pallas_call(
        functools.partial(mask_kernel, band_rows, band_cols, total_rows),
        grid=(tiles,),
        in_specs=[pl.BlockSpec(memory_space=pltpu.SMEM)],
        out_specs=pl.BlockSpec((1,) + shape, lambda t: (t, 0, 0)),
        out_shape=jax.ShapeDtypeStruct((tiles,) + shape, BF),
        cost_estimate=pl.CostEstimate(flops=10**7, bytes_accessed=2**21, transcendentals=0),
    )(start)


def attention_kernel(band_rows, band_cols, total_rows, head_width, extra, first, count, *refs):
    (place_ref, mask_ref, left_ref, right_ref, rows_a, rows_b, corners_a, corners_b,
     qkv_hbm, grad_hbm, w_hbm) = refs[:11]
    (dq_ref, out_a, out_b, mid_ref, to_left_ref, to_right_ref,
     halo_ref, spot_ref, q_ref, k_ref, v_ref, qt_ref, gt_ref, kt_ref, dqt_ref, dk_ref, dv_ref,
     own_refs, w_refs, own_sem, w_sem) = refs[11 + extra :]
    band_start = place_ref[0]
    even = place_ref[1] == 0
    tiles = band_rows // TILE_R
    queries = TILE_R * band_cols
    keys = REGION_R * KEY_COLS
    width = GROUP * head_width
    lanes = GROUP * queries
    region_rows = band_rows + 2 * MARGIN
    side = MARGIN * band_rows
    edge = MARGIN * band_cols
    corner = 2 * MARGIN * EDGE_R
    at_above = 2 * side
    at_below = at_above + edge
    at_cl = at_below + edge
    at_cr = at_cl + corner
    halves = [(i, slice(i * LANES, (i + 1) * LANES)) for i in range(width // LANES)]

    step = pl.program_id(0)
    groups = HEADS // GROUP

    def copies(slot):
        at = lambda part: pl.ds((part * groups + first + slot) * width, width)
        own = [
            pltpu.make_async_copy(source.at[:, at(part)], own_refs.at[slot, i], own_sem.at[slot, i])
            for i, (source, part) in enumerate(
                ((qkv_hbm, 0), (qkv_hbm, 1), (qkv_hbm, 2), (grad_hbm, 0))
            )
        ]
        weights = [
            pltpu.make_async_copy(w_hbm.at[:, at(1 + i)], w_refs.at[slot, i], w_sem.at[slot, i])
            for i in range(2)
        ]
        return weights + own

    @pl.when(step == 0)
    def _():
        for slot in range(count):
            for copy in copies(slot):
                copy.start()
        halo_ref[:side] = left_ref[...]
        halo_ref[side:at_above] = right_ref[...]
        for above, below, size, refs_ab in (
            (at_above, at_below, edge, (rows_a, rows_b)),
            (at_cl, at_cr, corner, (corners_a, corners_b)),
        ):
            for ref, at in zip(refs_ab, (jnp.where(even, below, above), jnp.where(even, above, below))):
                halo_ref[pl.ds(pl.multiple_of(at, 16), size), :] = ref[...]
        spot_ref[...] = jnp.zeros_like(spot_ref)

    def place(target, own, weights):
        fresh = dot(halo_ref[...], weights)
        for col in range(MARGIN):
            start = MARGIN * HALO_COLS + col
            for part, at in halves:
                spot_ref[part, pl.ds(start, band_rows, stride=HALO_COLS), :] = fresh[
                    col * band_rows : (col + 1) * band_rows, at
                ]
                spot_ref[part, pl.ds(start + MARGIN, band_rows, stride=HALO_COLS), :] = fresh[
                    side + col * band_rows : side + (col + 1) * band_rows, at
                ]
        for corner_at, skip, row in ((at_cl, PAD_R, 0), (at_cr, 0, MARGIN + band_rows)):
            for col in range(2 * MARGIN):
                base = corner_at + col * EDGE_R + skip
                spot = pl.ds(row * HALO_COLS + col, MARGIN, stride=HALO_COLS)
                for part, at in halves:
                    spot_ref[part, spot, :] = fresh[base : base + MARGIN, at]
        for row in range(region_rows):
            base = row * KEY_COLS
            inner = row - MARGIN
            if inner < 0:
                ours = fresh[at_above + row * band_cols : at_above + (row + 1) * band_cols].astype(BF)
            elif inner < band_rows:
                ours = own[inner * band_cols : (inner + 1) * band_cols, :]
            else:
                past = at_below + (inner - band_rows) * band_cols
                ours = fresh[past : past + band_cols].astype(BF)
            target[base : base + band_cols, :] = ours
            for part, at in halves:
                target[base + band_cols : base + KEY_COLS, at] = spot_ref[
                    part, row * HALO_COLS : (row + 1) * HALO_COLS, :
                ].astype(BF)

    for slot in range(count):

        @pl.when(step == slot)
        def _():
            for copy in copies(slot):
                copy.wait()

    grad_ref = own_refs.at[step, 3]
    place(k_ref, own_refs.at[step, 1], w_refs[step, 0])
    place(v_ref, own_refs.at[step, 2], w_refs[step, 1])
    q_ref[...] = own_refs[step, 0] * BF(head_width**-0.5)
    dk_ref[...] = jnp.zeros_like(dk_ref)
    dv_ref[...] = jnp.zeros_like(dv_ref)

    qt_ref[...] = q_ref[...].T
    gt_ref[...] = grad_ref[...].T
    kt_ref[...] = k_ref[...].T

    row_head = lax.broadcasted_iota(jnp.int32, (lanes, LANES), 0) // queries
    lane = lax.broadcasted_iota(jnp.int32, (lanes, LANES), 1)
    first_lanes = lane < head_width
    odd_row = (row_head & 1) == 1
    pair_heads = LANES // head_width
    block_of = [row_head == part * pair_heads + (lane >= head_width) for part, _ in halves]

    def swap_halves(value):
        return jnp.concatenate([value[:, head_width:], value[:, :head_width]], axis=1)

    def spread(rows):
        block = jnp.concatenate([rows] * GROUP, axis=0)
        return jnp.concatenate(
            [
                jnp.where(block_of[part], block[:, at], jnp.zeros_like(block[:, at]))
                for part, at in halves
            ],
            axis=1,
        )

    def spread_columns(ref, pair):
        both = ref[:, pl.ds(pl.multiple_of(pair * LANES, LANES), LANES)]
        turned = swap_halves(both)
        return [
            jnp.concatenate(
                [jnp.where(block_of[part], tile, jnp.zeros_like(tile)) for part, _ in halves], axis=1
            )
            for tile in (jnp.where(first_lanes, both, turned), jnp.where(first_lanes, turned, both))
        ]

    def one_tile(tile, qt_wide, gt_wide):
        top = region_top(tile, band_start, band_rows, total_rows)
        start = pl.multiple_of(top * KEY_COLS, TILE_R * KEY_COLS)
        region = pl.ds(start, keys)
        total = pl.ds(pl.multiple_of((top + PAD_R) * KEY_COLS, PAD_R * KEY_COLS), keys)
        mine = pl.ds(pl.multiple_of(tile * queries, queries), queries)
        mask = mask_ref[tile].astype(F32)
        scores = dot(k_ref[region, :], qt_wide) + jnp.concatenate([mask, mask], axis=1)
        dots = dot(v_ref[region, :], gt_wide)
        exponent = jnp.exp(scores - jnp.max(scores, axis=0, keepdims=True))
        inverse = 1.0 / jnp.sum(exponent, axis=0, keepdims=True)
        delta = jnp.sum(exponent * dots, axis=0, keepdims=True) * inverse
        attn = exponent * inverse
        dscore = (attn * (dots - delta)).astype(BF)
        dv = dot(attn.astype(BF), spread(grad_ref[mine, :]))
        dk = dot(dscore, spread(q_ref[mine, :]))
        for part, at in halves:
            dv_ref[part, total, :] += dv[:, at]
            dk_ref[part, total, :] += dk[:, at]
        dq = dot(kt_ref[:, region], dscore)
        return jnp.where(row_head < pair_heads, dq[:, :LANES], dq[:, LANES:])

    def one_pair(pair, carry):
        qt_wide = spread_columns(qt_ref, pair)
        gt_wide = spread_columns(gt_ref, pair)
        one, two = (one_tile(2 * pair + i, qt_wide[i], gt_wide[i]) for i in range(2))
        at = pl.ds(pl.multiple_of(pair * LANES, LANES), LANES)
        dqt_ref[:, at] = jnp.where(
            first_lanes,
            jnp.where(odd_row, swap_halves(one), one),
            jnp.where(odd_row, two, swap_halves(two)),
        )
        return carry

    lax.fori_loop(0, tiles // 2, one_pair, 0, unroll=2)
    dq_ref[...] = (dqt_ref[...].T * head_width**-0.5).astype(BF)

    middle = (PAD_R + MARGIN) * KEY_COLS
    below = (PAD_R + MARGIN + band_rows) * KEY_COLS
    for part, acc in enumerate((dk_ref, dv_ref)):
        for lane, at in halves:
            for out, own_at, side_at in (
                (out_a, jnp.where(even, below, PAD_R * KEY_COLS), jnp.where(even, below, 0)),
                (out_b, jnp.where(even, PAD_R * KEY_COLS, below), jnp.where(even, 0, below)),
            ):
                for row in range(MARGIN):
                    start = pl.multiple_of(own_at + row * KEY_COLS, KEY_COLS)
                    out[part, row * band_cols : (row + 1) * band_cols, at] = acc[
                        lane, pl.ds(start, band_cols), :
                    ].astype(BF)
                for pair in range(MARGIN):
                    here = slice(edge + pair * 2 * EDGE_R, edge + (pair + 1) * 2 * EDGE_R)
                    start = side_at + band_cols + 2 * pair
                    out[part, here, at] = jnp.concatenate(
                        [
                            acc[lane, pl.ds(start, EDGE_R, stride=KEY_COLS), :],
                            acc[lane, pl.ds(start + 1, EDGE_R, stride=KEY_COLS), :],
                        ],
                        axis=0,
                    ).astype(BF)
            for row in range(band_rows):
                base = middle + row * KEY_COLS
                mid_ref[part, row * band_cols : (row + 1) * band_cols, at] = acc[
                    lane, base : base + band_cols, :
                ].astype(BF)
            for col in range(MARGIN):
                here = slice(col * band_rows, (col + 1) * band_rows)
                start = middle + band_cols + col
                to_left_ref[part, here, at] = acc[
                    lane, pl.ds(start, band_rows, stride=KEY_COLS), :
                ].astype(BF)
                to_right_ref[part, here, at] = acc[
                    lane, pl.ds(start + MARGIN, band_rows, stride=KEY_COLS), :
                ].astype(BF)


def attention_grads(
    first, count, slots, start, masks, halo, qkv, grad_out, w_qkv, shape, before, after
):
    band_rows, band_cols, total_rows = shape
    tokens, width = grad_out.shape
    head_width = width // HEADS
    block = GROUP * head_width
    region_tokens = (band_rows + 2 * MARGIN) * KEY_COLS
    total_tokens = (band_rows + 2 * MARGIN + 2 * PAD_R) * KEY_COLS
    side = MARGIN * band_rows
    edge = MARGIN * (band_cols + 2 * EDGE_R)
    corner = 2 * MARGIN * EDGE_R
    halo_tokens = 2 * (side + MARGIN * band_cols + corner)
    whole = lambda g: (0, 0)
    column = lambda offset: (lambda g: (0, offset + first + g))
    slot = lambda g: (0, 0, first % slots + g)
    halves = [(2, edge), (2, edge), (2, tokens), (2, side), (2, side)]
    out_shape = [jax.ShapeDtypeStruct((tokens, width), BF)] + [
        jax.ShapeDtypeStruct(s + (slots * block,), BF) for s in halves
    ]
    aliases = {}
    if before:
        aliases = {11 + i: place for i, (place, _) in enumerate(before)}
    return pl.pallas_call(
        functools.partial(
            attention_kernel, band_rows, band_cols, total_rows, head_width,
            len(before) + len(after), first, count,
        ),
        grid=(count,),
        in_specs=[
            pl.BlockSpec(memory_space=pltpu.SMEM),
            pl.BlockSpec(masks.shape, lambda g: (0, 0, 0)),
        ]
        + [pl.BlockSpec(piece.shape, whole) for piece in halo]
        + [pl.BlockSpec(memory_space=pltpu.HBM)] * 3
        + [pl.BlockSpec(memory_space=pl.ANY)] * (len(before) + len(after)),
        out_specs=[pl.BlockSpec((tokens, block), column(0))]
        + [pl.BlockSpec(s + (block,), slot) for s in halves],
        out_shape=out_shape,
        input_output_aliases=aliases,
        scratch_shapes=[
            pltpu.VMEM((halo_tokens, width), BF),
            pltpu.VMEM((block // LANES, (band_rows + 2 * MARGIN) * HALO_COLS, LANES), F32),
            pltpu.VMEM((tokens, block), BF),
            pltpu.VMEM((region_tokens, block), BF),
            pltpu.VMEM((region_tokens, block), BF),
            pltpu.VMEM((block, tokens), BF),
            pltpu.VMEM((block, tokens), BF),
            pltpu.VMEM((block, region_tokens), BF),
            pltpu.VMEM((block, tokens), F32),
            pltpu.VMEM((block // LANES, total_tokens, LANES), F32),
            pltpu.VMEM((block // LANES, total_tokens, LANES), F32),
            pltpu.VMEM((count, 4, tokens, block), BF),
            pltpu.VMEM((count, 2, width, block), BF),
            pltpu.SemaphoreType.DMA((count, 4)),
            pltpu.SemaphoreType.DMA((count, 2)),
        ],
        compiler_params=pltpu.CompilerParams(
            dimension_semantics=("arbitrary",), vmem_limit_bytes=ATTENTION_MIB * MIB
        ),
        cost_estimate=pl.CostEstimate(
            flops=count * 14 * 10**9, bytes_accessed=count * 8 * MIB, transcendentals=count * 10**6
        ),
    )(start, masks, *halo, qkv, grad_out, w_qkv, *[a for _, a in before], *after)


def on_chip(kernel, out_shape, operands, after=(), scratch=(), flops=10**5, place=()):
    count = len(operands) + len(place)

    def run(*refs):
        kernel(*refs[:count], *refs[count + len(after) :])

    return pl.pallas_call(
        run,
        in_specs=[pl.BlockSpec(memory_space=pltpu.SMEM)] * len(place)
        + [pl.BlockSpec(memory_space=pltpu.VMEM)] * len(operands)
        + [pl.BlockSpec(memory_space=pl.ANY)] * len(after),
        out_specs=[pl.BlockSpec(memory_space=pltpu.VMEM)] * len(out_shape),
        out_shape=[jax.ShapeDtypeStruct(s, d) for s, d in out_shape],
        scratch_shapes=list(scratch),
        compiler_params=pltpu.CompilerParams(vmem_limit_bytes=24 * MIB),
        cost_estimate=pl.CostEstimate(flops=flops, bytes_accessed=10**4, transcendentals=0),
    )(*place, *operands, *after)


def lanes_of(width):
    return [(i, slice(i * LANES, (i + 1) * LANES)) for i in range(width // LANES)]


def project(own, w_qkv, after):
    tokens, width = own.shape
    columns = w_qkv.shape[1]
    block = 4 * LANES

    def kernel(own_ref, w_ref, *refs):
        refs[-1][...] = dot(own_ref[...], w_ref[...]).astype(BF)

    return pl.pallas_call(
        kernel,
        grid=(columns // block,),
        in_specs=[
            pl.BlockSpec((tokens, width), lambda g: (0, 0)),
            pl.BlockSpec((width, block), lambda g: (0, g)),
        ]
        + [pl.BlockSpec(memory_space=pl.ANY)] * len(after),
        out_specs=pl.BlockSpec((tokens, block), lambda g: (0, g)),
        out_shape=jax.ShapeDtypeStruct((tokens, columns), BF),
        compiler_params=pltpu.CompilerParams(vmem_limit_bytes=24 * MIB),
        cost_estimate=pl.CostEstimate(flops=10**9, bytes_accessed=MIB, transcendentals=0),
    )(own, w_qkv, *after)


def row_blocks(place, own, orders, after):
    tokens, width = own.shape
    devices = len(orders[0])
    size = width // devices
    step = max(1, 16 // size)

    def kernel(place_ref, own_ref, low_ref, high_ref, wide_ref):
        for at in range(0, width, 2 * LANES):
            wide_ref[at : at + 2 * LANES, :] = own_ref[:, at : at + 2 * LANES].astype(F32).T
        even = place_ref[1] == 0
        me = place_ref[2]
        for j in range(0, devices, step):
            rows = []
            for k in range(j, j + step):
                owner = me ^ jnp.where(even, int(orders[0][k]), int(orders[1][k]))
                rows.append(wide_ref[pl.ds(pl.multiple_of(owner * size, size), size), :])
            half, base = divmod(j * size, width // 2)
            block = rows[0] if step == 1 else jnp.concatenate(rows, axis=0)
            (low_ref, high_ref)[half][base : base + step * size, :] = block.astype(BF)

    out = ((width // 2, tokens), BF)
    scratch = [pltpu.VMEM((width, tokens), F32)]
    return on_chip(kernel, [out, out], [own], after=after, scratch=scratch, place=[place])


def pack_sides(own, band_rows, band_cols):
    tokens, width = own.shape

    def kernel(own_ref, last_ref, first_ref, wide_ref):
        for lane, at in lanes_of(width):
            wide_ref[lane] = own_ref[:, at].astype(F32)
            for col in range(MARGIN):
                here = slice(col * band_rows, (col + 1) * band_rows)
                last = pl.ds(band_cols - MARGIN + col, band_rows, stride=band_cols)
                last_ref[here, at] = wide_ref[lane, last, :].astype(BF)
                first = pl.ds(col, band_rows, stride=band_cols)
                first_ref[here, at] = wide_ref[lane, first, :].astype(BF)

    out = ((MARGIN * band_rows, width), BF)
    scratch = [pltpu.VMEM((width // LANES, tokens, LANES), F32)]
    return on_chip(kernel, [out, out], [own], scratch=scratch)


def pack_rows(place, own, band_cols, after):
    tokens, width = own.shape
    edge = MARGIN * band_cols

    def kernel(place_ref, own_ref, out_a, out_b):
        even = place_ref[1] == 0
        last, first = own_ref[tokens - edge :, :], own_ref[:edge, :]
        out_a[...] = jnp.where(even, last, first)
        out_b[...] = jnp.where(even, first, last)

    out = ((edge, width), BF)
    return on_chip(kernel, [out, out], [own], after=after, place=[place])


def pack_corners(place, left, right, band_rows, after):
    width = left.shape[1]

    def kernel(place_ref, left_ref, right_ref, out_a, out_b):
        even = place_ref[1] == 0
        for side, side_ref in enumerate((left_ref, right_ref)):
            for col in range(0, MARGIN, 2):
                base = (side * MARGIN + col) * EDGE_R
                last, first = (
                    jnp.concatenate(
                        [
                            side_ref[at : at + EDGE_R, :].astype(F32)
                            for at in (start, start + band_rows)
                        ]
                    )
                    for start in ((col + 1) * band_rows - EDGE_R, col * band_rows)
                )
                here = slice(base, base + 2 * EDGE_R)
                out_a[here, :] = jnp.where(even, last, first).astype(BF)
                out_b[here, :] = jnp.where(even, first, last).astype(BF)

    out = ((2 * MARGIN * EDGE_R, width), BF)
    return on_chip(kernel, [out, out], [left, right], after=after, place=[place])


def merge_sides(place, left, right, rim_a, rim_b, band_rows, band_cols, after=()):
    edge = MARGIN * band_cols

    def kernel(place_ref, left_ref, right_ref, a_ref, b_ref, ol_ref, or_ref):
        even = place_ref[1] == 0
        for part in range(2):
            for col in range(2 * MARGIN):
                source, target = (left_ref, ol_ref) if col < MARGIN else (right_ref, or_ref)
                base = (col % MARGIN) * band_rows
                pair = slice(edge + (col // 2) * 2 * EDGE_R, edge + (col // 2 + 1) * 2 * EDGE_R)
                odd = slice((col % 2) * EDGE_R, (col % 2 + 1) * EDGE_R)
                rows = source[part, base : base + band_rows, :].astype(F32)
                rim_a, rim_b = (ref[part, pair, :].astype(F32)[odd] for ref in (a_ref, b_ref))
                first = rows[:EDGE_R] + jnp.where(even, rim_b, rim_a)
                last = rows[band_rows - EDGE_R :] + jnp.where(even, rim_a, rim_b)
                target[part, base : base + band_rows, :] = jnp.concatenate(
                    [first, rows[EDGE_R : band_rows - EDGE_R], last], axis=0
                ).astype(BF)

    out = [(left.shape, BF), (right.shape, BF)]
    return on_chip(kernel, out, [left, right, rim_a, rim_b], after=after, place=[place])


def finish(place, mid, rim_a, rim_b, left, right, band_rows, band_cols, after, flops):
    _, tokens, width = mid.shape
    edge = MARGIN * band_cols

    def kernel(place_ref, mid_ref, a_ref, b_ref, left_ref, right_ref, out_ref, acc_ref):
        even = place_ref[1] == 0
        for part in range(2):
            for block in range(width // (2 * LANES)):
                for lane in range(2):
                    at = slice((2 * block + lane) * LANES, (2 * block + lane + 1) * LANES)
                    acc_ref[lane] = mid_ref[part, :, at].astype(F32)
                    from_a, from_b = (r[part, :edge, at].astype(F32) for r in (a_ref, b_ref))
                    acc_ref[lane, :edge, :] += jnp.where(even, from_b, from_a)
                    acc_ref[lane, tokens - edge :, :] += jnp.where(even, from_a, from_b)
                    for col in range(MARGIN):
                        here = slice(col * band_rows, (col + 1) * band_rows)
                        first = pl.ds(col, band_rows, stride=band_cols)
                        last = pl.ds(band_cols - MARGIN + col, band_rows, stride=band_cols)
                        acc_ref[lane, first, :] += left_ref[part, here, at].astype(F32)
                        acc_ref[lane, last, :] += right_ref[part, here, at].astype(F32)
                both = jnp.concatenate([acc_ref[0], acc_ref[1]], axis=1).astype(BF)
                start = part * width + block * 2 * LANES
                out_ref[:, start : start + 2 * LANES] = both

    out = [((tokens, 2 * width), BF)]
    scratch = [pltpu.VMEM((2, tokens, LANES), F32)]
    operands = [mid, rim_a, rim_b, left, right]
    return on_chip(kernel, out, operands, after, scratch, flops, [place])[0]


def grad_rows(rows, columns, scale, kind, after=()):
    features, count = rows.shape[0], len(columns)
    width = columns[0].shape[1]

    def kernel(rows_ref, *refs):
        for i, columns_ref in enumerate(refs[:count]):
            for start in range(0, width, 2 * LANES):
                part = dot(rows_ref[...], columns_ref[:, start : start + 2 * LANES])
                at = i * width + start
                refs[count][:, at : at + 2 * LANES] = (part * scale).astype(kind)

    return on_chip(kernel, [((features, count * width), kind)], [rows, *columns], after)[0]


def add_split(keep, received, after=()):
    half, columns = keep.shape[0] // 2, keep.shape[1]

    def kernel(keep_ref, received_ref, sums_ref, send_ref):
        sums_ref[...] = keep_ref[:half, :] + received_ref[:half, :].astype(F32)
        send_ref[...] = (keep_ref[half:, :] + received_ref[half:, :].astype(F32)).astype(BF)

    return on_chip(kernel, [((half, columns), F32), ((half, columns), BF)], [keep, received], after)


def add_blocks(keep, received, blocks):
    rows, columns = keep.shape
    size = rows // blocks

    def kernel(keep_ref, received_ref, sums_ref, *sends):
        total = keep_ref[...] + received_ref[...].astype(F32)
        sums_ref[...] = total[:size]
        for b in range(1, blocks):
            sends[b - 1][...] = total[b * size : (b + 1) * size].astype(BF)

    out = [((size, columns), F32)] + [((size, columns), BF)] * (blocks - 1)
    keep, *send = on_chip(kernel, out, [keep, received])
    return keep, send


def gather_sums(groups, places, width):
    flat = [a for group in groups for a in group]

    def kernel(*refs):
        out_ref = refs[-1]
        at = 0
        for group, moves in zip(groups, places):
            total = refs[at][...]
            for ref in refs[at + 1 : at + len(group)]:
                total = total + ref[...].astype(F32)
            at += len(group)
            for source, size, target in moves:
                out_ref[:, target : target + size] = total[:, source : source + size]

    return on_chip(kernel, [((flat[0].shape[0], width), F32)], flat)[0]


def shifted(array, axis, by, wrap):
    size = lax.axis_size(axis)
    route = [(i, (i + by) % size) for i in range(size) if wrap or 0 <= i + by < size]
    return lax.ppermute(array, axis, route)


def swapped(array_a, array_b, axis):
    size = lax.axis_size(axis)
    pairs = [(i, i + 1) for i in range(size - 1)]
    route = lambda chosen: chosen + [(j, i) for i, j in chosen]
    return [
        lax.ppermute(array, axis, route(pairs[offset::2]))
        for array, offset in ((array_a, 0), (array_b, 1))
    ]


def exchanged(array, axis, flip):
    return lax.ppermute(array, axis, [(i, i ^ flip) for i in range(lax.axis_size(axis))])


def bits_of(axis):
    return [(axis, 1 << b) for b in range((lax.axis_size(axis) - 1).bit_length())]


def reduce_stages():
    first, *lat_bits = bits_of("lat")
    bits = bits_of("dp") + lat_bits
    return first, list(zip(bits, reversed(bits)))


def feature_orders(first, stages):
    n_lon, n_lat = lax.axis_size("lon"), lax.axis_size("lat")
    unit = {"lon": 1, "lat": n_lon, "dp": n_lon * n_lat}
    lower = []
    for kind in range(2):
        order = np.arange(n_lon)
        for stage in reversed(stages):
            axis, bit = stage[kind]
            order = np.concatenate([order, order + unit[axis] * bit])
        lower.append(order)
    flip = unit[first[0]] * first[1]
    return [np.concatenate([lower[kind], lower[1 - kind] ^ flip]) for kind in range(2)]


def exchanged_stage(array, stage):
    n_lat, n_dp = lax.axis_size("lat"), lax.axis_size("dp")
    route = []
    for i in range(n_dp * n_lat):
        axis, bit = stage[i % n_lat % 2]
        route.append((i, i ^ (bit * n_lat if axis == "dp" else bit)))
    return lax.ppermute(array, ("dp", "lat"), route)


def body(inputs, grad_out, w_qkv):
    _, band_rows, band_cols, width = inputs.shape
    n_lat, n_lon, n_dp = lax.axis_size("lat"), lax.axis_size("lon"), lax.axis_size("dp")
    band_start = lax.axis_index("lat") * band_rows
    total_rows = band_rows * n_lat
    tokens = band_rows * band_cols
    slots = HEADS // GROUP // 2
    shape = (band_rows, band_cols, total_rows)
    own = inputs.reshape(tokens, width)
    flat_grad = grad_out.reshape(tokens, width)

    last_cols, first_cols = pack_sides(own, band_rows, band_cols)
    left = shifted(last_cols, "lon", 1, True)
    right = shifted(first_cols, "lon", -1, True)
    me = (lax.axis_index("dp") * n_lat + lax.axis_index("lat")) * n_lon + lax.axis_index("lon")
    start = jnp.stack([band_start, lax.axis_index("lat") % 2, me])
    rim_rows = swapped(*pack_rows(start, own, band_cols, [last_cols]), "lat")

    masks = window_masks(start, band_rows, band_cols, total_rows)
    qkv = project(own, w_qkv, [last_cols])
    first, stages = reduce_stages()
    half = width // 2
    rows_keep, rows_send = row_blocks(start, own, feature_orders(first, stages), [last_cols])
    corners = pack_corners(start, left, right, band_rows, [masks, qkv, rows_keep, rows_send])
    halo = (left, right, *rim_rows, *swapped(*corners, "lat"))
    scale = float(tokens * n_dp * n_lat * n_lon) ** -0.5

    attend = lambda first, count, before, after: attention_grads(
        first, count, slots, start, masks, halo, qkv, flat_grad, w_qkv, shape, before, after
    )

    def return_sides(grads, rims, after):
        to_left, to_right = merge_sides(
            start, grads[4], grads[5], *rims, band_rows, band_cols, after
        )
        from_right = shifted(to_left, "lon", -1, True)
        from_left = shifted(to_right, "lon", 1, True)
        return to_left, from_left, from_right

    one = attend(0, slots, [], [])
    rims_1 = swapped(one[1], one[2], "lat")
    two = attend(slots, 1, [(0, one[0])], [])
    sent, *sides_1 = return_sides(one, rims_1, [two[1]])
    two = attend(slots + 1, 1, list(enumerate(two)), [sent])
    rims_2 = swapped(two[1], two[2], "lat")
    dq = two[0]

    dkv_1 = finish(start, one[3], *rims_1, *sides_1, band_rows, band_cols, [dq], 2 * 10**9)
    sent, *sides_2 = return_sides(two, rims_2, [dkv_1])
    send = grad_rows(rows_send, [dq, dkv_1], scale, BF, after=[sent])
    received = exchanged(send, *first)
    keep = grad_rows(rows_keep, [dq, dkv_1], scale, F32, after=[send])
    keep, send = add_split(keep, received)

    dkv_2 = finish(start, two[3], *rims_2, *sides_2, band_rows, band_cols, [keep], FINISH_FLOPS)
    for stage in stages[:-1]:
        keep, send = add_split(keep, exchanged_stage(send, stage), [dkv_2])
    send_2 = grad_rows(rows_send, [dkv_2], scale, BF, after=[keep])
    received_2 = exchanged(send_2, *first)
    keep_2 = grad_rows(rows_keep, [dkv_2], scale, F32, after=[send_2])
    keep, send = add_blocks(keep, exchanged_stage(send, stages[-1]), n_lon)
    group_1 = [keep] + [exchanged(a, "lon", i + 1) for i, a in enumerate(send)]
    for stage in stages:
        keep_2, send_2 = add_split(keep_2, received_2)
        received_2 = exchanged_stage(send_2, stage)
    keep_2, send_2 = add_blocks(keep_2, received_2, n_lon)
    group_2 = [keep_2] + [exchanged(a, "lon", i + 1) for i, a in enumerate(send_2)]
    places = [
        [(0, width, 0), (width, half, width), (width + half, half, 2 * width)],
        [(0, half, width + half), (half, half, 2 * width + half)],
    ]
    grad_w = gather_sums([group_1, group_2], places, 3 * width)

    grad_proj = jnp.concatenate(
        [dq, dkv_1[:, :half], dkv_2[:, :half], dkv_1[:, half:], dkv_2[:, half:]], axis=1
    )
    grad_inputs = dot(grad_proj, w_qkv, NT).astype(BF).reshape(inputs.shape)
    return (grad_inputs, grad_w)


def solution(mesh):
    in_specs = (P("dp", "lat", "lon", None), P("dp", "lat", "lon", None), P())
    out_specs = (P("dp", "lat", "lon", None), P(("dp", "lat", "lon"), None))
    return jax.shard_map(body, mesh=mesh, in_specs=in_specs, out_specs=out_specs, check_vma=False)
```

```python
import functools

import jax
import jax.numpy as jnp
import numpy as np
from jax import lax
from jax.experimental import pallas as pl
from jax.experimental.pallas import tpu as pltpu
from jax.sharding import PartitionSpec as P

HEADS = 16
WIN = 13
MARGIN = WIN // 2
TILE_R = 4
GROUP = 4
KEY_COLS = 32
HALO_COLS = 16
REGION_R = 16
PAD_R = 2
EDGE_R = MARGIN + PAD_R
NEG = -1e30
BF = jnp.bfloat16
F32 = jnp.float32
MIB = 1024 * 1024
GATHER_FLOPS = 4 * 10**9
FINISH_FLOPS = 9 * 10**9
LANES = 128
ATTENTION_MIB = 46

NT = (((1,), (1,)), ((), ()))
TN = (((0,), (0,)), ((), ()))
NN = (((1,), (0,)), ((), ()))


def dot(a, b, dims=NN):
    return lax.dot_general(a, b, dims, preferred_element_type=F32)


def region_top(tile, band_start, band_rows, total_rows):
    lowest = jnp.where(band_start == 0, TILE_R, 0)
    highest = jnp.where(band_start + band_rows == total_rows, band_rows - 2 * TILE_R, band_rows)
    return jnp.clip(tile * TILE_R, lowest, highest)


def mask_kernel(band_rows, band_cols, total_rows, start_ref, mask_ref):
    band_start = start_ref[0]
    tile = pl.program_id(0)
    shape = mask_ref.shape[1:]
    first = region_top(tile, band_start, band_rows, total_rows)
    key = lax.broadcasted_iota(jnp.int32, shape, 0)
    query = lax.broadcasted_iota(jnp.int32, shape, 1) & (TILE_R * band_cols - 1)
    key_row = band_start - MARGIN + first + (key >> (KEY_COLS.bit_length() - 1))
    place = key & (KEY_COLS - 1)
    query_row = band_start + tile * TILE_R + (query >> (band_cols.bit_length() - 1))
    query_col = query & (band_cols - 1)
    window = jnp.clip(query_row - MARGIN, 0, total_rows - WIN)
    row_inside = (key_row >= window) & (key_row < window + WIN)
    key_col = jnp.where(
        place < band_cols,
        place,
        jnp.where(place < band_cols + MARGIN, place - band_cols - MARGIN, place - MARGIN),
    )
    col_inside = (jnp.abs(key_col - query_col) <= MARGIN) & (place < band_cols + 2 * MARGIN)
    mask_ref[0] = jnp.where(row_inside & col_inside, 0.0, NEG).astype(BF)


def window_masks(start, band_rows, band_cols, total_rows):
    tiles = band_rows // TILE_R
    shape = (REGION_R * KEY_COLS, 2 * TILE_R * band_cols)
    return pl.pallas_call(
        functools.partial(mask_kernel, band_rows, band_cols, total_rows),
        grid=(tiles,),
        in_specs=[pl.BlockSpec(memory_space=pltpu.SMEM)],
        out_specs=pl.BlockSpec((1,) + shape, lambda t: (t, 0, 0)),
        out_shape=jax.ShapeDtypeStruct((tiles,) + shape, BF),
        cost_estimate=pl.CostEstimate(flops=10**7, bytes_accessed=2**21, transcendentals=0),
    )(start)


def attention_kernel(band_rows, band_cols, total_rows, head_width, extra, first, count, *refs):
    (place_ref, mask_ref, left_ref, right_ref, rows_a, rows_b, corners_a, corners_b,
     qkv_hbm, grad_hbm, w_hbm) = refs[:11]
    (dq_ref, out_a, out_b, mid_ref, to_left_ref, to_right_ref,
     halo_ref, spot_ref, q_ref, k_ref, v_ref, dk_ref, dv_ref,
     own_refs, w_refs, own_sem, w_sem) = refs[11 + extra :]
    band_start = place_ref[0]
    even = place_ref[1] == 0
    tiles = band_rows // TILE_R
    queries = TILE_R * band_cols
    keys = REGION_R * KEY_COLS
    width = GROUP * head_width
    lanes = GROUP * queries
    region_rows = band_rows + 2 * MARGIN
    side = MARGIN * band_rows
    edge = MARGIN * band_cols
    corner = 2 * MARGIN * EDGE_R
    at_above = 2 * side
    at_below = at_above + edge
    at_cl = at_below + edge
    at_cr = at_cl + corner
    halves = [(i, slice(i * LANES, (i + 1) * LANES)) for i in range(width // LANES)]

    step = pl.program_id(0)
    groups = HEADS // GROUP

    def copies(slot, parts):
        at = lambda part: pl.ds((part * groups + first + slot) * width, width)
        for part, source, where, i in parts:
            target, sem = (w_refs, w_sem) if where else (own_refs, own_sem)
            yield pltpu.make_async_copy(source.at[:, at(part)], target.at[slot, i], sem.at[slot, i])

    for_k = ((1, w_hbm, 1, 0), (1, qkv_hbm, 0, 1))
    for_v = ((2, w_hbm, 1, 1), (2, qkv_hbm, 0, 2))
    for_q = ((0, qkv_hbm, 0, 0), (0, grad_hbm, 0, 3))

    def await_copies(parts):
        for slot in range(count):

            @pl.when(step == slot)
            def _():
                for copy in copies(slot, parts):
                    copy.wait()

    @pl.when(step == 0)
    def _():
        for slot in range(count):
            for copy in copies(slot, for_k + for_v + for_q):
                copy.start()
        halo_ref[:side] = left_ref[...]
        halo_ref[side:at_above] = right_ref[...]
        for above, below, size, refs_ab in (
            (at_above, at_below, edge, (rows_a, rows_b)),
            (at_cl, at_cr, corner, (corners_a, corners_b)),
        ):
            for ref, at in zip(refs_ab, (jnp.where(even, below, above), jnp.where(even, above, below))):
                halo_ref[pl.ds(pl.multiple_of(at, 16), size), :] = ref[...]
        spot_ref[...] = jnp.zeros_like(spot_ref)

    def place(target, own, weights):
        fresh = dot(halo_ref[...], weights)
        for col in range(MARGIN):
            start = MARGIN * HALO_COLS + col
            for part, at in halves:
                spot_ref[part, pl.ds(start, band_rows, stride=HALO_COLS), :] = fresh[
                    col * band_rows : (col + 1) * band_rows, at
                ]
                spot_ref[part, pl.ds(start + MARGIN, band_rows, stride=HALO_COLS), :] = fresh[
                    side + col * band_rows : side + (col + 1) * band_rows, at
                ]
        for corner_at, skip, row in ((at_cl, PAD_R, 0), (at_cr, 0, MARGIN + band_rows)):
            for col in range(2 * MARGIN):
                base = corner_at + col * EDGE_R + skip
                spot = pl.ds(row * HALO_COLS + col, MARGIN, stride=HALO_COLS)
                for part, at in halves:
                    spot_ref[part, spot, :] = fresh[base : base + MARGIN, at]
        for row in range(region_rows):
            base = row * KEY_COLS
            inner = row - MARGIN
            if inner < 0:
                ours = fresh[at_above + row * band_cols : at_above + (row + 1) * band_cols].astype(BF)
            elif inner < band_rows:
                ours = own[inner * band_cols : (inner + 1) * band_cols, :]
            else:
                past = at_below + (inner - band_rows) * band_cols
                ours = fresh[past : past + band_cols].astype(BF)
            target[base : base + band_cols, :] = ours
            for part, at in halves:
                target[base + band_cols : base + KEY_COLS, at] = spot_ref[
                    part, row * HALO_COLS : (row + 1) * HALO_COLS, :
                ].astype(BF)

    grad_ref = own_refs.at[step, 3]
    await_copies(for_k)
    place(k_ref, own_refs.at[step, 1], w_refs[step, 0])
    await_copies(for_v)
    place(v_ref, own_refs.at[step, 2], w_refs[step, 1])
    await_copies(for_q)
    q_ref[...] = own_refs[step, 0] * BF(head_width**-0.5)
    dk_ref[...] = jnp.zeros_like(dk_ref)
    dv_ref[...] = jnp.zeros_like(dv_ref)

    def spread(rows):
        block = jnp.concatenate([rows] * GROUP, axis=0)
        head_row = lax.broadcasted_iota(jnp.int32, (lanes, width), 0) // queries
        head_col = lax.broadcasted_iota(jnp.int32, (lanes, width), 1) // head_width
        return jnp.where(head_row == head_col, block, jnp.zeros_like(block))

    def one_tile(tile, carry):
        first = region_top(tile, band_start, band_rows, total_rows)
        region = pl.ds(pl.multiple_of(first * KEY_COLS, TILE_R * KEY_COLS), keys)
        total = pl.ds(pl.multiple_of((first + PAD_R) * KEY_COLS, PAD_R * KEY_COLS), keys)
        mine = pl.ds(pl.multiple_of(tile * queries, queries), queries)
        q_wide = spread(q_ref[mine, :])
        g_wide = spread(grad_ref[mine, :])
        mask = mask_ref[tile].astype(F32)
        scores = dot(k_ref[region, :], q_wide, NT) + jnp.concatenate([mask, mask], axis=1)
        dots = dot(v_ref[region, :], g_wide, NT)
        exponent = jnp.exp(scores - jnp.max(scores, axis=0, keepdims=True))
        inverse = 1.0 / jnp.sum(exponent, axis=0, keepdims=True)
        delta = jnp.sum(exponent * dots, axis=0, keepdims=True) * inverse
        attn = exponent * inverse
        dscore = (attn * (dots - delta)).astype(BF)
        dv = dot(attn.astype(BF), g_wide)
        dk = dot(dscore, q_wide)
        for part, at in halves:
            dv_ref[part, total, :] += dv[:, at]
            dk_ref[part, total, :] += dk[:, at]
        dq_wide = dot(dscore, k_ref[region, :], TN)
        head_col = lax.broadcasted_iota(jnp.int32, (queries, width), 1) // head_width
        dq = jnp.zeros((queries, width), F32)
        for head in range(GROUP):
            dq = jnp.where(head_col == head, dq_wide[head * queries : (head + 1) * queries], dq)
        dq_ref[mine, :] = (dq * head_width**-0.5).astype(BF)
        return carry

    lax.fori_loop(0, tiles, one_tile, 0, unroll=4)

    middle = (PAD_R + MARGIN) * KEY_COLS
    below = (PAD_R + MARGIN + band_rows) * KEY_COLS
    for part, acc in enumerate((dk_ref, dv_ref)):
        for lane, at in halves:
            for out, own_at, side_at in (
                (out_a, jnp.where(even, below, PAD_R * KEY_COLS), jnp.where(even, below, 0)),
                (out_b, jnp.where(even, PAD_R * KEY_COLS, below), jnp.where(even, 0, below)),
            ):
                for row in range(MARGIN):
                    start = pl.multiple_of(own_at + row * KEY_COLS, KEY_COLS)
                    out[part, row * band_cols : (row + 1) * band_cols, at] = acc[
                        lane, pl.ds(start, band_cols), :
                    ].astype(BF)
                for pair in range(MARGIN):
                    here = slice(edge + pair * 2 * EDGE_R, edge + (pair + 1) * 2 * EDGE_R)
                    start = side_at + band_cols + 2 * pair
                    out[part, here, at] = jnp.concatenate(
                        [
                            acc[lane, pl.ds(start, EDGE_R, stride=KEY_COLS), :],
                            acc[lane, pl.ds(start + 1, EDGE_R, stride=KEY_COLS), :],
                        ],
                        axis=0,
                    ).astype(BF)
            for row in range(band_rows):
                base = middle + row * KEY_COLS
                mid_ref[part, row * band_cols : (row + 1) * band_cols, at] = acc[
                    lane, base : base + band_cols, :
                ].astype(BF)
            for col in range(MARGIN):
                here = slice(col * band_rows, (col + 1) * band_rows)
                start = middle + band_cols + col
                to_left_ref[part, here, at] = acc[
                    lane, pl.ds(start, band_rows, stride=KEY_COLS), :
                ].astype(BF)
                to_right_ref[part, here, at] = acc[
                    lane, pl.ds(start + MARGIN, band_rows, stride=KEY_COLS), :
                ].astype(BF)


def attention_grads(
    first, count, slots, start, masks, halo, qkv, grad_out, w_qkv, shape, before, after
):
    band_rows, band_cols, total_rows = shape
    tokens, width = grad_out.shape
    head_width = width // HEADS
    block = GROUP * head_width
    region_tokens = (band_rows + 2 * MARGIN) * KEY_COLS
    total_tokens = (band_rows + 2 * MARGIN + 2 * PAD_R) * KEY_COLS
    side = MARGIN * band_rows
    edge = MARGIN * (band_cols + 2 * EDGE_R)
    corner = 2 * MARGIN * EDGE_R
    halo_tokens = 2 * (side + MARGIN * band_cols + corner)
    whole = lambda g: (0, 0)
    column = lambda offset: (lambda g: (0, offset + first + g))
    slot = lambda g: (0, 0, first % slots + g)
    halves = [(2, edge), (2, edge), (2, tokens), (2, side), (2, side)]
    out_shape = [jax.ShapeDtypeStruct((tokens, width), BF)] + [
        jax.ShapeDtypeStruct(s + (slots * block,), BF) for s in halves
    ]
    aliases = {}
    if before:
        aliases = {11 + i: place for i, (place, _) in enumerate(before)}
    return pl.pallas_call(
        functools.partial(
            attention_kernel, band_rows, band_cols, total_rows, head_width,
            len(before) + len(after), first, count,
        ),
        grid=(count,),
        in_specs=[
            pl.BlockSpec(memory_space=pltpu.SMEM),
            pl.BlockSpec(masks.shape, lambda g: (0, 0, 0)),
        ]
        + [pl.BlockSpec(piece.shape, whole) for piece in halo]
        + [pl.BlockSpec(memory_space=pltpu.HBM)] * 3
        + [pl.BlockSpec(memory_space=pl.ANY)] * (len(before) + len(after)),
        out_specs=[pl.BlockSpec((tokens, block), column(0))]
        + [pl.BlockSpec(s + (block,), slot) for s in halves],
        out_shape=out_shape,
        input_output_aliases=aliases,
        scratch_shapes=[
            pltpu.VMEM((halo_tokens, width), BF),
            pltpu.VMEM((block // LANES, (band_rows + 2 * MARGIN) * HALO_COLS, LANES), F32),
            pltpu.VMEM((tokens, block), BF),
            pltpu.VMEM((region_tokens, block), BF),
            pltpu.VMEM((region_tokens, block), BF),
            pltpu.VMEM((block // LANES, total_tokens, LANES), F32),
            pltpu.VMEM((block // LANES, total_tokens, LANES), F32),
            pltpu.VMEM((count, 4, tokens, block), BF),
            pltpu.VMEM((count, 2, width, block), BF),
            pltpu.SemaphoreType.DMA((count, 4)),
            pltpu.SemaphoreType.DMA((count, 2)),
        ],
        compiler_params=pltpu.CompilerParams(
            dimension_semantics=("arbitrary",), vmem_limit_bytes=ATTENTION_MIB * MIB
        ),
        cost_estimate=pl.CostEstimate(
            flops=count * 14 * 10**9, bytes_accessed=count * 8 * MIB, transcendentals=count * 10**6
        ),
    )(start, masks, *halo, qkv, grad_out, w_qkv, *[a for _, a in before], *after)


def on_chip(kernel, out_shape, operands, after=(), scratch=(), flops=10**5, place=()):
    count = len(operands) + len(place)

    def run(*refs):
        kernel(*refs[:count], *refs[count + len(after) :])

    return pl.pallas_call(
        run,
        in_specs=[pl.BlockSpec(memory_space=pltpu.SMEM)] * len(place)
        + [pl.BlockSpec(memory_space=pltpu.VMEM)] * len(operands)
        + [pl.BlockSpec(memory_space=pl.ANY)] * len(after),
        out_specs=[pl.BlockSpec(memory_space=pltpu.VMEM)] * len(out_shape),
        out_shape=[jax.ShapeDtypeStruct(s, d) for s, d in out_shape],
        scratch_shapes=list(scratch),
        compiler_params=pltpu.CompilerParams(vmem_limit_bytes=24 * MIB),
        cost_estimate=pl.CostEstimate(flops=flops, bytes_accessed=10**4, transcendentals=0),
    )(*place, *operands, *after)


def lanes_of(width):
    return [(i, slice(i * LANES, (i + 1) * LANES)) for i in range(width // LANES)]


def project(own, w_qkv, after):
    tokens, width = own.shape
    columns = w_qkv.shape[1]
    block = 4 * LANES

    def kernel(own_ref, w_ref, *refs):
        refs[-1][...] = dot(own_ref[...], w_ref[...]).astype(BF)

    return pl.pallas_call(
        kernel,
        grid=(columns // block,),
        in_specs=[
            pl.BlockSpec((tokens, width), lambda g: (0, 0)),
            pl.BlockSpec((width, block), lambda g: (0, g)),
        ]
        + [pl.BlockSpec(memory_space=pl.ANY)] * len(after),
        out_specs=pl.BlockSpec((tokens, block), lambda g: (0, g)),
        out_shape=jax.ShapeDtypeStruct((tokens, columns), BF),
        compiler_params=pltpu.CompilerParams(vmem_limit_bytes=24 * MIB),
        cost_estimate=pl.CostEstimate(flops=10**9, bytes_accessed=MIB, transcendentals=0),
    )(own, w_qkv, *after)


def input_grads(dq, dkv_1, dkv_2, w_qkv, after):
    tokens, width = dq.shape
    half = width // 2
    pieces = [(0, 0), (0, 1), (1, 0), (2, 0), (1, 1), (2, 1)]

    def kernel(*refs):
        w_ref, out_ref, acc_ref = refs[3], refs[-2], refs[-1]
        for step, (array, part) in enumerate(pieces):

            @pl.when(pl.program_id(0) == step)
            def _():
                product = dot(refs[array][:, part * half : (part + 1) * half], w_ref[...], NT)
                if step == 0:
                    acc_ref[...] = product
                elif step < len(pieces) - 1:
                    acc_ref[...] += product
                else:
                    out_ref[...] = (acc_ref[...] + product).astype(BF)

    whole = pl.BlockSpec((tokens, width), lambda g: (0, 0))
    return pl.pallas_call(
        kernel,
        grid=(len(pieces),),
        in_specs=[whole, whole, whole, pl.BlockSpec((width, half), lambda g: (0, g))]
        + [pl.BlockSpec(memory_space=pl.ANY)] * len(after),
        out_specs=whole,
        out_shape=jax.ShapeDtypeStruct((tokens, width), BF),
        scratch_shapes=[pltpu.VMEM((tokens, width), F32)],
        compiler_params=pltpu.CompilerParams(vmem_limit_bytes=24 * MIB),
        cost_estimate=pl.CostEstimate(flops=4 * 10**9, bytes_accessed=MIB, transcendentals=0),
    )(dq, dkv_1, dkv_2, w_qkv, *after)


def row_blocks(place, own, orders, after):
    tokens, width = own.shape
    devices = len(orders[0])
    size = width // devices
    step = max(1, 16 // size)

    def kernel(place_ref, own_ref, low_ref, high_ref, wide_ref):
        for at in range(0, width, 2 * LANES):
            wide_ref[at : at + 2 * LANES, :] = own_ref[:, at : at + 2 * LANES].astype(F32).T
        even = place_ref[1] == 0
        me = place_ref[2]
        for j in range(0, devices, step):
            rows = []
            for k in range(j, j + step):
                owner = me ^ jnp.where(even, int(orders[0][k]), int(orders[1][k]))
                rows.append(wide_ref[pl.ds(pl.multiple_of(owner * size, size), size), :])
            half, base = divmod(j * size, width // 2)
            block = rows[0] if step == 1 else jnp.concatenate(rows, axis=0)
            (low_ref, high_ref)[half][base : base + step * size, :] = block.astype(BF)

    out = ((width // 2, tokens), BF)
    scratch = [pltpu.VMEM((width, tokens), F32)]
    return on_chip(kernel, [out, out], [own], after=after, scratch=scratch, place=[place])


def pack_sides(own, band_rows, band_cols):
    tokens, width = own.shape

    def kernel(own_ref, last_ref, first_ref, wide_ref):
        for lane, at in lanes_of(width):
            wide_ref[lane] = own_ref[:, at].astype(F32)
            for col in range(MARGIN):
                here = slice(col * band_rows, (col + 1) * band_rows)
                last = pl.ds(band_cols - MARGIN + col, band_rows, stride=band_cols)
                last_ref[here, at] = wide_ref[lane, last, :].astype(BF)
                first = pl.ds(col, band_rows, stride=band_cols)
                first_ref[here, at] = wide_ref[lane, first, :].astype(BF)

    out = ((MARGIN * band_rows, width), BF)
    scratch = [pltpu.VMEM((width // LANES, tokens, LANES), F32)]
    return on_chip(kernel, [out, out], [own], scratch=scratch)


def pack_rows(place, own, band_cols, after):
    tokens, width = own.shape
    edge = MARGIN * band_cols

    def kernel(place_ref, own_ref, out_a, out_b):
        even = place_ref[1] == 0
        last, first = own_ref[tokens - edge :, :], own_ref[:edge, :]
        out_a[...] = jnp.where(even, last, first)
        out_b[...] = jnp.where(even, first, last)

    out = ((edge, width), BF)
    return on_chip(kernel, [out, out], [own], after=after, place=[place])


def pack_corners(place, left, right, band_rows, after):
    width = left.shape[1]

    def kernel(place_ref, left_ref, right_ref, out_a, out_b):
        even = place_ref[1] == 0
        for side, side_ref in enumerate((left_ref, right_ref)):
            for col in range(0, MARGIN, 2):
                base = (side * MARGIN + col) * EDGE_R
                last, first = (
                    jnp.concatenate(
                        [
                            side_ref[at : at + EDGE_R, :].astype(F32)
                            for at in (start, start + band_rows)
                        ]
                    )
                    for start in ((col + 1) * band_rows - EDGE_R, col * band_rows)
                )
                here = slice(base, base + 2 * EDGE_R)
                out_a[here, :] = jnp.where(even, last, first).astype(BF)
                out_b[here, :] = jnp.where(even, first, last).astype(BF)

    out = ((2 * MARGIN * EDGE_R, width), BF)
    return on_chip(kernel, [out, out], [left, right], after=after, place=[place])


def merge_sides(place, left, right, rim_a, rim_b, band_rows, band_cols, after=()):
    edge = MARGIN * band_cols

    def kernel(place_ref, left_ref, right_ref, a_ref, b_ref, ol_ref, or_ref):
        even = place_ref[1] == 0
        for part in range(2):
            for col in range(2 * MARGIN):
                source, target = (left_ref, ol_ref) if col < MARGIN else (right_ref, or_ref)
                base = (col % MARGIN) * band_rows
                pair = slice(edge + (col // 2) * 2 * EDGE_R, edge + (col // 2 + 1) * 2 * EDGE_R)
                odd = slice((col % 2) * EDGE_R, (col % 2 + 1) * EDGE_R)
                rows = source[part, base : base + band_rows, :].astype(F32)
                rim_a, rim_b = (ref[part, pair, :].astype(F32)[odd] for ref in (a_ref, b_ref))
                first = rows[:EDGE_R] + jnp.where(even, rim_b, rim_a)
                last = rows[band_rows - EDGE_R :] + jnp.where(even, rim_a, rim_b)
                target[part, base : base + band_rows, :] = jnp.concatenate(
                    [first, rows[EDGE_R : band_rows - EDGE_R], last], axis=0
                ).astype(BF)

    out = [(left.shape, BF), (right.shape, BF)]
    return on_chip(kernel, out, [left, right, rim_a, rim_b], after=after, place=[place])


def finish(place, mid, rim_a, rim_b, left, right, band_rows, band_cols, after, flops):
    _, tokens, width = mid.shape
    edge = MARGIN * band_cols

    def kernel(place_ref, mid_ref, a_ref, b_ref, left_ref, right_ref, out_ref, acc_ref):
        even = place_ref[1] == 0
        for part in range(2):
            for block in range(width // (2 * LANES)):
                for lane in range(2):
                    at = slice((2 * block + lane) * LANES, (2 * block + lane + 1) * LANES)
                    acc_ref[lane] = mid_ref[part, :, at].astype(F32)
                    from_a, from_b = (r[part, :edge, at].astype(F32) for r in (a_ref, b_ref))
                    acc_ref[lane, :edge, :] += jnp.where(even, from_b, from_a)
                    acc_ref[lane, tokens - edge :, :] += jnp.where(even, from_a, from_b)
                    for col in range(MARGIN):
                        here = slice(col * band_rows, (col + 1) * band_rows)
                        first = pl.ds(col, band_rows, stride=band_cols)
                        last = pl.ds(band_cols - MARGIN + col, band_rows, stride=band_cols)
                        acc_ref[lane, first, :] += left_ref[part, here, at].astype(F32)
                        acc_ref[lane, last, :] += right_ref[part, here, at].astype(F32)
                both = jnp.concatenate([acc_ref[0], acc_ref[1]], axis=1).astype(BF)
                start = part * width + block * 2 * LANES
                out_ref[:, start : start + 2 * LANES] = both

    out = [((tokens, 2 * width), BF)]
    scratch = [pltpu.VMEM((2, tokens, LANES), F32)]
    operands = [mid, rim_a, rim_b, left, right]
    return on_chip(kernel, out, operands, after, scratch, flops, [place])[0]


def grad_rows(rows, columns, scale, kind, after=()):
    features, count = rows.shape[0], len(columns)
    width = columns[0].shape[1]

    def kernel(rows_ref, *refs):
        for i, columns_ref in enumerate(refs[:count]):
            for start in range(0, width, 2 * LANES):
                part = dot(rows_ref[...], columns_ref[:, start : start + 2 * LANES])
                at = i * width + start
                refs[count][:, at : at + 2 * LANES] = (part * scale).astype(kind)

    return on_chip(kernel, [((features, count * width), kind)], [rows, *columns], after)[0]


def add_split(keep, received, after=()):
    half, columns = keep.shape[0] // 2, keep.shape[1]

    def kernel(keep_ref, received_ref, sums_ref, send_ref):
        sums_ref[...] = keep_ref[:half, :] + received_ref[:half, :].astype(F32)
        send_ref[...] = (keep_ref[half:, :] + received_ref[half:, :].astype(F32)).astype(BF)

    return on_chip(kernel, [((half, columns), F32), ((half, columns), BF)], [keep, received], after)


def add_blocks(place, keep, received, blocks, after):
    rows, columns = keep.shape
    size = rows // blocks

    def kernel(place_ref, keep_ref, received_ref, send_ref):
        me = place_ref[2] & (blocks - 1)
        for b in range(blocks):
            here = slice(b * size, (b + 1) * size)
            send_ref[me ^ b] = (keep_ref[here, :] + received_ref[here, :].astype(F32)).astype(BF)

    out = [((blocks, size, columns), BF)]
    return on_chip(kernel, out, [keep, received], after, place=[place])[0]


def sent_blocks(keep, received, blocks, after):
    rows, columns = keep.shape
    size = rows // blocks

    def kernel(keep_ref, received_ref, sums_ref, *sends):
        sums_ref[0] = keep_ref[:size, :] + received_ref[:size, :].astype(F32)
        for b in range(1, blocks):
            here = slice(b * size, (b + 1) * size)
            sends[b - 1][0] = (keep_ref[here, :] + received_ref[here, :].astype(F32)).astype(BF)

    shape = (1, size, columns)
    out = [(shape, F32)] + [(shape, BF)] * (blocks - 1)
    return on_chip(kernel, out, [keep, received], after)


def gather_sums(groups, places, width, flops):
    flat = [array for group in groups for array in group]

    def kernel(*refs):
        out_ref = refs[-1]
        at = 0
        for group, moves in zip(groups, places):
            mine = refs[at : at + len(group)]
            at += len(group)
            for source, size, target in moves:
                here = slice(source, source + size)
                parts = [ref[i, :, here].astype(F32) for ref in mine for i in range(ref.shape[0])]
                out_ref[:, target : target + size] = functools.reduce(lambda a, b: a + b, parts)

    return on_chip(kernel, [((flat[0].shape[1], width), F32)], flat, flops=flops)[0]


def shifted(array, axis, by, wrap):
    size = lax.axis_size(axis)
    route = [(i, (i + by) % size) for i in range(size) if wrap or 0 <= i + by < size]
    return lax.ppermute(array, axis, route)


def swapped(array_a, array_b, axis):
    size = lax.axis_size(axis)
    pairs = [(i, i + 1) for i in range(size - 1)]
    route = lambda chosen: chosen + [(j, i) for i, j in chosen]
    return [
        lax.ppermute(array, axis, route(pairs[offset::2]))
        for array, offset in ((array_a, 0), (array_b, 1))
    ]


def exchanged(array, axis, flip):
    return lax.ppermute(array, axis, [(i, i ^ flip) for i in range(lax.axis_size(axis))])


def bits_of(axis):
    return [(axis, 1 << b) for b in range((lax.axis_size(axis) - 1).bit_length())]


def reduce_stages():
    first, *lat_bits = bits_of("lat")
    bits = bits_of("dp") + lat_bits
    return first, list(zip(bits, reversed(bits)))


def feature_orders(first, stages):
    n_lon, n_lat = lax.axis_size("lon"), lax.axis_size("lat")
    unit = {"lon": 1, "lat": n_lon, "dp": n_lon * n_lat}
    lower = []
    for kind in range(2):
        order = np.arange(n_lon)
        for stage in reversed(stages):
            axis, bit = stage[kind]
            order = np.concatenate([order, order + unit[axis] * bit])
        lower.append(order)
    flip = unit[first[0]] * first[1]
    return [np.concatenate([lower[kind], lower[1 - kind] ^ flip]) for kind in range(2)]


def exchanged_stage(array, stage):
    n_lat, n_dp = lax.axis_size("lat"), lax.axis_size("dp")
    route = []
    for i in range(n_dp * n_lat):
        axis, bit = stage[i % n_lat % 2]
        route.append((i, i ^ (bit * n_lat if axis == "dp" else bit)))
    return lax.ppermute(array, ("dp", "lat"), route)


def body(inputs, grad_out, w_qkv):
    _, band_rows, band_cols, width = inputs.shape
    n_lat, n_lon, n_dp = lax.axis_size("lat"), lax.axis_size("lon"), lax.axis_size("dp")
    band_start = lax.axis_index("lat") * band_rows
    total_rows = band_rows * n_lat
    tokens = band_rows * band_cols
    slots = HEADS // GROUP // 2
    shape = (band_rows, band_cols, total_rows)
    own = inputs.reshape(tokens, width)
    flat_grad = grad_out.reshape(tokens, width)

    last_cols, first_cols = pack_sides(own, band_rows, band_cols)
    left = shifted(last_cols, "lon", 1, True)
    right = shifted(first_cols, "lon", -1, True)
    me = (lax.axis_index("dp") * n_lat + lax.axis_index("lat")) * n_lon + lax.axis_index("lon")
    start = jnp.stack([band_start, lax.axis_index("lat") % 2, me])
    rim_rows = swapped(*pack_rows(start, own, band_cols, [last_cols]), "lat")

    masks = window_masks(start, band_rows, band_cols, total_rows)
    qkv = project(own, w_qkv, [last_cols])
    first, stages = reduce_stages()
    half = width // 2
    rows_keep, rows_send = row_blocks(start, own, feature_orders(first, stages), [last_cols])
    corners = pack_corners(start, left, right, band_rows, [masks, qkv, rows_keep, rows_send])
    halo = (left, right, *rim_rows, *swapped(*corners, "lat"))
    scale = float(tokens * n_dp * n_lat * n_lon) ** -0.5

    attend = lambda first, count, before, after: attention_grads(
        first, count, slots, start, masks, halo, qkv, flat_grad, w_qkv, shape, before, after
    )

    def return_sides(grads, rims, after):
        to_left, to_right = merge_sides(
            start, grads[4], grads[5], *rims, band_rows, band_cols, after
        )
        from_right = shifted(to_left, "lon", -1, True)
        from_left = shifted(to_right, "lon", 1, True)
        return to_left, from_left, from_right

    one = attend(0, slots, [], [])
    rims_1 = swapped(one[1], one[2], "lat")
    two = attend(slots, 1, [(0, one[0])], [])
    sent, *sides_1 = return_sides(one, rims_1, [two[1]])
    two = attend(slots + 1, 1, list(enumerate(two)), [sent])
    rims_2 = swapped(two[1], two[2], "lat")
    dq = two[0]

    dkv_1 = finish(start, one[3], *rims_1, *sides_1, band_rows, band_cols, [dq], 2 * 10**9)
    sent, *sides_2 = return_sides(two, rims_2, [dkv_1])
    send = grad_rows(rows_send, [dq, dkv_1], scale, BF, after=[sent])
    received = exchanged(send, *first)
    keep = grad_rows(rows_keep, [dq, dkv_1], scale, F32, after=[send])
    keep, send = add_split(keep, received)

    dkv_2 = finish(start, two[3], *rims_2, *sides_2, band_rows, band_cols, [keep], FINISH_FLOPS)
    for stage in stages[:-1]:
        keep, send = add_split(keep, exchanged_stage(send, stage), [dkv_2])
    send_2 = grad_rows(rows_send, [dkv_2], scale, BF, after=[keep])
    received = exchanged_stage(send, stages[-1])
    received_2 = exchanged(send_2, *first)
    keep_2 = grad_rows(rows_keep, [dkv_2], scale, F32, after=[send_2])
    keep_2, send_2 = add_split(keep_2, received_2)
    received_2 = exchanged_stage(send_2, stages[0])
    grad_inputs = input_grads(dq, dkv_1, dkv_2, w_qkv, [send_2])
    keep, *send = sent_blocks(keep, received, n_lon, [grad_inputs])
    group_1 = [keep] + [exchanged(a, "lon", i + 1) for i, a in enumerate(send)]
    group_1 = [gather_sums([group_1], [[(0, 2 * width, 0)]], 2 * width, GATHER_FLOPS)[None]]
    for stage in stages[1:]:
        keep_2, send_2 = add_split(keep_2, received_2, [keep])
        received_2 = exchanged_stage(send_2, stage)
    send_2 = add_blocks(start, keep_2, received_2, n_lon, group_1)
    group_2 = [lax.all_to_all(send_2, "lon", 0, 0, tiled=True)]
    places = [
        [(0, width, 0), (width, half, width), (width + half, half, 2 * width)],
        [(0, half, width + half), (half, half, 2 * width + half)],
    ]
    grad_w = gather_sums([group_1, group_2], places, 3 * width, 10**5)

    return (grad_inputs.reshape(inputs.shape), grad_w)


def solution(mesh):
    in_specs = (P("dp", "lat", "lon", None), P("dp", "lat", "lon", None), P())
    out_specs = (P("dp", "lat", "lon", None), P(("dp", "lat", "lon"), None))
    return jax.shard_map(body, mesh=mesh, in_specs=in_specs, out_specs=out_specs, check_vma=False)
```

```python
import functools

import jax
import jax.numpy as jnp
import numpy as np
from jax import lax
from jax.experimental import pallas as pl
from jax.experimental.pallas import tpu as pltpu
from jax.sharding import PartitionSpec as P

HEADS = 16
WIN = 13
MARGIN = WIN // 2
TILE_R = 4
GROUP = 4
KEY_COLS = 32
HALO_COLS = 16
REGION_R = 16
PAD_R = 2
EDGE_R = MARGIN + PAD_R
NEG = -1e30
BF = jnp.bfloat16
F32 = jnp.float32
MIB = 1024 * 1024
GATHER_FLOPS = 4 * 10**9
FINISH_FLOPS = 9 * 10**9
LANES = 128
ATTENTION_MIB = 46

NT = (((1,), (1,)), ((), ()))
TN = (((0,), (0,)), ((), ()))
NN = (((1,), (0,)), ((), ()))


def dot(a, b, dims=NN):
    return lax.dot_general(a, b, dims, preferred_element_type=F32)


def region_top(tile, band_start, band_rows, total_rows):
    lowest = jnp.where(band_start == 0, TILE_R, 0)
    highest = jnp.where(band_start + band_rows == total_rows, band_rows - 2 * TILE_R, band_rows)
    return jnp.clip(tile * TILE_R, lowest, highest)


def mask_kernel(band_rows, band_cols, total_rows, start_ref, mask_ref):
    band_start = start_ref[0]
    tile = pl.program_id(0)
    shape = mask_ref.shape[1:]
    first = region_top(tile, band_start, band_rows, total_rows)
    key = lax.broadcasted_iota(jnp.int32, shape, 0)
    query = lax.broadcasted_iota(jnp.int32, shape, 1) & (TILE_R * band_cols - 1)
    key_row = band_start - MARGIN + first + (key >> (KEY_COLS.bit_length() - 1))
    place = key & (KEY_COLS - 1)
    query_row = band_start + tile * TILE_R + (query >> (band_cols.bit_length() - 1))
    query_col = query & (band_cols - 1)
    window = jnp.clip(query_row - MARGIN, 0, total_rows - WIN)
    row_inside = (key_row >= window) & (key_row < window + WIN)
    key_col = jnp.where(
        place < band_cols,
        place,
        jnp.where(place < band_cols + MARGIN, place - band_cols - MARGIN, place - MARGIN),
    )
    col_inside = (jnp.abs(key_col - query_col) <= MARGIN) & (place < band_cols + 2 * MARGIN)
    mask_ref[0] = jnp.where(row_inside & col_inside, 0.0, NEG).astype(BF)


def window_masks(start, band_rows, band_cols, total_rows):
    tiles = band_rows // TILE_R
    shape = (REGION_R * KEY_COLS, 2 * TILE_R * band_cols)
    return pl.pallas_call(
        functools.partial(mask_kernel, band_rows, band_cols, total_rows),
        grid=(tiles,),
        in_specs=[pl.BlockSpec(memory_space=pltpu.SMEM)],
        out_specs=pl.BlockSpec((1,) + shape, lambda t: (t, 0, 0)),
        out_shape=jax.ShapeDtypeStruct((tiles,) + shape, BF),
        cost_estimate=pl.CostEstimate(flops=10**7, bytes_accessed=2**21, transcendentals=0),
    )(start)


def attention_kernel(band_rows, band_cols, total_rows, head_width, extra, first, count, shift, *refs):
    (place_ref, mask_ref, left_ref, right_ref, rows_a, rows_b, corners_a, corners_b,
     qkv_hbm, grad_hbm, w_hbm) = refs[:11]
    before_a, before_b = refs[11 : 11 + shift], refs[11 + shift : 11 + 2 * shift]
    (dq_all, out_a_all, out_b_all, mid_all, to_left_all, to_right_all,
     halo_ref, spot_ref, q_ref, k_ref, v_ref, dk_ref, dv_ref,
     own_refs, w_refs, own_sem, w_sem) = refs[11 + extra :]
    band_start = place_ref[0]
    even = place_ref[1] == 0
    tiles = band_rows // TILE_R
    queries = TILE_R * band_cols
    keys = REGION_R * KEY_COLS
    width = GROUP * head_width
    lanes = GROUP * queries
    region_rows = band_rows + 2 * MARGIN
    side = MARGIN * band_rows
    edge = MARGIN * band_cols
    corner = 2 * MARGIN * EDGE_R
    at_above = 2 * side
    at_below = at_above + edge
    at_cl = at_below + edge
    at_cr = at_cl + corner
    halves = [(i, slice(i * LANES, (i + 1) * LANES)) for i in range(width // LANES)]

    step = pl.program_id(0)
    dq_ref, mid_ref, to_left_ref, to_right_ref = (
        ref.at[step] for ref in (dq_all, mid_all, to_left_all, to_right_all)
    )
    out_a, out_b = (ref.at[step + shift] for ref in (out_a_all, out_b_all))
    groups = HEADS // GROUP

    def copies(slot, parts):
        at = lambda part: pl.ds((part * groups + first + slot) * width, width)
        for part, source, where, i in parts:
            target, sem = (w_refs, w_sem) if where else (own_refs, own_sem)
            yield pltpu.make_async_copy(source.at[:, at(part)], target.at[slot, i], sem.at[slot, i])

    for_k = ((1, w_hbm, 1, 0), (1, qkv_hbm, 0, 1))
    for_v = ((2, w_hbm, 1, 1), (2, qkv_hbm, 0, 2))
    for_q = ((0, qkv_hbm, 0, 0), (0, grad_hbm, 0, 3))

    def await_copies(parts):
        for slot in range(count):

            @pl.when(step == slot)
            def _():
                for copy in copies(slot, parts):
                    copy.wait()

    @pl.when(step == 0)
    def _():
        for ref, kept in ((out_a_all, before_a), (out_b_all, before_b)):
            for i in range(shift):
                ref[i] = kept[0][i]
        for slot in range(count):
            for copy in copies(slot, for_k + for_v + for_q):
                copy.start()
        halo_ref[:side] = left_ref[...]
        halo_ref[side:at_above] = right_ref[...]
        for above, below, size, refs_ab in (
            (at_above, at_below, edge, (rows_a, rows_b)),
            (at_cl, at_cr, corner, (corners_a, corners_b)),
        ):
            for ref, at in zip(refs_ab, (jnp.where(even, below, above), jnp.where(even, above, below))):
                halo_ref[pl.ds(pl.multiple_of(at, 16), size), :] = ref[...]
        spot_ref[...] = jnp.zeros_like(spot_ref)

    def place(target, own, weights):
        fresh = dot(halo_ref[...], weights)
        for col in range(MARGIN):
            start = MARGIN * HALO_COLS + col
            for part, at in halves:
                spot_ref[part, pl.ds(start, band_rows, stride=HALO_COLS), :] = fresh[
                    col * band_rows : (col + 1) * band_rows, at
                ]
                spot_ref[part, pl.ds(start + MARGIN, band_rows, stride=HALO_COLS), :] = fresh[
                    side + col * band_rows : side + (col + 1) * band_rows, at
                ]
        for corner_at, skip, row in ((at_cl, PAD_R, 0), (at_cr, 0, MARGIN + band_rows)):
            for col in range(2 * MARGIN):
                base = corner_at + col * EDGE_R + skip
                spot = pl.ds(row * HALO_COLS + col, MARGIN, stride=HALO_COLS)
                for part, at in halves:
                    spot_ref[part, spot, :] = fresh[base : base + MARGIN, at]
        for row in range(region_rows):
            base = row * KEY_COLS
            inner = row - MARGIN
            if inner < 0:
                ours = fresh[at_above + row * band_cols : at_above + (row + 1) * band_cols].astype(BF)
            elif inner < band_rows:
                ours = own[inner * band_cols : (inner + 1) * band_cols, :]
            else:
                past = at_below + (inner - band_rows) * band_cols
                ours = fresh[past : past + band_cols].astype(BF)
            target[base : base + band_cols, :] = ours
            for part, at in halves:
                target[base + band_cols : base + KEY_COLS, at] = spot_ref[
                    part, row * HALO_COLS : (row + 1) * HALO_COLS, :
                ].astype(BF)

    grad_ref = own_refs.at[step, 3]
    await_copies(for_k)
    place(k_ref, own_refs.at[step, 1], w_refs[step, 0])
    await_copies(for_v)
    place(v_ref, own_refs.at[step, 2], w_refs[step, 1])
    await_copies(for_q)
    q_ref[...] = own_refs[step, 0] * BF(head_width**-0.5)
    dk_ref[...] = jnp.zeros_like(dk_ref)
    dv_ref[...] = jnp.zeros_like(dv_ref)

    def spread(rows):
        block = jnp.concatenate([rows] * GROUP, axis=0)
        head_row = lax.broadcasted_iota(jnp.int32, (lanes, width), 0) // queries
        head_col = lax.broadcasted_iota(jnp.int32, (lanes, width), 1) // head_width
        return jnp.where(head_row == head_col, block, jnp.zeros_like(block))

    def one_tile(tile, carry):
        first = region_top(tile, band_start, band_rows, total_rows)
        region = pl.ds(pl.multiple_of(first * KEY_COLS, TILE_R * KEY_COLS), keys)
        total = pl.ds(pl.multiple_of((first + PAD_R) * KEY_COLS, PAD_R * KEY_COLS), keys)
        mine = pl.ds(pl.multiple_of(tile * queries, queries), queries)
        q_wide = spread(q_ref[mine, :])
        g_wide = spread(grad_ref[mine, :])
        mask = mask_ref[tile].astype(F32)
        scores = dot(k_ref[region, :], q_wide, NT) + jnp.concatenate([mask, mask], axis=1)
        dots = dot(v_ref[region, :], g_wide, NT)
        exponent = jnp.exp(scores - jnp.max(scores, axis=0, keepdims=True))
        inverse = 1.0 / jnp.sum(exponent, axis=0, keepdims=True)
        delta = jnp.sum(exponent * dots, axis=0, keepdims=True) * inverse
        attn = exponent * inverse
        dscore = (attn * (dots - delta)).astype(BF)
        dv = dot(attn.astype(BF), g_wide)
        dk = dot(dscore, q_wide)
        for part, at in halves:
            dv_ref[part, total, :] += dv[:, at]
            dk_ref[part, total, :] += dk[:, at]
        dq_wide = dot(dscore, k_ref[region, :], TN)
        head_col = lax.broadcasted_iota(jnp.int32, (queries, width), 1) // head_width
        dq = jnp.zeros((queries, width), F32)
        for head in range(GROUP):
            dq = jnp.where(head_col == head, dq_wide[head * queries : (head + 1) * queries], dq)
        dq_ref[mine, :] = (dq * head_width**-0.5).astype(BF)
        return carry

    lax.fori_loop(0, tiles, one_tile, 0, unroll=4)

    middle = (PAD_R + MARGIN) * KEY_COLS
    below = (PAD_R + MARGIN + band_rows) * KEY_COLS
    for part, acc in enumerate((dk_ref, dv_ref)):
        for lane, at in halves:
            for out, own_at, side_at in (
                (out_a, jnp.where(even, below, PAD_R * KEY_COLS), jnp.where(even, below, 0)),
                (out_b, jnp.where(even, PAD_R * KEY_COLS, below), jnp.where(even, 0, below)),
            ):
                for row in range(MARGIN):
                    start = pl.multiple_of(own_at + row * KEY_COLS, KEY_COLS)
                    out[part, row * band_cols : (row + 1) * band_cols, at] = acc[
                        lane, pl.ds(start, band_cols), :
                    ].astype(BF)
                for pair in range(MARGIN):
                    here = slice(edge + pair * 2 * EDGE_R, edge + (pair + 1) * 2 * EDGE_R)
                    start = side_at + band_cols + 2 * pair
                    out[part, here, at] = jnp.concatenate(
                        [
                            acc[lane, pl.ds(start, EDGE_R, stride=KEY_COLS), :],
                            acc[lane, pl.ds(start + 1, EDGE_R, stride=KEY_COLS), :],
                        ],
                        axis=0,
                    ).astype(BF)
            for row in range(band_rows):
                base = middle + row * KEY_COLS
                mid_ref[part, row * band_cols : (row + 1) * band_cols, at] = acc[
                    lane, base : base + band_cols, :
                ].astype(BF)
            for col in range(MARGIN):
                here = slice(col * band_rows, (col + 1) * band_rows)
                start = middle + band_cols + col
                to_left_ref[part, here, at] = acc[
                    lane, pl.ds(start, band_rows, stride=KEY_COLS), :
                ].astype(BF)
                to_right_ref[part, here, at] = acc[
                    lane, pl.ds(start + MARGIN, band_rows, stride=KEY_COLS), :
                ].astype(BF)


def attention_grads(first, count, place, masks, halo, qkv, grad_out, w_qkv, shape, before, after):
    band_rows, band_cols, total_rows = shape
    tokens, width = grad_out.shape
    head_width = width // HEADS
    block = GROUP * head_width
    region_tokens = (band_rows + 2 * MARGIN) * KEY_COLS
    total_tokens = (band_rows + 2 * MARGIN + 2 * PAD_R) * KEY_COLS
    side = MARGIN * band_rows
    edge = MARGIN * (band_cols + 2 * EDGE_R)
    corner = 2 * MARGIN * EDGE_R
    halo_tokens = 2 * (side + MARGIN * band_cols + corner)
    shift = before[0].shape[0] if before else 0
    vmem = pl.BlockSpec(memory_space=pltpu.VMEM)
    shapes = [
        (count, tokens, block),
        (count + shift, 2, edge, block),
        (count + shift, 2, edge, block),
        (count, 2, tokens, block),
        (count, 2, side, block),
        (count, 2, side, block),
    ]
    return pl.pallas_call(
        functools.partial(
            attention_kernel, band_rows, band_cols, total_rows, head_width,
            len(before) + len(after), first, count, shift,
        ),
        grid=(count,),
        in_specs=[pl.BlockSpec(memory_space=pltpu.SMEM)]
        + [vmem] * (1 + len(halo))
        + [pl.BlockSpec(memory_space=pltpu.HBM)] * 3
        + [vmem] * len(before)
        + [pl.BlockSpec(memory_space=pl.ANY)] * len(after),
        out_specs=[vmem] * len(shapes),
        out_shape=[jax.ShapeDtypeStruct(s, BF) for s in shapes],
        scratch_shapes=[
            pltpu.VMEM((halo_tokens, width), BF),
            pltpu.VMEM((block // LANES, (band_rows + 2 * MARGIN) * HALO_COLS, LANES), F32),
            pltpu.VMEM((tokens, block), BF),
            pltpu.VMEM((region_tokens, block), BF),
            pltpu.VMEM((region_tokens, block), BF),
            pltpu.VMEM((block // LANES, total_tokens, LANES), F32),
            pltpu.VMEM((block // LANES, total_tokens, LANES), F32),
            pltpu.VMEM((count, 4, tokens, block), BF),
            pltpu.VMEM((count, 2, width, block), BF),
            pltpu.SemaphoreType.DMA((count, 4)),
            pltpu.SemaphoreType.DMA((count, 2)),
        ],
        compiler_params=pltpu.CompilerParams(
            dimension_semantics=("arbitrary",), vmem_limit_bytes=ATTENTION_MIB * MIB
        ),
        cost_estimate=pl.CostEstimate(
            flops=count * 14 * 10**9, bytes_accessed=count * 8 * MIB, transcendentals=count * 10**6
        ),
    )(place, masks, *halo, qkv, grad_out, w_qkv, *before, *after)


def on_chip(kernel, out_shape, operands, after=(), scratch=(), flops=10**5, place=()):
    count = len(operands) + len(place)

    def run(*refs):
        kernel(*refs[:count], *refs[count + len(after) :])

    return pl.pallas_call(
        run,
        in_specs=[pl.BlockSpec(memory_space=pltpu.SMEM)] * len(place)
        + [pl.BlockSpec(memory_space=pltpu.VMEM)] * len(operands)
        + [pl.BlockSpec(memory_space=pl.ANY)] * len(after),
        out_specs=[pl.BlockSpec(memory_space=pltpu.VMEM)] * len(out_shape),
        out_shape=[jax.ShapeDtypeStruct(s, d) for s, d in out_shape],
        scratch_shapes=list(scratch),
        compiler_params=pltpu.CompilerParams(vmem_limit_bytes=24 * MIB),
        cost_estimate=pl.CostEstimate(flops=flops, bytes_accessed=10**4, transcendentals=0),
    )(*place, *operands, *after)


def lanes_of(width):
    return [(i, slice(i * LANES, (i + 1) * LANES)) for i in range(width // LANES)]


def project(own, w_qkv, after):
    tokens, width = own.shape
    columns = w_qkv.shape[1]
    block = 4 * LANES

    def kernel(own_ref, w_ref, *refs):
        refs[-1][...] = dot(own_ref[...], w_ref[...]).astype(BF)

    return pl.pallas_call(
        kernel,
        grid=(columns // block,),
        in_specs=[
            pl.BlockSpec((tokens, width), lambda g: (0, 0)),
            pl.BlockSpec((width, block), lambda g: (0, g)),
        ]
        + [pl.BlockSpec(memory_space=pl.ANY)] * len(after),
        out_specs=pl.BlockSpec((tokens, block), lambda g: (0, g)),
        out_shape=jax.ShapeDtypeStruct((tokens, columns), BF),
        compiler_params=pltpu.CompilerParams(vmem_limit_bytes=24 * MIB),
        cost_estimate=pl.CostEstimate(flops=10**9, bytes_accessed=MIB, transcendentals=0),
    )(own, w_qkv, *after)


def input_grads(columns, w_qkv, after):
    tokens = columns[0].shape[-2]
    width, total = w_qkv.shape
    count = len(columns)
    pieces = list(pieces_of(columns))
    steps = len(pieces) // 2

    def kernel(*refs):
        w_ref, (out_ref, done_ref, acc_ref) = refs[count], refs[-3:]
        for step in range(steps):

            @pl.when(pl.program_id(0) == step)
            def _():
                both = [piece(refs, *where) for where in pieces[2 * step : 2 * step + 2]]
                product = dot(jnp.concatenate(both, axis=1), w_ref[...], NT)
                if step == 0:
                    acc_ref[...] = product
                elif step < steps - 1:
                    acc_ref[...] += product
                else:
                    out_ref[...] = (acc_ref[...] + product).astype(BF)
                    done_ref[...] = jnp.zeros_like(done_ref)

    return pl.pallas_call(
        kernel,
        grid=(steps,),
        in_specs=[pl.BlockSpec(memory_space=pltpu.VMEM)] * count
        + [pl.BlockSpec((width, total // steps), lambda g: (0, g))]
        + [pl.BlockSpec(memory_space=pl.ANY)] * len(after),
        out_specs=[
            pl.BlockSpec((tokens, width), lambda g: (0, 0)),
            pl.BlockSpec((8, LANES), lambda g: (0, 0)),
        ],
        out_shape=[
            jax.ShapeDtypeStruct((tokens, width), BF),
            jax.ShapeDtypeStruct((8, LANES), F32),
        ],
        scratch_shapes=[pltpu.VMEM((tokens, width), F32)],
        compiler_params=pltpu.CompilerParams(vmem_limit_bytes=24 * MIB),
        cost_estimate=pl.CostEstimate(flops=4 * 10**9, bytes_accessed=MIB, transcendentals=0),
    )(*columns, w_qkv, *after)


def row_blocks(place, own, orders, after):
    tokens, width = own.shape
    devices = len(orders[0])
    size = width // devices
    step = max(1, 16 // size)

    def kernel(place_ref, own_ref, low_ref, high_ref, wide_ref):
        for at in range(0, width, 2 * LANES):
            wide_ref[at : at + 2 * LANES, :] = own_ref[:, at : at + 2 * LANES].astype(F32).T
        even = place_ref[1] == 0
        me = place_ref[2]
        for j in range(0, devices, step):
            rows = []
            for k in range(j, j + step):
                owner = me ^ jnp.where(even, int(orders[0][k]), int(orders[1][k]))
                rows.append(wide_ref[pl.ds(pl.multiple_of(owner * size, size), size), :])
            half, base = divmod(j * size, width // 2)
            block = rows[0] if step == 1 else jnp.concatenate(rows, axis=0)
            (low_ref, high_ref)[half][base : base + step * size, :] = block.astype(BF)

    out = ((width // 2, tokens), BF)
    scratch = [pltpu.VMEM((width, tokens), F32)]
    return on_chip(kernel, [out, out], [own], after=after, scratch=scratch, place=[place])


def pack_sides(own, band_rows, band_cols):
    tokens, width = own.shape

    def kernel(own_ref, last_ref, first_ref, wide_ref):
        for lane, at in lanes_of(width):
            wide_ref[lane] = own_ref[:, at].astype(F32)
            for col in range(MARGIN):
                here = slice(col * band_rows, (col + 1) * band_rows)
                last = pl.ds(band_cols - MARGIN + col, band_rows, stride=band_cols)
                last_ref[here, at] = wide_ref[lane, last, :].astype(BF)
                first = pl.ds(col, band_rows, stride=band_cols)
                first_ref[here, at] = wide_ref[lane, first, :].astype(BF)

    out = ((MARGIN * band_rows, width), BF)
    scratch = [pltpu.VMEM((width // LANES, tokens, LANES), F32)]
    return on_chip(kernel, [out, out], [own], scratch=scratch)


def pack_rows(place, own, band_cols, after):
    tokens, width = own.shape
    edge = MARGIN * band_cols

    def kernel(place_ref, own_ref, out_a, out_b):
        even = place_ref[1] == 0
        last, first = own_ref[tokens - edge :, :], own_ref[:edge, :]
        out_a[...] = jnp.where(even, last, first)
        out_b[...] = jnp.where(even, first, last)

    out = ((edge, width), BF)
    return on_chip(kernel, [out, out], [own], after=after, place=[place])


def pack_corners(place, left, right, band_rows, after):
    width = left.shape[1]

    def kernel(place_ref, left_ref, right_ref, out_a, out_b):
        even = place_ref[1] == 0
        for side, side_ref in enumerate((left_ref, right_ref)):
            for col in range(0, MARGIN, 2):
                base = (side * MARGIN + col) * EDGE_R
                last, first = (
                    jnp.concatenate(
                        [
                            side_ref[at : at + EDGE_R, :].astype(F32)
                            for at in (start, start + band_rows)
                        ]
                    )
                    for start in ((col + 1) * band_rows - EDGE_R, col * band_rows)
                )
                here = slice(base, base + 2 * EDGE_R)
                out_a[here, :] = jnp.where(even, last, first).astype(BF)
                out_b[here, :] = jnp.where(even, first, last).astype(BF)

    out = ((2 * MARGIN * EDGE_R, width), BF)
    return on_chip(kernel, [out, out], [left, right], after=after, place=[place])


def merge_sides(place, lefts, rights, rim_a, rim_b, band_rows, band_cols, after=()):
    edge = MARGIN * band_cols
    calls = len(lefts)
    slots = rim_a.shape[0]
    each = slots // calls

    def kernel(place_ref, *refs):
        sides = refs[:calls], refs[calls : 2 * calls]
        a_ref, b_ref, *outs = refs[2 * calls :]
        even = place_ref[1] == 0
        for slot in range(slots):
            for part in range(2):
                for col in range(2 * MARGIN):
                    source = sides[col // MARGIN][slot // each]
                    base = (col % MARGIN) * band_rows
                    pair = slice(edge + (col // 2) * 2 * EDGE_R, edge + (col // 2 + 1) * 2 * EDGE_R)
                    odd = slice((col % 2) * EDGE_R, (col % 2 + 1) * EDGE_R)
                    rows = source[slot % each, part, base : base + band_rows, :].astype(F32)
                    from_a, from_b = (
                        ref[slot, part, pair, :].astype(F32)[odd] for ref in (a_ref, b_ref)
                    )
                    first = rows[:EDGE_R] + jnp.where(even, from_b, from_a)
                    last = rows[band_rows - EDGE_R :] + jnp.where(even, from_a, from_b)
                    outs[col // MARGIN][slot, part, base : base + band_rows, :] = jnp.concatenate(
                        [first, rows[EDGE_R : band_rows - EDGE_R], last], axis=0
                    ).astype(BF)

    out = ((slots,) + lefts[0].shape[1:], BF)
    return on_chip(kernel, [out, out], [*lefts, *rights, rim_a, rim_b], after, place=[place])


def finish(place, mids, rim_a, rim_b, left, right, parts, band_rows, band_cols, after, flops):
    calls = len(mids)
    slots, _, _, block = rim_a.shape
    each = slots // calls
    edge = MARGIN * band_cols
    tokens = band_rows * band_cols

    def kernel(place_ref, *refs):
        a_ref, b_ref, left_ref, right_ref, *outs, acc_ref = refs[calls:]
        even = place_ref[1] == 0
        for out_ref, part in zip(outs, parts):
            for slot in range(slots):
                for lane, at in lanes_of(block):
                    acc_ref[lane] = refs[slot // each][slot % each, part, :, at].astype(F32)
                    from_a, from_b = (
                        r[slot, part, :edge, at].astype(F32) for r in (a_ref, b_ref)
                    )
                    acc_ref[lane, :edge, :] += jnp.where(even, from_b, from_a)
                    acc_ref[lane, tokens - edge :, :] += jnp.where(even, from_a, from_b)
                    for col in range(MARGIN):
                        here = slice(col * band_rows, (col + 1) * band_rows)
                        first = pl.ds(col, band_rows, stride=band_cols)
                        last = pl.ds(band_cols - MARGIN + col, band_rows, stride=band_cols)
                        acc_ref[lane, first, :] += left_ref[slot, part, here, at].astype(F32)
                        acc_ref[lane, last, :] += right_ref[slot, part, here, at].astype(F32)
                    start = slot * block + lane * LANES
                    out_ref[:, start : start + LANES] = acc_ref[lane].astype(BF)

    out = [((tokens, slots * block), BF)] * len(parts)
    scratch = [pltpu.VMEM((block // LANES, tokens, LANES), F32)]
    operands = [*mids, rim_a, rim_b, left, right]
    return on_chip(kernel, out, operands, after, scratch, flops, [place])


def pieces_of(arrays):
    for i, array in enumerate(arrays):
        slots = range(array.shape[0]) if array.ndim == 3 else [None]
        for slot in slots:
            for start in range(0, array.shape[-1], 2 * LANES):
                yield i, slot, start


def piece(refs, i, slot, start):
    here = slice(start, start + 2 * LANES)
    return refs[i][:, here] if slot is None else refs[i][slot, :, here]


def grad_rows(rows, columns, scale, kind, after=()):
    features, count = rows.shape[0], len(columns)
    pieces = list(pieces_of(columns))

    def kernel(rows_ref, *refs):
        for at, where in enumerate(pieces):
            part = dot(rows_ref[...], piece(refs, *where))
            here = slice(at * 2 * LANES, (at + 1) * 2 * LANES)
            refs[count][:, here] = (part * scale).astype(kind)

    out = [((features, len(pieces) * 2 * LANES), kind)]
    return on_chip(kernel, out, [rows, *columns], after)[0]


def add_split(keep, received, after=()):
    half, columns = keep.shape[0] // 2, keep.shape[1]

    def kernel(keep_ref, received_ref, sums_ref, send_ref):
        sums_ref[...] = keep_ref[:half, :] + received_ref[:half, :].astype(F32)
        send_ref[...] = (keep_ref[half:, :] + received_ref[half:, :].astype(F32)).astype(BF)

    return on_chip(kernel, [((half, columns), F32), ((half, columns), BF)], [keep, received], after)


def sent_blocks(keep, received, blocks, after):
    rows, columns = keep.shape
    size = rows // blocks

    def kernel(keep_ref, received_ref, sums_ref, *sends):
        sums_ref[0] = keep_ref[:size, :] + received_ref[:size, :].astype(F32)
        for b in range(1, blocks):
            here = slice(b * size, (b + 1) * size)
            sends[b - 1][0] = (keep_ref[here, :] + received_ref[here, :].astype(F32)).astype(BF)

    shape = (1, size, columns)
    out = [(shape, F32)] + [(shape, BF)] * (blocks - 1)
    return on_chip(kernel, out, [keep, received], after)


def gather_sums(groups, places, width, after, flops):
    flat = [array for group in groups for array in group]

    def kernel(*refs):
        out_ref = refs[-1]
        at = 0
        for group, moves in zip(groups, places):
            mine = refs[at : at + len(group)]
            at += len(group)
            for source, size, target in moves:
                here = slice(source, source + size)
                parts = [ref[i, :, here].astype(F32) for ref in mine for i in range(ref.shape[0])]
                out_ref[:, target : target + size] = functools.reduce(lambda a, b: a + b, parts)

    return on_chip(kernel, [((flat[0].shape[1], width), F32)], flat, after, flops=flops)[0]


def shifted(array, axis, by, wrap):
    size = lax.axis_size(axis)
    route = [(i, (i + by) % size) for i in range(size) if wrap or 0 <= i + by < size]
    return lax.ppermute(array, axis, route)


def swapped(array_a, array_b, axis):
    size = lax.axis_size(axis)
    pairs = [(i, i + 1) for i in range(size - 1)]
    route = lambda chosen: chosen + [(j, i) for i, j in chosen]
    return [
        lax.ppermute(array, axis, route(pairs[offset::2]))
        for array, offset in ((array_a, 0), (array_b, 1))
    ]


def exchanged(array, axis, flip):
    return lax.ppermute(array, axis, [(i, i ^ flip) for i in range(lax.axis_size(axis))])


def bits_of(axis):
    return [(axis, 1 << b) for b in range((lax.axis_size(axis) - 1).bit_length())]


def reduce_stages():
    first, *lat_bits = bits_of("lat")
    bits = bits_of("dp") + lat_bits
    return first, list(zip(bits, reversed(bits)))


def feature_orders(first, stages):
    n_lon, n_lat = lax.axis_size("lon"), lax.axis_size("lat")
    unit = {"lon": 1, "lat": n_lon, "dp": n_lon * n_lat}
    lower = []
    for kind in range(2):
        order = np.arange(n_lon)
        for stage in reversed(stages):
            axis, bit = stage[kind]
            order = np.concatenate([order, order + unit[axis] * bit])
        lower.append(order)
    flip = unit[first[0]] * first[1]
    return [np.concatenate([lower[kind], lower[1 - kind] ^ flip]) for kind in range(2)]


def exchanged_stage(array, stage):
    n_lat, n_dp = lax.axis_size("lat"), lax.axis_size("dp")
    route = []
    for i in range(n_dp * n_lat):
        axis, bit = stage[i % n_lat % 2]
        route.append((i, i ^ (bit * n_lat if axis == "dp" else bit)))
    return lax.ppermute(array, ("dp", "lat"), route)


def body(inputs, grad_out, w_qkv):
    _, band_rows, band_cols, width = inputs.shape
    n_lat, n_lon, n_dp = lax.axis_size("lat"), lax.axis_size("lon"), lax.axis_size("dp")
    band_start = lax.axis_index("lat") * band_rows
    total_rows = band_rows * n_lat
    tokens = band_rows * band_cols
    slots = HEADS // GROUP // 2
    shape = (band_rows, band_cols, total_rows)
    own = inputs.reshape(tokens, width)
    flat_grad = grad_out.reshape(tokens, width)

    last_cols, first_cols = pack_sides(own, band_rows, band_cols)
    left = shifted(last_cols, "lon", 1, True)
    right = shifted(first_cols, "lon", -1, True)
    me = (lax.axis_index("dp") * n_lat + lax.axis_index("lat")) * n_lon + lax.axis_index("lon")
    start = jnp.stack([band_start, lax.axis_index("lat") % 2, me])
    rim_rows = swapped(*pack_rows(start, own, band_cols, [last_cols]), "lat")

    masks = window_masks(start, band_rows, band_cols, total_rows)
    qkv = project(own, w_qkv, [last_cols])
    first, stages = reduce_stages()
    half = width // 2
    rows_keep, rows_send = row_blocks(start, own, feature_orders(first, stages), [last_cols])
    corners = pack_corners(start, left, right, band_rows, [masks, qkv, rows_keep, rows_send])
    halo = (left, right, *rim_rows, *swapped(*corners, "lat"))
    scale = float(tokens * n_dp * n_lat * n_lon) ** -0.5

    attend = lambda first, count, before, after: attention_grads(
        first, count, start, masks, halo, qkv, flat_grad, w_qkv, shape, before, after
    )

    def return_sides(calls, rims, after):
        to_left, to_right = merge_sides(
            start, [c[4] for c in calls], [c[5] for c in calls], *rims, band_rows, band_cols, after
        )
        from_right = shifted(to_left, "lon", -1, True)
        from_left = shifted(to_right, "lon", 1, True)
        return to_left, from_left, from_right

    def finished(calls, rims, sides, parts, after, flops):
        mids = [c[3] for c in calls]
        return finish(start, mids, *rims, *sides, parts, band_rows, band_cols, after, flops)

    groups = HEADS // GROUP
    one = attend(0, slots, [], [])
    rims_1 = swapped(one[1], one[2], "lat")
    two = attend(slots, groups - slots - 1, [], [one[0]])
    sent, *sides_1 = return_sides([one], rims_1, [two[0]])
    three = attend(groups - 1, 1, [two[1], two[2]], [sent])
    rims_2 = swapped(three[1], three[2], "lat")
    dq = [one[0], two[0], three[0]]

    dk_1, dv_1 = finished([one], rims_1, sides_1, (0, 1), [three[0]], 2 * 10**9)
    sent, *sides_2 = return_sides([two, three], rims_2, [dk_1])
    send = grad_rows(rows_send, [*dq, dk_1, dv_1], scale, BF, after=[sent])
    received = exchanged(send, *first)
    keep = grad_rows(rows_keep, [*dq, dk_1, dv_1], scale, F32, after=[send])
    keep, send = add_split(keep, received)

    (dk_2,) = finished([two, three], rims_2, sides_2, (0,), [keep], FINISH_FLOPS)
    for stage in stages[:-1]:
        keep, send = add_split(keep, exchanged_stage(send, stage), [dk_2])
    received = exchanged_stage(send, stages[-1])
    (dv_2,) = finished([two, three], rims_2, sides_2, (1,), [keep], 10**5)
    send_2 = grad_rows(rows_send, [dk_2, dv_2], scale, BF)
    received_2 = exchanged(send_2, *first)
    keep_2 = grad_rows(rows_keep, [dk_2, dv_2], scale, F32, after=[send_2])
    keep, *send = sent_blocks(keep, received, n_lon, [keep_2])
    group_1 = [keep] + [exchanged(a, "lon", i + 1) for i, a in enumerate(send)]
    sum_1 = gather_sums([group_1], [[(0, 2 * width, 0)]], 2 * width, [], GATHER_FLOPS)[None]
    for stage in stages:
        keep_2, send_2 = add_split(keep_2, received_2, [keep])
        received_2 = exchanged_stage(send_2, stage)
    keep_2, *send_2 = sent_blocks(keep_2, received_2, n_lon, [sum_1])
    group_2 = [keep_2] + [exchanged(a, "lon", i + 1) for i, a in enumerate(send_2)]
    grad_inputs, done = input_grads([*dq, dk_1, dk_2, dv_1, dv_2], w_qkv, [keep_2])
    places = [
        [(0, width, 0), (width, half, width), (width + half, half, 2 * width)],
        [(0, half, width + half), (half, half, 2 * width + half)],
    ]
    grad_w = gather_sums([[sum_1], group_2], places, 3 * width, [done], 10**5)
    return (grad_inputs.reshape(inputs.shape), grad_w)


def solution(mesh):
    in_specs = (P("dp", "lat", "lon", None), P("dp", "lat", "lon", None), P())
    out_specs = (P("dp", "lat", "lon", None), P(("dp", "lat", "lon"), None))
    return jax.shard_map(body, mesh=mesh, in_specs=in_specs, out_specs=out_specs, check_vma=False)
```

```python
import functools

import jax
import jax.numpy as jnp
import numpy as np
from jax import lax
from jax.experimental import pallas as pl
from jax.experimental.pallas import tpu as pltpu
from jax.sharding import PartitionSpec as P

HEADS = 16
WIN = 13
MARGIN = WIN // 2
TILE_R = 4
GROUP = 4
KEY_COLS = 32
HALO_COLS = 16
REGION_R = 16
PAD_R = 2
EDGE_R = MARGIN + PAD_R
NEG = -1e30
BF = jnp.bfloat16
F32 = jnp.float32
MIB = 1024 * 1024
GATHER_FLOPS = 4 * 10**9
FINISH_FLOPS = 9 * 10**9
LANES = 128
ATTENTION_MIB = 32

NT = (((1,), (1,)), ((), ()))
TN = (((0,), (0,)), ((), ()))
NN = (((1,), (0,)), ((), ()))


def dot(a, b, dims=NN):
    return lax.dot_general(a, b, dims, preferred_element_type=F32)


def region_top(tile, band_start, band_rows, total_rows):
    lowest = jnp.where(band_start == 0, TILE_R, 0)
    highest = jnp.where(band_start + band_rows == total_rows, band_rows - 2 * TILE_R, band_rows)
    return jnp.clip(tile * TILE_R, lowest, highest)


def mask_kernel(band_rows, band_cols, total_rows, start_ref, mask_ref):
    band_start = start_ref[0]
    tile = pl.program_id(0)
    shape = mask_ref.shape[1:]
    first = region_top(tile, band_start, band_rows, total_rows)
    key = lax.broadcasted_iota(jnp.int32, shape, 0)
    query = lax.broadcasted_iota(jnp.int32, shape, 1) & (TILE_R * band_cols - 1)
    key_row = band_start - MARGIN + first + (key >> (KEY_COLS.bit_length() - 1))
    place = key & (KEY_COLS - 1)
    query_row = band_start + tile * TILE_R + (query >> (band_cols.bit_length() - 1))
    query_col = query & (band_cols - 1)
    window = jnp.clip(query_row - MARGIN, 0, total_rows - WIN)
    row_inside = (key_row >= window) & (key_row < window + WIN)
    key_col = jnp.where(
        place < band_cols,
        place,
        jnp.where(place < band_cols + MARGIN, place - band_cols - MARGIN, place - MARGIN),
    )
    col_inside = (jnp.abs(key_col - query_col) <= MARGIN) & (place < band_cols + 2 * MARGIN)
    mask_ref[0] = jnp.where(row_inside & col_inside, 0.0, NEG).astype(BF)


def window_masks(start, band_rows, band_cols, total_rows):
    tiles = band_rows // TILE_R
    shape = (REGION_R * KEY_COLS, 2 * TILE_R * band_cols)
    return pl.pallas_call(
        functools.partial(mask_kernel, band_rows, band_cols, total_rows),
        grid=(tiles,),
        in_specs=[pl.BlockSpec(memory_space=pltpu.SMEM)],
        out_specs=pl.BlockSpec((1,) + shape, lambda t: (t, 0, 0)),
        out_shape=jax.ShapeDtypeStruct((tiles,) + shape, BF),
        cost_estimate=pl.CostEstimate(flops=10**7, bytes_accessed=2**21, transcendentals=0),
    )(start)


def attention_kernel(band_rows, band_cols, total_rows, head_width, extra, first, count, shift, *refs):
    (place_ref, mask_ref, left_ref, right_ref, rows_a, rows_b, corners_a, corners_b,
     qkv_hbm, grad_hbm, w_hbm) = refs[:11]
    before_a, before_b = refs[11 : 11 + shift], refs[11 + shift : 11 + 2 * shift]
    (dq_all, out_a_all, out_b_all, mid_all, to_left_all, to_right_all,
     halo_ref, spot_ref, q_ref, k_ref, v_ref, dk_ref, dv_ref,
     own_refs, w_refs, own_sem, w_sem) = refs[11 + extra :]
    band_start = place_ref[0]
    even = place_ref[1] == 0
    tiles = band_rows // TILE_R
    queries = TILE_R * band_cols
    keys = REGION_R * KEY_COLS
    width = GROUP * head_width
    lanes = GROUP * queries
    region_rows = band_rows + 2 * MARGIN
    side = MARGIN * band_rows
    edge = MARGIN * band_cols
    corner = 2 * MARGIN * EDGE_R
    at_above = 2 * side
    at_below = at_above + edge
    at_cl = at_below + edge
    at_cr = at_cl + corner
    halves = [(i, slice(i * LANES, (i + 1) * LANES)) for i in range(width // LANES)]

    step = pl.program_id(0)
    dq_ref, mid_ref, to_left_ref, to_right_ref = (
        ref.at[step] for ref in (dq_all, mid_all, to_left_all, to_right_all)
    )
    out_a, out_b = (ref.at[step + shift] for ref in (out_a_all, out_b_all))
    groups = HEADS // GROUP

    def copies(slot, parts):
        at = lambda part: pl.ds((part * groups + first + slot) * width, width)
        for part, source, where, i in parts:
            target, sem = (w_refs, w_sem) if where else (own_refs, own_sem)
            yield pltpu.make_async_copy(source.at[:, at(part)], target.at[slot, i], sem.at[slot, i])

    for_k = ((1, w_hbm, 1, 0), (1, qkv_hbm, 0, 1))
    for_v = ((2, w_hbm, 1, 1), (2, qkv_hbm, 0, 2))
    for_q = ((0, qkv_hbm, 0, 0), (0, grad_hbm, 0, 3))

    def await_copies(parts):
        for slot in range(count):

            @pl.when(step == slot)
            def _():
                for copy in copies(slot, parts):
                    copy.wait()

    @pl.when(step == 0)
    def _():
        for ref, kept in ((out_a_all, before_a), (out_b_all, before_b)):
            for i in range(shift):
                ref[i] = kept[0][i]
        for slot in range(count):
            for copy in copies(slot, for_k + for_v + for_q):
                copy.start()
        halo_ref[:side] = left_ref[...]
        halo_ref[side:at_above] = right_ref[...]
        for above, below, size, refs_ab in (
            (at_above, at_below, edge, (rows_a, rows_b)),
            (at_cl, at_cr, corner, (corners_a, corners_b)),
        ):
            for ref, at in zip(refs_ab, (jnp.where(even, below, above), jnp.where(even, above, below))):
                halo_ref[pl.ds(pl.multiple_of(at, 16), size), :] = ref[...]
        spot_ref[...] = jnp.zeros_like(spot_ref)

    def place(target, own, weights):
        fresh = dot(halo_ref[...], weights)
        for col in range(MARGIN):
            start = MARGIN * HALO_COLS + col
            for part, at in halves:
                spot_ref[part, pl.ds(start, band_rows, stride=HALO_COLS), :] = fresh[
                    col * band_rows : (col + 1) * band_rows, at
                ]
                spot_ref[part, pl.ds(start + MARGIN, band_rows, stride=HALO_COLS), :] = fresh[
                    side + col * band_rows : side + (col + 1) * band_rows, at
                ]
        for corner_at, skip, row in ((at_cl, PAD_R, 0), (at_cr, 0, MARGIN + band_rows)):
            for col in range(2 * MARGIN):
                base = corner_at + col * EDGE_R + skip
                spot = pl.ds(row * HALO_COLS + col, MARGIN, stride=HALO_COLS)
                for part, at in halves:
                    spot_ref[part, spot, :] = fresh[base : base + MARGIN, at]
        for row in range(region_rows):
            base = row * KEY_COLS
            inner = row - MARGIN
            if inner < 0:
                ours = fresh[at_above + row * band_cols : at_above + (row + 1) * band_cols].astype(BF)
            elif inner < band_rows:
                ours = own[inner * band_cols : (inner + 1) * band_cols, :]
            else:
                past = at_below + (inner - band_rows) * band_cols
                ours = fresh[past : past + band_cols].astype(BF)
            target[base : base + band_cols, :] = ours
            for part, at in halves:
                target[base + band_cols : base + KEY_COLS, at] = spot_ref[
                    part, row * HALO_COLS : (row + 1) * HALO_COLS, :
                ].astype(BF)

    grad_ref = own_refs.at[step, 3]
    await_copies(for_k)
    place(k_ref, own_refs.at[step, 1], w_refs[step, 0])
    await_copies(for_v)
    place(v_ref, own_refs.at[step, 2], w_refs[step, 1])
    await_copies(for_q)
    q_ref[...] = own_refs[step, 0] * BF(head_width**-0.5)
    dk_ref[...] = jnp.zeros_like(dk_ref)
    dv_ref[...] = jnp.zeros_like(dv_ref)

    def spread(rows):
        block = jnp.concatenate([rows] * GROUP, axis=0)
        head_row = lax.broadcasted_iota(jnp.int32, (lanes, width), 0) // queries
        head_col = lax.broadcasted_iota(jnp.int32, (lanes, width), 1) // head_width
        return jnp.where(head_row == head_col, block, jnp.zeros_like(block))

    def one_tile(tile, carry):
        first = region_top(tile, band_start, band_rows, total_rows)
        region = pl.ds(pl.multiple_of(first * KEY_COLS, TILE_R * KEY_COLS), keys)
        total = pl.ds(pl.multiple_of((first + PAD_R) * KEY_COLS, PAD_R * KEY_COLS), keys)
        mine = pl.ds(pl.multiple_of(tile * queries, queries), queries)
        q_wide = spread(q_ref[mine, :])
        g_wide = spread(grad_ref[mine, :])
        mask = mask_ref[tile].astype(F32)
        scores = dot(k_ref[region, :], q_wide, NT) + jnp.concatenate([mask, mask], axis=1)
        dots = dot(v_ref[region, :], g_wide, NT)
        exponent = jnp.exp(scores - jnp.max(scores, axis=0, keepdims=True))
        inverse = 1.0 / jnp.sum(exponent, axis=0, keepdims=True)
        delta = jnp.sum(exponent * dots, axis=0, keepdims=True) * inverse
        attn = exponent * inverse
        dscore = (attn * (dots - delta)).astype(BF)
        dv = dot(attn.astype(BF), g_wide)
        dk = dot(dscore, q_wide)
        for part, at in halves:
            dv_ref[part, total, :] += dv[:, at]
            dk_ref[part, total, :] += dk[:, at]
        dq_wide = dot(dscore, k_ref[region, :], TN)
        head_col = lax.broadcasted_iota(jnp.int32, (queries, width), 1) // head_width
        dq = jnp.zeros((queries, width), F32)
        for head in range(GROUP):
            dq = jnp.where(head_col == head, dq_wide[head * queries : (head + 1) * queries], dq)
        dq_ref[mine, :] = (dq * head_width**-0.5).astype(BF)
        return carry

    lax.fori_loop(0, tiles, one_tile, 0, unroll=4)

    middle = (PAD_R + MARGIN) * KEY_COLS
    below = (PAD_R + MARGIN + band_rows) * KEY_COLS
    for part, acc in enumerate((dk_ref, dv_ref)):
        for lane, at in halves:
            for out, own_at, side_at in (
                (out_a, jnp.where(even, below, PAD_R * KEY_COLS), jnp.where(even, below, 0)),
                (out_b, jnp.where(even, PAD_R * KEY_COLS, below), jnp.where(even, 0, below)),
            ):
                for row in range(MARGIN):
                    start = pl.multiple_of(own_at + row * KEY_COLS, KEY_COLS)
                    out[part, row * band_cols : (row + 1) * band_cols, at] = acc[
                        lane, pl.ds(start, band_cols), :
                    ].astype(BF)
                for pair in range(MARGIN):
                    here = slice(edge + pair * 2 * EDGE_R, edge + (pair + 1) * 2 * EDGE_R)
                    start = side_at + band_cols + 2 * pair
                    out[part, here, at] = jnp.concatenate(
                        [
                            acc[lane, pl.ds(start, EDGE_R, stride=KEY_COLS), :],
                            acc[lane, pl.ds(start + 1, EDGE_R, stride=KEY_COLS), :],
                        ],
                        axis=0,
                    ).astype(BF)
            for row in range(band_rows):
                base = middle + row * KEY_COLS
                mid_ref[part, row * band_cols : (row + 1) * band_cols, at] = acc[
                    lane, base : base + band_cols, :
                ].astype(BF)
            for col in range(MARGIN):
                here = slice(col * band_rows, (col + 1) * band_rows)
                start = middle + band_cols + col
                to_left_ref[part, here, at] = acc[
                    lane, pl.ds(start, band_rows, stride=KEY_COLS), :
                ].astype(BF)
                to_right_ref[part, here, at] = acc[
                    lane, pl.ds(start + MARGIN, band_rows, stride=KEY_COLS), :
                ].astype(BF)


def attention_grads(first, count, place, masks, halo, qkv, grad_out, w_qkv, shape, before, after):
    band_rows, band_cols, total_rows = shape
    tokens, width = grad_out.shape
    head_width = width // HEADS
    block = GROUP * head_width
    region_tokens = (band_rows + 2 * MARGIN) * KEY_COLS
    total_tokens = (band_rows + 2 * MARGIN + 2 * PAD_R) * KEY_COLS
    side = MARGIN * band_rows
    edge = MARGIN * (band_cols + 2 * EDGE_R)
    corner = 2 * MARGIN * EDGE_R
    halo_tokens = 2 * (side + MARGIN * band_cols + corner)
    shift = before[0].shape[0] if before else 0
    vmem = pl.BlockSpec(memory_space=pltpu.VMEM)
    shapes = [
        (count, tokens, block),
        (count + shift, 2, edge, block),
        (count + shift, 2, edge, block),
        (count, 2, tokens, block),
        (count, 2, side, block),
        (count, 2, side, block),
    ]
    return pl.pallas_call(
        functools.partial(
            attention_kernel, band_rows, band_cols, total_rows, head_width,
            len(before) + len(after), first, count, shift,
        ),
        grid=(count,),
        in_specs=[pl.BlockSpec(memory_space=pltpu.SMEM)]
        + [vmem] * (1 + len(halo))
        + [pl.BlockSpec(memory_space=pltpu.HBM)] * 3
        + [vmem] * len(before)
        + [pl.BlockSpec(memory_space=pl.ANY)] * len(after),
        out_specs=[vmem] * len(shapes),
        out_shape=[jax.ShapeDtypeStruct(s, BF) for s in shapes],
        scratch_shapes=[
            pltpu.VMEM((halo_tokens, width), BF),
            pltpu.VMEM((block // LANES, (band_rows + 2 * MARGIN) * HALO_COLS, LANES), F32),
            pltpu.VMEM((tokens, block), BF),
            pltpu.VMEM((region_tokens, block), BF),
            pltpu.VMEM((region_tokens, block), BF),
            pltpu.VMEM((block // LANES, total_tokens, LANES), F32),
            pltpu.VMEM((block // LANES, total_tokens, LANES), F32),
            pltpu.VMEM((count, 4, tokens, block), BF),
            pltpu.VMEM((count, 2, width, block), BF),
            pltpu.SemaphoreType.DMA((count, 4)),
            pltpu.SemaphoreType.DMA((count, 2)),
        ],
        compiler_params=pltpu.CompilerParams(
            dimension_semantics=("arbitrary",), vmem_limit_bytes=ATTENTION_MIB * MIB
        ),
        cost_estimate=pl.CostEstimate(
            flops=count * 14 * 10**9, bytes_accessed=count * 8 * MIB, transcendentals=count * 10**6
        ),
    )(place, masks, *halo, qkv, grad_out, w_qkv, *before, *after)


def on_chip(kernel, out_shape, operands, after=(), scratch=(), flops=10**5, place=()):
    count = len(operands) + len(place)

    def run(*refs):
        kernel(*refs[:count], *refs[count + len(after) :])

    return pl.pallas_call(
        run,
        in_specs=[pl.BlockSpec(memory_space=pltpu.SMEM)] * len(place)
        + [pl.BlockSpec(memory_space=pltpu.VMEM)] * len(operands)
        + [pl.BlockSpec(memory_space=pl.ANY)] * len(after),
        out_specs=[pl.BlockSpec(memory_space=pltpu.VMEM)] * len(out_shape),
        out_shape=[jax.ShapeDtypeStruct(s, d) for s, d in out_shape],
        scratch_shapes=list(scratch),
        compiler_params=pltpu.CompilerParams(vmem_limit_bytes=24 * MIB),
        cost_estimate=pl.CostEstimate(flops=flops, bytes_accessed=10**4, transcendentals=0),
    )(*place, *operands, *after)


def lanes_of(width):
    return [(i, slice(i * LANES, (i + 1) * LANES)) for i in range(width // LANES)]


def project(own, w_qkv, after):
    tokens, width = own.shape
    columns = w_qkv.shape[1]
    block = 4 * LANES

    def kernel(own_ref, w_ref, *refs):
        refs[-1][...] = dot(own_ref[...], w_ref[...]).astype(BF)

    return pl.pallas_call(
        kernel,
        grid=(columns // block,),
        in_specs=[
            pl.BlockSpec((tokens, width), lambda g: (0, 0)),
            pl.BlockSpec((width, block), lambda g: (0, g)),
        ]
        + [pl.BlockSpec(memory_space=pl.ANY)] * len(after),
        out_specs=pl.BlockSpec((tokens, block), lambda g: (0, g)),
        out_shape=jax.ShapeDtypeStruct((tokens, columns), BF),
        compiler_params=pltpu.CompilerParams(vmem_limit_bytes=24 * MIB),
        cost_estimate=pl.CostEstimate(flops=10**9, bytes_accessed=MIB, transcendentals=0),
    )(own, w_qkv, *after)


def input_grads(columns, w_qkv, after):
    tokens = columns[0].shape[-2]
    width, total = w_qkv.shape
    count = len(columns)
    pieces = list(pieces_of(columns))
    steps = len(pieces) // 2

    def kernel(*refs):
        w_ref, (out_ref, done_ref, acc_ref) = refs[count], refs[-3:]
        for step in range(steps):

            @pl.when(pl.program_id(0) == step)
            def _():
                both = [piece(refs, *where) for where in pieces[2 * step : 2 * step + 2]]
                product = dot(jnp.concatenate(both, axis=1), w_ref[...], NT)
                if step == 0:
                    acc_ref[...] = product
                elif step < steps - 1:
                    acc_ref[...] += product
                else:
                    out_ref[...] = (acc_ref[...] + product).astype(BF)
                    done_ref[...] = jnp.zeros_like(done_ref)

    return pl.pallas_call(
        kernel,
        grid=(steps,),
        in_specs=[pl.BlockSpec(memory_space=pltpu.VMEM)] * count
        + [pl.BlockSpec((width, total // steps), lambda g: (0, g))]
        + [pl.BlockSpec(memory_space=pl.ANY)] * len(after),
        out_specs=[
            pl.BlockSpec((tokens, width), lambda g: (0, 0)),
            pl.BlockSpec((8, LANES), lambda g: (0, 0)),
        ],
        out_shape=[
            jax.ShapeDtypeStruct((tokens, width), BF),
            jax.ShapeDtypeStruct((8, LANES), F32),
        ],
        scratch_shapes=[pltpu.VMEM((tokens, width), F32)],
        compiler_params=pltpu.CompilerParams(vmem_limit_bytes=24 * MIB),
        cost_estimate=pl.CostEstimate(flops=4 * 10**9, bytes_accessed=MIB, transcendentals=0),
    )(*columns, w_qkv, *after)


def row_blocks(place, own, orders, after):
    tokens, width = own.shape
    devices = len(orders[0])
    size = width // devices
    step = max(1, 16 // size)

    def kernel(place_ref, own_ref, low_ref, high_ref, wide_ref):
        for at in range(0, width, 2 * LANES):
            wide_ref[at : at + 2 * LANES, :] = own_ref[:, at : at + 2 * LANES].astype(F32).T
        even = place_ref[1] == 0
        me = place_ref[2]
        for j in range(0, devices, step):
            rows = []
            for k in range(j, j + step):
                owner = me ^ jnp.where(even, int(orders[0][k]), int(orders[1][k]))
                rows.append(wide_ref[pl.ds(pl.multiple_of(owner * size, size), size), :])
            half, base = divmod(j * size, width // 2)
            block = rows[0] if step == 1 else jnp.concatenate(rows, axis=0)
            (low_ref, high_ref)[half][base : base + step * size, :] = block.astype(BF)

    out = ((width // 2, tokens), BF)
    scratch = [pltpu.VMEM((width, tokens), F32)]
    return on_chip(kernel, [out, out], [own], after=after, scratch=scratch, place=[place])


def pack_sides(own, band_rows, band_cols):
    tokens, width = own.shape

    def kernel(own_ref, last_ref, first_ref, wide_ref):
        for lane, at in lanes_of(width):
            wide_ref[lane] = own_ref[:, at].astype(F32)
            for col in range(MARGIN):
                here = slice(col * band_rows, (col + 1) * band_rows)
                last = pl.ds(band_cols - MARGIN + col, band_rows, stride=band_cols)
                last_ref[here, at] = wide_ref[lane, last, :].astype(BF)
                first = pl.ds(col, band_rows, stride=band_cols)
                first_ref[here, at] = wide_ref[lane, first, :].astype(BF)

    out = ((MARGIN * band_rows, width), BF)
    scratch = [pltpu.VMEM((width // LANES, tokens, LANES), F32)]
    return on_chip(kernel, [out, out], [own], scratch=scratch)


def pack_rows(place, own, band_cols, after):
    tokens, width = own.shape
    edge = MARGIN * band_cols

    def kernel(place_ref, own_ref, out_a, out_b):
        even = place_ref[1] == 0
        last, first = own_ref[tokens - edge :, :], own_ref[:edge, :]
        out_a[...] = jnp.where(even, last, first)
        out_b[...] = jnp.where(even, first, last)

    out = ((edge, width), BF)
    return on_chip(kernel, [out, out], [own], after=after, place=[place])


def pack_corners(place, left, right, band_rows, after):
    width = left.shape[1]

    def kernel(place_ref, left_ref, right_ref, out_a, out_b):
        even = place_ref[1] == 0
        for side, side_ref in enumerate((left_ref, right_ref)):
            for col in range(0, MARGIN, 2):
                base = (side * MARGIN + col) * EDGE_R
                last, first = (
                    jnp.concatenate(
                        [
                            side_ref[at : at + EDGE_R, :].astype(F32)
                            for at in (start, start + band_rows)
                        ]
                    )
                    for start in ((col + 1) * band_rows - EDGE_R, col * band_rows)
                )
                here = slice(base, base + 2 * EDGE_R)
                out_a[here, :] = jnp.where(even, last, first).astype(BF)
                out_b[here, :] = jnp.where(even, first, last).astype(BF)

    out = ((2 * MARGIN * EDGE_R, width), BF)
    return on_chip(kernel, [out, out], [left, right], after=after, place=[place])


def merge_sides(place, lefts, rights, rim_a, rim_b, band_rows, band_cols, after=()):
    edge = MARGIN * band_cols
    calls = len(lefts)
    slots = rim_a.shape[0]
    each = slots // calls

    def kernel(place_ref, *refs):
        sides = refs[:calls], refs[calls : 2 * calls]
        a_ref, b_ref, *outs = refs[2 * calls :]
        even = place_ref[1] == 0
        for slot in range(slots):
            for part in range(2):
                for col in range(2 * MARGIN):
                    source = sides[col // MARGIN][slot // each]
                    base = (col % MARGIN) * band_rows
                    pair = slice(edge + (col // 2) * 2 * EDGE_R, edge + (col // 2 + 1) * 2 * EDGE_R)
                    odd = slice((col % 2) * EDGE_R, (col % 2 + 1) * EDGE_R)
                    rows = source[slot % each, part, base : base + band_rows, :].astype(F32)
                    from_a, from_b = (
                        ref[slot, part, pair, :].astype(F32)[odd] for ref in (a_ref, b_ref)
                    )
                    first = rows[:EDGE_R] + jnp.where(even, from_b, from_a)
                    last = rows[band_rows - EDGE_R :] + jnp.where(even, from_a, from_b)
                    outs[col // MARGIN][slot, part, base : base + band_rows, :] = jnp.concatenate(
                        [first, rows[EDGE_R : band_rows - EDGE_R], last], axis=0
                    ).astype(BF)

    out = ((slots,) + lefts[0].shape[1:], BF)
    return on_chip(kernel, [out, out], [*lefts, *rights, rim_a, rim_b], after, place=[place])


def finish(place, mids, rim_a, rim_b, left, right, parts, band_rows, band_cols, after, flops):
    calls = len(mids)
    slots, _, _, block = rim_a.shape
    each = slots // calls
    edge = MARGIN * band_cols
    tokens = band_rows * band_cols

    def kernel(place_ref, *refs):
        a_ref, b_ref, left_ref, right_ref, *outs, acc_ref = refs[calls:]
        even = place_ref[1] == 0
        for out_ref, part in zip(outs, parts):
            for slot in range(slots):
                for lane, at in lanes_of(block):
                    acc_ref[lane] = refs[slot // each][slot % each, part, :, at].astype(F32)
                    from_a, from_b = (
                        r[slot, part, :edge, at].astype(F32) for r in (a_ref, b_ref)
                    )
                    acc_ref[lane, :edge, :] += jnp.where(even, from_b, from_a)
                    acc_ref[lane, tokens - edge :, :] += jnp.where(even, from_a, from_b)
                    for col in range(MARGIN):
                        here = slice(col * band_rows, (col + 1) * band_rows)
                        first = pl.ds(col, band_rows, stride=band_cols)
                        last = pl.ds(band_cols - MARGIN + col, band_rows, stride=band_cols)
                        acc_ref[lane, first, :] += left_ref[slot, part, here, at].astype(F32)
                        acc_ref[lane, last, :] += right_ref[slot, part, here, at].astype(F32)
                    start = slot * block + lane * LANES
                    out_ref[:, start : start + LANES] = acc_ref[lane].astype(BF)

    out = [((tokens, slots * block), BF)] * len(parts)
    scratch = [pltpu.VMEM((block // LANES, tokens, LANES), F32)]
    operands = [*mids, rim_a, rim_b, left, right]
    return on_chip(kernel, out, operands, after, scratch, flops, [place])


def pieces_of(arrays):
    for i, array in enumerate(arrays):
        slots = range(array.shape[0]) if array.ndim == 3 else [None]
        for slot in slots:
            for start in range(0, array.shape[-1], 2 * LANES):
                yield i, slot, start


def piece(refs, i, slot, start):
    here = slice(start, start + 2 * LANES)
    return refs[i][:, here] if slot is None else refs[i][slot, :, here]


def grad_rows(rows, columns, scale, kind, after=()):
    features, count = rows.shape[0], len(columns)
    pieces = list(pieces_of(columns))

    def kernel(rows_ref, *refs):
        for at, where in enumerate(pieces):
            part = dot(rows_ref[...], piece(refs, *where))
            here = slice(at * 2 * LANES, (at + 1) * 2 * LANES)
            refs[count][:, here] = (part * scale).astype(kind)

    out = [((features, len(pieces) * 2 * LANES), kind)]
    return on_chip(kernel, out, [rows, *columns], after)[0]


def add_split(keep, received, after=()):
    half, columns = keep.shape[0] // 2, keep.shape[1]

    def kernel(keep_ref, received_ref, sums_ref, send_ref):
        sums_ref[...] = keep_ref[:half, :] + received_ref[:half, :].astype(F32)
        send_ref[...] = (keep_ref[half:, :] + received_ref[half:, :].astype(F32)).astype(BF)

    return on_chip(kernel, [((half, columns), F32), ((half, columns), BF)], [keep, received], after)


def sent_blocks(keep, received, blocks, after):
    rows, columns = keep.shape
    size = rows // blocks

    def kernel(keep_ref, received_ref, sums_ref, *sends):
        sums_ref[0] = keep_ref[:size, :] + received_ref[:size, :].astype(F32)
        for b in range(1, blocks):
            here = slice(b * size, (b + 1) * size)
            sends[b - 1][0] = (keep_ref[here, :] + received_ref[here, :].astype(F32)).astype(BF)

    shape = (1, size, columns)
    out = [(shape, F32)] + [(shape, BF)] * (blocks - 1)
    return on_chip(kernel, out, [keep, received], after)


def gather_sums(groups, places, width, after, flops):
    flat = [array for group in groups for array in group]

    def kernel(*refs):
        out_ref = refs[-1]
        at = 0
        for group, moves in zip(groups, places):
            mine = refs[at : at + len(group)]
            at += len(group)
            for source, size, target in moves:
                here = slice(source, source + size)
                parts = [ref[i, :, here].astype(F32) for ref in mine for i in range(ref.shape[0])]
                out_ref[:, target : target + size] = functools.reduce(lambda a, b: a + b, parts)

    return on_chip(kernel, [((flat[0].shape[1], width), F32)], flat, after, flops=flops)[0]


def shifted(array, axis, by, wrap):
    size = lax.axis_size(axis)
    route = [(i, (i + by) % size) for i in range(size) if wrap or 0 <= i + by < size]
    return lax.ppermute(array, axis, route)


def swapped(array_a, array_b, axis):
    size = lax.axis_size(axis)
    pairs = [(i, i + 1) for i in range(size - 1)]
    route = lambda chosen: chosen + [(j, i) for i, j in chosen]
    return [
        lax.ppermute(array, axis, route(pairs[offset::2]))
        for array, offset in ((array_a, 0), (array_b, 1))
    ]


def exchanged(array, axis, flip):
    return lax.ppermute(array, axis, [(i, i ^ flip) for i in range(lax.axis_size(axis))])


def bits_of(axis):
    return [(axis, 1 << b) for b in range((lax.axis_size(axis) - 1).bit_length())]


def reduce_stages():
    first, *lat_bits = bits_of("lat")
    bits = bits_of("dp") + lat_bits
    return first, list(zip(bits, reversed(bits)))


def feature_orders(first, stages):
    n_lon, n_lat = lax.axis_size("lon"), lax.axis_size("lat")
    unit = {"lon": 1, "lat": n_lon, "dp": n_lon * n_lat}
    lower = []
    for kind in range(2):
        order = np.arange(n_lon)
        for stage in reversed(stages):
            axis, bit = stage[kind]
            order = np.concatenate([order, order + unit[axis] * bit])
        lower.append(order)
    flip = unit[first[0]] * first[1]
    return [np.concatenate([lower[kind], lower[1 - kind] ^ flip]) for kind in range(2)]


def exchanged_stage(array, stage):
    n_lat, n_dp = lax.axis_size("lat"), lax.axis_size("dp")
    route = []
    for i in range(n_dp * n_lat):
        axis, bit = stage[i % n_lat % 2]
        route.append((i, i ^ (bit * n_lat if axis == "dp" else bit)))
    return lax.ppermute(array, ("dp", "lat"), route)


def body(inputs, grad_out, w_qkv):
    _, band_rows, band_cols, width = inputs.shape
    n_lat, n_lon, n_dp = lax.axis_size("lat"), lax.axis_size("lon"), lax.axis_size("dp")
    band_start = lax.axis_index("lat") * band_rows
    total_rows = band_rows * n_lat
    tokens = band_rows * band_cols
    slots = HEADS // GROUP // 2
    shape = (band_rows, band_cols, total_rows)
    own = inputs.reshape(tokens, width)
    flat_grad = grad_out.reshape(tokens, width)

    last_cols, first_cols = pack_sides(own, band_rows, band_cols)
    left = shifted(last_cols, "lon", 1, True)
    right = shifted(first_cols, "lon", -1, True)
    me = (lax.axis_index("dp") * n_lat + lax.axis_index("lat")) * n_lon + lax.axis_index("lon")
    start = jnp.stack([band_start, lax.axis_index("lat") % 2, me])
    rim_rows = swapped(*pack_rows(start, own, band_cols, [last_cols]), "lat")

    masks = window_masks(start, band_rows, band_cols, total_rows)
    qkv = project(own, w_qkv, [last_cols])
    first, stages = reduce_stages()
    half = width // 2
    rows_keep, rows_send = row_blocks(start, own, feature_orders(first, stages), [last_cols])
    corners = pack_corners(start, left, right, band_rows, [masks, qkv, rows_keep, rows_send])
    halo = (left, right, *rim_rows, *swapped(*corners, "lat"))
    scale = float(tokens * n_dp * n_lat * n_lon) ** -0.5

    attend = lambda first, count, before, after: attention_grads(
        first, count, start, masks, halo, qkv, flat_grad, w_qkv, shape, before, after
    )

    def return_sides(calls, rims, after):
        to_left, to_right = merge_sides(
            start, [c[4] for c in calls], [c[5] for c in calls], *rims, band_rows, band_cols, after
        )
        from_right = shifted(to_left, "lon", -1, True)
        from_left = shifted(to_right, "lon", 1, True)
        return to_left, from_left, from_right

    def finished(calls, rims, sides, parts, after, flops):
        mids = [c[3] for c in calls]
        return finish(start, mids, *rims, *sides, parts, band_rows, band_cols, after, flops)

    groups = HEADS // GROUP
    one = attend(0, slots, [], [])
    rims_1 = swapped(one[1], one[2], "lat")
    two = attend(slots, groups - slots - 1, [], [one[0]])
    sent, *sides_1 = return_sides([one], rims_1, [two[0]])
    three = attend(groups - 1, 1, [two[1], two[2]], [sent])
    rims_2 = swapped(three[1], three[2], "lat")
    dq = [one[0], two[0], three[0]]

    dk_1, dv_1 = finished([one], rims_1, sides_1, (0, 1), [three[0]], 2 * 10**9)
    sent, *sides_2 = return_sides([two, three], rims_2, [dk_1])
    send = grad_rows(rows_send, [*dq, dk_1, dv_1], scale, BF, after=[sent])
    received = exchanged(send, *first)
    keep = grad_rows(rows_keep, [*dq, dk_1, dv_1], scale, F32, after=[send])
    keep, send = add_split(keep, received)

    (dk_2,) = finished([two, three], rims_2, sides_2, (0,), [keep], FINISH_FLOPS)
    for stage in stages[:-1]:
        keep, send = add_split(keep, exchanged_stage(send, stage), [dk_2])
    received = exchanged_stage(send, stages[-1])
    (dv_2,) = finished([two, three], rims_2, sides_2, (1,), [keep], 10**5)
    send_2 = grad_rows(rows_send, [dk_2, dv_2], scale, BF)
    received_2 = exchanged(send_2, *first)
    keep_2 = grad_rows(rows_keep, [dk_2, dv_2], scale, F32, after=[send_2])
    keep_2, send_2 = add_split(keep_2, received_2)
    received_2 = exchanged_stage(send_2, stages[0])
    grad_inputs, done = input_grads([*dq, dk_1, dk_2, dv_1, dv_2], w_qkv, [send_2])
    keep, *send = sent_blocks(keep, received, n_lon, [done])
    group_1 = [keep] + [exchanged(a, "lon", i + 1) for i, a in enumerate(send)]
    sum_1 = gather_sums([group_1], [[(0, 2 * width, 0)]], 2 * width, [], GATHER_FLOPS)[None]
    for stage in stages[1:]:
        keep_2, send_2 = add_split(keep_2, received_2, [keep])
        received_2 = exchanged_stage(send_2, stage)
    keep_2, *send_2 = sent_blocks(keep_2, received_2, n_lon, [])
    group_2 = [keep_2] + [exchanged(a, "lon", i + 1) for i, a in enumerate(send_2)]
    places = [
        [(0, width, 0), (width, half, width), (width + half, half, 2 * width)],
        [(0, half, width + half), (half, half, 2 * width + half)],
    ]
    grad_w = gather_sums([[sum_1], group_2], places, 3 * width, [], 10**5)
    return (grad_inputs.reshape(inputs.shape), grad_w)


def solution(mesh):
    in_specs = (P("dp", "lat", "lon", None), P("dp", "lat", "lon", None), P())
    out_specs = (P("dp", "lat", "lon", None), P(("dp", "lat", "lon"), None))
    return jax.shard_map(body, mesh=mesh, in_specs=in_specs, out_specs=out_specs, check_vma=False)
```

```python
import functools

import jax
import jax.numpy as jnp
import numpy as np
from jax import lax
from jax.experimental import pallas as pl
from jax.experimental.pallas import tpu as pltpu
from jax.sharding import PartitionSpec as P

HEADS = 16
WIN = 13
MARGIN = WIN // 2
TILE_R = 4
GROUP = 4
KEY_COLS = 32
HALO_COLS = 16
REGION_R = 16
PAD_R = 2
EDGE_R = MARGIN + PAD_R
NEG = -1e30
BF = jnp.bfloat16
F32 = jnp.float32
MIB = 1024 * 1024
FINISH_FLOPS = 9 * 10**9
LANES = 128
ATTENTION_MIB = 32

NT = (((1,), (1,)), ((), ()))
TN = (((0,), (0,)), ((), ()))
NN = (((1,), (0,)), ((), ()))


def dot(a, b, dims=NN):
    return lax.dot_general(a, b, dims, preferred_element_type=F32)


def region_top(tile, band_start, band_rows, total_rows):
    lowest = jnp.where(band_start == 0, TILE_R, 0)
    highest = jnp.where(band_start + band_rows == total_rows, band_rows - 2 * TILE_R, band_rows)
    return jnp.clip(tile * TILE_R, lowest, highest)


def mask_kernel(band_rows, band_cols, total_rows, start_ref, mask_ref):
    band_start = start_ref[0]
    tile = pl.program_id(0)
    shape = mask_ref.shape[1:]
    first = region_top(tile, band_start, band_rows, total_rows)
    key = lax.broadcasted_iota(jnp.int32, shape, 0)
    query = lax.broadcasted_iota(jnp.int32, shape, 1) & (TILE_R * band_cols - 1)
    key_row = band_start - MARGIN + first + (key >> (KEY_COLS.bit_length() - 1))
    place = key & (KEY_COLS - 1)
    query_row = band_start + tile * TILE_R + (query >> (band_cols.bit_length() - 1))
    query_col = query & (band_cols - 1)
    window = jnp.clip(query_row - MARGIN, 0, total_rows - WIN)
    row_inside = (key_row >= window) & (key_row < window + WIN)
    key_col = jnp.where(
        place < band_cols,
        place,
        jnp.where(place < band_cols + MARGIN, place - band_cols - MARGIN, place - MARGIN),
    )
    col_inside = (jnp.abs(key_col - query_col) <= MARGIN) & (place < band_cols + 2 * MARGIN)
    mask_ref[0] = jnp.where(row_inside & col_inside, 0.0, NEG).astype(BF)


def window_masks(start, band_rows, band_cols, total_rows):
    tiles = band_rows // TILE_R
    shape = (REGION_R * KEY_COLS, 2 * TILE_R * band_cols)
    return pl.pallas_call(
        functools.partial(mask_kernel, band_rows, band_cols, total_rows),
        grid=(tiles,),
        in_specs=[pl.BlockSpec(memory_space=pltpu.SMEM)],
        out_specs=pl.BlockSpec((1,) + shape, lambda t: (t, 0, 0)),
        out_shape=jax.ShapeDtypeStruct((tiles,) + shape, BF),
        cost_estimate=pl.CostEstimate(flops=10**7, bytes_accessed=2**21, transcendentals=0),
    )(start)


def attention_kernel(band_rows, band_cols, total_rows, head_width, extra, first, count, shift, *refs):
    (place_ref, mask_ref, left_ref, right_ref, rows_a, rows_b, corners_a, corners_b,
     qkv_hbm, grad_hbm, w_hbm) = refs[:11]
    before_a, before_b = refs[11 : 11 + shift], refs[11 + shift : 11 + 2 * shift]
    (dq_all, out_a_all, out_b_all, mid_all, to_left_all, to_right_all,
     halo_ref, spot_ref, q_ref, k_ref, v_ref, dk_ref, dv_ref,
     own_refs, w_refs, own_sem, w_sem) = refs[11 + extra :]
    band_start = place_ref[0]
    even = place_ref[1] == 0
    tiles = band_rows // TILE_R
    queries = TILE_R * band_cols
    keys = REGION_R * KEY_COLS
    width = GROUP * head_width
    lanes = GROUP * queries
    region_rows = band_rows + 2 * MARGIN
    side = MARGIN * band_rows
    edge = MARGIN * band_cols
    corner = 2 * MARGIN * EDGE_R
    at_above = 2 * side
    at_below = at_above + edge
    at_cl = at_below + edge
    at_cr = at_cl + corner
    halves = [(i, slice(i * LANES, (i + 1) * LANES)) for i in range(width // LANES)]

    step = pl.program_id(0)
    dq_ref, mid_ref, to_left_ref, to_right_ref = (
        ref.at[step] for ref in (dq_all, mid_all, to_left_all, to_right_all)
    )
    out_a, out_b = (ref.at[step + shift] for ref in (out_a_all, out_b_all))
    groups = HEADS // GROUP

    def copies(slot, parts):
        at = lambda part: pl.ds(pl.multiple_of((part * groups + first + slot) * width, width), width)
        for part, source, where, i in parts:
            target, sem = (w_refs, w_sem) if where else (own_refs, own_sem)
            yield pltpu.make_async_copy(source.at[:, at(part)], target.at[slot, i], sem.at[slot, i])

    for_k = ((1, w_hbm, 1, 0), (1, qkv_hbm, 0, 1))
    for_v = ((2, w_hbm, 1, 1), (2, qkv_hbm, 0, 2))
    for_q = ((0, qkv_hbm, 0, 0), (0, grad_hbm, 0, 3))

    @pl.when(step == 0)
    def _():
        for ref, kept in ((out_a_all, before_a), (out_b_all, before_b)):
            for i in range(shift):
                ref[i] = kept[0][i]
        for slot in range(count):
            for copy in copies(slot, for_k + for_v + for_q):
                copy.start()
        halo_ref[:side] = left_ref[...]
        halo_ref[side:at_above] = right_ref[...]
        for above, below, size, refs_ab in (
            (at_above, at_below, edge, (rows_a, rows_b)),
            (at_cl, at_cr, corner, (corners_a, corners_b)),
        ):
            for ref, at in zip(refs_ab, (jnp.where(even, below, above), jnp.where(even, above, below))):
                halo_ref[pl.ds(pl.multiple_of(at, 16), size), :] = ref[...]
        spot_ref[...] = jnp.zeros_like(spot_ref)

    def place(target, own, weights):
        fresh = dot(halo_ref[...], weights)
        for col in range(MARGIN):
            start = MARGIN * HALO_COLS + col
            for part, at in halves:
                spot_ref[part, pl.ds(start, band_rows, stride=HALO_COLS), :] = fresh[
                    col * band_rows : (col + 1) * band_rows, at
                ]
                spot_ref[part, pl.ds(start + MARGIN, band_rows, stride=HALO_COLS), :] = fresh[
                    side + col * band_rows : side + (col + 1) * band_rows, at
                ]
        for corner_at, skip, row in ((at_cl, PAD_R, 0), (at_cr, 0, MARGIN + band_rows)):
            for col in range(2 * MARGIN):
                base = corner_at + col * EDGE_R + skip
                spot = pl.ds(row * HALO_COLS + col, MARGIN, stride=HALO_COLS)
                for part, at in halves:
                    spot_ref[part, spot, :] = fresh[base : base + MARGIN, at]
        for row in range(region_rows):
            base = row * KEY_COLS
            inner = row - MARGIN
            if inner < 0:
                ours = fresh[at_above + row * band_cols : at_above + (row + 1) * band_cols].astype(BF)
            elif inner < band_rows:
                ours = own[inner * band_cols : (inner + 1) * band_cols, :]
            else:
                past = at_below + (inner - band_rows) * band_cols
                ours = fresh[past : past + band_cols].astype(BF)
            target[base : base + band_cols, :] = ours
            for part, at in halves:
                target[base + band_cols : base + KEY_COLS, at] = spot_ref[
                    part, row * HALO_COLS : (row + 1) * HALO_COLS, :
                ].astype(BF)

    grad_ref = own_refs.at[step, 3]
    for copy in copies(step, for_k + for_v + for_q):
        copy.wait()
    place(k_ref, own_refs.at[step, 1], w_refs[step, 0])
    place(v_ref, own_refs.at[step, 2], w_refs[step, 1])
    q_ref[...] = own_refs[step, 0] * BF(head_width**-0.5)
    dk_ref[...] = jnp.zeros_like(dk_ref)
    dv_ref[...] = jnp.zeros_like(dv_ref)

    def spread(rows):
        block = jnp.concatenate([rows] * GROUP, axis=0)
        head_row = lax.broadcasted_iota(jnp.int32, (lanes, width), 0) // queries
        head_col = lax.broadcasted_iota(jnp.int32, (lanes, width), 1) // head_width
        return jnp.where(head_row == head_col, block, jnp.zeros_like(block))

    def one_tile(tile, carry):
        first = region_top(tile, band_start, band_rows, total_rows)
        region = pl.ds(pl.multiple_of(first * KEY_COLS, TILE_R * KEY_COLS), keys)
        total = pl.ds(pl.multiple_of((first + PAD_R) * KEY_COLS, PAD_R * KEY_COLS), keys)
        mine = pl.ds(pl.multiple_of(tile * queries, queries), queries)
        q_wide = spread(q_ref[mine, :])
        g_wide = spread(grad_ref[mine, :])
        mask = mask_ref[tile].astype(F32)
        scores = dot(k_ref[region, :], q_wide, NT) + jnp.concatenate([mask, mask], axis=1)
        dots = dot(v_ref[region, :], g_wide, NT)
        exponent = jnp.exp(scores - jnp.max(scores, axis=0, keepdims=True))
        inverse = 1.0 / jnp.sum(exponent, axis=0, keepdims=True)
        delta = jnp.sum(exponent * dots, axis=0, keepdims=True) * inverse
        attn = exponent * inverse
        dscore = (attn * (dots - delta)).astype(BF)
        dv = dot(attn.astype(BF), g_wide)
        dk = dot(dscore, q_wide)
        for part, at in halves:
            dv_ref[part, total, :] += dv[:, at]
            dk_ref[part, total, :] += dk[:, at]
        dq_wide = dot(dscore, k_ref[region, :], TN)
        head_col = lax.broadcasted_iota(jnp.int32, (queries, width), 1) // head_width
        dq = jnp.zeros((queries, width), F32)
        for head in range(GROUP):
            dq = jnp.where(head_col == head, dq_wide[head * queries : (head + 1) * queries], dq)
        dq_ref[mine, :] = (dq * head_width**-0.5).astype(BF)
        return carry

    lax.fori_loop(0, tiles, one_tile, 0, unroll=8)

    middle = (PAD_R + MARGIN) * KEY_COLS
    below = (PAD_R + MARGIN + band_rows) * KEY_COLS
    for part, acc in enumerate((dk_ref, dv_ref)):
        for lane, at in halves:
            for out, own_at, side_at in (
                (out_a, jnp.where(even, below, PAD_R * KEY_COLS), jnp.where(even, below, 0)),
                (out_b, jnp.where(even, PAD_R * KEY_COLS, below), jnp.where(even, 0, below)),
            ):
                for row in range(MARGIN):
                    start = pl.multiple_of(own_at + row * KEY_COLS, KEY_COLS)
                    out[part, row * band_cols : (row + 1) * band_cols, at] = acc[
                        lane, pl.ds(start, band_cols), :
                    ].astype(BF)
                for pair in range(MARGIN):
                    here = slice(edge + pair * 2 * EDGE_R, edge + (pair + 1) * 2 * EDGE_R)
                    start = side_at + band_cols + 2 * pair
                    out[part, here, at] = jnp.concatenate(
                        [
                            acc[lane, pl.ds(start, EDGE_R, stride=KEY_COLS), :],
                            acc[lane, pl.ds(start + 1, EDGE_R, stride=KEY_COLS), :],
                        ],
                        axis=0,
                    ).astype(BF)
            for row in range(band_rows):
                base = middle + row * KEY_COLS
                mid_ref[part, row * band_cols : (row + 1) * band_cols, at] = acc[
                    lane, base : base + band_cols, :
                ].astype(BF)
            for col in range(MARGIN):
                here = slice(col * band_rows, (col + 1) * band_rows)
                start = middle + band_cols + col
                to_left_ref[part, here, at] = acc[
                    lane, pl.ds(start, band_rows, stride=KEY_COLS), :
                ].astype(BF)
                to_right_ref[part, here, at] = acc[
                    lane, pl.ds(start + MARGIN, band_rows, stride=KEY_COLS), :
                ].astype(BF)


def attention_grads(first, count, place, masks, halo, qkv, grad_out, w_qkv, shape, before, after):
    band_rows, band_cols, total_rows = shape
    tokens, width = grad_out.shape
    head_width = width // HEADS
    block = GROUP * head_width
    region_tokens = (band_rows + 2 * MARGIN) * KEY_COLS
    total_tokens = (band_rows + 2 * MARGIN + 2 * PAD_R) * KEY_COLS
    side = MARGIN * band_rows
    edge = MARGIN * (band_cols + 2 * EDGE_R)
    corner = 2 * MARGIN * EDGE_R
    halo_tokens = 2 * (side + MARGIN * band_cols + corner)
    shift = before[0].shape[0] if before else 0
    vmem = pl.BlockSpec(memory_space=pltpu.VMEM)
    shapes = [
        (count, tokens, block),
        (count + shift, 2, edge, block),
        (count + shift, 2, edge, block),
        (count, 2, tokens, block),
        (count, 2, side, block),
        (count, 2, side, block),
    ]
    return pl.pallas_call(
        functools.partial(
            attention_kernel, band_rows, band_cols, total_rows, head_width,
            len(before) + len(after), first, count, shift,
        ),
        grid=(count,),
        in_specs=[pl.BlockSpec(memory_space=pltpu.SMEM)]
        + [vmem] * (1 + len(halo))
        + [pl.BlockSpec(memory_space=pltpu.HBM)] * 3
        + [vmem] * len(before)
        + [pl.BlockSpec(memory_space=pl.ANY)] * len(after),
        out_specs=[vmem] * len(shapes),
        out_shape=[jax.ShapeDtypeStruct(s, BF) for s in shapes],
        scratch_shapes=[
            pltpu.VMEM((halo_tokens, width), BF),
            pltpu.VMEM((block // LANES, (band_rows + 2 * MARGIN) * HALO_COLS, LANES), F32),
            pltpu.VMEM((tokens, block), BF),
            pltpu.VMEM((region_tokens, block), BF),
            pltpu.VMEM((region_tokens, block), BF),
            pltpu.VMEM((block // LANES, total_tokens, LANES), F32),
            pltpu.VMEM((block // LANES, total_tokens, LANES), F32),
            pltpu.VMEM((count, 4, tokens, block), BF),
            pltpu.VMEM((count, 2, width, block), BF),
            pltpu.SemaphoreType.DMA((count, 4)),
            pltpu.SemaphoreType.DMA((count, 2)),
        ],
        compiler_params=pltpu.CompilerParams(
            dimension_semantics=("arbitrary",), vmem_limit_bytes=ATTENTION_MIB * MIB
        ),
        cost_estimate=pl.CostEstimate(
            flops=count * 14 * 10**9, bytes_accessed=count * 8 * MIB, transcendentals=count * 10**6
        ),
    )(place, masks, *halo, qkv, grad_out, w_qkv, *before, *after)


def on_chip(kernel, out_shape, operands, after=(), scratch=(), flops=10**5, place=()):
    count = len(operands) + len(place)

    def run(*refs):
        kernel(*refs[:count], *refs[count + len(after) :])

    return pl.pallas_call(
        run,
        in_specs=[pl.BlockSpec(memory_space=pltpu.SMEM)] * len(place)
        + [pl.BlockSpec(memory_space=pltpu.VMEM)] * len(operands)
        + [pl.BlockSpec(memory_space=pl.ANY)] * len(after),
        out_specs=[pl.BlockSpec(memory_space=pltpu.VMEM)] * len(out_shape),
        out_shape=[jax.ShapeDtypeStruct(s, d) for s, d in out_shape],
        scratch_shapes=list(scratch),
        compiler_params=pltpu.CompilerParams(vmem_limit_bytes=24 * MIB),
        cost_estimate=pl.CostEstimate(flops=flops, bytes_accessed=10**4, transcendentals=0),
    )(*place, *operands, *after)


def lanes_of(width):
    return [(i, slice(i * LANES, (i + 1) * LANES)) for i in range(width // LANES)]


def project(own, w_qkv, after):
    tokens, width = own.shape
    columns = w_qkv.shape[1]
    block = 4 * LANES

    def kernel(own_ref, w_ref, *refs):
        refs[-1][...] = dot(own_ref[...], w_ref[...]).astype(BF)

    return pl.pallas_call(
        kernel,
        grid=(columns // block,),
        in_specs=[
            pl.BlockSpec((tokens, width), lambda g: (0, 0)),
            pl.BlockSpec((width, block), lambda g: (0, g)),
        ]
        + [pl.BlockSpec(memory_space=pl.ANY)] * len(after),
        out_specs=pl.BlockSpec((tokens, block), lambda g: (0, g)),
        out_shape=jax.ShapeDtypeStruct((tokens, columns), BF),
        compiler_params=pltpu.CompilerParams(vmem_limit_bytes=24 * MIB),
        cost_estimate=pl.CostEstimate(flops=10**9, bytes_accessed=MIB, transcendentals=0),
    )(own, w_qkv, *after)


def input_grads(columns, w_qkv, after):
    tokens = columns[0].shape[-2]
    width, total = w_qkv.shape
    count = len(columns)
    pieces = list(pieces_of(columns))
    steps = len(pieces) // 2

    def kernel(*refs):
        w_ref, (out_ref, done_ref, acc_ref) = refs[count], refs[-3:]
        for step in range(steps):

            @pl.when(pl.program_id(0) == step)
            def _():
                both = [piece(refs, *where) for where in pieces[2 * step : 2 * step + 2]]
                product = dot(jnp.concatenate(both, axis=1), w_ref[...], NT)
                if step == 0:
                    acc_ref[...] = product
                elif step < steps - 1:
                    acc_ref[...] += product
                else:
                    out_ref[...] = (acc_ref[...] + product).astype(BF)
                    done_ref[...] = jnp.zeros_like(done_ref)

    return pl.pallas_call(
        kernel,
        grid=(steps,),
        in_specs=[pl.BlockSpec(memory_space=pltpu.VMEM)] * count
        + [pl.BlockSpec((width, total // steps), lambda g: (0, g))]
        + [pl.BlockSpec(memory_space=pl.ANY)] * len(after),
        out_specs=[
            pl.BlockSpec((tokens, width), lambda g: (0, 0)),
            pl.BlockSpec((8, LANES), lambda g: (0, 0)),
        ],
        out_shape=[
            jax.ShapeDtypeStruct((tokens, width), BF),
            jax.ShapeDtypeStruct((8, LANES), F32),
        ],
        scratch_shapes=[pltpu.VMEM((tokens, width), F32)],
        compiler_params=pltpu.CompilerParams(vmem_limit_bytes=24 * MIB),
        cost_estimate=pl.CostEstimate(flops=4 * 10**9, bytes_accessed=MIB, transcendentals=0),
    )(*columns, w_qkv, *after)


def row_blocks(place, own, orders, after):
    tokens, width = own.shape
    devices = len(orders[0])
    size = width // devices
    step = max(1, 16 // size)

    def kernel(place_ref, own_ref, low_ref, high_ref, wide_ref):
        for at in range(0, width, 2 * LANES):
            wide_ref[at : at + 2 * LANES, :] = own_ref[:, at : at + 2 * LANES].astype(F32).T
        even = place_ref[1] == 0
        me = place_ref[2]
        for j in range(0, devices, step):
            rows = []
            for k in range(j, j + step):
                owner = me ^ jnp.where(even, int(orders[0][k]), int(orders[1][k]))
                rows.append(wide_ref[pl.ds(pl.multiple_of(owner * size, size), size), :])
            half, base = divmod(j * size, width // 2)
            block = rows[0] if step == 1 else jnp.concatenate(rows, axis=0)
            (low_ref, high_ref)[half][base : base + step * size, :] = block.astype(BF)

    out = ((width // 2, tokens), BF)
    scratch = [pltpu.VMEM((width, tokens), F32)]
    return on_chip(kernel, [out, out], [own], after=after, scratch=scratch, place=[place])


def pack_sides(own, band_rows, band_cols):
    tokens, width = own.shape

    def kernel(own_ref, last_ref, first_ref, wide_ref):
        for lane, at in lanes_of(width):
            wide_ref[lane] = own_ref[:, at].astype(F32)
            for col in range(MARGIN):
                here = slice(col * band_rows, (col + 1) * band_rows)
                last = pl.ds(band_cols - MARGIN + col, band_rows, stride=band_cols)
                last_ref[here, at] = wide_ref[lane, last, :].astype(BF)
                first = pl.ds(col, band_rows, stride=band_cols)
                first_ref[here, at] = wide_ref[lane, first, :].astype(BF)

    out = ((MARGIN * band_rows, width), BF)
    scratch = [pltpu.VMEM((width // LANES, tokens, LANES), F32)]
    return on_chip(kernel, [out, out], [own], scratch=scratch)


def pack_rows(place, own, band_cols, after):
    tokens, width = own.shape
    edge = MARGIN * band_cols

    def kernel(place_ref, own_ref, out_a, out_b):
        even = place_ref[1] == 0
        last, first = own_ref[tokens - edge :, :], own_ref[:edge, :]
        out_a[...] = jnp.where(even, last, first)
        out_b[...] = jnp.where(even, first, last)

    out = ((edge, width), BF)
    return on_chip(kernel, [out, out], [own], after=after, place=[place])


def pack_corners(place, left, right, band_rows, after):
    width = left.shape[1]

    def kernel(place_ref, left_ref, right_ref, out_a, out_b):
        even = place_ref[1] == 0
        for side, side_ref in enumerate((left_ref, right_ref)):
            for col in range(0, MARGIN, 2):
                base = (side * MARGIN + col) * EDGE_R
                last, first = (
                    jnp.concatenate(
                        [
                            side_ref[at : at + EDGE_R, :].astype(F32)
                            for at in (start, start + band_rows)
                        ]
                    )
                    for start in ((col + 1) * band_rows - EDGE_R, col * band_rows)
                )
                here = slice(base, base + 2 * EDGE_R)
                out_a[here, :] = jnp.where(even, last, first).astype(BF)
                out_b[here, :] = jnp.where(even, first, last).astype(BF)

    out = ((2 * MARGIN * EDGE_R, width), BF)
    return on_chip(kernel, [out, out], [left, right], after=after, place=[place])


def merge_sides(place, lefts, rights, rim_a, rim_b, band_rows, band_cols, after=()):
    edge = MARGIN * band_cols
    calls = len(lefts)
    slots = rim_a.shape[0]
    each = slots // calls

    def kernel(place_ref, *refs):
        sides = refs[:calls], refs[calls : 2 * calls]
        a_ref, b_ref, *outs = refs[2 * calls :]
        even = place_ref[1] == 0
        for slot in range(slots):
            for part in range(2):
                for col in range(2 * MARGIN):
                    source = sides[col // MARGIN][slot // each]
                    base = (col % MARGIN) * band_rows
                    pair = slice(edge + (col // 2) * 2 * EDGE_R, edge + (col // 2 + 1) * 2 * EDGE_R)
                    odd = slice((col % 2) * EDGE_R, (col % 2 + 1) * EDGE_R)
                    rows = source[slot % each, part, base : base + band_rows, :].astype(F32)
                    from_a, from_b = (
                        ref[slot, part, pair, :].astype(F32)[odd] for ref in (a_ref, b_ref)
                    )
                    first = rows[:EDGE_R] + jnp.where(even, from_b, from_a)
                    last = rows[band_rows - EDGE_R :] + jnp.where(even, from_a, from_b)
                    outs[col // MARGIN][slot, part, base : base + band_rows, :] = jnp.concatenate(
                        [first, rows[EDGE_R : band_rows - EDGE_R], last], axis=0
                    ).astype(BF)

    out = ((slots,) + lefts[0].shape[1:], BF)
    return on_chip(kernel, [out, out], [*lefts, *rights, rim_a, rim_b], after, place=[place])


def finish(place, mids, rim_a, rim_b, left, right, parts, band_rows, band_cols, after, flops):
    calls = len(mids)
    slots, _, _, block = rim_a.shape
    each = slots // calls
    edge = MARGIN * band_cols
    tokens = band_rows * band_cols

    def kernel(place_ref, *refs):
        a_ref, b_ref, left_ref, right_ref, *outs, acc_ref = refs[calls:]
        even = place_ref[1] == 0
        for out_ref, part in zip(outs, parts):
            for slot in range(slots):
                for lane, at in lanes_of(block):
                    acc_ref[lane] = refs[slot // each][slot % each, part, :, at].astype(F32)
                    from_a, from_b = (
                        r[slot, part, :edge, at].astype(F32) for r in (a_ref, b_ref)
                    )
                    acc_ref[lane, :edge, :] += jnp.where(even, from_b, from_a)
                    acc_ref[lane, tokens - edge :, :] += jnp.where(even, from_a, from_b)
                    for col in range(MARGIN):
                        here = slice(col * band_rows, (col + 1) * band_rows)
                        first = pl.ds(col, band_rows, stride=band_cols)
                        last = pl.ds(band_cols - MARGIN + col, band_rows, stride=band_cols)
                        acc_ref[lane, first, :] += left_ref[slot, part, here, at].astype(F32)
                        acc_ref[lane, last, :] += right_ref[slot, part, here, at].astype(F32)
                    start = slot * block + lane * LANES
                    out_ref[:, start : start + LANES] = acc_ref[lane].astype(BF)

    out = [((tokens, slots * block), BF)] * len(parts)
    scratch = [pltpu.VMEM((block // LANES, tokens, LANES), F32)]
    operands = [*mids, rim_a, rim_b, left, right]
    return on_chip(kernel, out, operands, after, scratch, flops, [place])


def pieces_of(arrays):
    for i, array in enumerate(arrays):
        slots = range(array.shape[0]) if array.ndim == 3 else [None]
        for slot in slots:
            for start in range(0, array.shape[-1], 2 * LANES):
                yield i, slot, start


def piece(refs, i, slot, start):
    here = slice(start, start + 2 * LANES)
    return refs[i][:, here] if slot is None else refs[i][slot, :, here]


def grad_rows(rows, columns, scale, kind, after=()):
    features, count = rows.shape[0], len(columns)
    pieces = list(pieces_of(columns))

    def kernel(rows_ref, *refs):
        for at, where in enumerate(pieces):
            part = dot(rows_ref[...], piece(refs, *where))
            here = slice(at * 2 * LANES, (at + 1) * 2 * LANES)
            refs[count][:, here] = (part * scale).astype(kind)

    out = [((features, len(pieces) * 2 * LANES), kind)]
    return on_chip(kernel, out, [rows, *columns], after)[0]


def add_split(keep, received, after=()):
    half, columns = keep.shape[0] // 2, keep.shape[1]

    def kernel(keep_ref, received_ref, sums_ref, send_ref):
        sums_ref[...] = keep_ref[:half, :] + received_ref[:half, :].astype(F32)
        send_ref[...] = (keep_ref[half:, :] + received_ref[half:, :].astype(F32)).astype(BF)

    return on_chip(kernel, [((half, columns), F32), ((half, columns), BF)], [keep, received], after)


def gather_sums(groups, places, width):
    flat = [array for group in groups for array in group]

    def kernel(*refs):
        out_ref = refs[-1]
        for i, moves in enumerate(places):
            keep_ref, received_ref = refs[2 * i : 2 * i + 2]
            for source, size, target in moves:
                here = slice(source, source + size)
                total = keep_ref[:, here] + received_ref[:, here].astype(F32)
                out_ref[:, target : target + size] = total

    return on_chip(kernel, [((flat[0].shape[0], width), F32)], flat)[0]


def shifted(array, axis, by, wrap):
    size = lax.axis_size(axis)
    route = [(i, (i + by) % size) for i in range(size) if wrap or 0 <= i + by < size]
    return lax.ppermute(array, axis, route)


def swapped(array_a, array_b, axis):
    size = lax.axis_size(axis)
    pairs = [(i, i + 1) for i in range(size - 1)]
    route = lambda chosen: chosen + [(j, i) for i, j in chosen]
    return [
        lax.ppermute(array, axis, route(pairs[offset::2]))
        for array, offset in ((array_a, 0), (array_b, 1))
    ]


def exchanged(array, axis, flip):
    return lax.ppermute(array, axis, [(i, i ^ flip) for i in range(lax.axis_size(axis))])


def bits_of(axis):
    return [(axis, 1 << b) for b in range((lax.axis_size(axis) - 1).bit_length())]


def reduce_stages():
    first, *lat_bits = bits_of("lat")
    bits = bits_of("dp") + lat_bits
    return first, list(zip(bits, reversed(bits))) + [(bit, bit) for bit in bits_of("lon")]


def feature_orders(first, stages):
    n_lon, n_lat = lax.axis_size("lon"), lax.axis_size("lat")
    unit = {"lon": 1, "lat": n_lon, "dp": n_lon * n_lat}
    lower = []
    for kind in range(2):
        order = np.zeros(1, np.int64)
        for stage in reversed(stages):
            axis, bit = stage[kind]
            order = np.concatenate([order, order + unit[axis] * bit])
        lower.append(order)
    flip = unit[first[0]] * first[1]
    return [np.concatenate([lower[kind], lower[1 - kind] ^ flip]) for kind in range(2)]


def exchanged_stage(array, stage):
    if stage[0] == stage[1]:
        return exchanged(array, *stage[0])
    n_lat, n_dp = lax.axis_size("lat"), lax.axis_size("dp")
    route = []
    for i in range(n_dp * n_lat):
        axis, bit = stage[i % n_lat % 2]
        route.append((i, i ^ (bit * n_lat if axis == "dp" else bit)))
    return lax.ppermute(array, ("dp", "lat"), route)


def body(inputs, grad_out, w_qkv):
    _, band_rows, band_cols, width = inputs.shape
    n_lat, n_lon, n_dp = lax.axis_size("lat"), lax.axis_size("lon"), lax.axis_size("dp")
    band_start = lax.axis_index("lat") * band_rows
    total_rows = band_rows * n_lat
    tokens = band_rows * band_cols
    slots = HEADS // GROUP // 2
    shape = (band_rows, band_cols, total_rows)
    own = inputs.reshape(tokens, width)
    flat_grad = grad_out.reshape(tokens, width)

    last_cols, first_cols = pack_sides(own, band_rows, band_cols)
    left = shifted(last_cols, "lon", 1, True)
    right = shifted(first_cols, "lon", -1, True)
    me = (lax.axis_index("dp") * n_lat + lax.axis_index("lat")) * n_lon + lax.axis_index("lon")
    start = jnp.stack([band_start, lax.axis_index("lat") % 2, me])
    rim_rows = swapped(*pack_rows(start, own, band_cols, [last_cols]), "lat")

    masks = window_masks(start, band_rows, band_cols, total_rows)
    qkv = project(own, w_qkv, [last_cols])
    first, stages = reduce_stages()
    half = width // 2
    rows_keep, rows_send = row_blocks(start, own, feature_orders(first, stages), [last_cols])
    corners = pack_corners(start, left, right, band_rows, [masks, qkv, rows_keep, rows_send])
    halo = (left, right, *rim_rows, *swapped(*corners, "lat"))
    scale = float(tokens * n_dp * n_lat * n_lon) ** -0.5

    attend = lambda first, count, before, after: attention_grads(
        first, count, start, masks, halo, qkv, flat_grad, w_qkv, shape, before, after
    )

    def return_sides(calls, rims, after):
        to_left, to_right = merge_sides(
            start, [c[4] for c in calls], [c[5] for c in calls], *rims, band_rows, band_cols, after
        )
        from_right = shifted(to_left, "lon", -1, True)
        from_left = shifted(to_right, "lon", 1, True)
        return to_left, from_left, from_right

    def finished(calls, rims, sides, parts, after, flops):
        mids = [c[3] for c in calls]
        return finish(start, mids, *rims, *sides, parts, band_rows, band_cols, after, flops)

    groups = HEADS // GROUP
    one = attend(0, slots, [], [])
    rims_1 = swapped(one[1], one[2], "lat")
    two = attend(slots, groups - slots - 1, [], [one[0]])
    sent, *sides_1 = return_sides([one], rims_1, [two[0]])
    three = attend(groups - 1, 1, [two[1], two[2]], [sent])
    rims_2 = swapped(three[1], three[2], "lat")
    dq = [one[0], two[0], three[0]]

    dk_1, dv_1 = finished([one], rims_1, sides_1, (0, 1), [three[0]], 2 * 10**9)
    sent, *sides_2 = return_sides([two, three], rims_2, [dk_1])
    send = grad_rows(rows_send, [*dq, dk_1, dv_1], scale, BF, after=[sent])
    received = exchanged(send, *first)
    keep = grad_rows(rows_keep, [*dq, dk_1, dv_1], scale, F32, after=[send])
    keep, send = add_split(keep, received)

    (dk_2,) = finished([two, three], rims_2, sides_2, (0,), [keep], FINISH_FLOPS)
    received = exchanged_stage(send, stages[0])
    keep, send = add_split(keep, received, [dk_2])
    received = exchanged_stage(send, stages[1])
    (dv_2,) = finished([two, three], rims_2, sides_2, (1,), [keep], 10**5)
    send_2 = grad_rows(rows_send, [dk_2, dv_2], scale, BF)
    received_2 = exchanged(send_2, *first)
    keep_2 = grad_rows(rows_keep, [dk_2, dv_2], scale, F32, after=[send_2])
    keep_2, send_2 = add_split(keep_2, received_2)
    received_2 = exchanged_stage(send_2, stages[0])
    grad_inputs, done = input_grads([*dq, dk_1, dk_2, dv_1, dv_2], w_qkv, [send_2])
    keep, send = add_split(keep, received, [done])
    for i in range(2, len(stages)):
        received = exchanged_stage(send, stages[i])
        keep_2, send_2 = add_split(keep_2, received_2, [keep])
        received_2 = exchanged_stage(send_2, stages[i - 1])
        if i + 1 < len(stages):
            keep, send = add_split(keep, received, [keep_2])
    keep_2, send_2 = add_split(keep_2, received_2)
    received_2 = exchanged_stage(send_2, stages[-1])
    groups = [(keep, received), (keep_2, received_2)]
    places = [
        [(0, width, 0), (width, half, width), (width + half, half, 2 * width)],
        [(0, half, width + half), (half, half, 2 * width + half)],
    ]
    grad_w = gather_sums(groups, places, 3 * width)
    return (grad_inputs.reshape(inputs.shape), grad_w)


def solution(mesh):
    in_specs = (P("dp", "lat", "lon", None), P("dp", "lat", "lon", None), P())
    out_specs = (P("dp", "lat", "lon", None), P(("dp", "lat", "lon"), None))
    return jax.shard_map(body, mesh=mesh, in_specs=in_specs, out_specs=out_specs, check_vma=False)
```

```python
import functools

import jax
import jax.numpy as jnp
import numpy as np
from jax import lax
from jax.experimental import pallas as pl
from jax.experimental.pallas import tpu as pltpu
from jax.sharding import PartitionSpec as P

HEADS = 16
WIN = 13
MARGIN = WIN // 2
TILE_R = 4
GROUP = 4
KEY_COLS = 32
HALO_COLS = 16
REGION_R = 16
PAD_R = 2
EDGE_R = MARGIN + PAD_R
NEG = -1e30
BF = jnp.bfloat16
F32 = jnp.float32
MIB = 1024 * 1024
FINISH_FLOPS = 9 * 10**9
LANES = 128
ATTENTION_MIB = 32

NT = (((1,), (1,)), ((), ()))
TN = (((0,), (0,)), ((), ()))
NN = (((1,), (0,)), ((), ()))


def dot(a, b, dims=NN):
    return lax.dot_general(a, b, dims, preferred_element_type=F32)


def region_top(tile, band_start, band_rows, total_rows):
    lowest = jnp.where(band_start == 0, TILE_R, 0)
    highest = jnp.where(band_start + band_rows == total_rows, band_rows - 2 * TILE_R, band_rows)
    return jnp.clip(tile * TILE_R, lowest, highest)


def mask_kernel(band_rows, band_cols, total_rows, start_ref, mask_ref):
    band_start = start_ref[0]
    tile = pl.program_id(0)
    shape = mask_ref.shape[1:]
    first = region_top(tile, band_start, band_rows, total_rows)
    key = lax.broadcasted_iota(jnp.int32, shape, 0)
    query = lax.broadcasted_iota(jnp.int32, shape, 1) & (TILE_R * band_cols - 1)
    key_row = band_start - MARGIN + first + (key >> (KEY_COLS.bit_length() - 1))
    place = key & (KEY_COLS - 1)
    query_row = band_start + tile * TILE_R + (query >> (band_cols.bit_length() - 1))
    query_col = query & (band_cols - 1)
    window = jnp.clip(query_row - MARGIN, 0, total_rows - WIN)
    row_inside = (key_row >= window) & (key_row < window + WIN)
    key_col = jnp.where(
        place < band_cols,
        place,
        jnp.where(place < band_cols + MARGIN, place - band_cols - MARGIN, place - MARGIN),
    )
    col_inside = (jnp.abs(key_col - query_col) <= MARGIN) & (place < band_cols + 2 * MARGIN)
    mask_ref[0] = jnp.where(row_inside & col_inside, 0.0, NEG).astype(BF)


def window_masks(start, band_rows, band_cols, total_rows):
    tiles = band_rows // TILE_R
    shape = (REGION_R * KEY_COLS, 2 * TILE_R * band_cols)
    return pl.pallas_call(
        functools.partial(mask_kernel, band_rows, band_cols, total_rows),
        grid=(tiles,),
        in_specs=[pl.BlockSpec(memory_space=pltpu.SMEM)],
        out_specs=pl.BlockSpec((1,) + shape, lambda t: (t, 0, 0)),
        out_shape=jax.ShapeDtypeStruct((tiles,) + shape, BF),
        cost_estimate=pl.CostEstimate(flops=10**7, bytes_accessed=2**21, transcendentals=0),
    )(start)


def attention_kernel(band_rows, band_cols, total_rows, head_width, extra, first, count, shift, *refs):
    (place_ref, mask_ref, left_ref, right_ref, rows_a, rows_b, corners_a, corners_b,
     qkv_hbm, grad_hbm, w_hbm) = refs[:11]
    before_a, before_b = refs[11 : 11 + shift], refs[11 + shift : 11 + 2 * shift]
    (dq_all, out_a_all, out_b_all, mid_all, to_left_all, to_right_all,
     halo_ref, spot_ref, q_ref, k_ref, v_ref, dk_ref, dv_ref,
     own_refs, w_refs, own_sem, w_sem) = refs[11 + extra :]
    band_start = place_ref[0]
    even = place_ref[1] == 0
    tiles = band_rows // TILE_R
    queries = TILE_R * band_cols
    keys = REGION_R * KEY_COLS
    width = GROUP * head_width
    lanes = GROUP * queries
    region_rows = band_rows + 2 * MARGIN
    side = MARGIN * band_rows
    edge = MARGIN * band_cols
    corner = 2 * MARGIN * EDGE_R
    at_above = 2 * side
    at_below = at_above + edge
    at_cl = at_below + edge
    at_cr = at_cl + corner
    halves = [(i, slice(i * LANES, (i + 1) * LANES)) for i in range(width // LANES)]

    step = pl.program_id(0)
    dq_ref, mid_ref, to_left_ref, to_right_ref = (
        ref.at[step] for ref in (dq_all, mid_all, to_left_all, to_right_all)
    )
    out_a, out_b = (ref.at[step + shift] for ref in (out_a_all, out_b_all))
    groups = HEADS // GROUP

    def copies(slot, parts):
        at = lambda part: pl.ds(pl.multiple_of((part * groups + first + slot) * width, width), width)
        for part, source, where, i in parts:
            target, sem = (w_refs, w_sem) if where else (own_refs, own_sem)
            yield pltpu.make_async_copy(source.at[:, at(part)], target.at[slot, i], sem.at[slot, i])

    for_k = ((1, w_hbm, 1, 0), (1, qkv_hbm, 0, 1))
    for_v = ((2, w_hbm, 1, 1), (2, qkv_hbm, 0, 2))
    for_q = ((0, qkv_hbm, 0, 0), (0, grad_hbm, 0, 3))

    @pl.when(step == 0)
    def _():
        for ref, kept in ((out_a_all, before_a), (out_b_all, before_b)):
            for i in range(shift):
                ref[i] = kept[0][i]
        for slot in range(count):
            for copy in copies(slot, for_k + for_v + for_q):
                copy.start()
        halo_ref[:side] = left_ref[...]
        halo_ref[side:at_above] = right_ref[...]
        for above, below, size, refs_ab in (
            (at_above, at_below, edge, (rows_a, rows_b)),
            (at_cl, at_cr, corner, (corners_a, corners_b)),
        ):
            for ref, at in zip(refs_ab, (jnp.where(even, below, above), jnp.where(even, above, below))):
                halo_ref[pl.ds(pl.multiple_of(at, 16), size), :] = ref[...]
        spot_ref[...] = jnp.zeros_like(spot_ref)

    def place(target, own, weights):
        fresh = dot(halo_ref[...], weights)
        for col in range(MARGIN):
            start = MARGIN * HALO_COLS + col
            for part, at in halves:
                spot_ref[part, pl.ds(start, band_rows, stride=HALO_COLS), :] = fresh[
                    col * band_rows : (col + 1) * band_rows, at
                ]
                spot_ref[part, pl.ds(start + MARGIN, band_rows, stride=HALO_COLS), :] = fresh[
                    side + col * band_rows : side + (col + 1) * band_rows, at
                ]
        for corner_at, skip, row in ((at_cl, PAD_R, 0), (at_cr, 0, MARGIN + band_rows)):
            for col in range(2 * MARGIN):
                base = corner_at + col * EDGE_R + skip
                spot = pl.ds(row * HALO_COLS + col, MARGIN, stride=HALO_COLS)
                for part, at in halves:
                    spot_ref[part, spot, :] = fresh[base : base + MARGIN, at]
        for row in range(region_rows):
            base = row * KEY_COLS
            inner = row - MARGIN
            if inner < 0:
                ours = fresh[at_above + row * band_cols : at_above + (row + 1) * band_cols].astype(BF)
            elif inner < band_rows:
                ours = own[inner * band_cols : (inner + 1) * band_cols, :]
            else:
                past = at_below + (inner - band_rows) * band_cols
                ours = fresh[past : past + band_cols].astype(BF)
            target[base : base + band_cols, :] = ours
            for part, at in halves:
                target[base + band_cols : base + KEY_COLS, at] = spot_ref[
                    part, row * HALO_COLS : (row + 1) * HALO_COLS, :
                ].astype(BF)

    grad_ref = own_refs.at[step, 3]
    for copy in copies(step, for_k + for_v + for_q):
        copy.wait()
    place(k_ref, own_refs.at[step, 1], w_refs[step, 0])
    place(v_ref, own_refs.at[step, 2], w_refs[step, 1])
    q_ref[...] = own_refs[step, 0] * BF(head_width**-0.5)
    dk_ref[...] = jnp.zeros_like(dk_ref)
    dv_ref[...] = jnp.zeros_like(dv_ref)

    def spread(rows):
        block = jnp.concatenate([rows] * GROUP, axis=0)
        head_row = lax.broadcasted_iota(jnp.int32, (lanes, width), 0) // queries
        head_col = lax.broadcasted_iota(jnp.int32, (lanes, width), 1) // head_width
        return jnp.where(head_row == head_col, block, jnp.zeros_like(block))

    def one_tile(tile, carry):
        first = region_top(tile, band_start, band_rows, total_rows)
        region = pl.ds(pl.multiple_of(first * KEY_COLS, TILE_R * KEY_COLS), keys)
        total = pl.ds(pl.multiple_of((first + PAD_R) * KEY_COLS, PAD_R * KEY_COLS), keys)
        mine = pl.ds(pl.multiple_of(tile * queries, queries), queries)
        q_wide = spread(q_ref[mine, :])
        g_wide = spread(grad_ref[mine, :])
        mask = mask_ref[tile].astype(F32)
        scores = dot(k_ref[region, :], q_wide, NT) + jnp.concatenate([mask, mask], axis=1)
        dots = dot(v_ref[region, :], g_wide, NT)
        exponent = jnp.exp(scores - jnp.max(scores, axis=0, keepdims=True))
        inverse = 1.0 / jnp.sum(exponent, axis=0, keepdims=True)
        delta = jnp.sum(exponent * dots, axis=0, keepdims=True) * inverse
        attn = exponent * inverse
        dscore = (attn * (dots - delta)).astype(BF)
        dv = dot(attn.astype(BF), g_wide)
        dk = dot(dscore, q_wide)
        for part, at in halves:
            dv_ref[part, total, :] += dv[:, at]
            dk_ref[part, total, :] += dk[:, at]
        dq_wide = dot(dscore, k_ref[region, :], TN)
        head_col = lax.broadcasted_iota(jnp.int32, (queries, width), 1) // head_width
        dq = jnp.zeros((queries, width), F32)
        for head in range(GROUP):
            dq = jnp.where(head_col == head, dq_wide[head * queries : (head + 1) * queries], dq)
        dq_ref[mine, :] = (dq * head_width**-0.5).astype(BF)
        return carry

    lax.fori_loop(0, tiles, one_tile, 0, unroll=4)

    middle = (PAD_R + MARGIN) * KEY_COLS
    below = (PAD_R + MARGIN + band_rows) * KEY_COLS
    for part, acc in enumerate((dk_ref, dv_ref)):
        for lane, at in halves:
            for out, own_at, side_at in (
                (out_a, jnp.where(even, below, PAD_R * KEY_COLS), jnp.where(even, below, 0)),
                (out_b, jnp.where(even, PAD_R * KEY_COLS, below), jnp.where(even, 0, below)),
            ):
                for row in range(MARGIN):
                    start = pl.multiple_of(own_at + row * KEY_COLS, KEY_COLS)
                    out[part, row * band_cols : (row + 1) * band_cols, at] = acc[
                        lane, pl.ds(start, band_cols), :
                    ].astype(BF)
                for pair in range(MARGIN):
                    here = slice(edge + pair * 2 * EDGE_R, edge + (pair + 1) * 2 * EDGE_R)
                    start = side_at + band_cols + 2 * pair
                    out[part, here, at] = jnp.concatenate(
                        [
                            acc[lane, pl.ds(start, EDGE_R, stride=KEY_COLS), :],
                            acc[lane, pl.ds(start + 1, EDGE_R, stride=KEY_COLS), :],
                        ],
                        axis=0,
                    ).astype(BF)
            for row in range(band_rows):
                base = middle + row * KEY_COLS
                mid_ref[part, row * band_cols : (row + 1) * band_cols, at] = acc[
                    lane, base : base + band_cols, :
                ].astype(BF)
            for col in range(MARGIN):
                here = slice(col * band_rows, (col + 1) * band_rows)
                start = middle + band_cols + col
                to_left_ref[part, here, at] = acc[
                    lane, pl.ds(start, band_rows, stride=KEY_COLS), :
                ].astype(BF)
                to_right_ref[part, here, at] = acc[
                    lane, pl.ds(start + MARGIN, band_rows, stride=KEY_COLS), :
                ].astype(BF)


def attention_grads(first, count, place, masks, halo, qkv, grad_out, w_qkv, shape, before, after):
    band_rows, band_cols, total_rows = shape
    tokens, width = grad_out.shape
    head_width = width // HEADS
    block = GROUP * head_width
    region_tokens = (band_rows + 2 * MARGIN) * KEY_COLS
    total_tokens = (band_rows + 2 * MARGIN + 2 * PAD_R) * KEY_COLS
    side = MARGIN * band_rows
    edge = MARGIN * (band_cols + 2 * EDGE_R)
    corner = 2 * MARGIN * EDGE_R
    halo_tokens = 2 * (side + MARGIN * band_cols + corner)
    shift = before[0].shape[0] if before else 0
    vmem = pl.BlockSpec(memory_space=pltpu.VMEM)
    shapes = [
        (count, tokens, block),
        (count + shift, 2, edge, block),
        (count + shift, 2, edge, block),
        (count, 2, tokens, block),
        (count, 2, side, block),
        (count, 2, side, block),
    ]
    return pl.pallas_call(
        functools.partial(
            attention_kernel, band_rows, band_cols, total_rows, head_width,
            len(before) + len(after), first, count, shift,
        ),
        grid=(count,),
        in_specs=[pl.BlockSpec(memory_space=pltpu.SMEM)]
        + [vmem] * (1 + len(halo))
        + [pl.BlockSpec(memory_space=pltpu.HBM)] * 3
        + [vmem] * len(before)
        + [pl.BlockSpec(memory_space=pl.ANY)] * len(after),
        out_specs=[vmem] * len(shapes),
        out_shape=[jax.ShapeDtypeStruct(s, BF) for s in shapes],
        scratch_shapes=[
            pltpu.VMEM((halo_tokens, width), BF),
            pltpu.VMEM((block // LANES, (band_rows + 2 * MARGIN) * HALO_COLS, LANES), F32),
            pltpu.VMEM((tokens, block), BF),
            pltpu.VMEM((region_tokens, block), BF),
            pltpu.VMEM((region_tokens, block), BF),
            pltpu.VMEM((block // LANES, total_tokens, LANES), F32),
            pltpu.VMEM((block // LANES, total_tokens, LANES), F32),
            pltpu.VMEM((count, 4, tokens, block), BF),
            pltpu.VMEM((count, 2, width, block), BF),
            pltpu.SemaphoreType.DMA((count, 4)),
            pltpu.SemaphoreType.DMA((count, 2)),
        ],
        compiler_params=pltpu.CompilerParams(
            dimension_semantics=("arbitrary",), vmem_limit_bytes=ATTENTION_MIB * MIB
        ),
        cost_estimate=pl.CostEstimate(
            flops=count * 14 * 10**9, bytes_accessed=count * 8 * MIB, transcendentals=count * 10**6
        ),
    )(place, masks, *halo, qkv, grad_out, w_qkv, *before, *after)


def on_chip(kernel, out_shape, operands, after=(), scratch=(), flops=10**5, place=()):
    count = len(operands) + len(place)

    def run(*refs):
        kernel(*refs[:count], *refs[count + len(after) :])

    return pl.pallas_call(
        run,
        in_specs=[pl.BlockSpec(memory_space=pltpu.SMEM)] * len(place)
        + [pl.BlockSpec(memory_space=pltpu.VMEM)] * len(operands)
        + [pl.BlockSpec(memory_space=pl.ANY)] * len(after),
        out_specs=[pl.BlockSpec(memory_space=pltpu.VMEM)] * len(out_shape),
        out_shape=[jax.ShapeDtypeStruct(s, d) for s, d in out_shape],
        scratch_shapes=list(scratch),
        compiler_params=pltpu.CompilerParams(vmem_limit_bytes=24 * MIB),
        cost_estimate=pl.CostEstimate(flops=flops, bytes_accessed=10**4, transcendentals=0),
    )(*place, *operands, *after)


def lanes_of(width):
    return [(i, slice(i * LANES, (i + 1) * LANES)) for i in range(width // LANES)]


def project(own, w_qkv, after):
    tokens, width = own.shape
    columns = w_qkv.shape[1]
    block = 4 * LANES

    def kernel(own_ref, w_ref, *refs):
        refs[-1][...] = dot(own_ref[...], w_ref[...]).astype(BF)

    return pl.pallas_call(
        kernel,
        grid=(columns // block,),
        in_specs=[
            pl.BlockSpec((tokens, width), lambda g: (0, 0)),
            pl.BlockSpec((width, block), lambda g: (0, g)),
        ]
        + [pl.BlockSpec(memory_space=pl.ANY)] * len(after),
        out_specs=pl.BlockSpec((tokens, block), lambda g: (0, g)),
        out_shape=jax.ShapeDtypeStruct((tokens, columns), BF),
        compiler_params=pltpu.CompilerParams(vmem_limit_bytes=24 * MIB),
        cost_estimate=pl.CostEstimate(flops=10**9, bytes_accessed=MIB, transcendentals=0),
    )(own, w_qkv, *after)


def input_grads(columns, w_qkv, after):
    tokens = columns[0].shape[-2]
    width, total = w_qkv.shape
    count = len(columns)
    pieces = list(pieces_of(columns))
    steps = len(pieces) // 2

    def kernel(*refs):
        w_ref, (out_ref, done_ref, acc_ref) = refs[count], refs[-3:]
        for step in range(steps):

            @pl.when(pl.program_id(0) == step)
            def _():
                both = [piece(refs, *where) for where in pieces[2 * step : 2 * step + 2]]
                product = dot(jnp.concatenate(both, axis=1), w_ref[...], NT)
                if step == 0:
                    acc_ref[...] = product
                elif step < steps - 1:
                    acc_ref[...] += product
                else:
                    out_ref[...] = (acc_ref[...] + product).astype(BF)
                    done_ref[...] = jnp.zeros_like(done_ref)

    return pl.pallas_call(
        kernel,
        grid=(steps,),
        in_specs=[pl.BlockSpec(memory_space=pltpu.VMEM)] * count
        + [pl.BlockSpec((width, total // steps), lambda g: (0, g))]
        + [pl.BlockSpec(memory_space=pl.ANY)] * len(after),
        out_specs=[
            pl.BlockSpec((tokens, width), lambda g: (0, 0)),
            pl.BlockSpec((8, LANES), lambda g: (0, 0)),
        ],
        out_shape=[
            jax.ShapeDtypeStruct((tokens, width), BF),
            jax.ShapeDtypeStruct((8, LANES), F32),
        ],
        scratch_shapes=[pltpu.VMEM((tokens, width), F32)],
        compiler_params=pltpu.CompilerParams(vmem_limit_bytes=24 * MIB),
        cost_estimate=pl.CostEstimate(flops=4 * 10**9, bytes_accessed=MIB, transcendentals=0),
    )(*columns, w_qkv, *after)


def row_blocks(place, own, orders, after):
    tokens, width = own.shape
    devices = len(orders[0])
    size = width // devices
    step = max(1, 16 // size)

    def kernel(place_ref, own_ref, low_ref, high_ref, wide_ref):
        for at in range(0, width, 2 * LANES):
            wide_ref[at : at + 2 * LANES, :] = own_ref[:, at : at + 2 * LANES].astype(F32).T
        even = place_ref[1] == 0
        me = place_ref[2]
        for j in range(0, devices, step):
            rows = []
            for k in range(j, j + step):
                owner = me ^ jnp.where(even, int(orders[0][k]), int(orders[1][k]))
                rows.append(wide_ref[pl.ds(pl.multiple_of(owner * size, size), size), :])
            half, base = divmod(j * size, width // 2)
            block = rows[0] if step == 1 else jnp.concatenate(rows, axis=0)
            (low_ref, high_ref)[half][base : base + step * size, :] = block.astype(BF)

    out = ((width // 2, tokens), BF)
    scratch = [pltpu.VMEM((width, tokens), F32)]
    return on_chip(kernel, [out, out], [own], after=after, scratch=scratch, place=[place])


def pack_sides(own, band_rows, band_cols):
    tokens, width = own.shape

    def kernel(own_ref, last_ref, first_ref, wide_ref):
        for lane, at in lanes_of(width):
            wide_ref[lane] = own_ref[:, at].astype(F32)
            for col in range(MARGIN):
                here = slice(col * band_rows, (col + 1) * band_rows)
                last = pl.ds(band_cols - MARGIN + col, band_rows, stride=band_cols)
                last_ref[here, at] = wide_ref[lane, last, :].astype(BF)
                first = pl.ds(col, band_rows, stride=band_cols)
                first_ref[here, at] = wide_ref[lane, first, :].astype(BF)

    out = ((MARGIN * band_rows, width), BF)
    scratch = [pltpu.VMEM((width // LANES, tokens, LANES), F32)]
    return on_chip(kernel, [out, out], [own], scratch=scratch)


def pack_rows(place, own, band_cols, after):
    tokens, width = own.shape
    edge = MARGIN * band_cols

    def kernel(place_ref, own_ref, out_a, out_b):
        even = place_ref[1] == 0
        last, first = own_ref[tokens - edge :, :], own_ref[:edge, :]
        out_a[...] = jnp.where(even, last, first)
        out_b[...] = jnp.where(even, first, last)

    out = ((edge, width), BF)
    return on_chip(kernel, [out, out], [own], after=after, place=[place])


def pack_corners(place, left, right, band_rows, after):
    width = left.shape[1]

    def kernel(place_ref, left_ref, right_ref, out_a, out_b):
        even = place_ref[1] == 0
        for side, side_ref in enumerate((left_ref, right_ref)):
            for col in range(0, MARGIN, 2):
                base = (side * MARGIN + col) * EDGE_R
                last, first = (
                    jnp.concatenate(
                        [
                            side_ref[at : at + EDGE_R, :].astype(F32)
                            for at in (start, start + band_rows)
                        ]
                    )
                    for start in ((col + 1) * band_rows - EDGE_R, col * band_rows)
                )
                here = slice(base, base + 2 * EDGE_R)
                out_a[here, :] = jnp.where(even, last, first).astype(BF)
                out_b[here, :] = jnp.where(even, first, last).astype(BF)

    out = ((2 * MARGIN * EDGE_R, width), BF)
    return on_chip(kernel, [out, out], [left, right], after=after, place=[place])


def merge_sides(place, lefts, rights, rim_a, rim_b, band_rows, band_cols, after=()):
    edge = MARGIN * band_cols
    calls = len(lefts)
    slots = rim_a.shape[0]
    each = slots // calls

    def kernel(place_ref, *refs):
        sides = refs[:calls], refs[calls : 2 * calls]
        a_ref, b_ref, *outs = refs[2 * calls :]
        even = place_ref[1] == 0
        for slot in range(slots):
            for part in range(2):
                for col in range(2 * MARGIN):
                    source = sides[col // MARGIN][slot // each]
                    base = (col % MARGIN) * band_rows
                    pair = slice(edge + (col // 2) * 2 * EDGE_R, edge + (col // 2 + 1) * 2 * EDGE_R)
                    odd = slice((col % 2) * EDGE_R, (col % 2 + 1) * EDGE_R)
                    rows = source[slot % each, part, base : base + band_rows, :].astype(F32)
                    from_a, from_b = (
                        ref[slot, part, pair, :].astype(F32)[odd] for ref in (a_ref, b_ref)
                    )
                    first = rows[:EDGE_R] + jnp.where(even, from_b, from_a)
                    last = rows[band_rows - EDGE_R :] + jnp.where(even, from_a, from_b)
                    outs[col // MARGIN][slot, part, base : base + band_rows, :] = jnp.concatenate(
                        [first, rows[EDGE_R : band_rows - EDGE_R], last], axis=0
                    ).astype(BF)

    out = ((slots,) + lefts[0].shape[1:], BF)
    return on_chip(kernel, [out, out], [*lefts, *rights, rim_a, rim_b], after, place=[place])


def finish(place, mids, rim_a, rim_b, left, right, parts, band_rows, band_cols, after, flops):
    calls = len(mids)
    slots, _, _, block = rim_a.shape
    each = slots // calls
    edge = MARGIN * band_cols
    tokens = band_rows * band_cols

    def kernel(place_ref, *refs):
        a_ref, b_ref, left_ref, right_ref, *outs, acc_ref = refs[calls:]
        even = place_ref[1] == 0
        for out_ref, part in zip(outs, parts):
            for slot in range(slots):
                for lane, at in lanes_of(block):
                    acc_ref[lane] = refs[slot // each][slot % each, part, :, at].astype(F32)
                    from_a, from_b = (
                        r[slot, part, :edge, at].astype(F32) for r in (a_ref, b_ref)
                    )
                    acc_ref[lane, :edge, :] += jnp.where(even, from_b, from_a)
                    acc_ref[lane, tokens - edge :, :] += jnp.where(even, from_a, from_b)
                    for col in range(MARGIN):
                        here = slice(col * band_rows, (col + 1) * band_rows)
                        first = pl.ds(col, band_rows, stride=band_cols)
                        last = pl.ds(band_cols - MARGIN + col, band_rows, stride=band_cols)
                        acc_ref[lane, first, :] += left_ref[slot, part, here, at].astype(F32)
                        acc_ref[lane, last, :] += right_ref[slot, part, here, at].astype(F32)
                    start = slot * block + lane * LANES
                    out_ref[:, start : start + LANES] = acc_ref[lane].astype(BF)

    out = [((tokens, slots * block), BF)] * len(parts)
    scratch = [pltpu.VMEM((block // LANES, tokens, LANES), F32)]
    operands = [*mids, rim_a, rim_b, left, right]
    return on_chip(kernel, out, operands, after, scratch, flops, [place])


def pieces_of(arrays):
    for i, array in enumerate(arrays):
        slots = range(array.shape[0]) if array.ndim == 3 else [None]
        for slot in slots:
            for start in range(0, array.shape[-1], 2 * LANES):
                yield i, slot, start


def piece(refs, i, slot, start):
    here = slice(start, start + 2 * LANES)
    return refs[i][:, here] if slot is None else refs[i][slot, :, here]


def grad_rows(rows, columns, scale, kind, after=()):
    features, count = rows.shape[0], len(columns)
    pieces = list(pieces_of(columns))

    def kernel(rows_ref, *refs):
        for at, where in enumerate(pieces):
            part = dot(rows_ref[...], piece(refs, *where))
            here = slice(at * 2 * LANES, (at + 1) * 2 * LANES)
            refs[count][:, here] = (part * scale).astype(kind)

    out = [((features, len(pieces) * 2 * LANES), kind)]
    return on_chip(kernel, out, [rows, *columns], after)[0]


def add_split(keep, received, after=()):
    half, columns = keep.shape[0] // 2, keep.shape[1]

    def kernel(keep_ref, received_ref, sums_ref, send_ref):
        sums_ref[...] = keep_ref[:half, :] + received_ref[:half, :].astype(F32)
        send_ref[...] = (keep_ref[half:, :] + received_ref[half:, :].astype(F32)).astype(BF)

    return on_chip(kernel, [((half, columns), F32), ((half, columns), BF)], [keep, received], after)


def gather_sums(groups, places, width):
    flat = [array for group in groups for array in group]

    def kernel(*refs):
        out_ref = refs[-1]
        for i, moves in enumerate(places):
            keep_ref, received_ref = refs[2 * i : 2 * i + 2]
            for source, size, target in moves:
                here = slice(source, source + size)
                total = keep_ref[:, here] + received_ref[:, here].astype(F32)
                out_ref[:, target : target + size] = total

    return on_chip(kernel, [((flat[0].shape[0], width), F32)], flat)[0]


def shifted(array, axis, by, wrap):
    size = lax.axis_size(axis)
    route = [(i, (i + by) % size) for i in range(size) if wrap or 0 <= i + by < size]
    return lax.ppermute(array, axis, route)


def swapped(array_a, array_b, axis):
    size = lax.axis_size(axis)
    pairs = [(i, i + 1) for i in range(size - 1)]
    route = lambda chosen: chosen + [(j, i) for i, j in chosen]
    return [
        lax.ppermute(array, axis, route(pairs[offset::2]))
        for array, offset in ((array_a, 0), (array_b, 1))
    ]


def exchanged(array, axis, flip):
    return lax.ppermute(array, axis, [(i, i ^ flip) for i in range(lax.axis_size(axis))])


def bits_of(axis):
    return [(axis, 1 << b) for b in range((lax.axis_size(axis) - 1).bit_length())]


def reduce_stages():
    first, *lat_bits = bits_of("lat")
    bits = bits_of("dp") + lat_bits
    return first, list(zip(bits, reversed(bits))) + [(bit, bit) for bit in bits_of("lon")]


def feature_orders(first, stages):
    n_lon, n_lat = lax.axis_size("lon"), lax.axis_size("lat")
    unit = {"lon": 1, "lat": n_lon, "dp": n_lon * n_lat}
    lower = []
    for kind in range(2):
        order = np.zeros(1, np.int64)
        for stage in reversed(stages):
            axis, bit = stage[kind]
            order = np.concatenate([order, order + unit[axis] * bit])
        lower.append(order)
    flip = unit[first[0]] * first[1]
    return [np.concatenate([lower[kind], lower[1 - kind] ^ flip]) for kind in range(2)]


def exchanged_stage(array, stage):
    if stage[0] == stage[1]:
        return exchanged(array, *stage[0])
    n_lat, n_dp = lax.axis_size("lat"), lax.axis_size("dp")
    route = []
    for i in range(n_dp * n_lat):
        axis, bit = stage[i % n_lat % 2]
        route.append((i, i ^ (bit * n_lat if axis == "dp" else bit)))
    return lax.ppermute(array, ("dp", "lat"), route)


def body(inputs, grad_out, w_qkv):
    _, band_rows, band_cols, width = inputs.shape
    n_lat, n_lon, n_dp = lax.axis_size("lat"), lax.axis_size("lon"), lax.axis_size("dp")
    band_start = lax.axis_index("lat") * band_rows
    total_rows = band_rows * n_lat
    tokens = band_rows * band_cols
    slots = HEADS // GROUP // 2
    shape = (band_rows, band_cols, total_rows)
    own = inputs.reshape(tokens, width)
    flat_grad = grad_out.reshape(tokens, width)

    last_cols, first_cols = pack_sides(own, band_rows, band_cols)
    left = shifted(last_cols, "lon", 1, True)
    right = shifted(first_cols, "lon", -1, True)
    me = (lax.axis_index("dp") * n_lat + lax.axis_index("lat")) * n_lon + lax.axis_index("lon")
    start = jnp.stack([band_start, lax.axis_index("lat") % 2, me])
    rim_rows = swapped(*pack_rows(start, own, band_cols, [last_cols]), "lat")

    masks = window_masks(start, band_rows, band_cols, total_rows)
    qkv = project(own, w_qkv, [last_cols])
    first, stages = reduce_stages()
    half = width // 2
    rows_keep, rows_send = row_blocks(start, own, feature_orders(first, stages), [last_cols])
    corners = pack_corners(start, left, right, band_rows, [masks, qkv, rows_keep, rows_send])
    halo = (left, right, *rim_rows, *swapped(*corners, "lat"))
    scale = float(tokens * n_dp * n_lat * n_lon) ** -0.5

    attend = lambda first, count, before, after: attention_grads(
        first, count, start, masks, halo, qkv, flat_grad, w_qkv, shape, before, after
    )

    def return_sides(calls, rims, after):
        to_left, to_right = merge_sides(
            start, [c[4] for c in calls], [c[5] for c in calls], *rims, band_rows, band_cols, after
        )
        from_right = shifted(to_left, "lon", -1, True)
        from_left = shifted(to_right, "lon", 1, True)
        return to_left, from_left, from_right

    def finished(calls, rims, sides, parts, after, flops):
        mids = [c[3] for c in calls]
        return finish(start, mids, *rims, *sides, parts, band_rows, band_cols, after, flops)

    groups = HEADS // GROUP
    one = attend(0, slots, [], [])
    rims_1 = swapped(one[1], one[2], "lat")
    two = attend(slots, groups - slots - 1, [], [one[0]])
    sent, *sides_1 = return_sides([one], rims_1, [two[0]])
    three = attend(groups - 1, 1, [two[1], two[2]], [sent])
    rims_2 = swapped(three[1], three[2], "lat")
    dq = [one[0], two[0], three[0]]

    dk_1, dv_1 = finished([one], rims_1, sides_1, (0, 1), [three[0]], 2 * 10**9)
    sent, *sides_2 = return_sides([two, three], rims_2, [dk_1])
    send = grad_rows(rows_send, [*dq, dk_1, dv_1], scale, BF, after=[sent])
    received = exchanged(send, *first)
    keep = grad_rows(rows_keep, [*dq, dk_1, dv_1], scale, F32, after=[send])
    keep, send = add_split(keep, received)

    (dk_2,) = finished([two, three], rims_2, sides_2, (0,), [keep], FINISH_FLOPS)
    received = exchanged_stage(send, stages[0])
    keep, send = add_split(keep, received, [dk_2])
    received = exchanged_stage(send, stages[1])
    (dv_2,) = finished([two, three], rims_2, sides_2, (1,), [keep], 10**5)
    send_2 = grad_rows(rows_send, [dk_2, dv_2], scale, BF)
    received_2 = exchanged(send_2, *first)
    keep_2 = grad_rows(rows_keep, [dk_2, dv_2], scale, F32, after=[send_2])
    keep_2, send_2 = add_split(keep_2, received_2)
    received_2 = exchanged_stage(send_2, stages[0])
    grad_inputs, done = input_grads([*dq, dk_1, dk_2, dv_1, dv_2], w_qkv, [send_2])
    keep, send = add_split(keep, received, [done])
    for i in range(2, len(stages)):
        received = exchanged_stage(send, stages[i])
        keep_2, send_2 = add_split(keep_2, received_2, [keep])
        received_2 = exchanged_stage(send_2, stages[i - 1])
        if i + 1 < len(stages):
            keep, send = add_split(keep, received, [keep_2])
    keep_2, send_2 = add_split(keep_2, received_2)
    received_2 = exchanged_stage(send_2, stages[-1])
    groups = [(keep, received), (keep_2, received_2)]
    places = [
        [(0, width, 0), (width, half, width), (width + half, half, 2 * width)],
        [(0, half, width + half), (half, half, 2 * width + half)],
    ]
    grad_w = gather_sums(groups, places, 3 * width)
    return (grad_inputs.reshape(inputs.shape), grad_w)


def solution(mesh):
    in_specs = (P("dp", "lat", "lon", None), P("dp", "lat", "lon", None), P())
    out_specs = (P("dp", "lat", "lon", None), P(("dp", "lat", "lon"), None))
    return jax.shard_map(body, mesh=mesh, in_specs=in_specs, out_specs=out_specs, check_vma=False)
```

```python
import functools

import jax
import jax.numpy as jnp
import numpy as np
from jax import lax
from jax.experimental import pallas as pl
from jax.experimental.pallas import tpu as pltpu
from jax.sharding import PartitionSpec as P

HEADS = 16
WIN = 13
MARGIN = WIN // 2
TILE_R = 4
GROUP = 4
KEY_COLS = 32
HALO_COLS = 16
REGION_R = 16
PAD_R = 2
EDGE_R = MARGIN + PAD_R
NEG = -1e30
BF = jnp.bfloat16
F32 = jnp.float32
MIB = 1024 * 1024
FINISH_FLOPS = 9 * 10**9
LANES = 128
ATTENTION_MIB = 32

NT = (((1,), (1,)), ((), ()))
TN = (((0,), (0,)), ((), ()))
NN = (((1,), (0,)), ((), ()))


def dot(a, b, dims=NN):
    return lax.dot_general(a, b, dims, preferred_element_type=F32)


def region_top(tile, band_start, band_rows, total_rows):
    lowest = jnp.where(band_start == 0, TILE_R, 0)
    highest = jnp.where(band_start + band_rows == total_rows, band_rows - 2 * TILE_R, band_rows)
    return jnp.clip(tile * TILE_R, lowest, highest)


def mask_kernel(band_rows, band_cols, total_rows, start_ref, mask_ref):
    band_start = start_ref[0]
    tile = pl.program_id(0)
    shape = mask_ref.shape[1:]
    first = region_top(tile, band_start, band_rows, total_rows)
    key = lax.broadcasted_iota(jnp.int32, shape, 0)
    query = lax.broadcasted_iota(jnp.int32, shape, 1) & (TILE_R * band_cols - 1)
    key_row = band_start - MARGIN + first + (key >> (KEY_COLS.bit_length() - 1))
    place = key & (KEY_COLS - 1)
    query_row = band_start + tile * TILE_R + (query >> (band_cols.bit_length() - 1))
    query_col = query & (band_cols - 1)
    window = jnp.clip(query_row - MARGIN, 0, total_rows - WIN)
    row_inside = (key_row >= window) & (key_row < window + WIN)
    key_col = jnp.where(
        place < band_cols,
        place,
        jnp.where(place < band_cols + MARGIN, place - band_cols - MARGIN, place - MARGIN),
    )
    col_inside = (jnp.abs(key_col - query_col) <= MARGIN) & (place < band_cols + 2 * MARGIN)
    mask_ref[0] = jnp.where(row_inside & col_inside, 0.0, NEG).astype(BF)


def window_masks(start, band_rows, band_cols, total_rows):
    tiles = band_rows // TILE_R
    shape = (REGION_R * KEY_COLS, 2 * TILE_R * band_cols)
    return pl.pallas_call(
        functools.partial(mask_kernel, band_rows, band_cols, total_rows),
        grid=(tiles,),
        in_specs=[pl.BlockSpec(memory_space=pltpu.SMEM)],
        out_specs=pl.BlockSpec((1,) + shape, lambda t: (t, 0, 0)),
        out_shape=jax.ShapeDtypeStruct((tiles,) + shape, BF),
        cost_estimate=pl.CostEstimate(flops=10**7, bytes_accessed=2**21, transcendentals=0),
    )(start)


def attention_kernel(band_rows, band_cols, total_rows, head_width, extra, first, count, shift, *refs):
    (place_ref, mask_ref, take_ref, left_ref, right_ref, rows_a, rows_b, corners_a, corners_b,
     qkv_hbm, grad_hbm, w_hbm) = refs[:12]
    before_a, before_b = refs[12 : 12 + shift], refs[12 + shift : 12 + 2 * shift]
    (dq_all, out_a_all, out_b_all, mid_all, to_left_all, to_right_all,
     halo_ref, spot_ref, q_ref, k_ref, v_ref, dk_ref, dv_ref,
     side_ref, own_refs, w_refs, own_sem, w_sem) = refs[12 + extra :]
    band_start = place_ref[0]
    even = place_ref[1] == 0
    tiles = band_rows // TILE_R
    queries = TILE_R * band_cols
    keys = REGION_R * KEY_COLS
    width = GROUP * head_width
    lanes = GROUP * queries
    region_rows = band_rows + 2 * MARGIN
    side = MARGIN * band_rows
    edge = MARGIN * band_cols
    corner = 2 * MARGIN * EDGE_R
    at_above = 2 * side
    at_below = at_above + edge
    at_cl = at_below + edge
    at_cr = at_cl + corner
    halves = [(i, slice(i * LANES, (i + 1) * LANES)) for i in range(width // LANES)]

    step = pl.program_id(0)
    dq_ref, mid_ref, to_left_ref, to_right_ref = (
        ref.at[step] for ref in (dq_all, mid_all, to_left_all, to_right_all)
    )
    out_a, out_b = (ref.at[step + shift] for ref in (out_a_all, out_b_all))
    groups = HEADS // GROUP

    def copies(slot, parts):
        at = lambda part: pl.ds(pl.multiple_of((part * groups + first + slot) * width, width), width)
        for part, source, where, i in parts:
            target, sem = (w_refs, w_sem) if where else (own_refs, own_sem)
            yield pltpu.make_async_copy(source.at[:, at(part)], target.at[slot, i], sem.at[slot, i])

    for_k = ((1, w_hbm, 1, 0), (1, qkv_hbm, 0, 1))
    for_v = ((2, w_hbm, 1, 1), (2, qkv_hbm, 0, 2))
    for_q = ((0, qkv_hbm, 0, 0), (0, grad_hbm, 0, 3))

    @pl.when(step == 0)
    def _():
        for ref, kept in ((out_a_all, before_a), (out_b_all, before_b)):
            for i in range(shift):
                ref[i] = kept[0][i]
        for slot in range(count):
            for copy in copies(slot, for_k + for_v + for_q):
                copy.start()
        halo_ref[:side] = left_ref[...]
        halo_ref[side:at_above] = right_ref[...]
        for above, below, size, refs_ab in (
            (at_above, at_below, edge, (rows_a, rows_b)),
            (at_cl, at_cr, corner, (corners_a, corners_b)),
        ):
            for ref, at in zip(refs_ab, (jnp.where(even, below, above), jnp.where(even, above, below))):
                halo_ref[pl.ds(pl.multiple_of(at, 16), size), :] = ref[...]
        spot_ref[...] = jnp.zeros_like(spot_ref)

    def place(target, own, weights):
        fresh = dot(halo_ref[...], weights)
        for col in range(MARGIN):
            start = MARGIN * HALO_COLS + col
            for part, at in halves:
                spot_ref[part, pl.ds(start, band_rows, stride=HALO_COLS), :] = fresh[
                    col * band_rows : (col + 1) * band_rows, at
                ]
                spot_ref[part, pl.ds(start + MARGIN, band_rows, stride=HALO_COLS), :] = fresh[
                    side + col * band_rows : side + (col + 1) * band_rows, at
                ]
        for corner_at, skip, row in ((at_cl, PAD_R, 0), (at_cr, 0, MARGIN + band_rows)):
            for col in range(2 * MARGIN):
                base = corner_at + col * EDGE_R + skip
                spot = pl.ds(row * HALO_COLS + col, MARGIN, stride=HALO_COLS)
                for part, at in halves:
                    spot_ref[part, spot, :] = fresh[base : base + MARGIN, at]
        for row in range(region_rows):
            base = row * KEY_COLS
            inner = row - MARGIN
            if inner < 0:
                ours = fresh[at_above + row * band_cols : at_above + (row + 1) * band_cols].astype(BF)
            elif inner < band_rows:
                ours = own[inner * band_cols : (inner + 1) * band_cols, :]
            else:
                past = at_below + (inner - band_rows) * band_cols
                ours = fresh[past : past + band_cols].astype(BF)
            target[base : base + band_cols, :] = ours
            for part, at in halves:
                target[base + band_cols : base + KEY_COLS, at] = spot_ref[
                    part, row * HALO_COLS : (row + 1) * HALO_COLS, :
                ].astype(BF)

    grad_ref = own_refs.at[step, 3]
    for copy in copies(step, for_k + for_v + for_q):
        copy.wait()
    place(k_ref, own_refs.at[step, 1], w_refs[step, 0])
    place(v_ref, own_refs.at[step, 2], w_refs[step, 1])
    q_ref[...] = own_refs[step, 0] * BF(head_width**-0.5)
    dk_ref[...] = jnp.zeros_like(dk_ref)
    dv_ref[...] = jnp.zeros_like(dv_ref)

    def spread(rows):
        block = jnp.concatenate([rows] * GROUP, axis=0)
        head_row = lax.broadcasted_iota(jnp.int32, (lanes, width), 0) // queries
        head_col = lax.broadcasted_iota(jnp.int32, (lanes, width), 1) // head_width
        return jnp.where(head_row == head_col, block, jnp.zeros_like(block))

    def one_tile(tile, carry):
        first = region_top(tile, band_start, band_rows, total_rows)
        region = pl.ds(pl.multiple_of(first * KEY_COLS, TILE_R * KEY_COLS), keys)
        total = pl.ds(pl.multiple_of((first + PAD_R) * KEY_COLS, PAD_R * KEY_COLS), keys)
        mine = pl.ds(pl.multiple_of(tile * queries, queries), queries)
        q_wide = spread(q_ref[mine, :])
        g_wide = spread(grad_ref[mine, :])
        mask = mask_ref[tile].astype(F32)
        scores = dot(k_ref[region, :], q_wide, NT) + jnp.concatenate([mask, mask], axis=1)
        dots = dot(v_ref[region, :], g_wide, NT)
        exponent = jnp.exp(scores - jnp.max(scores, axis=0, keepdims=True))
        inverse = 1.0 / jnp.sum(exponent, axis=0, keepdims=True)
        delta = jnp.sum(exponent * dots, axis=0, keepdims=True) * inverse
        attn = exponent * inverse
        dscore = (attn * (dots - delta)).astype(BF)
        dv = dot(attn.astype(BF), g_wide)
        dk = dot(dscore, q_wide)
        for part, at in halves:
            dv_ref[part, total, :] += dv[:, at]
            dk_ref[part, total, :] += dk[:, at]
        dq_wide = dot(dscore, k_ref[region, :], TN)
        head_col = lax.broadcasted_iota(jnp.int32, (queries, width), 1) // head_width
        dq = jnp.zeros((queries, width), F32)
        for head in range(GROUP):
            dq = jnp.where(head_col == head, dq_wide[head * queries : (head + 1) * queries], dq)
        dq_ref[mine, :] = (dq * head_width**-0.5).astype(BF)
        return carry

    lax.fori_loop(0, tiles, one_tile, 0, unroll=4)

    middle = (PAD_R + MARGIN) * KEY_COLS
    below = (PAD_R + MARGIN + band_rows) * KEY_COLS
    for part, acc in enumerate((dk_ref, dv_ref)):
        for lane, at in halves:
            for out, own_at, side_at in (
                (out_a, jnp.where(even, below, PAD_R * KEY_COLS), jnp.where(even, below, 0)),
                (out_b, jnp.where(even, PAD_R * KEY_COLS, below), jnp.where(even, 0, below)),
            ):
                for row in range(MARGIN):
                    start = pl.multiple_of(own_at + row * KEY_COLS, KEY_COLS)
                    out[part, row * band_cols : (row + 1) * band_cols, at] = acc[
                        lane, pl.ds(start, band_cols), :
                    ].astype(BF)
                for pair in range(MARGIN):
                    here = slice(edge + pair * 2 * EDGE_R, edge + (pair + 1) * 2 * EDGE_R)
                    start = side_at + band_cols + 2 * pair
                    out[part, here, at] = jnp.concatenate(
                        [
                            acc[lane, pl.ds(start, EDGE_R, stride=KEY_COLS), :],
                            acc[lane, pl.ds(start + 1, EDGE_R, stride=KEY_COLS), :],
                        ],
                        axis=0,
                    ).astype(BF)
            for row in range(band_rows):
                base = middle + row * KEY_COLS
                mid_ref[part, row * band_cols : (row + 1) * band_cols, at] = acc[
                    lane, base : base + band_cols, :
                ].astype(BF)
            for row in range(band_rows):
                start = middle + row * KEY_COLS + band_cols
                side_ref[row * HALO_COLS : (row + 1) * HALO_COLS, at] = acc[
                    lane, start : start + HALO_COLS, :
                ].astype(BF)
        sides = dot(take_ref[...], side_ref[...]).astype(BF)
        to_left_ref[part] = sides[:side]
        to_right_ref[part] = sides[side:]


def attention_grads(first, count, place, masks, take, halo, qkv, grad_out, w_qkv, shape, before, after):
    band_rows, band_cols, total_rows = shape
    tokens, width = grad_out.shape
    head_width = width // HEADS
    block = GROUP * head_width
    region_tokens = (band_rows + 2 * MARGIN) * KEY_COLS
    total_tokens = (band_rows + 2 * MARGIN + 2 * PAD_R) * KEY_COLS
    side = MARGIN * band_rows
    edge = MARGIN * (band_cols + 2 * EDGE_R)
    corner = 2 * MARGIN * EDGE_R
    halo_tokens = 2 * (side + MARGIN * band_cols + corner)
    shift = before[0].shape[0] if before else 0
    vmem = pl.BlockSpec(memory_space=pltpu.VMEM)
    shapes = [
        (count, tokens, block),
        (count + shift, 2, edge, block),
        (count + shift, 2, edge, block),
        (count, 2, tokens, block),
        (count, 2, side, block),
        (count, 2, side, block),
    ]
    return pl.pallas_call(
        functools.partial(
            attention_kernel, band_rows, band_cols, total_rows, head_width,
            len(before) + len(after), first, count, shift,
        ),
        grid=(count,),
        in_specs=[pl.BlockSpec(memory_space=pltpu.SMEM)]
        + [vmem] * (2 + len(halo))
        + [pl.BlockSpec(memory_space=pltpu.HBM)] * 3
        + [vmem] * len(before)
        + [pl.BlockSpec(memory_space=pl.ANY)] * len(after),
        out_specs=[vmem] * len(shapes),
        out_shape=[jax.ShapeDtypeStruct(s, BF) for s in shapes],
        scratch_shapes=[
            pltpu.VMEM((halo_tokens, width), BF),
            pltpu.VMEM((block // LANES, (band_rows + 2 * MARGIN) * HALO_COLS, LANES), F32),
            pltpu.VMEM((tokens, block), BF),
            pltpu.VMEM((region_tokens, block), BF),
            pltpu.VMEM((region_tokens, block), BF),
            pltpu.VMEM((block // LANES, total_tokens, LANES), F32),
            pltpu.VMEM((block // LANES, total_tokens, LANES), F32),
            pltpu.VMEM((band_rows * HALO_COLS, block), BF),
            pltpu.VMEM((count, 4, tokens, block), BF),
            pltpu.VMEM((count, 2, width, block), BF),
            pltpu.SemaphoreType.DMA((count, 4)),
            pltpu.SemaphoreType.DMA((count, 2)),
        ],
        compiler_params=pltpu.CompilerParams(
            dimension_semantics=("arbitrary",), vmem_limit_bytes=ATTENTION_MIB * MIB
        ),
        cost_estimate=pl.CostEstimate(
            flops=count * 14 * 10**9, bytes_accessed=count * 8 * MIB, transcendentals=count * 10**6
        ),
    )(place, masks, take, *halo, qkv, grad_out, w_qkv, *before, *after)


def on_chip(kernel, out_shape, operands, after=(), scratch=(), flops=10**5, place=()):
    count = len(operands) + len(place)

    def run(*refs):
        kernel(*refs[:count], *refs[count + len(after) :])

    return pl.pallas_call(
        run,
        in_specs=[pl.BlockSpec(memory_space=pltpu.SMEM)] * len(place)
        + [pl.BlockSpec(memory_space=pltpu.VMEM)] * len(operands)
        + [pl.BlockSpec(memory_space=pl.ANY)] * len(after),
        out_specs=[pl.BlockSpec(memory_space=pltpu.VMEM)] * len(out_shape),
        out_shape=[jax.ShapeDtypeStruct(s, d) for s, d in out_shape],
        scratch_shapes=list(scratch),
        compiler_params=pltpu.CompilerParams(vmem_limit_bytes=24 * MIB),
        cost_estimate=pl.CostEstimate(flops=flops, bytes_accessed=10**4, transcendentals=0),
    )(*place, *operands, *after)


def lanes_of(width):
    return [(i, slice(i * LANES, (i + 1) * LANES)) for i in range(width // LANES)]


def project(own, w_qkv, after):
    tokens, width = own.shape
    columns = w_qkv.shape[1]
    block = 4 * LANES

    def kernel(own_ref, w_ref, *refs):
        refs[-1][...] = dot(own_ref[...], w_ref[...]).astype(BF)

    return pl.pallas_call(
        kernel,
        grid=(columns // block,),
        in_specs=[
            pl.BlockSpec((tokens, width), lambda g: (0, 0)),
            pl.BlockSpec((width, block), lambda g: (0, g)),
        ]
        + [pl.BlockSpec(memory_space=pl.ANY)] * len(after),
        out_specs=pl.BlockSpec((tokens, block), lambda g: (0, g)),
        out_shape=jax.ShapeDtypeStruct((tokens, columns), BF),
        compiler_params=pltpu.CompilerParams(vmem_limit_bytes=24 * MIB),
        cost_estimate=pl.CostEstimate(flops=10**9, bytes_accessed=MIB, transcendentals=0),
    )(own, w_qkv, *after)


def input_grads(columns, w_qkv, after):
    tokens = columns[0].shape[-2]
    width, total = w_qkv.shape
    count = len(columns)
    pieces = list(pieces_of(columns))
    steps = len(pieces) // 2

    def kernel(*refs):
        w_ref, (out_ref, done_ref, acc_ref) = refs[count], refs[-3:]
        for step in range(steps):

            @pl.when(pl.program_id(0) == step)
            def _():
                both = [piece(refs, *where) for where in pieces[2 * step : 2 * step + 2]]
                product = dot(jnp.concatenate(both, axis=1), w_ref[...], NT)
                if step == 0:
                    acc_ref[...] = product
                elif step < steps - 1:
                    acc_ref[...] += product
                else:
                    out_ref[...] = (acc_ref[...] + product).astype(BF)
                    done_ref[...] = jnp.zeros_like(done_ref)

    return pl.pallas_call(
        kernel,
        grid=(steps,),
        in_specs=[pl.BlockSpec(memory_space=pltpu.VMEM)] * count
        + [pl.BlockSpec((width, total // steps), lambda g: (0, g))]
        + [pl.BlockSpec(memory_space=pl.ANY)] * len(after),
        out_specs=[
            pl.BlockSpec((tokens, width), lambda g: (0, 0)),
            pl.BlockSpec((8, LANES), lambda g: (0, 0)),
        ],
        out_shape=[
            jax.ShapeDtypeStruct((tokens, width), BF),
            jax.ShapeDtypeStruct((8, LANES), F32),
        ],
        scratch_shapes=[pltpu.VMEM((tokens, width), F32)],
        compiler_params=pltpu.CompilerParams(vmem_limit_bytes=24 * MIB),
        cost_estimate=pl.CostEstimate(flops=4 * 10**9, bytes_accessed=MIB, transcendentals=0),
    )(*columns, w_qkv, *after)


def row_blocks(place, own, orders, after):
    tokens, width = own.shape
    devices = len(orders[0])
    size = width // devices
    step = max(1, 16 // size)

    def kernel(place_ref, own_ref, low_ref, high_ref, wide_ref):
        for at in range(0, width, 2 * LANES):
            wide_ref[at : at + 2 * LANES, :] = own_ref[:, at : at + 2 * LANES].astype(F32).T
        even = place_ref[1] == 0
        me = place_ref[2]
        for j in range(0, devices, step):
            rows = []
            for k in range(j, j + step):
                owner = me ^ jnp.where(even, int(orders[0][k]), int(orders[1][k]))
                rows.append(wide_ref[pl.ds(pl.multiple_of(owner * size, size), size), :])
            half, base = divmod(j * size, width // 2)
            block = rows[0] if step == 1 else jnp.concatenate(rows, axis=0)
            (low_ref, high_ref)[half][base : base + step * size, :] = block.astype(BF)

    out = ((width // 2, tokens), BF)
    scratch = [pltpu.VMEM((width, tokens), F32)]
    return on_chip(kernel, [out, out], [own], after=after, scratch=scratch, place=[place])


def pack_sides(own, band_rows, band_cols):
    tokens, width = own.shape

    def kernel(own_ref, last_ref, first_ref, wide_ref):
        for lane, at in lanes_of(width):
            wide_ref[lane] = own_ref[:, at].astype(F32)
            for col in range(MARGIN):
                here = slice(col * band_rows, (col + 1) * band_rows)
                last = pl.ds(band_cols - MARGIN + col, band_rows, stride=band_cols)
                last_ref[here, at] = wide_ref[lane, last, :].astype(BF)
                first = pl.ds(col, band_rows, stride=band_cols)
                first_ref[here, at] = wide_ref[lane, first, :].astype(BF)

    out = ((MARGIN * band_rows, width), BF)
    scratch = [pltpu.VMEM((width // LANES, tokens, LANES), F32)]
    return on_chip(kernel, [out, out], [own], scratch=scratch)


def pack_rows(place, own, band_cols, after):
    tokens, width = own.shape
    edge = MARGIN * band_cols

    def kernel(place_ref, own_ref, out_a, out_b):
        even = place_ref[1] == 0
        last, first = own_ref[tokens - edge :, :], own_ref[:edge, :]
        out_a[...] = jnp.where(even, last, first)
        out_b[...] = jnp.where(even, first, last)

    out = ((edge, width), BF)
    return on_chip(kernel, [out, out], [own], after=after, place=[place])


def pack_corners(place, left, right, band_rows, after):
    width = left.shape[1]

    def kernel(place_ref, left_ref, right_ref, out_a, out_b):
        even = place_ref[1] == 0
        for side, side_ref in enumerate((left_ref, right_ref)):
            for col in range(0, MARGIN, 2):
                base = (side * MARGIN + col) * EDGE_R
                last, first = (
                    jnp.concatenate(
                        [
                            side_ref[at : at + EDGE_R, :].astype(F32)
                            for at in (start, start + band_rows)
                        ]
                    )
                    for start in ((col + 1) * band_rows - EDGE_R, col * band_rows)
                )
                here = slice(base, base + 2 * EDGE_R)
                out_a[here, :] = jnp.where(even, last, first).astype(BF)
                out_b[here, :] = jnp.where(even, first, last).astype(BF)

    out = ((2 * MARGIN * EDGE_R, width), BF)
    return on_chip(kernel, [out, out], [left, right], after=after, place=[place])


def selectors(band_rows, band_cols, after):
    side = MARGIN * band_rows

    def kernel(take_ref, put_ref):
        sent = lax.broadcasted_iota(jnp.int32, take_ref.shape, 0)
        held = lax.broadcasted_iota(jnp.int32, take_ref.shape, 1)
        same_row = (sent & (band_rows - 1)) == (held >> (HALO_COLS.bit_length() - 1))
        same_col = (sent >> (band_rows.bit_length() - 1)) == (held & (HALO_COLS - 1))
        take_ref[...] = jnp.where(same_row & same_col, 1.0, 0.0).astype(BF)
        held = lax.broadcasted_iota(jnp.int32, put_ref.shape, 0)
        sent = lax.broadcasted_iota(jnp.int32, put_ref.shape, 1)
        same_row = (sent & (band_rows - 1)) == (held >> (band_cols.bit_length() - 1))
        col = sent >> (band_rows.bit_length() - 1)
        col = jnp.where(col < MARGIN, col, col + band_cols - 2 * MARGIN)
        same_col = col == (held & (band_cols - 1))
        put_ref[...] = jnp.where(same_row & same_col, 1.0, 0.0).astype(BF)

    out = [((2 * side, band_rows * HALO_COLS), BF), ((band_rows * band_cols, 2 * side), BF)]
    return on_chip(kernel, out, [], after)


def merge_sides(place, lefts, rights, rim_a, rim_b, band_rows, band_cols, after=()):
    edge = MARGIN * band_cols
    calls = len(lefts)
    slots = rim_a.shape[0]
    each = slots // calls

    def kernel(place_ref, *refs):
        sides = refs[:calls], refs[calls : 2 * calls]
        a_ref, b_ref, *outs = refs[2 * calls :]
        even = place_ref[1] == 0
        for slot in range(slots):
            for part in range(2):
                for col in range(2 * MARGIN):
                    source = sides[col // MARGIN][slot // each]
                    base = (col % MARGIN) * band_rows
                    pair = slice(edge + (col // 2) * 2 * EDGE_R, edge + (col // 2 + 1) * 2 * EDGE_R)
                    odd = slice((col % 2) * EDGE_R, (col % 2 + 1) * EDGE_R)
                    rows = source[slot % each, part, base : base + band_rows, :].astype(F32)
                    from_a, from_b = (
                        ref[slot, part, pair, :].astype(F32)[odd] for ref in (a_ref, b_ref)
                    )
                    first = rows[:EDGE_R] + jnp.where(even, from_b, from_a)
                    last = rows[band_rows - EDGE_R :] + jnp.where(even, from_a, from_b)
                    outs[col // MARGIN][slot, part, base : base + band_rows, :] = jnp.concatenate(
                        [first, rows[EDGE_R : band_rows - EDGE_R], last], axis=0
                    ).astype(BF)

    out = ((slots,) + lefts[0].shape[1:], BF)
    return on_chip(kernel, [out, out], [*lefts, *rights, rim_a, rim_b], after, place=[place])


def finish(place, mids, rim_a, rim_b, left, right, put, parts, band_rows, band_cols, after, flops):
    calls = len(mids)
    slots, _, _, block = rim_a.shape
    each = slots // calls
    edge = MARGIN * band_cols
    tokens = band_rows * band_cols

    def kernel(place_ref, *refs):
        a_ref, b_ref, left_ref, right_ref, put_ref, *outs, acc_ref = refs[calls:]
        even = place_ref[1] == 0
        for out_ref, part in zip(outs, parts):
            for slot in range(slots):
                sides = jnp.concatenate([left_ref[slot, part], right_ref[slot, part]], axis=0)
                acc_ref[...] = dot(put_ref[...], sides) + refs[slot // each][
                    slot % each, part
                ].astype(F32)
                from_a, from_b = (r[slot, part, :edge, :].astype(F32) for r in (a_ref, b_ref))
                acc_ref[:edge, :] += jnp.where(even, from_b, from_a)
                acc_ref[tokens - edge :, :] += jnp.where(even, from_a, from_b)
                out_ref[:, slot * block : (slot + 1) * block] = acc_ref[...].astype(BF)

    out = [((tokens, slots * block), BF)] * len(parts)
    scratch = [pltpu.VMEM((tokens, block), F32)]
    operands = [*mids, rim_a, rim_b, left, right, put]
    return on_chip(kernel, out, operands, after, scratch, flops, [place])


def pieces_of(arrays):
    for i, array in enumerate(arrays):
        slots = range(array.shape[0]) if array.ndim == 3 else [None]
        for slot in slots:
            for start in range(0, array.shape[-1], 2 * LANES):
                yield i, slot, start


def piece(refs, i, slot, start):
    here = slice(start, start + 2 * LANES)
    return refs[i][:, here] if slot is None else refs[i][slot, :, here]


def grad_rows(rows, columns, scale, kind, after=()):
    features, count = rows.shape[0], len(columns)
    pieces = list(pieces_of(columns))

    def kernel(rows_ref, *refs):
        for at, where in enumerate(pieces):
            part = dot(rows_ref[...], piece(refs, *where))
            here = slice(at * 2 * LANES, (at + 1) * 2 * LANES)
            refs[count][:, here] = (part * scale).astype(kind)

    out = [((features, len(pieces) * 2 * LANES), kind)]
    return on_chip(kernel, out, [rows, *columns], after)[0]


def add_split(keep, received, after=()):
    half, columns = keep.shape[0] // 2, keep.shape[1]

    def kernel(keep_ref, received_ref, sums_ref, send_ref):
        sums_ref[...] = keep_ref[:half, :] + received_ref[:half, :].astype(F32)
        send_ref[...] = (keep_ref[half:, :] + received_ref[half:, :].astype(F32)).astype(BF)

    return on_chip(kernel, [((half, columns), F32), ((half, columns), BF)], [keep, received], after)


def gather_sums(groups, places, width):
    flat = [array for group in groups for array in group]

    def kernel(*refs):
        out_ref = refs[-1]
        for i, moves in enumerate(places):
            keep_ref, received_ref = refs[2 * i : 2 * i + 2]
            for source, size, target in moves:
                here = slice(source, source + size)
                total = keep_ref[:, here] + received_ref[:, here].astype(F32)
                out_ref[:, target : target + size] = total

    return on_chip(kernel, [((flat[0].shape[0], width), F32)], flat)[0]


def shifted(array, axis, by, wrap):
    size = lax.axis_size(axis)
    route = [(i, (i + by) % size) for i in range(size) if wrap or 0 <= i + by < size]
    return lax.ppermute(array, axis, route)


def swapped(array_a, array_b, axis):
    size = lax.axis_size(axis)
    pairs = [(i, i + 1) for i in range(size - 1)]
    route = lambda chosen: chosen + [(j, i) for i, j in chosen]
    return [
        lax.ppermute(array, axis, route(pairs[offset::2]))
        for array, offset in ((array_a, 0), (array_b, 1))
    ]


def exchanged(array, axis, flip):
    return lax.ppermute(array, axis, [(i, i ^ flip) for i in range(lax.axis_size(axis))])


def bits_of(axis):
    return [(axis, 1 << b) for b in range((lax.axis_size(axis) - 1).bit_length())]


def reduce_stages():
    first, *lat_bits = bits_of("lat")
    bits = bits_of("dp") + lat_bits
    return first, list(zip(bits, reversed(bits))) + [(bit, bit) for bit in bits_of("lon")]


def feature_orders(first, stages):
    n_lon, n_lat = lax.axis_size("lon"), lax.axis_size("lat")
    unit = {"lon": 1, "lat": n_lon, "dp": n_lon * n_lat}
    lower = []
    for kind in range(2):
        order = np.zeros(1, np.int64)
        for stage in reversed(stages):
            axis, bit = stage[kind]
            order = np.concatenate([order, order + unit[axis] * bit])
        lower.append(order)
    flip = unit[first[0]] * first[1]
    return [np.concatenate([lower[kind], lower[1 - kind] ^ flip]) for kind in range(2)]


def exchanged_stage(array, stage):
    if stage[0] == stage[1]:
        return exchanged(array, *stage[0])
    n_lat, n_dp = lax.axis_size("lat"), lax.axis_size("dp")
    route = []
    for i in range(n_dp * n_lat):
        axis, bit = stage[i % n_lat % 2]
        route.append((i, i ^ (bit * n_lat if axis == "dp" else bit)))
    return lax.ppermute(array, ("dp", "lat"), route)


def body(inputs, grad_out, w_qkv):
    _, band_rows, band_cols, width = inputs.shape
    n_lat, n_lon, n_dp = lax.axis_size("lat"), lax.axis_size("lon"), lax.axis_size("dp")
    band_start = lax.axis_index("lat") * band_rows
    total_rows = band_rows * n_lat
    tokens = band_rows * band_cols
    slots = HEADS // GROUP // 2
    shape = (band_rows, band_cols, total_rows)
    own = inputs.reshape(tokens, width)
    flat_grad = grad_out.reshape(tokens, width)

    last_cols, first_cols = pack_sides(own, band_rows, band_cols)
    left = shifted(last_cols, "lon", 1, True)
    right = shifted(first_cols, "lon", -1, True)
    me = (lax.axis_index("dp") * n_lat + lax.axis_index("lat")) * n_lon + lax.axis_index("lon")
    start = jnp.stack([band_start, lax.axis_index("lat") % 2, me])
    rim_rows = swapped(*pack_rows(start, own, band_cols, [last_cols]), "lat")

    take, put = selectors(band_rows, band_cols, [last_cols])
    masks = window_masks(start, band_rows, band_cols, total_rows)
    qkv = project(own, w_qkv, [last_cols])
    first, stages = reduce_stages()
    half = width // 2
    rows_keep, rows_send = row_blocks(start, own, feature_orders(first, stages), [last_cols])
    corners = pack_corners(start, left, right, band_rows, [masks, take, qkv, rows_keep, rows_send])
    halo = (left, right, *rim_rows, *swapped(*corners, "lat"))
    scale = float(tokens * n_dp * n_lat * n_lon) ** -0.5

    attend = lambda first, count, before, after: attention_grads(
        first, count, start, masks, take, halo, qkv, flat_grad, w_qkv, shape, before, after
    )

    def return_sides(calls, rims, after):
        to_left, to_right = merge_sides(
            start, [c[4] for c in calls], [c[5] for c in calls], *rims, band_rows, band_cols, after
        )
        from_right = shifted(to_left, "lon", -1, True)
        from_left = shifted(to_right, "lon", 1, True)
        return to_left, from_left, from_right

    def finished(calls, rims, sides, parts, after, flops):
        mids = [c[3] for c in calls]
        return finish(start, mids, *rims, *sides, put, parts, band_rows, band_cols, after, flops)

    groups = HEADS // GROUP
    one = attend(0, slots, [], [])
    rims_1 = swapped(one[1], one[2], "lat")
    two = attend(slots, groups - slots - 1, [], [one[0]])
    sent, *sides_1 = return_sides([one], rims_1, [two[0]])
    three = attend(groups - 1, 1, [two[1], two[2]], [sent])
    rims_2 = swapped(three[1], three[2], "lat")
    dq = [one[0], two[0], three[0]]

    dk_1, dv_1 = finished([one], rims_1, sides_1, (0, 1), [three[0]], 2 * 10**9)
    sent, *sides_2 = return_sides([two, three], rims_2, [dk_1])
    send = grad_rows(rows_send, [*dq, dk_1, dv_1], scale, BF, after=[sent])
    received = exchanged(send, *first)
    keep = grad_rows(rows_keep, [*dq, dk_1, dv_1], scale, F32, after=[send])
    keep, send = add_split(keep, received)

    (dk_2,) = finished([two, three], rims_2, sides_2, (0,), [keep], FINISH_FLOPS)
    received = exchanged_stage(send, stages[0])
    keep, send = add_split(keep, received, [dk_2])
    received = exchanged_stage(send, stages[1])
    (dv_2,) = finished([two, three], rims_2, sides_2, (1,), [keep], 10**5)
    send_2 = grad_rows(rows_send, [dk_2, dv_2], scale, BF)
    received_2 = exchanged(send_2, *first)
    keep_2 = grad_rows(rows_keep, [dk_2, dv_2], scale, F32, after=[send_2])
    keep_2, send_2 = add_split(keep_2, received_2)
    received_2 = exchanged_stage(send_2, stages[0])
    grad_inputs, done = input_grads([*dq, dk_1, dk_2, dv_1, dv_2], w_qkv, [send_2])
    keep, send = add_split(keep, received, [done])
    for i in range(2, len(stages)):
        received = exchanged_stage(send, stages[i])
        keep_2, send_2 = add_split(keep_2, received_2, [keep])
        received_2 = exchanged_stage(send_2, stages[i - 1])
        if i + 1 < len(stages):
            keep, send = add_split(keep, received, [keep_2])
    keep_2, send_2 = add_split(keep_2, received_2)
    received_2 = exchanged_stage(send_2, stages[-1])
    groups = [(keep, received), (keep_2, received_2)]
    places = [
        [(0, width, 0), (width, half, width), (width + half, half, 2 * width)],
        [(0, half, width + half), (half, half, 2 * width + half)],
    ]
    grad_w = gather_sums(groups, places, 3 * width)
    return (grad_inputs.reshape(inputs.shape), grad_w)


def solution(mesh):
    in_specs = (P("dp", "lat", "lon", None), P("dp", "lat", "lon", None), P())
    out_specs = (P("dp", "lat", "lon", None), P(("dp", "lat", "lon"), None))
    return jax.shard_map(body, mesh=mesh, in_specs=in_specs, out_specs=out_specs, check_vma=False)
```

```python
import functools

import jax
import jax.numpy as jnp
import numpy as np
from jax import lax
from jax.experimental import pallas as pl
from jax.experimental.pallas import tpu as pltpu
from jax.sharding import PartitionSpec as P

HEADS = 16
WIN = 13
MARGIN = WIN // 2
TILE_R = 4
GROUP = 4
KEY_COLS = 32
HALO_COLS = 16
REGION_R = 16
PAD_R = 2
EDGE_R = MARGIN + PAD_R
NEG = -1e30
BF = jnp.bfloat16
F32 = jnp.float32
MIB = 1024 * 1024
FINISH_FLOPS = 9 * 10**9
LANES = 128
ATTENTION_MIB = 32

NT = (((1,), (1,)), ((), ()))
TN = (((0,), (0,)), ((), ()))
NN = (((1,), (0,)), ((), ()))


def dot(a, b, dims=NN):
    return lax.dot_general(a, b, dims, preferred_element_type=F32)


def region_top(tile, band_start, band_rows, total_rows):
    lowest = jnp.where(band_start == 0, TILE_R, 0)
    highest = jnp.where(band_start + band_rows == total_rows, band_rows - 2 * TILE_R, band_rows)
    return jnp.clip(tile * TILE_R, lowest, highest)


def mask_kernel(band_rows, band_cols, total_rows, start_ref, mask_ref):
    band_start = start_ref[0]
    tile = pl.program_id(0)
    shape = mask_ref.shape[1:]
    first = region_top(tile, band_start, band_rows, total_rows)
    key = lax.broadcasted_iota(jnp.int32, shape, 0)
    query = lax.broadcasted_iota(jnp.int32, shape, 1) & (TILE_R * band_cols - 1)
    key_row = band_start - MARGIN + first + (key >> (KEY_COLS.bit_length() - 1))
    place = key & (KEY_COLS - 1)
    query_row = band_start + tile * TILE_R + (query >> (band_cols.bit_length() - 1))
    query_col = query & (band_cols - 1)
    window = jnp.clip(query_row - MARGIN, 0, total_rows - WIN)
    row_inside = (key_row >= window) & (key_row < window + WIN)
    key_col = jnp.where(
        place < band_cols,
        place,
        jnp.where(place < band_cols + MARGIN, place - band_cols - MARGIN, place - MARGIN),
    )
    col_inside = (jnp.abs(key_col - query_col) <= MARGIN) & (place < band_cols + 2 * MARGIN)
    mask_ref[0] = jnp.where(row_inside & col_inside, 0.0, NEG).astype(BF)


def window_masks(start, band_rows, band_cols, total_rows):
    tiles = band_rows // TILE_R
    shape = (REGION_R * KEY_COLS, 2 * TILE_R * band_cols)
    return pl.pallas_call(
        functools.partial(mask_kernel, band_rows, band_cols, total_rows),
        grid=(tiles,),
        in_specs=[pl.BlockSpec(memory_space=pltpu.SMEM)],
        out_specs=pl.BlockSpec((1,) + shape, lambda t: (t, 0, 0)),
        out_shape=jax.ShapeDtypeStruct((tiles,) + shape, BF),
        cost_estimate=pl.CostEstimate(flops=10**7, bytes_accessed=2**21, transcendentals=0),
    )(start)


def attention_kernel(band_rows, band_cols, total_rows, head_width, extra, first, count, shift, *refs):
    (place_ref, mask_ref, take_ref, left_ref, right_ref, rows_a, rows_b, corners_a, corners_b,
     qkv_hbm, grad_hbm, w_hbm) = refs[:12]
    before_a, before_b = refs[12 : 12 + shift], refs[12 + shift : 12 + 2 * shift]
    (dq_all, out_a_all, out_b_all, mid_all, to_left_all, to_right_all,
     halo_ref, spot_ref, q_ref, k_ref, v_ref, dk_ref, dv_ref,
     side_ref, own_refs, w_refs, own_sem, w_sem) = refs[12 + extra :]
    band_start = place_ref[0]
    even = place_ref[1] == 0
    tiles = band_rows // TILE_R
    queries = TILE_R * band_cols
    keys = REGION_R * KEY_COLS
    width = GROUP * head_width
    lanes = GROUP * queries
    region_rows = band_rows + 2 * MARGIN
    side = MARGIN * band_rows
    edge = MARGIN * band_cols
    corner = 2 * MARGIN * EDGE_R
    at_above = 2 * side
    at_below = at_above + edge
    at_cl = at_below + edge
    at_cr = at_cl + corner
    halves = [(i, slice(i * LANES, (i + 1) * LANES)) for i in range(width // LANES)]

    step = pl.program_id(0)
    dq_ref, mid_ref, to_left_ref, to_right_ref = (
        ref.at[step] for ref in (dq_all, mid_all, to_left_all, to_right_all)
    )
    out_a, out_b = (ref.at[step + shift] for ref in (out_a_all, out_b_all))
    groups = HEADS // GROUP

    def copies(slot, parts):
        at = lambda part: pl.ds(pl.multiple_of((part * groups + first + slot) * width, width), width)
        for part, source, where, i in parts:
            target, sem = (w_refs, w_sem) if where else (own_refs, own_sem)
            yield pltpu.make_async_copy(source.at[:, at(part)], target.at[slot, i], sem.at[slot, i])

    for_k = ((1, w_hbm, 1, 0), (1, qkv_hbm, 0, 1))
    for_v = ((2, w_hbm, 1, 1), (2, qkv_hbm, 0, 2))
    for_q = ((0, qkv_hbm, 0, 0), (0, grad_hbm, 0, 3))

    @pl.when(step == 0)
    def _():
        for ref, kept in ((out_a_all, before_a), (out_b_all, before_b)):
            for i in range(shift):
                ref[i] = kept[0][i]
        for slot in range(count):
            for copy in copies(slot, for_k + for_v + for_q):
                copy.start()
        halo_ref[:side] = left_ref[...]
        halo_ref[side:at_above] = right_ref[...]
        for above, below, size, refs_ab in (
            (at_above, at_below, edge, (rows_a, rows_b)),
            (at_cl, at_cr, corner, (corners_a, corners_b)),
        ):
            for ref, at in zip(refs_ab, (jnp.where(even, below, above), jnp.where(even, above, below))):
                halo_ref[pl.ds(pl.multiple_of(at, 16), size), :] = ref[...]
        spot_ref[...] = jnp.zeros_like(spot_ref)

    def place(target, own, weights):
        fresh = dot(halo_ref[...], weights)
        for col in range(MARGIN):
            start = MARGIN * HALO_COLS + col
            for part, at in halves:
                spot_ref[part, pl.ds(start, band_rows, stride=HALO_COLS), :] = fresh[
                    col * band_rows : (col + 1) * band_rows, at
                ]
                spot_ref[part, pl.ds(start + MARGIN, band_rows, stride=HALO_COLS), :] = fresh[
                    side + col * band_rows : side + (col + 1) * band_rows, at
                ]
        for corner_at, skip, row in ((at_cl, PAD_R, 0), (at_cr, 0, MARGIN + band_rows)):
            for col in range(2 * MARGIN):
                base = corner_at + col * EDGE_R + skip
                spot = pl.ds(row * HALO_COLS + col, MARGIN, stride=HALO_COLS)
                for part, at in halves:
                    spot_ref[part, spot, :] = fresh[base : base + MARGIN, at]
        for row in range(region_rows):
            base = row * KEY_COLS
            inner = row - MARGIN
            if inner < 0:
                ours = fresh[at_above + row * band_cols : at_above + (row + 1) * band_cols].astype(BF)
            elif inner < band_rows:
                ours = own[inner * band_cols : (inner + 1) * band_cols, :]
            else:
                past = at_below + (inner - band_rows) * band_cols
                ours = fresh[past : past + band_cols].astype(BF)
            target[base : base + band_cols, :] = ours
            for part, at in halves:
                target[base + band_cols : base + KEY_COLS, at] = spot_ref[
                    part, row * HALO_COLS : (row + 1) * HALO_COLS, :
                ].astype(BF)

    grad_ref = own_refs.at[step, 3]
    for copy in copies(step, for_k + for_v + for_q):
        copy.wait()
    place(k_ref, own_refs.at[step, 1], w_refs[step, 0])
    place(v_ref, own_refs.at[step, 2], w_refs[step, 1])
    q_ref[...] = own_refs[step, 0] * BF(head_width**-0.5)
    dk_ref[...] = jnp.zeros_like(dk_ref)
    dv_ref[...] = jnp.zeros_like(dv_ref)

    def spread(rows):
        block = jnp.concatenate([rows] * GROUP, axis=0)
        head_row = lax.broadcasted_iota(jnp.int32, (lanes, width), 0) // queries
        head_col = lax.broadcasted_iota(jnp.int32, (lanes, width), 1) // head_width
        return jnp.where(head_row == head_col, block, jnp.zeros_like(block))

    def one_tile(tile, carry):
        first = region_top(tile, band_start, band_rows, total_rows)
        region = pl.ds(pl.multiple_of(first * KEY_COLS, TILE_R * KEY_COLS), keys)
        total = pl.ds(pl.multiple_of((first + PAD_R) * KEY_COLS, PAD_R * KEY_COLS), keys)
        mine = pl.ds(pl.multiple_of(tile * queries, queries), queries)
        q_wide = spread(q_ref[mine, :])
        g_wide = spread(grad_ref[mine, :])
        mask = mask_ref[tile].astype(F32)
        scores = dot(k_ref[region, :], q_wide, NT) + jnp.concatenate([mask, mask], axis=1)
        dots = dot(v_ref[region, :], g_wide, NT)
        exponent = jnp.exp(scores - jnp.max(scores, axis=0, keepdims=True))
        inverse = 1.0 / jnp.sum(exponent, axis=0, keepdims=True)
        delta = jnp.sum(exponent * dots, axis=0, keepdims=True) * inverse
        attn = exponent * inverse
        dscore = (attn * (dots - delta)).astype(BF)
        dv = dot(attn.astype(BF), g_wide)
        dk = dot(dscore, q_wide)
        for part, at in halves:
            dv_ref[part, total, :] += dv[:, at]
            dk_ref[part, total, :] += dk[:, at]
        dq_wide = dot(dscore, k_ref[region, :], TN)
        head_col = lax.broadcasted_iota(jnp.int32, (queries, width), 1) // head_width
        dq = jnp.zeros((queries, width), F32)
        for head in range(GROUP):
            dq = jnp.where(head_col == head, dq_wide[head * queries : (head + 1) * queries], dq)
        dq_ref[mine, :] = (dq * head_width**-0.5).astype(BF)
        return carry

    lax.fori_loop(0, tiles, one_tile, 0, unroll=8)

    middle = (PAD_R + MARGIN) * KEY_COLS
    below = (PAD_R + MARGIN + band_rows) * KEY_COLS
    for part, acc in enumerate((dk_ref, dv_ref)):
        for lane, at in halves:
            for out, own_at, side_at in (
                (out_a, jnp.where(even, below, PAD_R * KEY_COLS), jnp.where(even, below, 0)),
                (out_b, jnp.where(even, PAD_R * KEY_COLS, below), jnp.where(even, 0, below)),
            ):
                for row in range(MARGIN):
                    start = pl.multiple_of(own_at + row * KEY_COLS, KEY_COLS)
                    out[part, row * band_cols : (row + 1) * band_cols, at] = acc[
                        lane, pl.ds(start, band_cols), :
                    ].astype(BF)
                for pair in range(MARGIN):
                    here = slice(edge + pair * 2 * EDGE_R, edge + (pair + 1) * 2 * EDGE_R)
                    start = side_at + band_cols + 2 * pair
                    out[part, here, at] = jnp.concatenate(
                        [
                            acc[lane, pl.ds(start, EDGE_R, stride=KEY_COLS), :],
                            acc[lane, pl.ds(start + 1, EDGE_R, stride=KEY_COLS), :],
                        ],
                        axis=0,
                    ).astype(BF)
            for row in range(band_rows):
                base = middle + row * KEY_COLS
                mid_ref[part, row * band_cols : (row + 1) * band_cols, at] = acc[
                    lane, base : base + band_cols, :
                ].astype(BF)
            for row in range(band_rows):
                start = middle + row * KEY_COLS + band_cols
                side_ref[row * HALO_COLS : (row + 1) * HALO_COLS, at] = acc[
                    lane, start : start + HALO_COLS, :
                ].astype(BF)
        sides = dot(take_ref[...], side_ref[...]).astype(BF)
        to_left_ref[part] = sides[:side]
        to_right_ref[part] = sides[side:]


def attention_grads(first, count, place, masks, take, halo, qkv, grad_out, w_qkv, shape, before, after):
    band_rows, band_cols, total_rows = shape
    tokens, width = grad_out.shape
    head_width = width // HEADS
    block = GROUP * head_width
    region_tokens = (band_rows + 2 * MARGIN) * KEY_COLS
    total_tokens = (band_rows + 2 * MARGIN + 2 * PAD_R) * KEY_COLS
    side = MARGIN * band_rows
    edge = MARGIN * (band_cols + 2 * EDGE_R)
    corner = 2 * MARGIN * EDGE_R
    halo_tokens = 2 * (side + MARGIN * band_cols + corner)
    shift = before[0].shape[0] if before else 0
    vmem = pl.BlockSpec(memory_space=pltpu.VMEM)
    shapes = [
        (count, tokens, block),
        (count + shift, 2, edge, block),
        (count + shift, 2, edge, block),
        (count, 2, tokens, block),
        (count, 2, side, block),
        (count, 2, side, block),
    ]
    return pl.pallas_call(
        functools.partial(
            attention_kernel, band_rows, band_cols, total_rows, head_width,
            len(before) + len(after), first, count, shift,
        ),
        grid=(count,),
        in_specs=[pl.BlockSpec(memory_space=pltpu.SMEM)]
        + [vmem] * (2 + len(halo))
        + [pl.BlockSpec(memory_space=pltpu.HBM)] * 3
        + [vmem] * len(before)
        + [pl.BlockSpec(memory_space=pl.ANY)] * len(after),
        out_specs=[vmem] * len(shapes),
        out_shape=[jax.ShapeDtypeStruct(s, BF) for s in shapes],
        scratch_shapes=[
            pltpu.VMEM((halo_tokens, width), BF),
            pltpu.VMEM((block // LANES, (band_rows + 2 * MARGIN) * HALO_COLS, LANES), F32),
            pltpu.VMEM((tokens, block), BF),
            pltpu.VMEM((region_tokens, block), BF),
            pltpu.VMEM((region_tokens, block), BF),
            pltpu.VMEM((block // LANES, total_tokens, LANES), F32),
            pltpu.VMEM((block // LANES, total_tokens, LANES), F32),
            pltpu.VMEM((band_rows * HALO_COLS, block), BF),
            pltpu.VMEM((count, 4, tokens, block), BF),
            pltpu.VMEM((count, 2, width, block), BF),
            pltpu.SemaphoreType.DMA((count, 4)),
            pltpu.SemaphoreType.DMA((count, 2)),
        ],
        compiler_params=pltpu.CompilerParams(
            dimension_semantics=("arbitrary",), vmem_limit_bytes=ATTENTION_MIB * MIB
        ),
        cost_estimate=pl.CostEstimate(
            flops=count * 14 * 10**9, bytes_accessed=count * 8 * MIB, transcendentals=count * 10**6
        ),
    )(place, masks, take, *halo, qkv, grad_out, w_qkv, *before, *after)


def on_chip(kernel, out_shape, operands, after=(), scratch=(), flops=10**5, place=()):
    count = len(operands) + len(place)

    def run(*refs):
        kernel(*refs[:count], *refs[count + len(after) :])

    return pl.pallas_call(
        run,
        in_specs=[pl.BlockSpec(memory_space=pltpu.SMEM)] * len(place)
        + [pl.BlockSpec(memory_space=pltpu.VMEM)] * len(operands)
        + [pl.BlockSpec(memory_space=pl.ANY)] * len(after),
        out_specs=[pl.BlockSpec(memory_space=pltpu.VMEM)] * len(out_shape),
        out_shape=[jax.ShapeDtypeStruct(s, d) for s, d in out_shape],
        scratch_shapes=list(scratch),
        compiler_params=pltpu.CompilerParams(vmem_limit_bytes=24 * MIB),
        cost_estimate=pl.CostEstimate(flops=flops, bytes_accessed=10**4, transcendentals=0),
    )(*place, *operands, *after)


def lanes_of(width):
    return [(i, slice(i * LANES, (i + 1) * LANES)) for i in range(width // LANES)]


def project(own, w_qkv, after):
    tokens, width = own.shape
    columns = w_qkv.shape[1]
    block = 4 * LANES

    def kernel(own_ref, w_ref, *refs):
        def part(n, carry):
            at = pl.ds(pl.multiple_of(n * 2 * LANES, 2 * LANES), 2 * LANES)
            refs[-1][:, at] = dot(own_ref[...], w_ref[:, at]).astype(BF)
            return carry

        lax.fori_loop(0, block // (2 * LANES), part, 0)

    return pl.pallas_call(
        kernel,
        grid=(columns // block,),
        in_specs=[
            pl.BlockSpec((tokens, width), lambda g: (0, 0)),
            pl.BlockSpec((width, block), lambda g: (0, g)),
        ]
        + [pl.BlockSpec(memory_space=pl.ANY)] * len(after),
        out_specs=pl.BlockSpec((tokens, block), lambda g: (0, g)),
        out_shape=jax.ShapeDtypeStruct((tokens, columns), BF),
        compiler_params=pltpu.CompilerParams(vmem_limit_bytes=24 * MIB),
        cost_estimate=pl.CostEstimate(flops=10**9, bytes_accessed=MIB, transcendentals=0),
    )(own, w_qkv, *after)


def input_grads(columns, w_qkv, after):
    tokens = columns[0].shape[-2]
    width, total = w_qkv.shape
    count = len(columns)
    pieces = list(pieces_of(columns))
    steps = len(pieces) // 2

    def kernel(*refs):
        w_ref, (out_ref, done_ref, acc_ref) = refs[count], refs[-3:]
        for step in range(steps):

            @pl.when(pl.program_id(0) == step)
            def _():
                both = [piece(refs, *where) for where in pieces[2 * step : 2 * step + 2]]
                chunk = jnp.concatenate(both, axis=1)

                def add(n, carry):
                    at = pl.ds(pl.multiple_of(n * 2 * LANES, 2 * LANES), 2 * LANES)
                    product = dot(chunk, w_ref[at, :], NT)
                    if step == 0:
                        acc_ref[:, at] = product
                    elif step < steps - 1:
                        acc_ref[:, at] += product
                    else:
                        out_ref[:, at] = (acc_ref[:, at] + product).astype(BF)
                    return carry

                lax.fori_loop(0, width // (2 * LANES), add, 0)
                if step == steps - 1:
                    done_ref[...] = jnp.zeros_like(done_ref)

    return pl.pallas_call(
        kernel,
        grid=(steps,),
        in_specs=[pl.BlockSpec(memory_space=pltpu.VMEM)] * count
        + [pl.BlockSpec((width, total // steps), lambda g: (0, g))]
        + [pl.BlockSpec(memory_space=pl.ANY)] * len(after),
        out_specs=[
            pl.BlockSpec((tokens, width), lambda g: (0, 0)),
            pl.BlockSpec((8, LANES), lambda g: (0, 0)),
        ],
        out_shape=[
            jax.ShapeDtypeStruct((tokens, width), BF),
            jax.ShapeDtypeStruct((8, LANES), F32),
        ],
        scratch_shapes=[pltpu.VMEM((tokens, width), F32)],
        compiler_params=pltpu.CompilerParams(vmem_limit_bytes=24 * MIB),
        cost_estimate=pl.CostEstimate(flops=4 * 10**9, bytes_accessed=MIB, transcendentals=0),
    )(*columns, w_qkv, *after)


def row_blocks(place, own, orders, after):
    tokens, width = own.shape
    devices = len(orders[0])
    size = width // devices
    step = max(1, 16 // size)

    def kernel(place_ref, own_ref, low_ref, high_ref, wide_ref):
        for at in range(0, width, 2 * LANES):
            wide_ref[at : at + 2 * LANES, :] = own_ref[:, at : at + 2 * LANES].astype(F32).T
        even = place_ref[1] == 0
        me = place_ref[2]
        for j in range(0, devices, step):
            rows = []
            for k in range(j, j + step):
                owner = me ^ jnp.where(even, int(orders[0][k]), int(orders[1][k]))
                rows.append(wide_ref[pl.ds(pl.multiple_of(owner * size, size), size), :])
            half, base = divmod(j * size, width // 2)
            block = rows[0] if step == 1 else jnp.concatenate(rows, axis=0)
            (low_ref, high_ref)[half][base : base + step * size, :] = block.astype(BF)

    out = ((width // 2, tokens), BF)
    scratch = [pltpu.VMEM((width, tokens), F32)]
    return on_chip(kernel, [out, out], [own], after=after, scratch=scratch, place=[place])


def pack_sides(own, band_rows, band_cols):
    tokens, width = own.shape

    def kernel(own_ref, last_ref, first_ref, wide_ref):
        for lane, at in lanes_of(width):
            wide_ref[lane] = own_ref[:, at].astype(F32)
            for col in range(MARGIN):
                here = slice(col * band_rows, (col + 1) * band_rows)
                last = pl.ds(band_cols - MARGIN + col, band_rows, stride=band_cols)
                last_ref[here, at] = wide_ref[lane, last, :].astype(BF)
                first = pl.ds(col, band_rows, stride=band_cols)
                first_ref[here, at] = wide_ref[lane, first, :].astype(BF)

    out = ((MARGIN * band_rows, width), BF)
    scratch = [pltpu.VMEM((width // LANES, tokens, LANES), F32)]
    return on_chip(kernel, [out, out], [own], scratch=scratch)


def pack_rows(place, own, band_cols, after):
    tokens, width = own.shape
    edge = MARGIN * band_cols

    def kernel(place_ref, own_ref, out_a, out_b):
        even = place_ref[1] == 0
        last, first = own_ref[tokens - edge :, :], own_ref[:edge, :]
        out_a[...] = jnp.where(even, last, first)
        out_b[...] = jnp.where(even, first, last)

    out = ((edge, width), BF)
    return on_chip(kernel, [out, out], [own], after=after, place=[place])


def pack_corners(place, left, right, band_rows, after):
    width = left.shape[1]

    def kernel(place_ref, left_ref, right_ref, out_a, out_b):
        even = place_ref[1] == 0
        for side, side_ref in enumerate((left_ref, right_ref)):
            for col in range(0, MARGIN, 2):
                base = (side * MARGIN + col) * EDGE_R
                last, first = (
                    jnp.concatenate(
                        [
                            side_ref[at : at + EDGE_R, :].astype(F32)
                            for at in (start, start + band_rows)
                        ]
                    )
                    for start in ((col + 1) * band_rows - EDGE_R, col * band_rows)
                )
                here = slice(base, base + 2 * EDGE_R)
                out_a[here, :] = jnp.where(even, last, first).astype(BF)
                out_b[here, :] = jnp.where(even, first, last).astype(BF)

    out = ((2 * MARGIN * EDGE_R, width), BF)
    return on_chip(kernel, [out, out], [left, right], after=after, place=[place])


def selectors(band_rows, band_cols, after):
    side = MARGIN * band_rows

    def kernel(take_ref, put_ref):
        sent = lax.broadcasted_iota(jnp.int32, take_ref.shape, 0)
        held = lax.broadcasted_iota(jnp.int32, take_ref.shape, 1)
        same_row = (sent & (band_rows - 1)) == (held >> (HALO_COLS.bit_length() - 1))
        same_col = (sent >> (band_rows.bit_length() - 1)) == (held & (HALO_COLS - 1))
        take_ref[...] = jnp.where(same_row & same_col, 1.0, 0.0).astype(BF)
        held = lax.broadcasted_iota(jnp.int32, put_ref.shape, 0)
        sent = lax.broadcasted_iota(jnp.int32, put_ref.shape, 1)
        same_row = (sent & (band_rows - 1)) == (held >> (band_cols.bit_length() - 1))
        col = sent >> (band_rows.bit_length() - 1)
        col = jnp.where(col < MARGIN, col, col + band_cols - 2 * MARGIN)
        same_col = col == (held & (band_cols - 1))
        put_ref[...] = jnp.where(same_row & same_col, 1.0, 0.0).astype(BF)

    out = [((2 * side, band_rows * HALO_COLS), BF), ((band_rows * band_cols, 2 * side), BF)]
    return on_chip(kernel, out, [], after)


def merge_sides(place, lefts, rights, rim_a, rim_b, band_rows, band_cols, after=()):
    edge = MARGIN * band_cols
    calls = len(lefts)
    slots = rim_a.shape[0]
    each = slots // calls

    def kernel(place_ref, *refs):
        sides = refs[:calls], refs[calls : 2 * calls]
        a_ref, b_ref, *outs = refs[2 * calls :]
        even = place_ref[1] == 0
        for slot in range(slots):
            for part in range(2):
                for col in range(2 * MARGIN):
                    source = sides[col // MARGIN][slot // each]
                    base = (col % MARGIN) * band_rows
                    pair = slice(edge + (col // 2) * 2 * EDGE_R, edge + (col // 2 + 1) * 2 * EDGE_R)
                    odd = slice((col % 2) * EDGE_R, (col % 2 + 1) * EDGE_R)
                    rows = source[slot % each, part, base : base + band_rows, :].astype(F32)
                    from_a, from_b = (
                        ref[slot, part, pair, :].astype(F32)[odd] for ref in (a_ref, b_ref)
                    )
                    first = rows[:EDGE_R] + jnp.where(even, from_b, from_a)
                    last = rows[band_rows - EDGE_R :] + jnp.where(even, from_a, from_b)
                    outs[col // MARGIN][slot, part, base : base + band_rows, :] = jnp.concatenate(
                        [first, rows[EDGE_R : band_rows - EDGE_R], last], axis=0
                    ).astype(BF)

    out = ((slots,) + lefts[0].shape[1:], BF)
    return on_chip(kernel, [out, out], [*lefts, *rights, rim_a, rim_b], after, place=[place])


def finish(place, mids, rim_a, rim_b, left, right, put, parts, band_rows, band_cols, after, flops):
    calls = len(mids)
    slots, _, _, block = rim_a.shape
    each = slots // calls
    edge = MARGIN * band_cols
    tokens = band_rows * band_cols

    def kernel(place_ref, *refs):
        a_ref, b_ref, left_ref, right_ref, put_ref, *outs, acc_ref = refs[calls:]
        even = place_ref[1] == 0
        for out_ref, part in zip(outs, parts):
            for slot in range(slots):
                sides = jnp.concatenate([left_ref[slot, part], right_ref[slot, part]], axis=0)
                acc_ref[...] = dot(put_ref[...], sides) + refs[slot // each][
                    slot % each, part
                ].astype(F32)
                from_a, from_b = (r[slot, part, :edge, :].astype(F32) for r in (a_ref, b_ref))
                acc_ref[:edge, :] += jnp.where(even, from_b, from_a)
                acc_ref[tokens - edge :, :] += jnp.where(even, from_a, from_b)
                out_ref[:, slot * block : (slot + 1) * block] = acc_ref[...].astype(BF)

    out = [((tokens, slots * block), BF)] * len(parts)
    scratch = [pltpu.VMEM((tokens, block), F32)]
    operands = [*mids, rim_a, rim_b, left, right, put]
    return on_chip(kernel, out, operands, after, scratch, flops, [place])


def pieces_of(arrays):
    for i, array in enumerate(arrays):
        slots = range(array.shape[0]) if array.ndim == 3 else [None]
        for slot in slots:
            for start in range(0, array.shape[-1], 2 * LANES):
                yield i, slot, start


def piece(refs, i, slot, start):
    here = slice(start, start + 2 * LANES)
    return refs[i][:, here] if slot is None else refs[i][slot, :, here]


def grad_rows(rows, columns, scale, kind, after=()):
    features, count = rows.shape[0], len(columns)
    pieces = list(pieces_of(columns))

    def kernel(rows_ref, *refs):
        for at, where in enumerate(pieces):
            part = dot(rows_ref[...], piece(refs, *where))
            here = slice(at * 2 * LANES, (at + 1) * 2 * LANES)
            refs[count][:, here] = (part * scale).astype(kind)

    out = [((features, len(pieces) * 2 * LANES), kind)]
    return on_chip(kernel, out, [rows, *columns], after)[0]


def add_split(keep, received, after=()):
    half, columns = keep.shape[0] // 2, keep.shape[1]

    def kernel(keep_ref, received_ref, sums_ref, send_ref):
        sums_ref[...] = keep_ref[:half, :] + received_ref[:half, :].astype(F32)
        send_ref[...] = (keep_ref[half:, :] + received_ref[half:, :].astype(F32)).astype(BF)

    return on_chip(kernel, [((half, columns), F32), ((half, columns), BF)], [keep, received], after)


def gather_sums(groups, places, width):
    flat = [array for group in groups for array in group]

    def kernel(*refs):
        out_ref = refs[-1]
        for i, moves in enumerate(places):
            keep_ref, received_ref = refs[2 * i : 2 * i + 2]
            for source, size, target in moves:
                here = slice(source, source + size)
                total = keep_ref[:, here] + received_ref[:, here].astype(F32)
                out_ref[:, target : target + size] = total

    return on_chip(kernel, [((flat[0].shape[0], width), F32)], flat)[0]


def shifted(array, axis, by, wrap):
    size = lax.axis_size(axis)
    route = [(i, (i + by) % size) for i in range(size) if wrap or 0 <= i + by < size]
    return lax.ppermute(array, axis, route)


def swapped(array_a, array_b, axis):
    size = lax.axis_size(axis)
    pairs = [(i, i + 1) for i in range(size - 1)]
    route = lambda chosen: chosen + [(j, i) for i, j in chosen]
    return [
        lax.ppermute(array, axis, route(pairs[offset::2]))
        for array, offset in ((array_a, 0), (array_b, 1))
    ]


def exchanged(array, axis, flip):
    return lax.ppermute(array, axis, [(i, i ^ flip) for i in range(lax.axis_size(axis))])


def bits_of(axis):
    return [(axis, 1 << b) for b in range((lax.axis_size(axis) - 1).bit_length())]


def reduce_stages():
    first, *lat_bits = bits_of("lat")
    bits = bits_of("dp") + lat_bits
    return first, list(zip(bits, reversed(bits))) + [(bit, bit) for bit in bits_of("lon")]


def feature_orders(first, stages):
    n_lon, n_lat = lax.axis_size("lon"), lax.axis_size("lat")
    unit = {"lon": 1, "lat": n_lon, "dp": n_lon * n_lat}
    lower = []
    for kind in range(2):
        order = np.zeros(1, np.int64)
        for stage in reversed(stages):
            axis, bit = stage[kind]
            order = np.concatenate([order, order + unit[axis] * bit])
        lower.append(order)
    flip = unit[first[0]] * first[1]
    return [np.concatenate([lower[kind], lower[1 - kind] ^ flip]) for kind in range(2)]


def exchanged_stage(array, stage):
    if stage[0] == stage[1]:
        return exchanged(array, *stage[0])
    n_lat, n_dp = lax.axis_size("lat"), lax.axis_size("dp")
    route = []
    for i in range(n_dp * n_lat):
        axis, bit = stage[i % n_lat % 2]
        route.append((i, i ^ (bit * n_lat if axis == "dp" else bit)))
    return lax.ppermute(array, ("dp", "lat"), route)


def body(inputs, grad_out, w_qkv):
    _, band_rows, band_cols, width = inputs.shape
    n_lat, n_lon, n_dp = lax.axis_size("lat"), lax.axis_size("lon"), lax.axis_size("dp")
    band_start = lax.axis_index("lat") * band_rows
    total_rows = band_rows * n_lat
    tokens = band_rows * band_cols
    slots = HEADS // GROUP // 2
    shape = (band_rows, band_cols, total_rows)
    own = inputs.reshape(tokens, width)
    flat_grad = grad_out.reshape(tokens, width)

    last_cols, first_cols = pack_sides(own, band_rows, band_cols)
    left = shifted(last_cols, "lon", 1, True)
    right = shifted(first_cols, "lon", -1, True)
    me = (lax.axis_index("dp") * n_lat + lax.axis_index("lat")) * n_lon + lax.axis_index("lon")
    start = jnp.stack([band_start, lax.axis_index("lat") % 2, me])
    rim_rows = swapped(*pack_rows(start, own, band_cols, [last_cols]), "lat")

    take, put = selectors(band_rows, band_cols, [last_cols])
    masks = window_masks(start, band_rows, band_cols, total_rows)
    qkv = project(own, w_qkv, [last_cols])
    first, stages = reduce_stages()
    half = width // 2
    rows_keep, rows_send = row_blocks(start, own, feature_orders(first, stages), [last_cols])
    corners = pack_corners(start, left, right, band_rows, [masks, qkv, rows_keep, rows_send])
    halo = (left, right, *rim_rows, *swapped(*corners, "lat"))
    scale = float(tokens * n_dp * n_lat * n_lon) ** -0.5

    attend = lambda first, count, before, after: attention_grads(
        first, count, start, masks, take, halo, qkv, flat_grad, w_qkv, shape, before, after
    )

    def return_sides(calls, rims, after):
        to_left, to_right = merge_sides(
            start, [c[4] for c in calls], [c[5] for c in calls], *rims, band_rows, band_cols, after
        )
        from_right = shifted(to_left, "lon", -1, True)
        from_left = shifted(to_right, "lon", 1, True)
        return to_left, from_left, from_right

    def finished(calls, rims, sides, parts, after, flops):
        mids = [c[3] for c in calls]
        return finish(start, mids, *rims, *sides, put, parts, band_rows, band_cols, after, flops)

    groups = HEADS // GROUP
    one = attend(0, slots, [], [])
    rims_1 = swapped(one[1], one[2], "lat")
    two = attend(slots, groups - slots - 1, [], [one[0]])
    sent, *sides_1 = return_sides([one], rims_1, [two[0]])
    three = attend(groups - 1, 1, [two[1], two[2]], [sent])
    rims_2 = swapped(three[1], three[2], "lat")
    dq = [one[0], two[0], three[0]]

    dk_1, dv_1 = finished([one], rims_1, sides_1, (0, 1), [three[0]], 2 * 10**9)
    sent, *sides_2 = return_sides([two, three], rims_2, [dk_1])
    send = grad_rows(rows_send, [*dq, dk_1, dv_1], scale, BF, after=[sent])
    received = exchanged(send, *first)
    keep = grad_rows(rows_keep, [*dq, dk_1, dv_1], scale, F32, after=[send])
    keep, send = add_split(keep, received)

    (dk_2,) = finished([two, three], rims_2, sides_2, (0,), [keep], FINISH_FLOPS)
    received = exchanged_stage(send, stages[0])
    keep, send = add_split(keep, received, [dk_2])
    received = exchanged_stage(send, stages[1])
    (dv_2,) = finished([two, three], rims_2, sides_2, (1,), [keep], 10**5)
    send_2 = grad_rows(rows_send, [dk_2, dv_2], scale, BF)
    received_2 = exchanged(send_2, *first)
    keep_2 = grad_rows(rows_keep, [dk_2, dv_2], scale, F32, after=[send_2])
    keep_2, send_2 = add_split(keep_2, received_2)
    received_2 = exchanged_stage(send_2, stages[0])
    grad_inputs, done = input_grads([*dq, dk_1, dk_2, dv_1, dv_2], w_qkv, [send_2])
    keep, send = add_split(keep, received, [done])
    for i in range(2, len(stages)):
        received = exchanged_stage(send, stages[i])
        keep_2, send_2 = add_split(keep_2, received_2, [keep])
        received_2 = exchanged_stage(send_2, stages[i - 1])
        if i + 1 < len(stages):
            keep, send = add_split(keep, received, [keep_2])
    keep_2, send_2 = add_split(keep_2, received_2)
    received_2 = exchanged_stage(send_2, stages[-1])
    groups = [(keep, received), (keep_2, received_2)]
    places = [
        [(0, width, 0), (width, half, width), (width + half, half, 2 * width)],
        [(0, half, width + half), (half, half, 2 * width + half)],
    ]
    grad_w = gather_sums(groups, places, 3 * width)
    return (grad_inputs.reshape(inputs.shape), grad_w)


def solution(mesh):
    in_specs = (P("dp", "lat", "lon", None), P("dp", "lat", "lon", None), P())
    out_specs = (P("dp", "lat", "lon", None), P(("dp", "lat", "lon"), None))
    return jax.shard_map(body, mesh=mesh, in_specs=in_specs, out_specs=out_specs, check_vma=False)
```

```python
import functools

import jax
import jax.numpy as jnp
import numpy as np
from jax import lax
from jax.experimental import pallas as pl
from jax.experimental.pallas import tpu as pltpu
from jax.sharding import PartitionSpec as P

HEADS = 16
WIN = 13
MARGIN = WIN // 2
TILE_R = 4
GROUP = 4
KEY_COLS = 32
HALO_COLS = 16
REGION_R = 16
PAD_R = 2
EDGE_R = MARGIN + PAD_R
NEG = -1e30
BF = jnp.bfloat16
F32 = jnp.float32
MIB = 1024 * 1024
FINISH_FLOPS = 9 * 10**9
LANES = 128
ATTENTION_MIB = 32

NT = (((1,), (1,)), ((), ()))
TN = (((0,), (0,)), ((), ()))
NN = (((1,), (0,)), ((), ()))


def dot(a, b, dims=NN):
    return lax.dot_general(a, b, dims, preferred_element_type=F32)


def region_top(tile, band_start, band_rows, total_rows):
    lowest = jnp.where(band_start == 0, TILE_R, 0)
    highest = jnp.where(band_start + band_rows == total_rows, band_rows - 2 * TILE_R, band_rows)
    return jnp.clip(tile * TILE_R, lowest, highest)


def mask_kernel(band_rows, band_cols, total_rows, start_ref, mask_ref):
    band_start = start_ref[0]
    tile = pl.program_id(0)
    shape = mask_ref.shape[1:]
    first = region_top(tile, band_start, band_rows, total_rows)
    key = lax.broadcasted_iota(jnp.int32, shape, 0)
    query = lax.broadcasted_iota(jnp.int32, shape, 1) & (TILE_R * band_cols - 1)
    key_row = band_start - MARGIN + first + (key >> (KEY_COLS.bit_length() - 1))
    place = key & (KEY_COLS - 1)
    query_row = band_start + tile * TILE_R + (query >> (band_cols.bit_length() - 1))
    query_col = query & (band_cols - 1)
    window = jnp.clip(query_row - MARGIN, 0, total_rows - WIN)
    row_inside = (key_row >= window) & (key_row < window + WIN)
    key_col = jnp.where(
        place < band_cols,
        place,
        jnp.where(place < band_cols + MARGIN, place - band_cols - MARGIN, place - MARGIN),
    )
    col_inside = (jnp.abs(key_col - query_col) <= MARGIN) & (place < band_cols + 2 * MARGIN)
    mask_ref[0] = jnp.where(row_inside & col_inside, 0.0, NEG).astype(BF)


def window_masks(start, band_rows, band_cols, total_rows):
    tiles = band_rows // TILE_R
    shape = (REGION_R * KEY_COLS, 2 * TILE_R * band_cols)
    return pl.pallas_call(
        functools.partial(mask_kernel, band_rows, band_cols, total_rows),
        grid=(tiles,),
        in_specs=[pl.BlockSpec(memory_space=pltpu.SMEM)],
        out_specs=pl.BlockSpec((1,) + shape, lambda t: (t, 0, 0)),
        out_shape=jax.ShapeDtypeStruct((tiles,) + shape, BF),
        cost_estimate=pl.CostEstimate(flops=10**7, bytes_accessed=2**21, transcendentals=0),
    )(start)


def attention_kernel(band_rows, band_cols, total_rows, head_width, extra, first, count, shift, *refs):
    (place_ref, mask_ref, take_ref, left_ref, right_ref, rows_a, rows_b, corners_a, corners_b,
     qkv_hbm, grad_hbm, w_hbm) = refs[:12]
    before_a, before_b = refs[12 : 12 + shift], refs[12 + shift : 12 + 2 * shift]
    (dq_all, out_a_all, out_b_all, mid_all, to_left_all, to_right_all,
     halo_ref, spot_ref, q_ref, k_ref, v_ref, dk_ref, dv_ref,
     side_ref, own_refs, w_refs, own_sem, w_sem) = refs[12 + extra :]
    band_start = place_ref[0]
    even = place_ref[1] == 0
    tiles = band_rows // TILE_R
    queries = TILE_R * band_cols
    keys = REGION_R * KEY_COLS
    width = GROUP * head_width
    lanes = GROUP * queries
    region_rows = band_rows + 2 * MARGIN
    side = MARGIN * band_rows
    edge = MARGIN * band_cols
    corner = 2 * MARGIN * EDGE_R
    at_above = 2 * side
    at_below = at_above + edge
    at_cl = at_below + edge
    at_cr = at_cl + corner
    halves = [(i, slice(i * LANES, (i + 1) * LANES)) for i in range(width // LANES)]

    step = pl.program_id(0)
    dq_ref, mid_ref, to_left_ref, to_right_ref = (
        ref.at[step] for ref in (dq_all, mid_all, to_left_all, to_right_all)
    )
    out_a, out_b = (ref.at[step + shift] for ref in (out_a_all, out_b_all))
    groups = HEADS // GROUP

    def copies(slot, parts):
        at = lambda part: pl.ds(pl.multiple_of((part * groups + first + slot) * width, width), width)
        for part, source, where, i in parts:
            target, sem = (w_refs, w_sem) if where else (own_refs, own_sem)
            yield pltpu.make_async_copy(source.at[:, at(part)], target.at[slot, i], sem.at[slot, i])

    for_k = ((1, w_hbm, 1, 0), (1, qkv_hbm, 0, 1))
    for_v = ((2, w_hbm, 1, 1), (2, qkv_hbm, 0, 2))
    for_q = ((0, qkv_hbm, 0, 0), (0, grad_hbm, 0, 3))

    @pl.when(step == 0)
    def _():
        for ref, kept in ((out_a_all, before_a), (out_b_all, before_b)):
            for i in range(shift):
                ref[i] = kept[0][i]
        for slot in range(count):
            for copy in copies(slot, for_k + for_v + for_q):
                copy.start()
        halo_ref[:side] = left_ref[...]
        halo_ref[side:at_above] = right_ref[...]
        for above, below, size, refs_ab in (
            (at_above, at_below, edge, (rows_a, rows_b)),
            (at_cl, at_cr, corner, (corners_a, corners_b)),
        ):
            for ref, at in zip(refs_ab, (jnp.where(even, below, above), jnp.where(even, above, below))):
                halo_ref[pl.ds(pl.multiple_of(at, 16), size), :] = ref[...]
        spot_ref[...] = jnp.zeros_like(spot_ref)

    def place(target, own, weights):
        fresh = dot(halo_ref[...], weights)
        for col in range(MARGIN):
            start = MARGIN * HALO_COLS + col
            for part, at in halves:
                spot_ref[part, pl.ds(start, band_rows, stride=HALO_COLS), :] = fresh[
                    col * band_rows : (col + 1) * band_rows, at
                ]
                spot_ref[part, pl.ds(start + MARGIN, band_rows, stride=HALO_COLS), :] = fresh[
                    side + col * band_rows : side + (col + 1) * band_rows, at
                ]
        for corner_at, skip, row in ((at_cl, PAD_R, 0), (at_cr, 0, MARGIN + band_rows)):
            for col in range(2 * MARGIN):
                base = corner_at + col * EDGE_R + skip
                spot = pl.ds(row * HALO_COLS + col, MARGIN, stride=HALO_COLS)
                for part, at in halves:
                    spot_ref[part, spot, :] = fresh[base : base + MARGIN, at]
        for row in range(region_rows):
            base = row * KEY_COLS
            inner = row - MARGIN
            if inner < 0:
                ours = fresh[at_above + row * band_cols : at_above + (row + 1) * band_cols].astype(BF)
            elif inner < band_rows:
                ours = own[inner * band_cols : (inner + 1) * band_cols, :]
            else:
                past = at_below + (inner - band_rows) * band_cols
                ours = fresh[past : past + band_cols].astype(BF)
            target[base : base + band_cols, :] = ours
            for part, at in halves:
                target[base + band_cols : base + KEY_COLS, at] = spot_ref[
                    part, row * HALO_COLS : (row + 1) * HALO_COLS, :
                ].astype(BF)

    grad_ref = own_refs.at[step, 3]
    for copy in copies(step, for_k + for_v + for_q):
        copy.wait()
    place(k_ref, own_refs.at[step, 1], w_refs[step, 0])
    place(v_ref, own_refs.at[step, 2], w_refs[step, 1])
    q_ref[...] = own_refs[step, 0] * BF(head_width**-0.5)
    dk_ref[...] = jnp.zeros_like(dk_ref)
    dv_ref[...] = jnp.zeros_like(dv_ref)

    def spread(rows):
        block = jnp.concatenate([rows] * GROUP, axis=0)
        head_row = lax.broadcasted_iota(jnp.int32, (lanes, width), 0) // queries
        head_col = lax.broadcasted_iota(jnp.int32, (lanes, width), 1) // head_width
        return jnp.where(head_row == head_col, block, jnp.zeros_like(block))

    def one_tile(tile, carry):
        first = region_top(tile, band_start, band_rows, total_rows)
        region = pl.ds(pl.multiple_of(first * KEY_COLS, TILE_R * KEY_COLS), keys)
        total = pl.ds(pl.multiple_of((first + PAD_R) * KEY_COLS, PAD_R * KEY_COLS), keys)
        mine = pl.ds(pl.multiple_of(tile * queries, queries), queries)
        q_wide = spread(q_ref[mine, :])
        g_wide = spread(grad_ref[mine, :])
        mask = mask_ref[tile].astype(F32)
        scores = dot(k_ref[region, :], q_wide, NT) + jnp.concatenate([mask, mask], axis=1)
        dots = dot(v_ref[region, :], g_wide, NT)
        exponent = jnp.exp(scores - jnp.max(scores, axis=0, keepdims=True))
        inverse = 1.0 / jnp.sum(exponent, axis=0, keepdims=True)
        delta = jnp.sum(exponent * dots, axis=0, keepdims=True) * inverse
        attn = exponent * inverse
        dscore = (attn * (dots - delta)).astype(BF)
        dv = dot(attn.astype(BF), g_wide)
        dk = dot(dscore, q_wide)
        for part, at in halves:
            dv_ref[part, total, :] += dv[:, at]
            dk_ref[part, total, :] += dk[:, at]
        dq_wide = dot(dscore, k_ref[region, :], TN)
        head_col = lax.broadcasted_iota(jnp.int32, (queries, width), 1) // head_width
        dq = jnp.zeros((queries, width), F32)
        for head in range(GROUP):
            dq = jnp.where(head_col == head, dq_wide[head * queries : (head + 1) * queries], dq)
        dq_ref[mine, :] = (dq * head_width**-0.5).astype(BF)
        return carry

    lax.fori_loop(0, tiles, one_tile, 0, unroll=8)

    middle = (PAD_R + MARGIN) * KEY_COLS
    below = (PAD_R + MARGIN + band_rows) * KEY_COLS
    for part, acc in enumerate((dk_ref, dv_ref)):
        for lane, at in halves:
            for out, own_at, side_at in (
                (out_a, jnp.where(even, below, PAD_R * KEY_COLS), jnp.where(even, below, 0)),
                (out_b, jnp.where(even, PAD_R * KEY_COLS, below), jnp.where(even, 0, below)),
            ):
                for row in range(MARGIN):
                    start = pl.multiple_of(own_at + row * KEY_COLS, KEY_COLS)
                    out[part, row * band_cols : (row + 1) * band_cols, at] = acc[
                        lane, pl.ds(start, band_cols), :
                    ].astype(BF)
                for pair in range(MARGIN):
                    here = slice(edge + pair * 2 * EDGE_R, edge + (pair + 1) * 2 * EDGE_R)
                    start = side_at + band_cols + 2 * pair
                    out[part, here, at] = jnp.concatenate(
                        [
                            acc[lane, pl.ds(start, EDGE_R, stride=KEY_COLS), :],
                            acc[lane, pl.ds(start + 1, EDGE_R, stride=KEY_COLS), :],
                        ],
                        axis=0,
                    ).astype(BF)
            for row in range(band_rows):
                base = middle + row * KEY_COLS
                mid_ref[part, row * band_cols : (row + 1) * band_cols, at] = acc[
                    lane, base : base + band_cols, :
                ].astype(BF)
            for row in range(band_rows):
                start = middle + row * KEY_COLS + band_cols
                side_ref[row * HALO_COLS : (row + 1) * HALO_COLS, at] = acc[
                    lane, start : start + HALO_COLS, :
                ].astype(BF)
        sides = dot(take_ref[...], side_ref[...]).astype(BF)
        to_left_ref[part] = sides[:side]
        to_right_ref[part] = sides[side:]


def attention_grads(first, count, place, masks, take, halo, qkv, grad_out, w_qkv, shape, before, after):
    band_rows, band_cols, total_rows = shape
    tokens, width = grad_out.shape
    head_width = width // HEADS
    block = GROUP * head_width
    region_tokens = (band_rows + 2 * MARGIN) * KEY_COLS
    total_tokens = (band_rows + 2 * MARGIN + 2 * PAD_R) * KEY_COLS
    side = MARGIN * band_rows
    edge = MARGIN * (band_cols + 2 * EDGE_R)
    corner = 2 * MARGIN * EDGE_R
    halo_tokens = 2 * (side + MARGIN * band_cols + corner)
    shift = before[0].shape[0] if before else 0
    vmem = pl.BlockSpec(memory_space=pltpu.VMEM)
    shapes = [
        (count, tokens, block),
        (count + shift, 2, edge, block),
        (count + shift, 2, edge, block),
        (count, 2, tokens, block),
        (count, 2, side, block),
        (count, 2, side, block),
    ]
    return pl.pallas_call(
        functools.partial(
            attention_kernel, band_rows, band_cols, total_rows, head_width,
            len(before) + len(after), first, count, shift,
        ),
        grid=(count,),
        in_specs=[pl.BlockSpec(memory_space=pltpu.SMEM)]
        + [vmem] * (2 + len(halo))
        + [pl.BlockSpec(memory_space=pltpu.HBM)] * 3
        + [vmem] * len(before)
        + [pl.BlockSpec(memory_space=pl.ANY)] * len(after),
        out_specs=[vmem] * len(shapes),
        out_shape=[jax.ShapeDtypeStruct(s, BF) for s in shapes],
        scratch_shapes=[
            pltpu.VMEM((halo_tokens, width), BF),
            pltpu.VMEM((block // LANES, (band_rows + 2 * MARGIN) * HALO_COLS, LANES), F32),
            pltpu.VMEM((tokens, block), BF),
            pltpu.VMEM((region_tokens, block), BF),
            pltpu.VMEM((region_tokens, block), BF),
            pltpu.VMEM((block // LANES, total_tokens, LANES), F32),
            pltpu.VMEM((block // LANES, total_tokens, LANES), F32),
            pltpu.VMEM((band_rows * HALO_COLS, block), BF),
            pltpu.VMEM((count, 4, tokens, block), BF),
            pltpu.VMEM((count, 2, width, block), BF),
            pltpu.SemaphoreType.DMA((count, 4)),
            pltpu.SemaphoreType.DMA((count, 2)),
        ],
        compiler_params=pltpu.CompilerParams(
            dimension_semantics=("arbitrary",), vmem_limit_bytes=ATTENTION_MIB * MIB
        ),
        cost_estimate=pl.CostEstimate(
            flops=count * 14 * 10**9, bytes_accessed=count * 8 * MIB, transcendentals=count * 10**6
        ),
    )(place, masks, take, *halo, qkv, grad_out, w_qkv, *before, *after)


def on_chip(kernel, out_shape, operands, after=(), scratch=(), flops=10**5, place=()):
    count = len(operands) + len(place)

    def run(*refs):
        kernel(*refs[:count], *refs[count + len(after) :])

    return pl.pallas_call(
        run,
        in_specs=[pl.BlockSpec(memory_space=pltpu.SMEM)] * len(place)
        + [pl.BlockSpec(memory_space=pltpu.VMEM)] * len(operands)
        + [pl.BlockSpec(memory_space=pl.ANY)] * len(after),
        out_specs=[pl.BlockSpec(memory_space=pltpu.VMEM)] * len(out_shape),
        out_shape=[jax.ShapeDtypeStruct(s, d) for s, d in out_shape],
        scratch_shapes=list(scratch),
        compiler_params=pltpu.CompilerParams(vmem_limit_bytes=24 * MIB),
        cost_estimate=pl.CostEstimate(flops=flops, bytes_accessed=10**4, transcendentals=0),
    )(*place, *operands, *after)


def lanes_of(width):
    return [(i, slice(i * LANES, (i + 1) * LANES)) for i in range(width // LANES)]


def project(own, w_qkv, after):
    tokens, width = own.shape
    columns = w_qkv.shape[1]
    block = 4 * LANES

    def kernel(own_ref, w_ref, *refs):
        refs[-1][...] = dot(own_ref[...], w_ref[...]).astype(BF)

    return pl.pallas_call(
        kernel,
        grid=(columns // block,),
        in_specs=[
            pl.BlockSpec((tokens, width), lambda g: (0, 0)),
            pl.BlockSpec((width, block), lambda g: (0, g)),
        ]
        + [pl.BlockSpec(memory_space=pl.ANY)] * len(after),
        out_specs=pl.BlockSpec((tokens, block), lambda g: (0, g)),
        out_shape=jax.ShapeDtypeStruct((tokens, columns), BF),
        compiler_params=pltpu.CompilerParams(vmem_limit_bytes=24 * MIB),
        cost_estimate=pl.CostEstimate(flops=10**9, bytes_accessed=MIB, transcendentals=0),
    )(own, w_qkv, *after)


def input_grads(columns, w_qkv, after):
    tokens = columns[0].shape[-2]
    width, total = w_qkv.shape
    count = len(columns)
    pieces = list(pieces_of(columns))
    steps = len(pieces) // 2

    def kernel(*refs):
        w_ref, (out_ref, done_ref, acc_ref, chunk_ref) = refs[count], refs[-4:]
        now = pl.program_id(0)
        for step in range(steps):

            @pl.when(now == step)
            def _():
                for half, where in enumerate(pieces[2 * step : 2 * step + 2]):
                    chunk_ref[:, half * 2 * LANES : (half + 1) * 2 * LANES] = piece(refs, *where)

        @pl.when(now == 0)
        def _():
            acc_ref[...] = jnp.zeros_like(acc_ref)

        acc_ref[...] += dot(chunk_ref[...], w_ref[...], NT)

        @pl.when(now == steps - 1)
        def _():
            out_ref[...] = acc_ref[...].astype(BF)
            done_ref[...] = jnp.zeros_like(done_ref)

    return pl.pallas_call(
        kernel,
        grid=(steps,),
        in_specs=[pl.BlockSpec(memory_space=pltpu.VMEM)] * count
        + [pl.BlockSpec((width, total // steps), lambda g: (0, g))]
        + [pl.BlockSpec(memory_space=pl.ANY)] * len(after),
        out_specs=[
            pl.BlockSpec((tokens, width), lambda g: (0, 0)),
            pl.BlockSpec((8, LANES), lambda g: (0, 0)),
        ],
        out_shape=[
            jax.ShapeDtypeStruct((tokens, width), BF),
            jax.ShapeDtypeStruct((8, LANES), F32),
        ],
        scratch_shapes=[pltpu.VMEM((tokens, width), F32), pltpu.VMEM((tokens, 4 * LANES), BF)],
        compiler_params=pltpu.CompilerParams(vmem_limit_bytes=24 * MIB),
        cost_estimate=pl.CostEstimate(flops=4 * 10**9, bytes_accessed=MIB, transcendentals=0),
    )(*columns, w_qkv, *after)


def row_blocks(place, own, orders, after):
    tokens, width = own.shape
    devices = len(orders[0])
    size = width // devices
    step = max(1, 16 // size)

    def kernel(place_ref, own_ref, low_ref, high_ref, wide_ref):
        for at in range(0, width, 2 * LANES):
            wide_ref[at : at + 2 * LANES, :] = own_ref[:, at : at + 2 * LANES].astype(F32).T
        even = place_ref[1] == 0
        me = place_ref[2]
        for j in range(0, devices, step):
            rows = []
            for k in range(j, j + step):
                owner = me ^ jnp.where(even, int(orders[0][k]), int(orders[1][k]))
                rows.append(wide_ref[pl.ds(pl.multiple_of(owner * size, size), size), :])
            half, base = divmod(j * size, width // 2)
            block = rows[0] if step == 1 else jnp.concatenate(rows, axis=0)
            (low_ref, high_ref)[half][base : base + step * size, :] = block.astype(BF)

    out = ((width // 2, tokens), BF)
    scratch = [pltpu.VMEM((width, tokens), F32)]
    return on_chip(kernel, [out, out], [own], after=after, scratch=scratch, place=[place])


def pack_sides(own, band_rows, band_cols):
    tokens, width = own.shape

    def kernel(own_ref, last_ref, first_ref, wide_ref):
        for lane, at in lanes_of(width):
            wide_ref[lane] = own_ref[:, at].astype(F32)
            for col in range(MARGIN):
                here = slice(col * band_rows, (col + 1) * band_rows)
                last = pl.ds(band_cols - MARGIN + col, band_rows, stride=band_cols)
                last_ref[here, at] = wide_ref[lane, last, :].astype(BF)
                first = pl.ds(col, band_rows, stride=band_cols)
                first_ref[here, at] = wide_ref[lane, first, :].astype(BF)

    out = ((MARGIN * band_rows, width), BF)
    scratch = [pltpu.VMEM((width // LANES, tokens, LANES), F32)]
    return on_chip(kernel, [out, out], [own], scratch=scratch)


def pack_rows(place, own, band_cols, after):
    tokens, width = own.shape
    edge = MARGIN * band_cols

    def kernel(place_ref, own_ref, out_a, out_b):
        even = place_ref[1] == 0
        last, first = own_ref[tokens - edge :, :], own_ref[:edge, :]
        out_a[...] = jnp.where(even, last, first)
        out_b[...] = jnp.where(even, first, last)

    out = ((edge, width), BF)
    return on_chip(kernel, [out, out], [own], after=after, place=[place])


def pack_corners(place, left, right, band_rows, after):
    width = left.shape[1]

    def kernel(place_ref, left_ref, right_ref, out_a, out_b):
        even = place_ref[1] == 0
        for side, side_ref in enumerate((left_ref, right_ref)):
            for col in range(0, MARGIN, 2):
                base = (side * MARGIN + col) * EDGE_R
                last, first = (
                    jnp.concatenate(
                        [
                            side_ref[at : at + EDGE_R, :].astype(F32)
                            for at in (start, start + band_rows)
                        ]
                    )
                    for start in ((col + 1) * band_rows - EDGE_R, col * band_rows)
                )
                here = slice(base, base + 2 * EDGE_R)
                out_a[here, :] = jnp.where(even, last, first).astype(BF)
                out_b[here, :] = jnp.where(even, first, last).astype(BF)

    out = ((2 * MARGIN * EDGE_R, width), BF)
    return on_chip(kernel, [out, out], [left, right], after=after, place=[place])


def selectors(band_rows, band_cols, after):
    side = MARGIN * band_rows

    def kernel(take_ref, put_ref):
        sent = lax.broadcasted_iota(jnp.int32, take_ref.shape, 0)
        held = lax.broadcasted_iota(jnp.int32, take_ref.shape, 1)
        same_row = (sent & (band_rows - 1)) == (held >> (HALO_COLS.bit_length() - 1))
        same_col = (sent >> (band_rows.bit_length() - 1)) == (held & (HALO_COLS - 1))
        take_ref[...] = jnp.where(same_row & same_col, 1.0, 0.0).astype(BF)
        held = lax.broadcasted_iota(jnp.int32, put_ref.shape, 0)
        sent = lax.broadcasted_iota(jnp.int32, put_ref.shape, 1)
        same_row = (sent & (band_rows - 1)) == (held >> (band_cols.bit_length() - 1))
        col = sent >> (band_rows.bit_length() - 1)
        col = jnp.where(col < MARGIN, col, col + band_cols - 2 * MARGIN)
        same_col = col == (held & (band_cols - 1))
        put_ref[...] = jnp.where(same_row & same_col, 1.0, 0.0).astype(BF)

    out = [((2 * side, band_rows * HALO_COLS), BF), ((band_rows * band_cols, 2 * side), BF)]
    return on_chip(kernel, out, [], after)


def merge_sides(place, lefts, rights, rim_a, rim_b, band_rows, band_cols, after=()):
    edge = MARGIN * band_cols
    calls = len(lefts)
    slots = rim_a.shape[0]
    each = slots // calls

    def kernel(place_ref, *refs):
        sides = refs[:calls], refs[calls : 2 * calls]
        a_ref, b_ref, *outs = refs[2 * calls :]
        even = place_ref[1] == 0
        for slot in range(slots):
            for part in range(2):
                for col in range(2 * MARGIN):
                    source = sides[col // MARGIN][slot // each]
                    base = (col % MARGIN) * band_rows
                    pair = slice(edge + (col // 2) * 2 * EDGE_R, edge + (col // 2 + 1) * 2 * EDGE_R)
                    odd = slice((col % 2) * EDGE_R, (col % 2 + 1) * EDGE_R)
                    rows = source[slot % each, part, base : base + band_rows, :].astype(F32)
                    from_a, from_b = (
                        ref[slot, part, pair, :].astype(F32)[odd] for ref in (a_ref, b_ref)
                    )
                    first = rows[:EDGE_R] + jnp.where(even, from_b, from_a)
                    last = rows[band_rows - EDGE_R :] + jnp.where(even, from_a, from_b)
                    outs[col // MARGIN][slot, part, base : base + band_rows, :] = jnp.concatenate(
                        [first, rows[EDGE_R : band_rows - EDGE_R], last], axis=0
                    ).astype(BF)

    out = ((slots,) + lefts[0].shape[1:], BF)
    return on_chip(kernel, [out, out], [*lefts, *rights, rim_a, rim_b], after, place=[place])


def finish(place, mids, rim_a, rim_b, left, right, put, parts, band_rows, band_cols, after, flops):
    calls = len(mids)
    slots, _, _, block = rim_a.shape
    each = slots // calls
    edge = MARGIN * band_cols
    tokens = band_rows * band_cols

    def kernel(place_ref, *refs):
        a_ref, b_ref, left_ref, right_ref, put_ref, *outs, acc_ref = refs[calls:]
        even = place_ref[1] == 0
        for out_ref, part in zip(outs, parts):
            for slot in range(slots):
                sides = jnp.concatenate([left_ref[slot, part], right_ref[slot, part]], axis=0)
                acc_ref[...] = dot(put_ref[...], sides) + refs[slot // each][
                    slot % each, part
                ].astype(F32)
                from_a, from_b = (r[slot, part, :edge, :].astype(F32) for r in (a_ref, b_ref))
                acc_ref[:edge, :] += jnp.where(even, from_b, from_a)
                acc_ref[tokens - edge :, :] += jnp.where(even, from_a, from_b)
                out_ref[:, slot * block : (slot + 1) * block] = acc_ref[...].astype(BF)

    out = [((tokens, slots * block), BF)] * len(parts)
    scratch = [pltpu.VMEM((tokens, block), F32)]
    operands = [*mids, rim_a, rim_b, left, right, put]
    return on_chip(kernel, out, operands, after, scratch, flops, [place])


def pieces_of(arrays):
    for i, array in enumerate(arrays):
        slots = range(array.shape[0]) if array.ndim == 3 else [None]
        for slot in slots:
            for start in range(0, array.shape[-1], 2 * LANES):
                yield i, slot, start


def piece(refs, i, slot, start):
    here = slice(start, start + 2 * LANES)
    return refs[i][:, here] if slot is None else refs[i][slot, :, here]


def grad_rows(rows, columns, scale, kind, after=()):
    features, count = rows.shape[0], len(columns)
    pieces = list(pieces_of(columns))

    def kernel(rows_ref, *refs):
        for at, where in enumerate(pieces):
            part = dot(rows_ref[...], piece(refs, *where))
            here = slice(at * 2 * LANES, (at + 1) * 2 * LANES)
            refs[count][:, here] = (part * scale).astype(kind)

    out = [((features, len(pieces) * 2 * LANES), kind)]
    return on_chip(kernel, out, [rows, *columns], after)[0]


def add_split(keep, received, after=()):
    half, columns = keep.shape[0] // 2, keep.shape[1]

    def kernel(keep_ref, received_ref, sums_ref, send_ref):
        sums_ref[...] = keep_ref[:half, :] + received_ref[:half, :].astype(F32)
        send_ref[...] = (keep_ref[half:, :] + received_ref[half:, :].astype(F32)).astype(BF)

    return on_chip(kernel, [((half, columns), F32), ((half, columns), BF)], [keep, received], after)


def gather_sums(groups, places, width):
    flat = [array for group in groups for array in group]

    def kernel(*refs):
        out_ref = refs[-1]
        for i, moves in enumerate(places):
            keep_ref, received_ref = refs[2 * i : 2 * i + 2]
            for source, size, target in moves:
                here = slice(source, source + size)
                total = keep_ref[:, here] + received_ref[:, here].astype(F32)
                out_ref[:, target : target + size] = total

    return on_chip(kernel, [((flat[0].shape[0], width), F32)], flat)[0]


def shifted(array, axis, by, wrap):
    size = lax.axis_size(axis)
    route = [(i, (i + by) % size) for i in range(size) if wrap or 0 <= i + by < size]
    return lax.ppermute(array, axis, route)


def swapped(array_a, array_b, axis):
    size = lax.axis_size(axis)
    pairs = [(i, i + 1) for i in range(size - 1)]
    route = lambda chosen: chosen + [(j, i) for i, j in chosen]
    return [
        lax.ppermute(array, axis, route(pairs[offset::2]))
        for array, offset in ((array_a, 0), (array_b, 1))
    ]


def exchanged(array, axis, flip):
    return lax.ppermute(array, axis, [(i, i ^ flip) for i in range(lax.axis_size(axis))])


def bits_of(axis):
    return [(axis, 1 << b) for b in range((lax.axis_size(axis) - 1).bit_length())]


def reduce_stages():
    first, *lat_bits = bits_of("lat")
    bits = bits_of("dp") + lat_bits
    return first, list(zip(bits, reversed(bits))) + [(bit, bit) for bit in bits_of("lon")]


def feature_orders(first, stages):
    n_lon, n_lat = lax.axis_size("lon"), lax.axis_size("lat")
    unit = {"lon": 1, "lat": n_lon, "dp": n_lon * n_lat}
    lower = []
    for kind in range(2):
        order = np.zeros(1, np.int64)
        for stage in reversed(stages):
            axis, bit = stage[kind]
            order = np.concatenate([order, order + unit[axis] * bit])
        lower.append(order)
    flip = unit[first[0]] * first[1]
    return [np.concatenate([lower[kind], lower[1 - kind] ^ flip]) for kind in range(2)]


def exchanged_stage(array, stage):
    if stage[0] == stage[1]:
        return exchanged(array, *stage[0])
    n_lat, n_dp = lax.axis_size("lat"), lax.axis_size("dp")
    route = []
    for i in range(n_dp * n_lat):
        axis, bit = stage[i % n_lat % 2]
        route.append((i, i ^ (bit * n_lat if axis == "dp" else bit)))
    return lax.ppermute(array, ("dp", "lat"), route)


def body(inputs, grad_out, w_qkv):
    _, band_rows, band_cols, width = inputs.shape
    n_lat, n_lon, n_dp = lax.axis_size("lat"), lax.axis_size("lon"), lax.axis_size("dp")
    band_start = lax.axis_index("lat") * band_rows
    total_rows = band_rows * n_lat
    tokens = band_rows * band_cols
    slots = HEADS // GROUP // 2
    shape = (band_rows, band_cols, total_rows)
    own = inputs.reshape(tokens, width)
    flat_grad = grad_out.reshape(tokens, width)

    last_cols, first_cols = pack_sides(own, band_rows, band_cols)
    left = shifted(last_cols, "lon", 1, True)
    right = shifted(first_cols, "lon", -1, True)
    me = (lax.axis_index("dp") * n_lat + lax.axis_index("lat")) * n_lon + lax.axis_index("lon")
    start = jnp.stack([band_start, lax.axis_index("lat") % 2, me])
    rim_rows = swapped(*pack_rows(start, own, band_cols, [last_cols]), "lat")

    take, put = selectors(band_rows, band_cols, [last_cols])
    masks = window_masks(start, band_rows, band_cols, total_rows)
    qkv = project(own, w_qkv, [last_cols])
    first, stages = reduce_stages()
    half = width // 2
    rows_keep, rows_send = row_blocks(start, own, feature_orders(first, stages), [last_cols])
    corners = pack_corners(start, left, right, band_rows, [masks, qkv, rows_keep, rows_send])
    halo = (left, right, *rim_rows, *swapped(*corners, "lat"))
    scale = float(tokens * n_dp * n_lat * n_lon) ** -0.5

    attend = lambda first, count, before, after: attention_grads(
        first, count, start, masks, take, halo, qkv, flat_grad, w_qkv, shape, before, after
    )

    def return_sides(calls, rims, after):
        to_left, to_right = merge_sides(
            start, [c[4] for c in calls], [c[5] for c in calls], *rims, band_rows, band_cols, after
        )
        from_right = shifted(to_left, "lon", -1, True)
        from_left = shifted(to_right, "lon", 1, True)
        return to_left, from_left, from_right

    def finished(calls, rims, sides, parts, after, flops):
        mids = [c[3] for c in calls]
        return finish(start, mids, *rims, *sides, put, parts, band_rows, band_cols, after, flops)

    groups = HEADS // GROUP
    one = attend(0, slots, [], [])
    rims_1 = swapped(one[1], one[2], "lat")
    two = attend(slots, groups - slots - 1, [], [one[0]])
    sent, *sides_1 = return_sides([one], rims_1, [two[0]])
    three = attend(groups - 1, 1, [two[1], two[2]], [sent])
    rims_2 = swapped(three[1], three[2], "lat")
    dq = [one[0], two[0], three[0]]

    dk_1, dv_1 = finished([one], rims_1, sides_1, (0, 1), [three[0]], 2 * 10**9)
    sent, *sides_2 = return_sides([two, three], rims_2, [dk_1])
    send = grad_rows(rows_send, [*dq, dk_1, dv_1], scale, BF, after=[sent])
    received = exchanged(send, *first)
    keep = grad_rows(rows_keep, [*dq, dk_1, dv_1], scale, F32, after=[send])
    keep, send = add_split(keep, received)

    (dk_2,) = finished([two, three], rims_2, sides_2, (0,), [keep], FINISH_FLOPS)
    received = exchanged_stage(send, stages[0])
    keep, send = add_split(keep, received, [dk_2])
    received = exchanged_stage(send, stages[1])
    (dv_2,) = finished([two, three], rims_2, sides_2, (1,), [keep], 10**5)
    send_2 = grad_rows(rows_send, [dk_2, dv_2], scale, BF)
    received_2 = exchanged(send_2, *first)
    keep_2 = grad_rows(rows_keep, [dk_2, dv_2], scale, F32, after=[send_2])
    keep_2, send_2 = add_split(keep_2, received_2)
    received_2 = exchanged_stage(send_2, stages[0])
    grad_inputs, done = input_grads([*dq, dk_1, dk_2, dv_1, dv_2], w_qkv, [send_2])
    keep, send = add_split(keep, received, [done])
    for i in range(2, len(stages)):
        received = exchanged_stage(send, stages[i])
        keep_2, send_2 = add_split(keep_2, received_2, [keep])
        received_2 = exchanged_stage(send_2, stages[i - 1])
        if i + 1 < len(stages):
            keep, send = add_split(keep, received, [keep_2])
    keep_2, send_2 = add_split(keep_2, received_2)
    received_2 = exchanged_stage(send_2, stages[-1])
    groups = [(keep, received), (keep_2, received_2)]
    places = [
        [(0, width, 0), (width, half, width), (width + half, half, 2 * width)],
        [(0, half, width + half), (half, half, 2 * width + half)],
    ]
    grad_w = gather_sums(groups, places, 3 * width)
    return (grad_inputs.reshape(inputs.shape), grad_w)


def solution(mesh):
    in_specs = (P("dp", "lat", "lon", None), P("dp", "lat", "lon", None), P())
    out_specs = (P("dp", "lat", "lon", None), P(("dp", "lat", "lon"), None))
    return jax.shard_map(body, mesh=mesh, in_specs=in_specs, out_specs=out_specs, check_vma=False)
```

```python
import functools

import jax
import jax.numpy as jnp
import numpy as np
from jax import lax
from jax.experimental import pallas as pl
from jax.experimental.pallas import tpu as pltpu
from jax.sharding import PartitionSpec as P

HEADS = 16
WIN = 13
MARGIN = WIN // 2
TILE_R = 4
GROUP = 4
KEY_COLS = 32
HALO_COLS = 16
REGION_R = 16
PAD_R = 2
EDGE_R = MARGIN + PAD_R
NEG = -1e30
BF = jnp.bfloat16
F32 = jnp.float32
MIB = 1024 * 1024
FINISH_FLOPS = 9 * 10**9
LANES = 128
ATTENTION_MIB = 32

NT = (((1,), (1,)), ((), ()))
TN = (((0,), (0,)), ((), ()))
NN = (((1,), (0,)), ((), ()))


def dot(a, b, dims=NN):
    return lax.dot_general(a, b, dims, preferred_element_type=F32)


def region_top(tile, band_start, band_rows, total_rows):
    lowest = jnp.where(band_start == 0, TILE_R, 0)
    highest = jnp.where(band_start + band_rows == total_rows, band_rows - 2 * TILE_R, band_rows)
    return jnp.clip(tile * TILE_R, lowest, highest)


def mask_kernel(band_rows, band_cols, total_rows, start_ref, mask_ref):
    band_start = start_ref[0]
    tile = pl.program_id(0)
    shape = mask_ref.shape[1:]
    first = region_top(tile, band_start, band_rows, total_rows)
    key = lax.broadcasted_iota(jnp.int32, shape, 0)
    query = lax.broadcasted_iota(jnp.int32, shape, 1) & (TILE_R * band_cols - 1)
    key_row = band_start - MARGIN + first + (key >> (KEY_COLS.bit_length() - 1))
    place = key & (KEY_COLS - 1)
    query_row = band_start + tile * TILE_R + (query >> (band_cols.bit_length() - 1))
    query_col = query & (band_cols - 1)
    window = jnp.clip(query_row - MARGIN, 0, total_rows - WIN)
    row_inside = (key_row >= window) & (key_row < window + WIN)
    key_col = jnp.where(
        place < band_cols,
        place,
        jnp.where(place < band_cols + MARGIN, place - band_cols - MARGIN, place - MARGIN),
    )
    col_inside = (jnp.abs(key_col - query_col) <= MARGIN) & (place < band_cols + 2 * MARGIN)
    mask_ref[0] = jnp.where(row_inside & col_inside, 0.0, NEG).astype(BF)


def window_masks(start, band_rows, band_cols, total_rows):
    tiles = band_rows // TILE_R
    shape = (REGION_R * KEY_COLS, 2 * TILE_R * band_cols)
    return pl.pallas_call(
        functools.partial(mask_kernel, band_rows, band_cols, total_rows),
        grid=(tiles,),
        in_specs=[pl.BlockSpec(memory_space=pltpu.SMEM)],
        out_specs=pl.BlockSpec((1,) + shape, lambda t: (t, 0, 0)),
        out_shape=jax.ShapeDtypeStruct((tiles,) + shape, BF),
        cost_estimate=pl.CostEstimate(flops=10**7, bytes_accessed=2**21, transcendentals=0),
    )(start)


def attention_kernel(band_rows, band_cols, total_rows, head_width, extra, first, count, shift, *refs):
    (place_ref, mask_ref, take_ref, left_ref, right_ref, rows_a, rows_b, corners_a, corners_b,
     qkv_hbm, grad_hbm, w_hbm) = refs[:12]
    before_a, before_b = refs[12 : 12 + shift], refs[12 + shift : 12 + 2 * shift]
    (dq_all, out_a_all, out_b_all, mid_all, to_left_all, to_right_all,
     halo_ref, spot_ref, q_ref, k_ref, v_ref, dk_ref, dv_ref,
     side_ref, own_refs, w_refs, own_sem, w_sem) = refs[12 + extra :]
    band_start = place_ref[0]
    even = place_ref[1] == 0
    tiles = band_rows // TILE_R
    queries = TILE_R * band_cols
    keys = REGION_R * KEY_COLS
    width = GROUP * head_width
    lanes = GROUP * queries
    region_rows = band_rows + 2 * MARGIN
    side = MARGIN * band_rows
    edge = MARGIN * band_cols
    corner = 2 * MARGIN * EDGE_R
    at_above = 2 * side
    at_below = at_above + edge
    at_cl = at_below + edge
    at_cr = at_cl + corner
    halves = [(i, slice(i * LANES, (i + 1) * LANES)) for i in range(width // LANES)]

    step = pl.program_id(0)
    dq_ref, mid_ref, to_left_ref, to_right_ref = (
        ref.at[step] for ref in (dq_all, mid_all, to_left_all, to_right_all)
    )
    out_a, out_b = (ref.at[step + shift] for ref in (out_a_all, out_b_all))
    groups = HEADS // GROUP

    def copies(slot, parts):
        at = lambda part: pl.ds(pl.multiple_of((part * groups + first + slot) * width, width), width)
        for part, source, where, i in parts:
            target, sem = (w_refs, w_sem) if where else (own_refs, own_sem)
            yield pltpu.make_async_copy(source.at[:, at(part)], target.at[slot, i], sem.at[slot, i])

    for_k = ((1, w_hbm, 1, 0), (1, qkv_hbm, 0, 1))
    for_v = ((2, w_hbm, 1, 1), (2, qkv_hbm, 0, 2))
    for_q = ((0, qkv_hbm, 0, 0), (0, grad_hbm, 0, 3))

    @pl.when(step == 0)
    def _():
        for ref, kept in ((out_a_all, before_a), (out_b_all, before_b)):
            for i in range(shift):
                ref[i] = kept[0][i]
        for slot in range(count):
            for copy in copies(slot, for_k + for_v + for_q):
                copy.start()
        halo_ref[:side] = left_ref[...]
        halo_ref[side:at_above] = right_ref[...]
        for above, below, size, refs_ab in (
            (at_above, at_below, edge, (rows_a, rows_b)),
            (at_cl, at_cr, corner, (corners_a, corners_b)),
        ):
            for ref, at in zip(refs_ab, (jnp.where(even, below, above), jnp.where(even, above, below))):
                halo_ref[pl.ds(pl.multiple_of(at, 16), size), :] = ref[...]
        spot_ref[...] = jnp.zeros_like(spot_ref)

    def place(target, own, weights):
        fresh = dot(halo_ref[...], weights)
        for col in range(MARGIN):
            start = MARGIN * HALO_COLS + col
            for part, at in halves:
                spot_ref[part, pl.ds(start, band_rows, stride=HALO_COLS), :] = fresh[
                    col * band_rows : (col + 1) * band_rows, at
                ]
                spot_ref[part, pl.ds(start + MARGIN, band_rows, stride=HALO_COLS), :] = fresh[
                    side + col * band_rows : side + (col + 1) * band_rows, at
                ]
        for corner_at, skip, row in ((at_cl, PAD_R, 0), (at_cr, 0, MARGIN + band_rows)):
            for col in range(2 * MARGIN):
                base = corner_at + col * EDGE_R + skip
                spot = pl.ds(row * HALO_COLS + col, MARGIN, stride=HALO_COLS)
                for part, at in halves:
                    spot_ref[part, spot, :] = fresh[base : base + MARGIN, at]
        for row in range(region_rows):
            base = row * KEY_COLS
            inner = row - MARGIN
            if inner < 0:
                ours = fresh[at_above + row * band_cols : at_above + (row + 1) * band_cols].astype(BF)
            elif inner < band_rows:
                ours = own[inner * band_cols : (inner + 1) * band_cols, :]
            else:
                past = at_below + (inner - band_rows) * band_cols
                ours = fresh[past : past + band_cols].astype(BF)
            target[base : base + band_cols, :] = ours
            for part, at in halves:
                target[base + band_cols : base + KEY_COLS, at] = spot_ref[
                    part, row * HALO_COLS : (row + 1) * HALO_COLS, :
                ].astype(BF)

    grad_ref = own_refs.at[step, 3]
    for copy in copies(step, for_k + for_v + for_q):
        copy.wait()
    place(k_ref, own_refs.at[step, 1], w_refs[step, 0])
    place(v_ref, own_refs.at[step, 2], w_refs[step, 1])
    q_ref[...] = own_refs[step, 0] * BF(head_width**-0.5)
    dk_ref[...] = jnp.zeros_like(dk_ref)
    dv_ref[...] = jnp.zeros_like(dv_ref)

    def spread(rows):
        block = jnp.concatenate([rows] * GROUP, axis=0)
        head_row = lax.broadcasted_iota(jnp.int32, (lanes, width), 0) // queries
        head_col = lax.broadcasted_iota(jnp.int32, (lanes, width), 1) // head_width
        return jnp.where(head_row == head_col, block, jnp.zeros_like(block))

    def one_tile(tile, carry):
        first = region_top(tile, band_start, band_rows, total_rows)
        region = pl.ds(pl.multiple_of(first * KEY_COLS, TILE_R * KEY_COLS), keys)
        total = pl.ds(pl.multiple_of((first + PAD_R) * KEY_COLS, PAD_R * KEY_COLS), keys)
        mine = pl.ds(pl.multiple_of(tile * queries, queries), queries)
        q_wide = spread(q_ref[mine, :])
        g_wide = spread(grad_ref[mine, :])
        mask = mask_ref[tile].astype(F32)
        scores = dot(k_ref[region, :], q_wide, NT) + jnp.concatenate([mask, mask], axis=1)
        dots = dot(v_ref[region, :], g_wide, NT)
        exponent = jnp.exp(scores - jnp.max(scores, axis=0, keepdims=True))
        inverse = 1.0 / jnp.sum(exponent, axis=0, keepdims=True)
        delta = jnp.sum(exponent * dots, axis=0, keepdims=True) * inverse
        attn = exponent * inverse
        dscore = (attn * (dots - delta)).astype(BF)
        dv = dot(attn.astype(BF), g_wide)
        dk = dot(dscore, q_wide)
        for part, at in halves:
            dv_ref[part, total, :] += dv[:, at]
            dk_ref[part, total, :] += dk[:, at]
        dq_wide = dot(dscore, k_ref[region, :], TN)
        head_col = lax.broadcasted_iota(jnp.int32, (queries, width), 1) // head_width
        dq = jnp.zeros((queries, width), F32)
        for head in range(GROUP):
            dq = jnp.where(head_col == head, dq_wide[head * queries : (head + 1) * queries], dq)
        dq_ref[mine, :] = (dq * head_width**-0.5).astype(BF)
        return carry

    lax.fori_loop(0, tiles, one_tile, 0, unroll=8)

    middle = (PAD_R + MARGIN) * KEY_COLS
    below = (PAD_R + MARGIN + band_rows) * KEY_COLS
    for part, acc in enumerate((dk_ref, dv_ref)):
        for lane, at in halves:
            for out, own_at, side_at in (
                (out_a, jnp.where(even, below, PAD_R * KEY_COLS), jnp.where(even, below, 0)),
                (out_b, jnp.where(even, PAD_R * KEY_COLS, below), jnp.where(even, 0, below)),
            ):
                for row in range(MARGIN):
                    start = pl.multiple_of(own_at + row * KEY_COLS, KEY_COLS)
                    out[part, row * band_cols : (row + 1) * band_cols, at] = acc[
                        lane, pl.ds(start, band_cols), :
                    ].astype(BF)
                for pair in range(MARGIN):
                    here = slice(edge + pair * 2 * EDGE_R, edge + (pair + 1) * 2 * EDGE_R)
                    start = side_at + band_cols + 2 * pair
                    out[part, here, at] = jnp.concatenate(
                        [
                            acc[lane, pl.ds(start, EDGE_R, stride=KEY_COLS), :],
                            acc[lane, pl.ds(start + 1, EDGE_R, stride=KEY_COLS), :],
                        ],
                        axis=0,
                    ).astype(BF)
            for row in range(band_rows):
                base = middle + row * KEY_COLS
                mid_ref[part, row * band_cols : (row + 1) * band_cols, at] = acc[
                    lane, base : base + band_cols, :
                ].astype(BF)
            for row in range(band_rows):
                start = middle + row * KEY_COLS + band_cols
                side_ref[row * HALO_COLS : (row + 1) * HALO_COLS, at] = acc[
                    lane, start : start + HALO_COLS, :
                ].astype(BF)
        sides = dot(take_ref[...], side_ref[...]).astype(BF)
        to_left_ref[part] = sides[:side]
        to_right_ref[part] = sides[side:]


def attention_grads(first, count, place, masks, take, halo, qkv, grad_out, w_qkv, shape, before, after):
    band_rows, band_cols, total_rows = shape
    tokens, width = grad_out.shape
    head_width = width // HEADS
    block = GROUP * head_width
    region_tokens = (band_rows + 2 * MARGIN) * KEY_COLS
    total_tokens = (band_rows + 2 * MARGIN + 2 * PAD_R) * KEY_COLS
    side = MARGIN * band_rows
    edge = MARGIN * (band_cols + 2 * EDGE_R)
    corner = 2 * MARGIN * EDGE_R
    halo_tokens = 2 * (side + MARGIN * band_cols + corner)
    shift = before[0].shape[0] if before else 0
    vmem = pl.BlockSpec(memory_space=pltpu.VMEM)
    shapes = [
        (count, tokens, block),
        (count + shift, 2, edge, block),
        (count + shift, 2, edge, block),
        (count, 2, tokens, block),
        (count, 2, side, block),
        (count, 2, side, block),
    ]
    return pl.pallas_call(
        functools.partial(
            attention_kernel, band_rows, band_cols, total_rows, head_width,
            len(before) + len(after), first, count, shift,
        ),
        grid=(count,),
        in_specs=[pl.BlockSpec(memory_space=pltpu.SMEM)]
        + [vmem] * (2 + len(halo))
        + [pl.BlockSpec(memory_space=pltpu.HBM)] * 3
        + [vmem] * len(before)
        + [pl.BlockSpec(memory_space=pl.ANY)] * len(after),
        out_specs=[vmem] * len(shapes),
        out_shape=[jax.ShapeDtypeStruct(s, BF) for s in shapes],
        scratch_shapes=[
            pltpu.VMEM((halo_tokens, width), BF),
            pltpu.VMEM((block // LANES, (band_rows + 2 * MARGIN) * HALO_COLS, LANES), F32),
            pltpu.VMEM((tokens, block), BF),
            pltpu.VMEM((region_tokens, block), BF),
            pltpu.VMEM((region_tokens, block), BF),
            pltpu.VMEM((block // LANES, total_tokens, LANES), F32),
            pltpu.VMEM((block // LANES, total_tokens, LANES), F32),
            pltpu.VMEM((band_rows * HALO_COLS, block), BF),
            pltpu.VMEM((count, 4, tokens, block), BF),
            pltpu.VMEM((count, 2, width, block), BF),
            pltpu.SemaphoreType.DMA((count, 4)),
            pltpu.SemaphoreType.DMA((count, 2)),
        ],
        compiler_params=pltpu.CompilerParams(
            dimension_semantics=("arbitrary",), vmem_limit_bytes=ATTENTION_MIB * MIB
        ),
        cost_estimate=pl.CostEstimate(
            flops=count * 14 * 10**9, bytes_accessed=count * 8 * MIB, transcendentals=count * 10**6
        ),
    )(place, masks, take, *halo, qkv, grad_out, w_qkv, *before, *after)


def on_chip(kernel, out_shape, operands, after=(), scratch=(), flops=10**5, place=()):
    count = len(operands) + len(place)

    def run(*refs):
        kernel(*refs[:count], *refs[count + len(after) :])

    return pl.pallas_call(
        run,
        in_specs=[pl.BlockSpec(memory_space=pltpu.SMEM)] * len(place)
        + [pl.BlockSpec(memory_space=pltpu.VMEM)] * len(operands)
        + [pl.BlockSpec(memory_space=pl.ANY)] * len(after),
        out_specs=[pl.BlockSpec(memory_space=pltpu.VMEM)] * len(out_shape),
        out_shape=[jax.ShapeDtypeStruct(s, d) for s, d in out_shape],
        scratch_shapes=list(scratch),
        compiler_params=pltpu.CompilerParams(vmem_limit_bytes=24 * MIB),
        cost_estimate=pl.CostEstimate(flops=flops, bytes_accessed=10**4, transcendentals=0),
    )(*place, *operands, *after)


def lanes_of(width):
    return [(i, slice(i * LANES, (i + 1) * LANES)) for i in range(width // LANES)]


def project(own, w_qkv, after):
    tokens, width = own.shape
    columns = w_qkv.shape[1]
    block = 4 * LANES

    def kernel(own_ref, w_ref, *refs):
        refs[-1][...] = dot(own_ref[...], w_ref[...]).astype(BF)

    return pl.pallas_call(
        kernel,
        grid=(columns // block,),
        in_specs=[
            pl.BlockSpec((tokens, width), lambda g: (0, 0)),
            pl.BlockSpec((width, block), lambda g: (0, g)),
        ]
        + [pl.BlockSpec(memory_space=pl.ANY)] * len(after),
        out_specs=pl.BlockSpec((tokens, block), lambda g: (0, g)),
        out_shape=jax.ShapeDtypeStruct((tokens, columns), BF),
        compiler_params=pltpu.CompilerParams(vmem_limit_bytes=24 * MIB),
        cost_estimate=pl.CostEstimate(flops=10**9, bytes_accessed=MIB, transcendentals=0),
    )(own, w_qkv, *after)


def input_grads(columns, w_qkv, after):
    tokens = columns[0].shape[-2]
    width, total = w_qkv.shape
    count = len(columns)
    pieces = list(pieces_of(columns))
    steps = len(pieces) // 2

    def kernel(*refs):
        w_ref, (out_ref, done_ref, acc_ref, chunk_ref) = refs[count], refs[-4:]
        now = pl.program_id(0)
        for step in range(steps):

            @pl.when(now == step)
            def _():
                for half, where in enumerate(pieces[2 * step : 2 * step + 2]):
                    chunk_ref[:, half * 2 * LANES : (half + 1) * 2 * LANES] = piece(refs, *where)

        @pl.when(now == 0)
        def _():
            acc_ref[...] = jnp.zeros_like(acc_ref)

        acc_ref[...] += dot(chunk_ref[...], w_ref[...], NT)

        @pl.when(now == steps - 1)
        def _():
            out_ref[...] = acc_ref[...].astype(BF)
            done_ref[...] = jnp.zeros_like(done_ref)

    return pl.pallas_call(
        kernel,
        grid=(steps,),
        in_specs=[pl.BlockSpec(memory_space=pltpu.VMEM)] * count
        + [pl.BlockSpec((width, total // steps), lambda g: (0, g))]
        + [pl.BlockSpec(memory_space=pl.ANY)] * len(after),
        out_specs=[
            pl.BlockSpec((tokens, width), lambda g: (0, 0)),
            pl.BlockSpec((8, LANES), lambda g: (0, 0)),
        ],
        out_shape=[
            jax.ShapeDtypeStruct((tokens, width), BF),
            jax.ShapeDtypeStruct((8, LANES), F32),
        ],
        scratch_shapes=[pltpu.VMEM((tokens, width), F32), pltpu.VMEM((tokens, 4 * LANES), BF)],
        compiler_params=pltpu.CompilerParams(vmem_limit_bytes=24 * MIB),
        cost_estimate=pl.CostEstimate(flops=4 * 10**9, bytes_accessed=MIB, transcendentals=0),
    )(*columns, w_qkv, *after)


def row_blocks(place, own, orders, after):
    tokens, width = own.shape
    devices = len(orders[0])
    size = width // devices
    step = max(1, 16 // size)

    def kernel(place_ref, own_ref, low_ref, high_ref, wide_ref):
        for at in range(0, width, 2 * LANES):
            wide_ref[at : at + 2 * LANES, :] = own_ref[:, at : at + 2 * LANES].astype(F32).T
        even = place_ref[1] == 0
        me = place_ref[2]
        for j in range(0, devices, step):
            rows = []
            for k in range(j, j + step):
                owner = me ^ jnp.where(even, int(orders[0][k]), int(orders[1][k]))
                rows.append(wide_ref[pl.ds(pl.multiple_of(owner * size, size), size), :])
            half, base = divmod(j * size, width // 2)
            block = rows[0] if step == 1 else jnp.concatenate(rows, axis=0)
            (low_ref, high_ref)[half][base : base + step * size, :] = block.astype(BF)

    out = ((width // 2, tokens), BF)
    scratch = [pltpu.VMEM((width, tokens), F32)]
    return on_chip(kernel, [out, out], [own], after=after, scratch=scratch, place=[place])


def pack_sides(own, band_rows, band_cols):
    tokens, width = own.shape

    def kernel(own_ref, last_ref, first_ref, wide_ref):
        for lane, at in lanes_of(width):
            wide_ref[lane] = own_ref[:, at].astype(F32)
            for col in range(MARGIN):
                here = slice(col * band_rows, (col + 1) * band_rows)
                last = pl.ds(band_cols - MARGIN + col, band_rows, stride=band_cols)
                last_ref[here, at] = wide_ref[lane, last, :].astype(BF)
                first = pl.ds(col, band_rows, stride=band_cols)
                first_ref[here, at] = wide_ref[lane, first, :].astype(BF)

    out = ((MARGIN * band_rows, width), BF)
    scratch = [pltpu.VMEM((width // LANES, tokens, LANES), F32)]
    return on_chip(kernel, [out, out], [own], scratch=scratch)


def pack_rows(place, own, band_cols, after):
    tokens, width = own.shape
    edge = MARGIN * band_cols

    def kernel(place_ref, own_ref, out_a, out_b):
        even = place_ref[1] == 0
        last, first = own_ref[tokens - edge :, :], own_ref[:edge, :]
        out_a[...] = jnp.where(even, last, first)
        out_b[...] = jnp.where(even, first, last)

    out = ((edge, width), BF)
    return on_chip(kernel, [out, out], [own], after=after, place=[place])


def pack_corners(place, left, right, band_rows, after):
    width = left.shape[1]

    def kernel(place_ref, left_ref, right_ref, out_a, out_b):
        even = place_ref[1] == 0
        for side, side_ref in enumerate((left_ref, right_ref)):
            for col in range(0, MARGIN, 2):
                base = (side * MARGIN + col) * EDGE_R
                last, first = (
                    jnp.concatenate(
                        [
                            side_ref[at : at + EDGE_R, :].astype(F32)
                            for at in (start, start + band_rows)
                        ]
                    )
                    for start in ((col + 1) * band_rows - EDGE_R, col * band_rows)
                )
                here = slice(base, base + 2 * EDGE_R)
                out_a[here, :] = jnp.where(even, last, first).astype(BF)
                out_b[here, :] = jnp.where(even, first, last).astype(BF)

    out = ((2 * MARGIN * EDGE_R, width), BF)
    return on_chip(kernel, [out, out], [left, right], after=after, place=[place])


def selectors(band_rows, band_cols, after):
    side = MARGIN * band_rows

    def kernel(take_ref, put_ref):
        sent = lax.broadcasted_iota(jnp.int32, take_ref.shape, 0)
        held = lax.broadcasted_iota(jnp.int32, take_ref.shape, 1)
        same_row = (sent & (band_rows - 1)) == (held >> (HALO_COLS.bit_length() - 1))
        same_col = (sent >> (band_rows.bit_length() - 1)) == (held & (HALO_COLS - 1))
        take_ref[...] = jnp.where(same_row & same_col, 1.0, 0.0).astype(BF)
        held = lax.broadcasted_iota(jnp.int32, put_ref.shape, 0)
        sent = lax.broadcasted_iota(jnp.int32, put_ref.shape, 1)
        same_row = (sent & (band_rows - 1)) == (held >> (band_cols.bit_length() - 1))
        col = sent >> (band_rows.bit_length() - 1)
        col = jnp.where(col < MARGIN, col, col + band_cols - 2 * MARGIN)
        same_col = col == (held & (band_cols - 1))
        put_ref[...] = jnp.where(same_row & same_col, 1.0, 0.0).astype(BF)

    out = [((2 * side, band_rows * HALO_COLS), BF), ((band_rows * band_cols, 2 * side), BF)]
    return on_chip(kernel, out, [], after)


def merge_sides(place, lefts, rights, rim_a, rim_b, band_rows, band_cols, after=()):
    edge = MARGIN * band_cols
    calls = len(lefts)
    slots = rim_a.shape[0]
    each = slots // calls

    def kernel(place_ref, *refs):
        sides = refs[:calls], refs[calls : 2 * calls]
        a_ref, b_ref, *outs = refs[2 * calls :]
        even = place_ref[1] == 0
        for slot in range(slots):
            for part in range(2):
                for col in range(2 * MARGIN):
                    source = sides[col // MARGIN][slot // each]
                    base = (col % MARGIN) * band_rows
                    pair = slice(edge + (col // 2) * 2 * EDGE_R, edge + (col // 2 + 1) * 2 * EDGE_R)
                    odd = slice((col % 2) * EDGE_R, (col % 2 + 1) * EDGE_R)
                    rows = source[slot % each, part, base : base + band_rows, :].astype(F32)
                    from_a, from_b = (
                        ref[slot, part, pair, :].astype(F32)[odd] for ref in (a_ref, b_ref)
                    )
                    first = rows[:EDGE_R] + jnp.where(even, from_b, from_a)
                    last = rows[band_rows - EDGE_R :] + jnp.where(even, from_a, from_b)
                    outs[col // MARGIN][slot, part, base : base + band_rows, :] = jnp.concatenate(
                        [first, rows[EDGE_R : band_rows - EDGE_R], last], axis=0
                    ).astype(BF)

    out = ((slots,) + lefts[0].shape[1:], BF)
    return on_chip(kernel, [out, out], [*lefts, *rights, rim_a, rim_b], after, place=[place])


def finish(place, mids, rim_a, rim_b, left, right, put, parts, band_rows, band_cols, after, flops):
    calls = len(mids)
    slots, _, _, block = rim_a.shape
    each = slots // calls
    edge = MARGIN * band_cols
    tokens = band_rows * band_cols

    def kernel(place_ref, *refs):
        a_ref, b_ref, left_ref, right_ref, put_ref, *outs, acc_ref = refs[calls:]
        even = place_ref[1] == 0
        for out_ref, part in zip(outs, parts):
            for slot in range(slots):
                sides = jnp.concatenate([left_ref[slot, part], right_ref[slot, part]], axis=0)
                acc_ref[...] = dot(put_ref[...], sides) + refs[slot // each][
                    slot % each, part
                ].astype(F32)
                from_a, from_b = (r[slot, part, :edge, :].astype(F32) for r in (a_ref, b_ref))
                acc_ref[:edge, :] += jnp.where(even, from_b, from_a)
                acc_ref[tokens - edge :, :] += jnp.where(even, from_a, from_b)
                out_ref[:, slot * block : (slot + 1) * block] = acc_ref[...].astype(BF)

    out = [((tokens, slots * block), BF)] * len(parts)
    scratch = [pltpu.VMEM((tokens, block), F32)]
    operands = [*mids, rim_a, rim_b, left, right, put]
    return on_chip(kernel, out, operands, after, scratch, flops, [place])


def pieces_of(arrays):
    for i, array in enumerate(arrays):
        slots = range(array.shape[0]) if array.ndim == 3 else [None]
        for slot in slots:
            for start in range(0, array.shape[-1], 2 * LANES):
                yield i, slot, start


def piece(refs, i, slot, start):
    here = slice(start, start + 2 * LANES)
    return refs[i][:, here] if slot is None else refs[i][slot, :, here]


def grad_rows(rows, columns, scale, kind, after=()):
    features, count = rows.shape[0], len(columns)
    pieces = list(pieces_of(columns))

    def kernel(rows_ref, *refs):
        for at, where in enumerate(pieces):
            part = dot(rows_ref[...], piece(refs, *where))
            here = slice(at * 2 * LANES, (at + 1) * 2 * LANES)
            refs[count][:, here] = (part * scale).astype(kind)

    out = [((features, len(pieces) * 2 * LANES), kind)]
    return on_chip(kernel, out, [rows, *columns], after)[0]


def add_split(keep, received, after=()):
    half, columns = keep.shape[0] // 2, keep.shape[1]

    def kernel(keep_ref, received_ref, sums_ref, send_ref):
        sums_ref[...] = keep_ref[:half, :] + received_ref[:half, :].astype(F32)
        send_ref[...] = (keep_ref[half:, :] + received_ref[half:, :].astype(F32)).astype(BF)

    return on_chip(kernel, [((half, columns), F32), ((half, columns), BF)], [keep, received], after)


def gather_sums(groups, places, width):
    flat = [array for group in groups for array in group]

    def kernel(*refs):
        out_ref = refs[-1]
        for i, moves in enumerate(places):
            keep_ref, received_ref = refs[2 * i : 2 * i + 2]
            for source, size, target in moves:
                here = slice(source, source + size)
                total = keep_ref[:, here] + received_ref[:, here].astype(F32)
                out_ref[:, target : target + size] = total

    return on_chip(kernel, [((flat[0].shape[0], width), F32)], flat)[0]


def shifted(array, axis, by, wrap):
    size = lax.axis_size(axis)
    route = [(i, (i + by) % size) for i in range(size) if wrap or 0 <= i + by < size]
    return lax.ppermute(array, axis, route)


def swapped(array_a, array_b, axis):
    size = lax.axis_size(axis)
    pairs = [(i, i + 1) for i in range(size - 1)]
    route = lambda chosen: chosen + [(j, i) for i, j in chosen]
    return [
        lax.ppermute(array, axis, route(pairs[offset::2]))
        for array, offset in ((array_a, 0), (array_b, 1))
    ]


def exchanged(array, axis, flip):
    return lax.ppermute(array, axis, [(i, i ^ flip) for i in range(lax.axis_size(axis))])


def bits_of(axis):
    return [(axis, 1 << b) for b in range((lax.axis_size(axis) - 1).bit_length())]


def reduce_stages():
    first, *lat_bits = bits_of("lat")
    bits = bits_of("dp") + lat_bits
    return first, list(zip(bits, reversed(bits))) + [(bit, bit) for bit in bits_of("lon")]


def feature_orders(first, stages):
    n_lon, n_lat = lax.axis_size("lon"), lax.axis_size("lat")
    unit = {"lon": 1, "lat": n_lon, "dp": n_lon * n_lat}
    lower = []
    for kind in range(2):
        order = np.zeros(1, np.int64)
        for stage in reversed(stages):
            axis, bit = stage[kind]
            order = np.concatenate([order, order + unit[axis] * bit])
        lower.append(order)
    flip = unit[first[0]] * first[1]
    return [np.concatenate([lower[kind], lower[1 - kind] ^ flip]) for kind in range(2)]


def exchanged_stage(array, stage):
    if stage[0] == stage[1]:
        return exchanged(array, *stage[0])
    n_lat, n_dp = lax.axis_size("lat"), lax.axis_size("dp")
    route = []
    for i in range(n_dp * n_lat):
        axis, bit = stage[i % n_lat % 2]
        route.append((i, i ^ (bit * n_lat if axis == "dp" else bit)))
    return lax.ppermute(array, ("dp", "lat"), route)


def body(inputs, grad_out, w_qkv):
    _, band_rows, band_cols, width = inputs.shape
    n_lat, n_lon, n_dp = lax.axis_size("lat"), lax.axis_size("lon"), lax.axis_size("dp")
    band_start = lax.axis_index("lat") * band_rows
    total_rows = band_rows * n_lat
    tokens = band_rows * band_cols
    slots = HEADS // GROUP // 2
    shape = (band_rows, band_cols, total_rows)
    own = inputs.reshape(tokens, width)
    flat_grad = grad_out.reshape(tokens, width)

    last_cols, first_cols = pack_sides(own, band_rows, band_cols)
    left = shifted(last_cols, "lon", 1, True)
    right = shifted(first_cols, "lon", -1, True)
    me = (lax.axis_index("dp") * n_lat + lax.axis_index("lat")) * n_lon + lax.axis_index("lon")
    start = jnp.stack([band_start, lax.axis_index("lat") % 2, me])
    rim_rows = swapped(*pack_rows(start, own, band_cols, [last_cols]), "lat")

    take, put = selectors(band_rows, band_cols, [last_cols])
    masks = window_masks(start, band_rows, band_cols, total_rows)
    qkv = project(own, w_qkv, [last_cols])
    first, stages = reduce_stages()
    half = width // 2
    rows_keep, rows_send = row_blocks(start, own, feature_orders(first, stages), [last_cols])
    corners = pack_corners(start, left, right, band_rows, [masks, qkv])
    halo = (left, right, *rim_rows, *swapped(*corners, "lat"))
    scale = float(tokens * n_dp * n_lat * n_lon) ** -0.5

    attend = lambda first, count, before, after: attention_grads(
        first, count, start, masks, take, halo, qkv, flat_grad, w_qkv, shape, before, after
    )

    def return_sides(calls, rims, after):
        to_left, to_right = merge_sides(
            start, [c[4] for c in calls], [c[5] for c in calls], *rims, band_rows, band_cols, after
        )
        from_right = shifted(to_left, "lon", -1, True)
        from_left = shifted(to_right, "lon", 1, True)
        return to_left, from_left, from_right

    def finished(calls, rims, sides, parts, after, flops):
        mids = [c[3] for c in calls]
        return finish(start, mids, *rims, *sides, put, parts, band_rows, band_cols, after, flops)

    groups = HEADS // GROUP
    one = attend(0, slots, [], [rows_keep])
    rims_1 = swapped(one[1], one[2], "lat")
    two = attend(slots, groups - slots - 1, [], [one[0]])
    sent, *sides_1 = return_sides([one], rims_1, [two[0]])
    three = attend(groups - 1, 1, [two[1], two[2]], [sent])
    rims_2 = swapped(three[1], three[2], "lat")
    dq = [one[0], two[0], three[0]]

    dk_1, dv_1 = finished([one], rims_1, sides_1, (0, 1), [three[0]], 2 * 10**9)
    sent, *sides_2 = return_sides([two, three], rims_2, [dk_1])
    send = grad_rows(rows_send, [*dq, dk_1, dv_1], scale, BF, after=[sent])
    received = exchanged(send, *first)
    keep = grad_rows(rows_keep, [*dq, dk_1, dv_1], scale, F32, after=[send])
    keep, send = add_split(keep, received)

    (dk_2,) = finished([two, three], rims_2, sides_2, (0,), [keep], FINISH_FLOPS)
    received = exchanged_stage(send, stages[0])
    keep, send = add_split(keep, received, [dk_2])
    received = exchanged_stage(send, stages[1])
    (dv_2,) = finished([two, three], rims_2, sides_2, (1,), [keep], 10**5)
    send_2 = grad_rows(rows_send, [dk_2, dv_2], scale, BF)
    received_2 = exchanged(send_2, *first)
    keep_2 = grad_rows(rows_keep, [dk_2, dv_2], scale, F32, after=[send_2])
    keep_2, send_2 = add_split(keep_2, received_2)
    received_2 = exchanged_stage(send_2, stages[0])
    grad_inputs, done = input_grads([*dq, dk_1, dk_2, dv_1, dv_2], w_qkv, [send_2])
    keep, send = add_split(keep, received, [done])
    for i in range(2, len(stages)):
        received = exchanged_stage(send, stages[i])
        keep_2, send_2 = add_split(keep_2, received_2, [keep])
        received_2 = exchanged_stage(send_2, stages[i - 1])
        if i + 1 < len(stages):
            keep, send = add_split(keep, received, [keep_2])
    keep_2, send_2 = add_split(keep_2, received_2)
    received_2 = exchanged_stage(send_2, stages[-1])
    groups = [(keep, received), (keep_2, received_2)]
    places = [
        [(0, width, 0), (width, half, width), (width + half, half, 2 * width)],
        [(0, half, width + half), (half, half, 2 * width + half)],
    ]
    grad_w = gather_sums(groups, places, 3 * width)
    return (grad_inputs.reshape(inputs.shape), grad_w)


def solution(mesh):
    in_specs = (P("dp", "lat", "lon", None), P("dp", "lat", "lon", None), P())
    out_specs = (P("dp", "lat", "lon", None), P(("dp", "lat", "lon"), None))
    return jax.shard_map(body, mesh=mesh, in_specs=in_specs, out_specs=out_specs, check_vma=False)
```
